32 devices in a mesh: inline: 8 (over y, x, core), crosslin: 4 (over z).
Axes of the slice: x: 2, y: 2, z: 4, core: 2. Of those that a mesh axis runs over, the one named last changes fastest.
Arguments:
- traces: float32 [4096, 4, 1024], P(('inline', 'crosslin')), may hold values from -6 to 6
- destination: int32 [4096, 1], P(('inline', 'crosslin')), may hold values from 0 to 31; in each aligned block of 128 rows (0 to 127, 128 to 255, ...) at most 8 rows name the same one
- bin_index: int32 [4096, 4], P(('inline', 'crosslin')), may hold values from 0 to 1023
- dip_inline: int32 [256, 128], P('inline', 'crosslin'), may hold values from -2 to 2
- dip_cross: int32 [256, 128], P('inline', 'crosslin'), may hold values from -2 to 2
Outputs:
- smoothed: float32 [256, 128, 1024], P('inline', 'crosslin')
The draws below stay inside these ranges and needn't reach their ends.
Inputs may be any that keep to these rules, and one draw needn't show every extreme that they name: `destination`: at most 8 of one device's blocks name the same tile, and that many are reached.
All inputs are finite; a program needn't handle non-finite values.
Results may differ from the reference program's by a relative error of at most 0.00009.
Values sent between devices are 32-bit elements; how exact they have to be, the bound alone decides.
No kernel may reach another device: no remote copies, remote signals or barrier semaphores. Data moves between devices by JAX's collectives and lax.ppermute only.
A program may use at most 64 MiB of HBM per device.

```python
import math
import jax
import jax.numpy as jnp
import numpy as np
from jax import lax

NS = 1024
BT = 4
SB = 128
BI = 32
BX = 32
HALF = 7
DMAX = 2
CAP = 8
BINS = 1024
BLOCKS = 4096
NBI = 256
NBX = 128
N_CROSSLIN = 4
DEVICES = 32


def place_ends(entries, stream_key, low, top_value):
    shape = entries.shape
    index_at = [jax.random.randint(jax.random.fold_in(stream_key, axis), (), 0, shape[axis]) for axis in range(len(shape))]
    entries = entries.at[tuple(index_at)].set(low)
    longest = shape.index(max(shape))
    index_at[longest] = (index_at[longest] + 1) % shape[longest]
    return entries.at[tuple(index_at)].set(top_value)


def level_of(rng, shape, cuts, low, largest):
    factor_of = 1.0
    for axis_at, parts in cuts:
        steps = jax.random.uniform(jax.random.fold_in(jax.random.fold_in(rng, 6), axis_at), (parts,), jnp.float32, low / len(cuts), largest / len(cuts))
        factor_of = factor_of * jnp.repeat(jnp.exp(steps), shape[axis_at] // parts).reshape((-1,) + (1,) * (len(shape) - 1 - axis_at))
    return factor_of


def shared_out(key, own, number, rows, number_of, top, limit, slope):
    order = jax.random.permutation(key, number_of)
    heavy_load, ordinary = portions_of(number_of, rows * top, limit, slope, True), portions_of(number_of, rows * top, limit, slope, False)
    places = jnp.arange(number_of)

    def named(lengths, turn):
        used = int((lengths > 0).sum())
        fixed = max(1, used // 4)
        moved = fixed + (places - fixed + turn * (used - fixed)) % max(1, number_of - fixed)
        return jnp.zeros((number_of,), jnp.int32).at[order[jnp.where(places < fixed, places, moved)]].set(jnp.asarray(lengths, jnp.int32))

    lengths = jnp.where(number % 4 == 0, named(heavy_load, number // 4), named(ordinary, number - number // 4 - 1))
    mixed = jax.random.permutation(jax.random.fold_in(own, 3), number_of)
    giver, sink = mixed[0:number_of // 2 * 2:2], mixed[1:number_of // 2 * 2:2]
    room = jnp.minimum(lengths[giver] - 1, limit - lengths[sink]) // 2
    room = jnp.where((giver == order[0]) | (sink == order[0]) | (lengths[sink] == 0), 0, jnp.maximum(room, 0))
    moved = jax.random.randint(jax.random.fold_in(own, 4), (number_of // 2,), 0, 1 << 20) % (room + 1)
    lengths = lengths.at[giver].add(-moved).at[sink].add(moved)
    members = jnp.searchsorted(jnp.cumsum(lengths), jnp.arange(rows * top), side="right").astype(jnp.int32)
    table = members.reshape(top, rows).T
    table = table[jax.random.permutation(jax.random.fold_in(own, 1), rows)]
    turn = jax.random.randint(jax.random.fold_in(own, 2), (rows, 1), 0, top)
    return jnp.take_along_axis(table, (jnp.arange(top)[None, :] + turn) % top, axis=1)


def portions_of(amount, total, bound, slope, full):
    portions = [(1 << 20) // math.isqrt(grade ** slope) + 1 for grade in range(1, amount + 1)]
    largest = bound if full else min(bound, max(-(-total // amount), total * portions[0] // sum(portions)))
    least = 1 if total - largest >= amount - 1 else 0
    counts, surplus = [largest] + [least] * (amount - 1), total - largest - least * (amount - 1)
    while surplus > 0:
        candidates = [i for i in range(1, amount) if counts[i] < largest] or [i for i in range(1, amount) if counts[i] < bound]
        mass, budget = sum([portions[i] for i in candidates]), surplus
        for i in candidates:
            more = min(bound - counts[i], max(1, budget * portions[i] // mass), surplus)
            counts[i] = counts[i] + more
            surplus = surplus - more
    return np.array(counts)


def centred(key, shape, scale, limit, cuts=(), held_as=jnp.bfloat16):
    array = jax.random.normal(key, shape, jnp.float32) * scale
    if len(cuts) > 0:
        array = level_of(key, shape, cuts, -0.22, 0.18) * array
    return jnp.clip(array, min=-limit, max=limit).astype(held_as)


def setup_inputs(seed: int = 0) -> dict:
    key_list = jax.random.split(jax.random.key(seed), 6)
    traces = centred(key_list[0], (BLOCKS, BT, NS), 1.0, 6.0, ((0, 32),), jnp.float32)
    destination_keys = jax.random.split(jax.random.fold_in(key_list[1], 1), BLOCKS // SB)
    destination_turns = jax.random.permutation(jax.random.fold_in(key_list[1], 3), BLOCKS // SB)
    destination = jax.vmap(lambda own, number: shared_out(jax.random.fold_in(key_list[1], 2), own, number, SB, DEVICES, 1, CAP, 1))(destination_keys, destination_turns).reshape((BLOCKS, 1))
    bin_index = place_ends(jax.random.randint(key_list[2], (BLOCKS, BT), 0, BINS), jax.random.fold_in(key_list[2], 1), 0, BINS - 1).astype(jnp.int32)
    dip_inline = place_ends(jax.random.randint(key_list[3], (NBI, NBX), -DMAX, DMAX + 1), jax.random.fold_in(key_list[3], 1), -DMAX, DMAX).astype(jnp.int32)
    dip_cross = place_ends(jax.random.randint(key_list[4], (NBI, NBX), -DMAX, DMAX + 1), jax.random.fold_in(key_list[4], 1), -DMAX, DMAX).astype(jnp.int32)
    return dict(traces=traces, destination=destination, bin_index=bin_index, dip_inline=dip_inline, dip_cross=dip_cross)


def steer(padded, dip_index, along_dim):
    margin = HALF * DMAX
    samples = padded.shape[-1] - 2 * margin
    extent = padded.shape[along_dim] - 2 * HALF
    result = jnp.zeros(dip_index.shape + (samples,), jnp.float32)
    for dip_value in range(-DMAX, DMAX + 1):
        running = jnp.zeros(dip_index.shape + (samples,), jnp.float32)
        for offset in range(-HALF, HALF + 1):
            weight = (HALF + 1 - abs(offset)) / float((HALF + 1) ** 2)
            shifted = lax.slice_in_dim(padded, HALF + offset, HALF + offset + extent, axis=along_dim)
            begin = margin + dip_value * offset
            shifted = shifted[..., begin:begin + samples]
            running = running + weight * shifted
        result = jnp.where((dip_index == dip_value)[..., None], running, result)
    return result


def pad_grid(gridded, along_dim):
    margin = HALF * DMAX
    widths = [(0, 0), (0, 0), (margin, margin)]
    widths[along_dim] = (HALF, HALF)
    return jnp.pad(gridded, widths)


def reference(traces, destination, bin_index, dip_inline, dip_cross):
    target = destination[:, 0]
    row_index = (target // N_CROSSLIN)[:, None] * BI + bin_index // BX
    col_index = (target % N_CROSSLIN)[:, None] * BX + bin_index % BX
    segment = (row_index * NBX + col_index).reshape(-1).astype(jnp.int32)
    samples = traces.shape[-1]
    summed = jax.ops.segment_sum(traces.reshape(-1, samples), segment, num_segments=NBI * NBX)
    fold_count = jax.ops.segment_sum(jnp.ones(segment.shape, jnp.float32), segment, num_segments=NBI * NBX)
    stacked = (summed / jnp.maximum(fold_count, 1.0)[:, None]).reshape(NBI, NBX, samples)
    first_pass = steer(pad_grid(stacked, 0), dip_inline, 0)
    second_pass = steer(pad_grid(first_pass, 1), dip_cross, 1)
    return steer(pad_grid(second_pass, 0), dip_inline, 0)
```

```python
import functools

import jax
import jax.numpy as jnp
from jax import lax
from jax.experimental import pallas as pl
from jax.experimental.pallas import tpu as pltpu
from jax.sharding import PartitionSpec as P

HALF = 7
LANES = 128
SUB = 8


def weight(offset):
    return (HALF + 1 - abs(offset)) / float((HALF + 1) ** 2)


def take_lanes(cells, index):
    return jnp.take_along_axis(cells, index, axis=1, mode="promise_in_bounds")


def steer_kernel(dip_ref, low_ref, own_ref, high_ref, out_ref, rows_ref, *, swap):
    tiles, extent = own_ref.shape[:2]
    rows_ref[:, 0:HALF] = low_ref[...]
    rows_ref[:, HALF : HALF + extent] = own_ref[...]
    rows_ref[:, HALF + extent :] = high_ref[...]
    lane = lax.broadcasted_iota(jnp.int32, (SUB, LANES), 1)
    nothing = jnp.zeros((SUB, LANES), jnp.float32)

    def one_row(row, _):
        dip = dip_ref[row]
        upward = dip > 0
        totals = [weight(0) * rows_ref[t, row + HALF] for t in range(tiles)]
        for offset in range(1, HALF + 1):
            moved = dip * offset
            pair = []
            for side, shift in ((1, moved), (-1, -moved)):
                index = (lane + shift) & (LANES - 1)
                outside = (lane < shift) | (lane >= LANES + shift)
                row_tiles = [rows_ref[t, row + HALF + side * offset] for t in range(tiles)]
                shifted = []
                for t in range(tiles):
                    before = row_tiles[t - 1] if t > 0 else nothing
                    after = row_tiles[t + 1] if t + 1 < tiles else nothing
                    if side > 0:
                        beside = jnp.where(upward, after, before)
                    else:
                        beside = jnp.where(upward, before, after)
                    merged = jnp.where(outside, beside, row_tiles[t])
                    shifted.append(take_lanes(merged, index))
                pair.append(shifted)
            for t in range(tiles):
                totals[t] = totals[t] + weight(offset) * (pair[0][t] + pair[1][t])
        for t in range(tiles):
            if swap:
                out_ref[t, pl.ds(row, SUB, stride=extent), :] = totals[t]
            else:
                out_ref[row, :, pl.ds(t * LANES, LANES)] = totals[t]
        return 0

    lax.fori_loop(0, extent, one_row, 0)


def steer(low, own, high, dip, swap):
    tiles, extent, across, _ = own.shape
    dip_lanes = jnp.broadcast_to(dip[:, :, None], (extent, across, LANES))
    if swap:
        out_shape = jax.ShapeDtypeStruct((tiles, across * extent, LANES), jnp.float32)
        out_spec = pl.BlockSpec((tiles, SUB * extent, LANES), lambda i: (0, i, 0))
    else:
        out_shape = jax.ShapeDtypeStruct((extent, across, tiles * LANES), jnp.float32)
        out_spec = pl.BlockSpec((extent, SUB, tiles * LANES), lambda i: (0, i, 0))
    result = pl.pallas_call(
        functools.partial(steer_kernel, swap=swap),
        grid=(across // SUB,),
        in_specs=[
            pl.BlockSpec((extent, SUB, LANES), lambda i: (0, i, 0)),
            pl.BlockSpec((tiles, HALF, SUB, LANES), lambda i: (0, 0, i, 0)),
            pl.BlockSpec((tiles, extent, SUB, LANES), lambda i: (0, 0, i, 0)),
            pl.BlockSpec((tiles, HALF, SUB, LANES), lambda i: (0, 0, i, 0)),
        ],
        out_specs=out_spec,
        out_shape=out_shape,
        scratch_shapes=[pltpu.VMEM((tiles, extent + 2 * HALF, SUB, LANES), jnp.float32)],
        compiler_params=pltpu.CompilerParams(vmem_limit_bytes=32 * 2**20),
        cost_estimate=pl.CostEstimate(
            flops=60 * extent * across * tiles * LANES,
            bytes_accessed=8 * extent * across * tiles * LANES,
            transcendentals=0,
        ),
    )(dip_lanes, low, own, high)
    if swap:
        result = result.reshape(tiles, across, extent, LANES)
    return result


def ends(cells, axis):
    count = lax.axis_size(axis)
    tail = cells[:, cells.shape[1] - HALF :]
    head = cells[:, :HALF]
    low = lax.ppermute(tail, axis, [(i, i + 1) for i in range(count - 1)])
    high = lax.ppermute(head, axis, [(i + 1, i) for i in range(count - 1)])
    return low, high


def on_device(traces, destination, bin_index, dip_inline, dip_cross):
    held_blocks, block_rows, samples = traces.shape
    rows_inline = lax.axis_size("inline")
    cols_cross = lax.axis_size("crosslin")
    devices = rows_inline * cols_cross
    capacity = 2 * held_blocks // devices
    tile_rows, tile_cols = dip_inline.shape
    bin_total = tile_rows * tile_cols
    target = destination[:, 0]
    positions = jnp.arange(held_blocks, dtype=jnp.int32)
    earlier = (target[:, None] == target[None, :]) & (positions[None, :] < positions[:, None])
    ranking = jnp.sum(earlier.astype(jnp.int32), axis=1)
    slot_index = target * capacity + ranking
    slot_range = jnp.arange(devices * capacity, dtype=jnp.int32)
    matches = slot_range[:, None] == slot_index[None, :]
    source = jnp.sum(jnp.where(matches, positions[None, :], 0), axis=1)
    filled = jnp.any(matches, axis=1)
    outgoing = jnp.where(filled[:, None, None], traces[source], 0.0)
    outgoing_bins = jnp.where(filled[:, None], bin_index[source], bin_total)
    outgoing = outgoing.reshape(devices, capacity, block_rows, samples)
    outgoing_bins = outgoing_bins.reshape(devices, capacity, block_rows)
    arrived, arrived_bins = (
        lax.all_to_all(outgoing, ("inline", "crosslin"), split_axis=0, concat_axis=0, tiled=True),
        lax.all_to_all(
            outgoing_bins, ("inline", "crosslin"), split_axis=0, concat_axis=0, tiled=True
        ),
    )
    arrived_rows = arrived.reshape(-1, samples)
    arrived_bins = arrived_bins.reshape(-1)
    member = (jnp.arange(bin_total, dtype=jnp.int32)[:, None] == arrived_bins[None, :]).astype(
        jnp.float32
    )
    summed = jnp.dot(
        member, arrived_rows, precision=lax.Precision.HIGHEST, preferred_element_type=jnp.float32
    )
    fold_count = jnp.sum(member, axis=1)
    stacked = (summed / jnp.maximum(fold_count, 1.0)[:, None]).reshape(
        tile_rows, tile_cols, samples
    )
    stacked = jnp.moveaxis(stacked.reshape(tile_rows, tile_cols, -1, LANES), 2, 0)
    low, high = ends(stacked, "inline")
    first_pass = steer(low, stacked, high, dip_inline, True)
    low, high = ends(first_pass, "crosslin")
    second_pass = steer(low, first_pass, high, dip_cross.T, True)
    low, high = ends(second_pass, "inline")
    return steer(low, second_pass, high, dip_inline, False)


def solution(mesh):
    return jax.shard_map(
        on_device,
        mesh=mesh,
        in_specs=(
            P(("inline", "crosslin"), None, None),
            P(("inline", "crosslin"), None),
            P(("inline", "crosslin"), None),
            P("inline", "crosslin"),
            P("inline", "crosslin"),
        ),
        out_specs=P("inline", "crosslin", None),
        check_vma=False,
    )
```

```python
import functools

import jax
import jax.numpy as jnp
from jax import lax
from jax.experimental import pallas as pl
from jax.experimental.pallas import tpu as pltpu
from jax.sharding import PartitionSpec as P

HALF = 7
DMAX = 2
LANES = 128
PHASES = 8
LINES = 8
REACH = -(-HALF * DMAX // PHASES)
SPAN = (2 * REACH + 1) * PHASES
BOTH = ("inline", "crosslin")


def weight(offset):
    return (HALF + 1 - abs(offset)) / float((HALF + 1) ** 2)


def fill_interleave(table_ref, time_dim):
    size = table_ref.shape[0]
    time = lax.broadcasted_iota(jnp.int32, (size, size), time_dim)
    place = lax.broadcasted_iota(jnp.int32, (size, size), 1 - time_dim)
    hit = time == (place & (LANES - 1)) * PHASES + place // LANES
    table_ref[...] = jnp.where(hit, 1.0, 0.0).astype(jnp.bfloat16)


def move_samples(rows, table_ref):
    upper = rows.astype(jnp.bfloat16)
    rest = (rows - upper.astype(jnp.float32)).astype(jnp.bfloat16)
    table = table_ref[...]
    moved = jnp.dot(upper, table, preferred_element_type=jnp.float32)
    return moved + jnp.dot(rest, table, preferred_element_type=jnp.float32)


def pack_kernel(target_ref, traces_ref, out_ref, table_ref, tiles_ref, used_ref, sem, *, capacity):
    held, block_rows, samples = traces_ref.shape
    devices = used_ref.shape[0]
    block_span = block_rows * PHASES
    group = 32
    fill_interleave(table_ref, 0)

    def clear(device, _):
        used_ref[device] = 0
        return 0

    lax.fori_loop(0, devices, clear, 0)

    def one_group(g, _):
        rows = traces_ref[pl.ds(g * group, group)].reshape(group * block_rows, samples)
        moved = move_samples(rows, table_ref)
        for eight in range(group * block_rows // 8):
            for phase in range(PHASES):
                tiles_ref[
                    pl.ds(g * group * block_span + eight * 8 * PHASES + phase, 8, stride=PHASES), :
                ] = moved[eight * 8 : eight * 8 + 8, phase * LANES : (phase + 1) * LANES]

        def send_block(i, _):
            block = g * group + i
            device = target_ref[block]
            rank = used_ref[device]
            used_ref[device] = rank + 1
            pltpu.make_async_copy(
                tiles_ref.at[pl.ds(block * block_span, block_span), :],
                out_ref.at[device * capacity + rank],
                sem,
            ).start()
            return 0

        lax.fori_loop(0, group, send_block, 0)
        return 0

    lax.fori_loop(0, held // group, one_group, 0)
    pltpu.make_async_copy(tiles_ref, tiles_ref, sem).wait()


def pack(traces, target, devices, capacity):
    held, block_rows, samples = traces.shape
    return pl.pallas_call(
        functools.partial(pack_kernel, capacity=capacity),
        in_specs=[
            pl.BlockSpec(memory_space=pltpu.SMEM),
            pl.BlockSpec(memory_space=pltpu.VMEM),
        ],
        out_specs=pl.BlockSpec(memory_space=pl.ANY),
        out_shape=jax.ShapeDtypeStruct(
            (devices * capacity, block_rows * PHASES, LANES), jnp.float32
        ),
        scratch_shapes=[
            pltpu.VMEM((samples, samples), jnp.bfloat16),
            pltpu.VMEM((held * block_rows * PHASES, LANES), jnp.float32),
            pltpu.SMEM((devices,), jnp.int32),
            pltpu.SemaphoreType.DMA,
        ],
        compiler_params=pltpu.CompilerParams(vmem_limit_bytes=32 * 2**20),
    )(target, traces)


def bin_kernel(bins_ref, scale_ref, blocks_ref, out_ref, even_ref, odd_ref):
    step = pl.program_id(0)
    slots, block_span, _ = blocks_ref.shape
    block_rows = block_span // PHASES
    bin_total = out_ref.shape[0]
    unroll = 8

    @pl.when(step == 0)
    def _():
        def clear(i, _):
            for j in range(unroll):
                even_ref[i * unroll + j] = jnp.zeros((PHASES, LANES), jnp.float32)
                odd_ref[i * unroll + j] = jnp.zeros((PHASES, LANES), jnp.float32)
            return 0

        lax.fori_loop(0, bin_total // unroll, clear, 0)

    def add_slot(slot, _):
        first = (step * slots + slot) * block_rows
        for j in range(block_rows):
            total_ref = odd_ref if j % 2 else even_ref
            place = bins_ref[first + j]
            total_ref[place] += blocks_ref[slot, j * PHASES : (j + 1) * PHASES]
        return 0

    lax.fori_loop(0, slots, add_slot, 0)

    @pl.when(step == pl.num_programs(0) - 1)
    def _():
        def finish(i, _):
            for j in range(unroll):
                place = i * unroll + j
                out_ref[place] = (even_ref[place] + odd_ref[place]) * scale_ref[place]
            return 0

        lax.fori_loop(0, bin_total // unroll, finish, 0)


def stack_bins(blocks, bins, scale):
    slots, block_span, _ = blocks.shape
    bin_total = scale.shape[0]
    steps = 8
    return pl.pallas_call(
        bin_kernel,
        grid=(steps,),
        in_specs=[
            pl.BlockSpec(memory_space=pltpu.SMEM),
            pl.BlockSpec(memory_space=pltpu.SMEM),
            pl.BlockSpec((slots // steps, block_span, LANES), lambda i: (i, 0, 0)),
        ],
        out_specs=pl.BlockSpec((bin_total, PHASES, LANES), lambda i: (0, 0, 0)),
        out_shape=jax.ShapeDtypeStruct((bin_total, PHASES, LANES), jnp.float32),
        scratch_shapes=[
            pltpu.VMEM((bin_total + 8, PHASES, LANES), jnp.float32),
            pltpu.VMEM((bin_total + 8, PHASES, LANES), jnp.float32),
        ],
        compiler_params=pltpu.CompilerParams(vmem_limit_bytes=40 * 2**20),
    )(bins, scale, blocks)


def steer_line(dip_of, cell_of, put, extent, spread_ref):
    lane = lax.broadcasted_iota(jnp.int32, (PHASES, LANES), 1)
    for place in range(extent + 2 * HALF):
        cell = cell_of(place)
        for reach in range(-REACH, REACH + 1):
            moved = cell
            if reach:
                moved = pltpu.roll(cell, (-reach) % LANES, axis=1)
                inside = lane < LANES - reach if reach > 0 else lane >= -reach
                moved = jnp.where(inside, moved, 0.0)
            spread_ref[pl.ds(place * SPAN + (reach + REACH) * PHASES, PHASES), :] = moved
    for place in range(extent):
        dip = dip_of(place)
        centre = (place + HALF) * SPAN + REACH * PHASES

        def tap(offset):
            return spread_ref[pl.ds(centre + offset * SPAN + dip * offset, PHASES), :]

        total = weight(0) * tap(0)
        for offset in range(1, HALF + 1):
            total = total + weight(offset) * (tap(offset) + tap(-offset))
        put(place, total)


def steer_kernel(dip_ref, low_ref, own_ref, high_ref, out_ref, spread_a, spread_b, *more, along):
    extent = own_ref.shape[along]
    start = pl.program_id(0) * LINES
    final = len(more) > 0
    if final:
        staged_ref, table_ref = more

        @pl.when(pl.program_id(0) == 0)
        def _():
            fill_interleave(table_ref, 1)

    def at(place, line):
        return (place, line) if along == 0 else (line, place)

    def one_line(line, spread_ref):
        def cell_of(place):
            if place < HALF:
                return low_ref[at(place, line)]
            if place < HALF + extent:
                return own_ref[at(place - HALF, line)]
            return high_ref[at(place - HALF - extent, line)]

        def put(place, value):
            if final:
                staged_ref[pl.ds((place * LINES + line) * PHASES, PHASES), :] = value
            else:
                out_ref[at(place, line)] = value

        steer_line(lambda place: dip_ref[at(place, start + line)], cell_of, put, extent, spread_ref)

    def two_lines(i, _):
        one_line(2 * i, spread_a)
        one_line(2 * i + 1, spread_b)
        return 0

    lax.fori_loop(0, LINES // 2, two_lines, 0)
    if final:
        rows = jnp.concatenate(
            [
                jnp.concatenate(
                    [
                        staged_ref[pl.ds(place * LINES * PHASES + phase, LINES, stride=PHASES), :]
                        for phase in range(PHASES)
                    ],
                    axis=1,
                )
                for place in range(extent)
            ],
            axis=0,
        )
        out_ref[...] = move_samples(rows, table_ref).reshape(out_ref.shape)


def steer(low, own, high, dip, along, final=False):
    rows, cols = own.shape[:2]
    extent = own.shape[along]
    samples = PHASES * LANES

    def block(count):
        if along == 0:
            return pl.BlockSpec((count, LINES, PHASES, LANES), lambda i: (0, i, 0, 0))
        return pl.BlockSpec((LINES, count, PHASES, LANES), lambda i: (i, 0, 0, 0))

    spread = pltpu.VMEM(((extent + 2 * HALF) * SPAN, LANES), jnp.float32)
    scratch = [spread, spread]
    out_shape, out_spec = jax.ShapeDtypeStruct(own.shape, jnp.float32), block(extent)
    if final:
        out_shape = jax.ShapeDtypeStruct((rows, cols, samples), jnp.float32)
        out_spec = pl.BlockSpec((rows, LINES, samples), lambda i: (0, i, 0))
        scratch += [
            pltpu.VMEM((extent * LINES * PHASES, LANES), jnp.float32),
            pltpu.VMEM((samples, samples), jnp.bfloat16),
        ]
    return pl.pallas_call(
        functools.partial(steer_kernel, along=along),
        grid=(own.shape[1 - along] // LINES,),
        in_specs=[
            pl.BlockSpec(memory_space=pltpu.SMEM),
            block(HALF),
            block(extent),
            block(HALF),
        ],
        out_specs=out_spec,
        out_shape=out_shape,
        scratch_shapes=scratch,
        compiler_params=pltpu.CompilerParams(vmem_limit_bytes=40 * 2**20),
        cost_estimate=pl.CostEstimate(
            flops=30 * rows * cols * samples,
            bytes_accessed=8 * rows * cols * samples,
            transcendentals=0,
        ),
    )(dip, low, own, high)


def ends(cells, axis, along):
    count = lax.axis_size(axis)
    size = cells.shape[along]
    tail = lax.slice_in_dim(cells, size - HALF, size, axis=along)
    head = lax.slice_in_dim(cells, 0, HALF, axis=along)
    low = lax.ppermute(tail, axis, [(i, i + 1) for i in range(count - 1)])
    high = lax.ppermute(head, axis, [(i + 1, i) for i in range(count - 1)])
    return low, high


def arrived_bins(destination, bin_index, devices, capacity, bin_total):
    held = destination.shape[0]
    mine = lax.axis_index("inline") * lax.axis_size("crosslin") + lax.axis_index("crosslin")
    listed = lax.all_gather(jnp.concatenate([destination, bin_index], axis=1), BOTH, axis=0, tiled=True)
    listed = listed.reshape(devices, held, -1)
    hit = listed[:, :, 0] == mine
    rank = jnp.cumsum(hit.astype(jnp.int32), axis=1) - 1
    slots = jnp.arange(capacity, dtype=jnp.int32)
    chosen = hit[:, None, :] & (rank[:, None, :] == slots[None, :, None])
    bins = jnp.sum(jnp.where(chosen[..., None], listed[:, None, :, 1:], 0), axis=2)
    bins = jnp.where(jnp.any(chosen, axis=2)[..., None], bins, bin_total).reshape(-1)
    fold = jnp.sum(
        (jnp.arange(bin_total, dtype=jnp.int32)[:, None] == bins[None, :]).astype(jnp.float32), axis=1
    )
    return bins, 1.0 / jnp.maximum(fold, 1.0)


def on_device(traces, destination, bin_index, dip_inline, dip_cross):
    held = traces.shape[0]
    devices = lax.axis_size("inline") * lax.axis_size("crosslin")
    capacity = 2 * held // devices
    tile_rows, tile_cols = dip_inline.shape
    bins, scale = arrived_bins(destination, bin_index, devices, capacity, tile_rows * tile_cols)
    outgoing = pack(traces, destination.reshape(-1), devices, capacity)
    arrived = lax.all_to_all(outgoing, BOTH, split_axis=0, concat_axis=0, tiled=True)
    stacked = stack_bins(arrived, bins, scale).reshape(tile_rows, tile_cols, PHASES, LANES)
    low, high = ends(stacked, "inline", 0)
    first_pass = steer(low, stacked, high, dip_inline, 0)
    low, high = ends(first_pass, "crosslin", 1)
    second_pass = steer(low, first_pass, high, dip_cross, 1)
    low, high = ends(second_pass, "inline", 0)
    return steer(low, second_pass, high, dip_inline, 0, final=True)


def solution(mesh):
    return jax.shard_map(
        on_device,
        mesh=mesh,
        in_specs=(
            P(BOTH, None, None),
            P(BOTH, None),
            P(BOTH, None),
            P("inline", "crosslin"),
            P("inline", "crosslin"),
        ),
        out_specs=P("inline", "crosslin", None),
        check_vma=False,
    )
```

```python
import functools

import jax
import jax.numpy as jnp
from jax import lax
from jax.experimental import pallas as pl
from jax.experimental.pallas import tpu as pltpu
from jax.sharding import PartitionSpec as P

HALF = 7
DMAX = 2
LANES = 128
PHASES = 8
LINES = 8
PARTS = 2
REACH = -(-HALF * DMAX // PHASES)
SPAN = (2 * REACH + 1) * PHASES
BOTH = ("inline", "crosslin")
MIB = 2**20


def weight(offset):
    return (HALF + 1 - abs(offset)) / float((HALF + 1) ** 2)


def fill_interleave(table_ref, time_dim):
    size = table_ref.shape[0]
    time = lax.broadcasted_iota(jnp.int32, (size, size), time_dim)
    place = lax.broadcasted_iota(jnp.int32, (size, size), 1 - time_dim)
    hit = time == (place & (LANES - 1)) * PHASES + place // LANES
    table_ref[...] = jnp.where(hit, 1.0, 0.0).astype(jnp.bfloat16)


def move_samples(rows, table_ref):
    count = rows.shape[0]
    upper = rows.astype(jnp.bfloat16)
    rest = (rows - upper.astype(jnp.float32)).astype(jnp.bfloat16)
    both = jnp.concatenate([upper, rest], axis=0)
    moved = jnp.dot(both, table_ref[...], preferred_element_type=jnp.float32)
    return moved[:count] + moved[count:]


def pack_kernel(target_ref, lists_ref, traces_ref, out_ref, table_ref, tiles_ref, used_ref, sem, *more, part, capacity):
    held, block_rows, samples = traces_ref.shape
    share = block_rows // PARTS
    devices = used_ref.shape[0]
    span = share * PHASES
    fill_interleave(table_ref, 0)
    rows = traces_ref[:, part * share : (part + 1) * share, :].reshape(held * share, samples)
    moved = move_samples(rows, table_ref)
    for eight in range(held * share // 8):
        for phase in range(PHASES):
            tiles_ref[pl.ds(eight * 8 * PHASES + phase, 8, stride=PHASES), :] = moved[
                eight * 8 : eight * 8 + 8, phase * LANES : (phase + 1) * LANES
            ]

    def clear(device, _):
        used_ref[device] = 0
        return 0

    lax.fori_loop(0, devices, clear, 0)
    if more:
        listed_ref, listed_sem = more
        room = listed_ref.shape[1]
        listed_ref[...] = jnp.full(listed_ref.shape, -1.0, jnp.float32)

    def send_block(block, _):
        device = target_ref[block]
        rank = used_ref[device]
        used_ref[device] = rank + 1
        pltpu.make_async_copy(
            tiles_ref.at[pl.ds(pl.multiple_of(block * span, 8), span), :],
            out_ref.at[device, pl.ds(pl.multiple_of(rank * span, 8), span), :],
            sem,
        ).start()
        if more:
            listed_ref[device, pl.ds(rank, 1), :] = lists_ref[pl.ds(block, 1), :]
        return 0

    lax.fori_loop(0, held, send_block, 0, unroll=4)
    if more:
        copy = pltpu.make_async_copy(
            listed_ref, out_ref.at[:, capacity * span : capacity * span + room, :], listed_sem
        )
        copy.start()
        copy.wait()
    pltpu.make_async_copy(tiles_ref, tiles_ref, sem).wait()


def pack(traces, target, lists, devices, capacity, part):
    held, block_rows, samples = traces.shape
    span = block_rows // PARTS * PHASES
    room = -(-capacity // 8) * 8
    scratch = [
        pltpu.VMEM((samples, samples), jnp.bfloat16),
        pltpu.VMEM((held * span, LANES), jnp.float32),
        pltpu.SMEM((devices,), jnp.int32),
        pltpu.SemaphoreType.DMA,
    ]
    rows = capacity * span
    if part == 0:
        scratch += [pltpu.VMEM((devices, room, LANES), jnp.float32), pltpu.SemaphoreType.DMA]
        rows += room
    return pl.pallas_call(
        functools.partial(pack_kernel, part=part, capacity=capacity),
        in_specs=[
            pl.BlockSpec(memory_space=pltpu.SMEM),
            pl.BlockSpec(memory_space=pltpu.VMEM),
            pl.BlockSpec(memory_space=pltpu.VMEM),
        ],
        out_specs=pl.BlockSpec(memory_space=pl.ANY),
        out_shape=jax.ShapeDtypeStruct((devices, rows, LANES), jnp.float32),
        scratch_shapes=scratch,
        compiler_params=pltpu.CompilerParams(vmem_limit_bytes=32 * MIB),
        cost_estimate=pl.CostEstimate(
            flops=4 * samples * samples * held, bytes_accessed=4 * MIB, transcendentals=0
        ),
    )(target, lists, traces)


def bin_kernel(bins_ref, scale_ref, blocks_ref, *refs, part, capacity, last):
    if last:
        before_ref, out_ref, even_ref, odd_ref = refs
    else:
        out_ref, even_ref, odd_ref = refs
    step = pl.program_id(0)
    senders = blocks_ref.shape[0]
    bin_total = out_ref.shape[0]
    block_rows = bins_ref.shape[0] // (senders * pl.num_programs(0) * capacity)
    share = block_rows // PARTS
    unroll = 8

    @pl.when(step == 0)
    def _():
        def clear(i, _):
            for j in range(unroll):
                even_ref[i * unroll + j] = jnp.zeros((PHASES, LANES), jnp.float32)
                odd_ref[i * unroll + j] = jnp.zeros((PHASES, LANES), jnp.float32)
            return 0

        lax.fori_loop(0, bin_total // unroll, clear, 0)

    def add_sender(sender, _):
        first = (step * senders + sender) * (capacity * block_rows) + part * share
        for rank in range(capacity):
            for j in range(share):
                total_ref = odd_ref if j % 2 else even_ref
                place = bins_ref[first + rank * block_rows + j]
                row = (rank * share + j) * PHASES
                total_ref[place] += blocks_ref[sender, row : row + PHASES, :]
        return 0

    lax.fori_loop(0, senders, add_sender, 0)

    @pl.when(step == pl.num_programs(0) - 1)
    def _():
        def finish(i, _):
            for j in range(unroll):
                place = i * unroll + j
                total = even_ref[place] + odd_ref[place]
                if last:
                    total = (total + before_ref[place]) * scale_ref[place]
                out_ref[place] = total
            return 0

        lax.fori_loop(0, bin_total // unroll, finish, 0)


def stack_bins(blocks, bins, scale, capacity, part, before):
    devices, rows, _ = blocks.shape
    bin_total = scale.shape[0]
    steps = 8
    last = part == PARTS - 1
    whole = pl.BlockSpec((bin_total, PHASES, LANES), lambda i: (0, 0, 0))
    return pl.pallas_call(
        functools.partial(bin_kernel, part=part, capacity=capacity, last=last),
        grid=(steps,),
        in_specs=[
            pl.BlockSpec(memory_space=pltpu.SMEM),
            pl.BlockSpec(memory_space=pltpu.SMEM),
            pl.BlockSpec((devices // steps, rows, LANES), lambda i: (i, 0, 0)),
        ]
        + [whole] * last,
        out_specs=whole,
        out_shape=jax.ShapeDtypeStruct((bin_total, PHASES, LANES), jnp.float32),
        scratch_shapes=[
            pltpu.VMEM((bin_total + 8, PHASES, LANES), jnp.float32),
            pltpu.VMEM((bin_total + 8, PHASES, LANES), jnp.float32),
        ],
        compiler_params=pltpu.CompilerParams(vmem_limit_bytes=40 * MIB),
        cost_estimate=pl.CostEstimate(
            flops=8 * MIB, bytes_accessed=12 * MIB, transcendentals=0
        ),
    )(bins, scale, blocks, *([before] if last else []))


def steer_line(dip_of, cell_of, put, extent, spread_ref):
    lane = lax.broadcasted_iota(jnp.int32, (PHASES, LANES), 1)
    for place in range(extent + 2 * HALF):
        cell = cell_of(place)
        for reach in range(-REACH, REACH + 1):
            moved = cell
            if reach:
                moved = pltpu.roll(cell, (-reach) % LANES, axis=1)
                inside = lane < LANES - reach if reach > 0 else lane >= -reach
                moved = jnp.where(inside, moved, 0.0)
            spread_ref[pl.ds(place * SPAN + (reach + REACH) * PHASES, PHASES), :] = moved
    for place in range(extent):
        centre = (place + HALF) * SPAN + REACH * PHASES
        pace = dip_of(place) + SPAN
        above = below = centre
        total = weight(0) * spread_ref[pl.ds(centre, PHASES), :]
        for offset in range(1, HALF + 1):
            above = above + pace
            below = below - pace
            both = spread_ref[pl.ds(above, PHASES), :] + spread_ref[pl.ds(below, PHASES), :]
            total = total + weight(offset) * both
        put(place, total)


def steer_kernel(dip_ref, *refs, along, places, block_of, final):
    inputs = 1 + max(index for index, _ in places)
    pieces, refs = refs[:inputs], refs[inputs:]
    if final is not None:
        if final > 0:
            refs = refs[1:]
        out_ref, spread_a, spread_b, staged_ref, table_ref = refs

        @pl.when(pl.program_id(0) == 0)
        def _():
            fill_interleave(table_ref, 1)

    else:
        out_ref, spread_a, spread_b = refs
    extent = len(places) - 2 * HALF
    start = block_of(pl.program_id(0)) * LINES

    def at(place, line):
        return (place, line) if along == 0 else (line, place)

    def one_line(line, spread_ref):
        def cell_of(place):
            index, local = places[place]
            return pieces[index][at(local, line)]

        def put(place, value):
            if final is not None:
                staged_ref[pl.ds((place * LINES + line) * PHASES, PHASES), :] = value
            else:
                out_ref[at(place, line)] = value

        steer_line(lambda place: dip_ref[at(place, start + line)], cell_of, put, extent, spread_ref)

    def two_lines(i, _):
        one_line(2 * i, spread_a)
        one_line(2 * i + 1, spread_b)
        return 0

    lax.fori_loop(0, LINES // 2, two_lines, 0)
    if final is not None:
        rows = jnp.concatenate(
            [
                jnp.concatenate(
                    [
                        staged_ref[pl.ds(place * LINES * PHASES + phase, LINES, stride=PHASES), :]
                        for phase in range(PHASES)
                    ],
                    axis=1,
                )
                for place in range(extent)
            ],
            axis=0,
        )
        out_ref[...] = move_samples(rows, table_ref).reshape(out_ref.shape)


def steer(pieces, order, dip, along, steps, block_of, final=None, before=None):
    extent = dip.shape[along]
    lines = dip.shape[1 - along]
    samples = PHASES * LANES
    places = [(index, first + i) for index, first, count in order for i in range(count)]

    def spec(array, whole):
        chosen = block_of if whole else lambda i: i
        if along == 0:
            return pl.BlockSpec((array.shape[0], LINES, PHASES, LANES), lambda i: (0, chosen(i), 0, 0))
        return pl.BlockSpec((LINES, array.shape[1], PHASES, LANES), lambda i: (chosen(i), 0, 0, 0))

    in_specs = [pl.BlockSpec(memory_space=pltpu.SMEM)] + [spec(*piece) for piece in pieces]
    operands = [dip] + [array for array, _ in pieces]
    spread = pltpu.VMEM((len(places) * SPAN, LANES), jnp.float32)
    scratch = [spread, spread]
    aliases = {}
    if final is not None:
        out_shape = jax.ShapeDtypeStruct((extent, lines, samples), jnp.float32)
        out_spec = pl.BlockSpec((extent, LINES, samples), lambda i: (0, block_of(i), 0))
        scratch += [
            pltpu.VMEM((extent * LINES * PHASES, LANES), jnp.float32),
            pltpu.VMEM((samples, samples), jnp.bfloat16),
        ]
        if final > 0:
            aliases = {len(operands): 0}
            in_specs.append(pl.BlockSpec(memory_space=pl.ANY))
            operands.append(before)
    else:
        shape = (extent, steps * LINES) if along == 0 else (steps * LINES, extent)
        out_shape = jax.ShapeDtypeStruct(shape + (PHASES, LANES), jnp.float32)
        out_spec = spec(out_shape, False)
    return pl.pallas_call(
        functools.partial(steer_kernel, along=along, places=places, block_of=block_of, final=final),
        grid=(steps,),
        in_specs=in_specs,
        out_specs=out_spec,
        out_shape=out_shape,
        scratch_shapes=scratch,
        input_output_aliases=aliases,
        compiler_params=pltpu.CompilerParams(vmem_limit_bytes=40 * MIB),
        cost_estimate=pl.CostEstimate(
            flops=30 * extent * steps * LINES * samples,
            bytes_accessed=16 * extent * steps * LINES * samples,
            transcendentals=0,
        ),
    )(*operands)


def swap_ends(head, tail, axis):
    count = lax.axis_size(axis)
    low = lax.ppermute(tail, axis, [(i, i + 1) for i in range(count - 1)])
    high = lax.ppermute(head, axis, [(i + 1, i) for i in range(count - 1)])
    return low, high


def outer_of(cells, dim):
    size = cells.shape[dim]
    return jnp.concatenate(
        [lax.slice_in_dim(cells, 0, LINES, axis=dim), lax.slice_in_dim(cells, size - LINES, size, axis=dim)],
        axis=dim,
    )


def inner_of(cells, dim):
    return lax.slice_in_dim(cells, LINES, cells.shape[dim] - LINES, axis=dim)


def smooth(stacked, dip_inline, dip_cross):
    rows, cols = dip_inline.shape
    row_blocks, col_blocks = rows // LINES, cols // LINES
    steps_in = lambda blocks: blocks - 2
    inner = lambda i: i + 1
    outer = lambda blocks: lambda i: i * (blocks - 1)

    head, tail = stacked[:HALF], stacked[rows - HALF :]
    order = [(0, 0, HALF), (1, 0, rows), (2, 0, HALF)]
    firsts = []
    for pick, steps, block_of in (
        (outer_of, 2, outer(col_blocks)),
        (inner_of, col_blocks - 2, inner),
    ):
        low, high = swap_ends(pick(head, 1), pick(tail, 1), "inline")
        firsts.append(
            steer([(low, False), (stacked, True), (high, False)], order, dip_inline, 0, steps, block_of)
        )
    border, middle = firsts

    head, tail = border[:, :HALF], border[:, 2 * LINES - HALF :]
    order = [(0, 0, HALF), (1, 0, LINES), (2, 0, cols - 2 * LINES), (1, LINES, LINES), (3, 0, HALF)]
    seconds = []
    for pick, steps, block_of in (
        (outer_of, 2, outer(row_blocks)),
        (inner_of, row_blocks - 2, inner),
    ):
        low, high = swap_ends(pick(head, 0), pick(tail, 0), "crosslin")
        seconds.append(
            steer(
                [(low, False), (border, True), (middle, True), (high, False)],
                order, dip_cross, 1, steps, block_of,
            )
        )
    border, middle = seconds

    head, tail = border[:HALF], border[2 * LINES - HALF :]
    order = [(0, 0, HALF), (1, 0, LINES), (2, 0, rows - 2 * LINES), (1, LINES, LINES), (3, 0, HALF)]
    half = col_blocks // 2
    result = None
    for group in range(2):
        begin, steps = (0, half) if group == 0 else (half, col_blocks - half)
        pick = lambda cells: cells[:, begin * LINES : (begin + steps) * LINES]
        low, high = swap_ends(pick(head), pick(tail), "inline")
        result = steer(
            [(low, False), (border, True), (middle, True), (high, False)],
            order, dip_inline, 0, steps, functools.partial(lambda begin, i: i + begin, begin),
            final=group, before=result,
        )
    return result


def on_device(traces, destination, bin_index, dip_inline, dip_cross):
    held, block_rows, _ = traces.shape
    devices = lax.axis_size("inline") * lax.axis_size("crosslin")
    capacity = 2 * held // devices
    tile_rows, tile_cols = dip_inline.shape
    bin_total = tile_rows * tile_cols
    target = destination.reshape(-1)
    lists = jnp.pad(bin_index.astype(jnp.float32), ((0, 0), (0, LANES - block_rows)))
    arrived = [
        lax.all_to_all(
            pack(traces, target, lists, devices, capacity, part), BOTH, split_axis=0, concat_axis=0, tiled=True
        )
        for part in range(PARTS)
    ]
    room = capacity * block_rows // PARTS * PHASES
    listed = arrived[0][:, room : room + capacity, :block_rows].astype(jnp.int32)
    bins = jnp.where(listed < 0, bin_total, listed).reshape(-1)
    fold = jnp.sum(
        (jnp.arange(bin_total, dtype=jnp.int32)[:, None] == bins[None, :]).astype(jnp.float32), axis=1
    )
    scale = 1.0 / jnp.maximum(fold, 1.0)
    total = None
    for part in range(PARTS):
        total = stack_bins(arrived[part], bins, scale, capacity, part, total)
    return smooth(total.reshape(tile_rows, tile_cols, PHASES, LANES), dip_inline, dip_cross)


def solution(mesh):
    return jax.shard_map(
        on_device,
        mesh=mesh,
        in_specs=(
            P(BOTH, None, None),
            P(BOTH, None),
            P(BOTH, None),
            P("inline", "crosslin"),
            P("inline", "crosslin"),
        ),
        out_specs=P("inline", "crosslin", None),
        check_vma=False,
    )
```

```python
import functools

import jax
import jax.numpy as jnp
from jax import lax
from jax.experimental import pallas as pl
from jax.experimental.pallas import tpu as pltpu
from jax.sharding import PartitionSpec as P

HALF = 7
DMAX = 2
LANES = 128
PHASES = 8
LINES = 8
PARTS = 2
REACH = -(-HALF * DMAX // PHASES)
PAIR = 2 * PHASES
GROUP = 16
BOTH = ("inline", "crosslin")
MIB = 2**20


def weight(offset):
    return (HALF + 1 - abs(offset)) / float((HALF + 1) ** 2)


def fill_interleave(table_ref, time_dim):
    size = table_ref.shape[0]
    time = lax.broadcasted_iota(jnp.int32, (size, size), time_dim)
    place = lax.broadcasted_iota(jnp.int32, (size, size), 1 - time_dim)
    hit = time == (place & (LANES - 1)) * PHASES + place // LANES
    table_ref[...] = jnp.where(hit, 1.0, 0.0).astype(jnp.bfloat16)


def move_samples(rows, table_ref):
    count = rows.shape[0]
    upper = rows.astype(jnp.bfloat16)
    rest = (rows - upper.astype(jnp.float32)).astype(jnp.bfloat16)
    both = jnp.concatenate([upper, rest], axis=0)
    moved = jnp.dot(both, table_ref[...], preferred_element_type=jnp.float32)
    return moved[:count] + moved[count:]


def pack_kernel(target_ref, lists_ref, traces_ref, out_ref, table_ref, tiles_ref, used_ref, sem, *more, part, capacity):
    held, block_rows, samples = traces_ref.shape
    share = block_rows // PARTS
    devices = used_ref.shape[0]
    span = share * PHASES
    fill_interleave(table_ref, 0)
    rows = traces_ref[:, part * share : (part + 1) * share, :].reshape(held * share, samples)
    moved = move_samples(rows, table_ref)
    for eight in range(held * share // 8):
        for phase in range(PHASES):
            tiles_ref[pl.ds(eight * 8 * PHASES + phase, 8, stride=PHASES), :] = moved[
                eight * 8 : eight * 8 + 8, phase * LANES : (phase + 1) * LANES
            ]

    def clear(device, _):
        used_ref[device] = 0
        return 0

    lax.fori_loop(0, devices, clear, 0)
    if more:
        listed_ref, listed_sem = more
        room = listed_ref.shape[1]
        listed_ref[...] = jnp.full(listed_ref.shape, -1.0, jnp.float32)

    def send_block(block, _):
        device = target_ref[block]
        rank = used_ref[device]
        used_ref[device] = rank + 1
        pltpu.make_async_copy(
            tiles_ref.at[pl.ds(pl.multiple_of(block * span, 8), span), :],
            out_ref.at[device, pl.ds(pl.multiple_of(rank * span, 8), span), :],
            sem,
        ).start()
        if more:
            listed_ref[device, pl.ds(rank, 1), :] = lists_ref[pl.ds(block, 1), :]
        return 0

    lax.fori_loop(0, held, send_block, 0, unroll=4)
    if more:
        copy = pltpu.make_async_copy(
            listed_ref, out_ref.at[:, capacity * span : capacity * span + room, :], listed_sem
        )
        copy.start()
        copy.wait()
    pltpu.make_async_copy(tiles_ref, tiles_ref, sem).wait()


def pack(traces, target, lists, devices, capacity, part):
    held, block_rows, samples = traces.shape
    span = block_rows // PARTS * PHASES
    room = -(-capacity // 8) * 8
    scratch = [
        pltpu.VMEM((samples, samples), jnp.bfloat16),
        pltpu.VMEM((held * span, LANES), jnp.float32),
        pltpu.SMEM((devices,), jnp.int32),
        pltpu.SemaphoreType.DMA,
    ]
    rows = capacity * span
    if part == 0:
        scratch += [pltpu.VMEM((devices, room, LANES), jnp.float32), pltpu.SemaphoreType.DMA]
        rows += room
    return pl.pallas_call(
        functools.partial(pack_kernel, part=part, capacity=capacity),
        in_specs=[
            pl.BlockSpec(memory_space=pltpu.SMEM),
            pl.BlockSpec(memory_space=pltpu.VMEM),
            pl.BlockSpec(memory_space=pltpu.VMEM),
        ],
        out_specs=pl.BlockSpec(memory_space=pl.ANY),
        out_shape=jax.ShapeDtypeStruct((devices, rows, LANES), jnp.float32),
        scratch_shapes=scratch,
        compiler_params=pltpu.CompilerParams(vmem_limit_bytes=32 * MIB),
        cost_estimate=pl.CostEstimate(
            flops=4 * samples * samples * held, bytes_accessed=4 * MIB, transcendentals=0
        ),
    )(target, lists, traces)


def bin_kernel(bins_ref, scale_ref, blocks_ref, *refs, part, capacity, last):
    if last:
        before_ref, out_ref, even_ref, odd_ref = refs
    else:
        out_ref, even_ref, odd_ref = refs
    step = pl.program_id(0)
    senders = blocks_ref.shape[0]
    bin_total = out_ref.shape[0]
    block_rows = bins_ref.shape[0] // (senders * pl.num_programs(0) * capacity)
    share = block_rows // PARTS
    unroll = 8

    @pl.when(step == 0)
    def _():
        def clear(i, _):
            for j in range(unroll):
                even_ref[i * unroll + j] = jnp.zeros((PHASES, LANES), jnp.float32)
                odd_ref[i * unroll + j] = jnp.zeros((PHASES, LANES), jnp.float32)
            return 0

        lax.fori_loop(0, bin_total // unroll, clear, 0)

    def add_sender(sender, _):
        first = (step * senders + sender) * (capacity * block_rows) + part * share
        for rank in range(capacity):
            for j in range(share):
                total_ref = odd_ref if j % 2 else even_ref
                place = bins_ref[first + rank * block_rows + j]
                row = (rank * share + j) * PHASES
                total_ref[place] += blocks_ref[sender, row : row + PHASES, :]
        return 0

    lax.fori_loop(0, senders, add_sender, 0)

    @pl.when(step == pl.num_programs(0) - 1)
    def _():
        def finish(i, _):
            for j in range(unroll):
                place = i * unroll + j
                total = even_ref[place] + odd_ref[place]
                if last:
                    total = (total + before_ref[place]) * scale_ref[place]
                out_ref[place] = total
            return 0

        lax.fori_loop(0, bin_total // unroll, finish, 0)


def stack_bins(blocks, bins, scale, capacity, part, before):
    devices, rows, _ = blocks.shape
    bin_total = scale.shape[0]
    steps = 8
    last = part == PARTS - 1
    whole = pl.BlockSpec((bin_total, PHASES, LANES), lambda i: (0, 0, 0))
    return pl.pallas_call(
        functools.partial(bin_kernel, part=part, capacity=capacity, last=last),
        grid=(steps,),
        in_specs=[
            pl.BlockSpec(memory_space=pltpu.SMEM),
            pl.BlockSpec(memory_space=pltpu.SMEM),
            pl.BlockSpec((devices // steps, rows, LANES), lambda i: (i, 0, 0)),
        ]
        + [whole] * last,
        out_specs=whole,
        out_shape=jax.ShapeDtypeStruct((bin_total, PHASES, LANES), jnp.float32),
        scratch_shapes=[
            pltpu.VMEM((bin_total + 8, PHASES, LANES), jnp.float32),
            pltpu.VMEM((bin_total + 8, PHASES, LANES), jnp.float32),
        ],
        compiler_params=pltpu.CompilerParams(vmem_limit_bytes=40 * MIB),
        cost_estimate=pl.CostEstimate(
            flops=8 * MIB, bytes_accessed=12 * MIB, transcendentals=0
        ),
    )(bins, scale, blocks, *([before] if last else []))


def steer_line(dip_ref, line, cell_of, put, extent, halves_ref, taps_refs, spots_ref, weights_ref):
    for pair in range((extent + 2 * HALF) // 2):
        cells = jnp.concatenate([cell_of(2 * pair), cell_of(2 * pair + 1)], axis=0)
        upper = cells.astype(jnp.bfloat16)
        halves_ref[pair * PAIR : (pair + 1) * PAIR, :LANES] = upper
        rest = (cells - upper.astype(jnp.float32)).astype(jnp.bfloat16)
        halves_ref[pair * PAIR : (pair + 1) * PAIR, LANES:] = rest
    row = lax.broadcasted_iota(jnp.int32, (PAIR, LANES), 0)
    column = lax.broadcasted_iota(jnp.int32, (PAIR, LANES), 1)
    phase_gap = ((row & (PHASES - 1)) - (column & (PHASES - 1))).astype(jnp.float32).astype(jnp.bfloat16)
    lane = lax.broadcasted_iota(jnp.int32, (PHASES, LANES), 1)
    none = jnp.zeros((PAIR, LANES), jnp.bfloat16)
    reaches = range(-REACH, REACH + 1)
    for group in range(extent // GROUP):
        taps_ref = taps_refs[group % 2]
        for pair in range(GROUP // 2):
            first = (group * GROUP // 2 + pair) * PAIR
            dip = dip_ref[line, first : first + PAIR, :]
            for half in range(2):
                block = pl.ds((pair * 2 + half) * PAIR, PAIR)
                move = phase_gap + dip * spots_ref[block, :]
                weights = weights_ref[block, :]
                for reach in reaches:
                    begin = (pair * len(reaches) + reach + REACH) * PAIR
                    taps_ref[begin : begin + PAIR, half * LANES : (half + 1) * LANES] = jnp.where(
                        move == jnp.bfloat16(reach * PHASES), weights, none
                    )
        start = group * GROUP * PHASES
        both = jnp.dot(
            taps_ref[...], halves_ref[start : start + 2 * LANES, :], preferred_element_type=jnp.float32
        )
        for pair in range(GROUP // 2):
            for member in range(2):
                total = None
                for reach in reaches:
                    begin = (pair * len(reaches) + reach + REACH) * PAIR + member * PHASES
                    part = both[begin : begin + PHASES, :LANES] + both[begin : begin + PHASES, LANES:]
                    if reach:
                        part = pltpu.roll(part, (-reach) % LANES, axis=1)
                        inside = lane < LANES - reach if reach > 0 else lane >= -reach
                        part = jnp.where(inside, part, 0.0)
                    total = part if total is None else total + part
                put(group * GROUP + 2 * pair + member, total)


def fill_weights(spots_ref, weights_ref):
    row = lax.broadcasted_iota(jnp.int32, (PAIR, LANES), 0)
    column = lax.broadcasted_iota(jnp.int32, (PAIR, LANES), 1)
    for pair in range(GROUP // 2):
        for half in range(2):
            block = pl.ds((pair * 2 + half) * PAIR, PAIR)
            spot = half * PAIR + column // PHASES - HALF - 2 * pair - row // PHASES
            share = jnp.maximum(HALF + 1 - jnp.abs(spot), 0).astype(jnp.float32) / (HALF + 1) ** 2
            spots_ref[block, :] = jnp.clip(spot, -HALF - 1, HALF + 1).astype(jnp.float32).astype(jnp.bfloat16)
            weights_ref[block, :] = share.astype(jnp.bfloat16)


def steer_kernel(dip_ref, *refs, along, places, final):
    inputs = 1 + max(index for index, _ in places)
    pieces, refs = refs[:inputs], refs[inputs:]
    if final is not None and final > 0:
        refs = refs[1:]
    out_ref, halves_a, halves_b, taps_a, taps_b, spots_ref, weights_ref, *more = refs
    if final is not None:
        staged_ref, table_ref = more
    extent = len(places) - 2 * HALF

    @pl.when(pl.program_id(0) == 0)
    def _():
        fill_weights(spots_ref, weights_ref)
        for halves_ref in (halves_a, halves_b):
            filled = len(places) * PHASES
            halves_ref[filled:, :] = jnp.zeros((halves_ref.shape[0] - filled, 2 * LANES), jnp.bfloat16)
        if final is not None:
            fill_interleave(table_ref, 1)

    def at(place, line):
        return (place, line) if along == 0 else (line, place)

    def one_line(line, halves_ref):
        def cell_of(place):
            index, local = places[place]
            return pieces[index][at(local, line)]

        def put(place, value):
            if final is not None:
                staged_ref[pl.ds((place * LINES + line) * PHASES, PHASES), :] = value
            else:
                out_ref[at(place, line)] = value

        steer_line(
            dip_ref, line, cell_of, put, extent, halves_ref, (taps_a, taps_b), spots_ref, weights_ref
        )

    def two_lines(i, _):
        one_line(2 * i, halves_a)
        one_line(2 * i + 1, halves_b)
        return 0

    lax.fori_loop(0, LINES // 2, two_lines, 0)
    if final is not None:
        rows = jnp.concatenate(
            [
                jnp.concatenate(
                    [
                        staged_ref[pl.ds(place * LINES * PHASES + phase, LINES, stride=PHASES), :]
                        for phase in range(PHASES)
                    ],
                    axis=1,
                )
                for place in range(extent)
            ],
            axis=0,
        )
        out_ref[...] = move_samples(rows, table_ref).reshape(out_ref.shape)


def steer(pieces, order, dip, along, steps, block_of, final=None, before=None):
    lines, extent = dip.shape[0], dip.shape[1] // PHASES
    samples = PHASES * LANES
    places = [(index, first + i) for index, first, count in order for i in range(count)]

    def spec(array, whole):
        chosen = block_of if whole else lambda i: i
        if along == 0:
            return pl.BlockSpec((array.shape[0], LINES, PHASES, LANES), lambda i: (0, chosen(i), 0, 0))
        return pl.BlockSpec((LINES, array.shape[1], PHASES, LANES), lambda i: (chosen(i), 0, 0, 0))

    in_specs = [pl.BlockSpec((LINES, extent * PHASES, LANES), lambda i: (block_of(i), 0, 0))]
    in_specs += [spec(*piece) for piece in pieces]
    operands = [dip] + [array for array, _ in pieces]
    halves = pltpu.VMEM((extent * PHASES + LANES, 2 * LANES), jnp.bfloat16)
    taps = pltpu.VMEM((GROUP * (2 * REACH + 1) * PHASES, 2 * LANES), jnp.bfloat16)
    constant = pltpu.VMEM((GROUP * PAIR, LANES), jnp.bfloat16)
    scratch = [halves, halves, taps, taps, constant, constant]
    aliases = {}
    if final is not None:
        out_shape = jax.ShapeDtypeStruct((extent, lines, samples), jnp.float32)
        out_spec = pl.BlockSpec((extent, LINES, samples), lambda i: (0, block_of(i), 0))
        scratch += [
            pltpu.VMEM((extent * LINES * PHASES, LANES), jnp.float32),
            pltpu.VMEM((samples, samples), jnp.bfloat16),
        ]
        if final > 0:
            aliases = {len(operands): 0}
            in_specs.append(pl.BlockSpec(memory_space=pl.ANY))
            operands.append(before)
    else:
        shape = (extent, steps * LINES) if along == 0 else (steps * LINES, extent)
        out_shape = jax.ShapeDtypeStruct(shape + (PHASES, LANES), jnp.float32)
        out_spec = spec(out_shape, False)
    return pl.pallas_call(
        functools.partial(steer_kernel, along=along, places=places, final=final),
        grid=(steps,),
        in_specs=in_specs,
        out_specs=out_spec,
        out_shape=out_shape,
        scratch_shapes=scratch,
        input_output_aliases=aliases,
        compiler_params=pltpu.CompilerParams(vmem_limit_bytes=40 * MIB),
        cost_estimate=pl.CostEstimate(
            flops=30 * extent * steps * LINES * samples,
            bytes_accessed=16 * extent * steps * LINES * samples,
            transcendentals=0,
        ),
    )(*operands)


def swap_ends(head, tail, axis):
    count = lax.axis_size(axis)
    low = lax.ppermute(tail, axis, [(i, i + 1) for i in range(count - 1)])
    high = lax.ppermute(head, axis, [(i + 1, i) for i in range(count - 1)])
    return low, high


def outer_of(cells, dim):
    size = cells.shape[dim]
    return jnp.concatenate(
        [lax.slice_in_dim(cells, 0, LINES, axis=dim), lax.slice_in_dim(cells, size - LINES, size, axis=dim)],
        axis=dim,
    )


def inner_of(cells, dim):
    return lax.slice_in_dim(cells, LINES, cells.shape[dim] - LINES, axis=dim)


def dip_tiles(dip):
    lines, extent = dip.shape
    tiles = jnp.broadcast_to(dip.astype(jnp.bfloat16)[:, :, None, None], (lines, extent, PHASES, LANES))
    return tiles.reshape(lines, extent * PHASES, LANES)


def smooth(stacked, dip_inline, dip_cross):
    rows, cols = dip_inline.shape
    dip_inline, dip_cross = dip_tiles(dip_inline.T), dip_tiles(dip_cross)
    row_blocks, col_blocks = rows // LINES, cols // LINES
    steps_in = lambda blocks: blocks - 2
    inner = lambda i: i + 1
    outer = lambda blocks: lambda i: i * (blocks - 1)

    head, tail = stacked[:HALF], stacked[rows - HALF :]
    order = [(0, 0, HALF), (1, 0, rows), (2, 0, HALF)]
    firsts = []
    for pick, steps, block_of in (
        (outer_of, 2, outer(col_blocks)),
        (inner_of, col_blocks - 2, inner),
    ):
        low, high = swap_ends(pick(head, 1), pick(tail, 1), "inline")
        firsts.append(
            steer([(low, False), (stacked, True), (high, False)], order, dip_inline, 0, steps, block_of)
        )
    border, middle = firsts

    head, tail = border[:, :HALF], border[:, 2 * LINES - HALF :]
    order = [(0, 0, HALF), (1, 0, LINES), (2, 0, cols - 2 * LINES), (1, LINES, LINES), (3, 0, HALF)]
    seconds = []
    for pick, steps, block_of in (
        (outer_of, 2, outer(row_blocks)),
        (inner_of, row_blocks - 2, inner),
    ):
        low, high = swap_ends(pick(head, 0), pick(tail, 0), "crosslin")
        seconds.append(
            steer(
                [(low, False), (border, True), (middle, True), (high, False)],
                order, dip_cross, 1, steps, block_of,
            )
        )
    border, middle = seconds

    head, tail = border[:HALF], border[2 * LINES - HALF :]
    order = [(0, 0, HALF), (1, 0, LINES), (2, 0, rows - 2 * LINES), (1, LINES, LINES), (3, 0, HALF)]
    half = col_blocks // 2
    result = None
    for group in range(2):
        begin, steps = (0, half) if group == 0 else (half, col_blocks - half)
        pick = lambda cells: cells[:, begin * LINES : (begin + steps) * LINES]
        low, high = swap_ends(pick(head), pick(tail), "inline")
        result = steer(
            [(low, False), (border, True), (middle, True), (high, False)],
            order, dip_inline, 0, steps, functools.partial(lambda begin, i: i + begin, begin),
            final=group, before=result,
        )
    return result


def on_device(traces, destination, bin_index, dip_inline, dip_cross):
    held, block_rows, _ = traces.shape
    devices = lax.axis_size("inline") * lax.axis_size("crosslin")
    capacity = 2 * held // devices
    tile_rows, tile_cols = dip_inline.shape
    bin_total = tile_rows * tile_cols
    target = destination.reshape(-1)
    lists = jnp.pad(bin_index.astype(jnp.float32), ((0, 0), (0, LANES - block_rows)))
    arrived = [
        lax.all_to_all(
            pack(traces, target, lists, devices, capacity, part), BOTH, split_axis=0, concat_axis=0, tiled=True
        )
        for part in range(PARTS)
    ]
    room = capacity * block_rows // PARTS * PHASES
    listed = arrived[0][:, room : room + capacity, :block_rows].astype(jnp.int32)
    bins = jnp.where(listed < 0, bin_total, listed).reshape(-1)
    fold = jnp.sum(
        (jnp.arange(bin_total, dtype=jnp.int32)[:, None] == bins[None, :]).astype(jnp.float32), axis=1
    )
    scale = 1.0 / jnp.maximum(fold, 1.0)
    total = None
    for part in range(PARTS):
        total = stack_bins(arrived[part], bins, scale, capacity, part, total)
    return smooth(total.reshape(tile_rows, tile_cols, PHASES, LANES), dip_inline, dip_cross)


def solution(mesh):
    return jax.shard_map(
        on_device,
        mesh=mesh,
        in_specs=(
            P(BOTH, None, None),
            P(BOTH, None),
            P(BOTH, None),
            P("inline", "crosslin"),
            P("inline", "crosslin"),
        ),
        out_specs=P("inline", "crosslin", None),
        check_vma=False,
    )
```

```python
import functools

import jax
import jax.numpy as jnp
import numpy as np
from jax import lax
from jax.experimental import pallas as pl
from jax.experimental.pallas import tpu as pltpu
from jax.sharding import PartitionSpec as P

HALF = 7
DMAX = 2
LANES = 128
PHASES = 8
PAIR = 2 * PHASES
WIDE = 2 * LANES
BORDER = 8
REACH = -(-HALF * DMAX // PHASES)
REACHES = range(-REACH, REACH + 1)
BOTH = ("inline", "crosslin")
MIB = 2**20
VMEM = pl.BlockSpec(memory_space=pltpu.VMEM)
SMEM = pl.BlockSpec(memory_space=pltpu.SMEM)
ANY = pl.BlockSpec(memory_space=pl.ANY)
HBM = pl.BlockSpec(memory_space=pltpu.HBM)
F32, BF16, I32 = jnp.float32, jnp.bfloat16, jnp.int32


def interleave_table(samples):
    table = np.zeros((samples, samples), np.float32)
    time = np.arange(samples)
    table[time, time % PHASES * LANES + time // PHASES] = 1.0
    return table


def move_samples(rows, table):
    count = rows.shape[0]
    upper = rows.astype(BF16)
    rest = (rows - upper.astype(F32)).astype(BF16)
    both = jnp.concatenate([upper, rest], axis=0)
    moved = jnp.dot(both, table, preferred_element_type=F32)
    return moved[:count] + moved[count:]


def pack_kernel(target_ref, bins_ref, traces_ref, table_ref, out_ref, tiles_ref, used_ref, listed_ref, sem, listed_sem, *, capacity):
    held, block_rows, samples = traces_ref.shape
    devices, room, _ = listed_ref.shape
    span = block_rows * PHASES
    groups = 2
    lane = lax.broadcasted_iota(I32, (1, LANES), 1)
    listed_ref[...] = jnp.full(listed_ref.shape, -1.0, F32)

    def clear(device, _):
        used_ref[device] = 0
        return 0

    lax.fori_loop(0, devices, clear, 0)

    def send_block(block, _):
        device = target_ref[block]
        rank = used_ref[device]
        used_ref[device] = rank + 1
        pltpu.make_async_copy(
            tiles_ref.at[pl.ds(pl.multiple_of(block * span, 8), span), :],
            out_ref.at[device, pl.ds(pl.multiple_of(rank * span, 8), span), :],
            sem,
        ).start()
        row = jnp.zeros((1, LANES), I32)
        for j in range(block_rows):
            row = jnp.where(lane == j, bins_ref[j, block], row)
        listed_ref[device, pl.ds(rank, 1), :] = row.astype(F32)
        return 0

    for group in range(groups):
        count = held // groups
        rows = traces_ref[group * count : (group + 1) * count].reshape(count * block_rows, samples)
        moved = move_samples(rows, table_ref[...])
        for eight in range(count * block_rows // 8):
            for phase in range(PHASES):
                first = (group * count * block_rows + eight * 8) * PHASES + phase
                tiles_ref[pl.ds(first, 8, stride=PHASES), :] = moved[
                    eight * 8 : eight * 8 + 8, phase * LANES : (phase + 1) * LANES
                ]
        lax.fori_loop(group * count, (group + 1) * count, send_block, 0, unroll=4)
    copy = pltpu.make_async_copy(
        listed_ref, out_ref.at[:, capacity * span : capacity * span + room, :], listed_sem
    )
    copy.start()
    copy.wait()
    pltpu.make_async_copy(tiles_ref, tiles_ref, sem).wait()


def pack(traces, target, bins, table, devices, capacity):
    held, block_rows, samples = traces.shape
    span = block_rows * PHASES
    room = -(-capacity // 8) * 8
    return pl.pallas_call(
        functools.partial(pack_kernel, capacity=capacity),
        in_specs=[SMEM, SMEM, VMEM, VMEM],
        out_specs=HBM,
        out_shape=jax.ShapeDtypeStruct((devices, capacity * span + room, LANES), F32),
        scratch_shapes=[
            pltpu.VMEM((held * span, LANES), F32),
            pltpu.SMEM((devices,), I32),
            pltpu.VMEM((devices, room, LANES), F32),
            pltpu.SemaphoreType.DMA,
            pltpu.SemaphoreType.DMA,
        ],
        compiler_params=pltpu.CompilerParams(vmem_limit_bytes=20 * MIB),
    )(target, bins, traces, table)


def bin_kernel(blocks_ref, out_ref, head_ref, tail_ref, even_ref, odd_ref, listed_ref, places_ref, fold_ref, sems, *, capacity, edge):
    devices, rows, _ = blocks_ref.shape
    room = listed_ref.shape[1]
    bin_total = out_ref.shape[0]
    block_rows = (rows - room) // (capacity * PHASES)
    unroll = 8
    listed = blocks_ref[:, rows - room :, :]
    listed_ref[...] = jnp.where(listed < 0, float(bin_total), listed).astype(I32)
    copy = pltpu.make_async_copy(listed_ref, places_ref, sems.at[0])
    copy.start()
    nothing = jnp.zeros((PHASES, LANES), F32)

    def clear(i, _):
        for j in range(unroll):
            even_ref[i * unroll + j] = nothing
            odd_ref[i * unroll + j] = nothing
            fold_ref[i * unroll + j] = 0
        return 0

    lax.fori_loop(0, bin_total // unroll, clear, 0)
    fold_ref[bin_total] = 0
    copy.wait()

    def add_sender(sender, _):
        for rank in range(capacity):
            for j in range(block_rows):
                total_ref = odd_ref if j % 2 else even_ref
                place = places_ref[sender, rank, j]
                row = (rank * block_rows + j) * PHASES
                total_ref[place] += blocks_ref[sender, row : row + PHASES, :]
                fold_ref[place] = fold_ref[place] + 1
        return 0

    lax.fori_loop(0, devices, add_sender, 0)

    def finish(i, _):
        for j in range(unroll):
            place = i * unroll + j
            fold = jnp.full((PHASES, LANES), jnp.maximum(fold_ref[place], 1).astype(F32))
            out_ref[place] = (even_ref[place] + odd_ref[place]) / fold
        return 0

    lax.fori_loop(0, edge // unroll, finish, 0)
    head_copy = pltpu.make_async_copy(out_ref.at[pl.ds(0, edge)], head_ref, sems.at[1])
    head_copy.start()
    lax.fori_loop((bin_total - edge) // unroll, bin_total // unroll, finish, 0)
    tail_copy = pltpu.make_async_copy(out_ref.at[pl.ds(bin_total - edge, edge)], tail_ref, sems.at[2])
    tail_copy.start()
    lax.fori_loop(edge // unroll, (bin_total - edge) // unroll, finish, 0)
    head_copy.wait()
    tail_copy.wait()


def stack_bins(blocks, tile_rows, tile_cols, capacity):
    devices = blocks.shape[0]
    bin_total = tile_rows * tile_cols
    edge = HALF * tile_cols
    room = -(-capacity // 8) * 8
    stacked, head, tail = pl.pallas_call(
        functools.partial(bin_kernel, capacity=capacity, edge=edge),
        in_specs=[VMEM],
        out_specs=[VMEM, HBM, HBM],
        out_shape=[
            jax.ShapeDtypeStruct((bin_total, PHASES, LANES), F32),
            jax.ShapeDtypeStruct((edge, PHASES, LANES), F32),
            jax.ShapeDtypeStruct((edge, PHASES, LANES), F32),
        ],
        scratch_shapes=[
            pltpu.VMEM((bin_total + 8, PHASES, LANES), F32),
            pltpu.VMEM((bin_total + 8, PHASES, LANES), F32),
            pltpu.VMEM((devices, room, LANES), I32),
            pltpu.SMEM((devices, room, LANES), I32),
            pltpu.SMEM((bin_total + 8,), I32),
            pltpu.SemaphoreType.DMA((3,)),
        ],
        compiler_params=pltpu.CompilerParams(vmem_limit_bytes=20 * MIB),
    )(blocks)
    shape = (tile_cols, PHASES, LANES)
    return stacked.reshape((tile_rows,) + shape), head.reshape((HALF,) + shape), tail.reshape((HALF,) + shape)


def fill_weights(spots_ref, weights_ref):
    row = lax.broadcasted_iota(I32, (PAIR, LANES), 0)
    column = lax.broadcasted_iota(I32, (PAIR, LANES), 1)
    for pair in range(spots_ref.shape[0] // (2 * PAIR)):
        for half in range(2):
            block = pl.ds((pair * 2 + half) * PAIR, PAIR)
            spot = half * PAIR + column // PHASES - HALF - 2 * pair - row // PHASES
            share = jnp.maximum(HALF + 1 - jnp.abs(spot), 0).astype(F32) / (HALF + 1) ** 2
            spots_ref[block, :] = jnp.clip(spot, -HALF - 1, HALF + 1).astype(F32).astype(BF16)
            weights_ref[block, :] = share.astype(BF16)


def steer_window(dip_of, cells, first, count, put, halves_ref, spots_ref, weights_ref):
    for pair in range(len(cells) // 2):
        both = jnp.concatenate([cells[2 * pair](), cells[2 * pair + 1]()], axis=0)
        upper = both.astype(BF16)
        halves_ref[pair * PAIR : (pair + 1) * PAIR, :LANES] = upper
        rest = (both - upper.astype(F32)).astype(BF16)
        halves_ref[pair * PAIR : (pair + 1) * PAIR, LANES:] = rest
    row = lax.broadcasted_iota(I32, (PAIR, LANES), 0)
    column = lax.broadcasted_iota(I32, (PAIR, LANES), 1)
    phase_gap = ((row & (PHASES - 1)) - (column & (PHASES - 1))).astype(F32).astype(BF16)
    lane = lax.broadcasted_iota(I32, (PHASES, LANES), 1)
    none = jnp.zeros((PAIR, LANES), BF16)
    taps = []
    for pair in range(count // 2):
        dip = dip_of(first // 2 + pair)
        moves, weights = [], []
        for half in range(2):
            block = pl.ds((pair * 2 + half) * PAIR, PAIR)
            moves.append(phase_gap + dip * spots_ref[block, :])
            weights.append(weights_ref[block, :])
        for reach in REACHES:
            taps.append(
                jnp.concatenate(
                    [jnp.where(moves[h] == jnp.bfloat16(reach * PHASES), weights[h], none) for h in range(2)],
                    axis=1,
                )
            )
    sums = jnp.dot(jnp.concatenate(taps, axis=0), halves_ref[...], preferred_element_type=F32)
    for pair in range(count // 2):
        for member in range(2):
            total = None
            for reach in REACHES:
                begin = (pair * len(REACHES) + reach + REACH) * PAIR + member * PHASES
                part = sums[begin : begin + PHASES, :LANES] + sums[begin : begin + PHASES, LANES:]
                if reach:
                    part = pltpu.roll(part, (-reach) % LANES, axis=1)
                    inside = lane < LANES - reach if reach > 0 else lane >= -reach
                    part = jnp.where(inside, part, 0.0)
                total = part if total is None else total + part
            put(first + 2 * pair + member, total)


def steer_kernel(dip_ref, *refs, along, whole, lines, line_of, windows, local_of, edges, final, chained, pieces_count):
    pieces, refs = refs[:pieces_count], refs[pieces_count:]
    if final:
        table_ref, refs = refs[0], refs[1:]
    if chained:
        refs = refs[1:]
    out_ref, refs = refs[0], refs[1:]
    edge_refs, refs = refs[: len(edges)], refs[len(edges) :]
    spots_ref, weights_ref, sems, *refs = refs
    halves = refs[: 2 * len(windows)]
    if final:
        staged_ref, result_ref = refs[2 * len(windows) :]
    fill_weights(spots_ref, weights_ref)
    for i, halves_ref in enumerate(halves):
        filled = len(windows[i % len(windows)][2]) * PHASES
        if filled < WIDE:
            halves_ref[filled:, :] = jnp.zeros((WIDE - filled, WIDE), BF16)

    def at(place, line):
        return (place, line) if along == 0 else (line, place)

    def one_line(line, parity):
        full = line_of(line)

        def cell(index, local):
            return lambda: pieces[index][at(local, full if whole[index] else line)]

        def put(place, value):
            if final:
                staged_ref[pl.ds((local_of(place) * final + line % final) * PHASES, PHASES), :] = value
            else:
                out_ref[at(local_of(place), line)] = value

        for i, (first, count, places) in enumerate(windows):
            steer_window(
                lambda pair: dip_ref[full, pair * PAIR : (pair + 1) * PAIR, :],
                [cell(*place) for place in places],
                first, count, put, halves[parity * len(windows) + i], spots_ref, weights_ref,
            )

    def two_lines(i, _):
        one_line(2 * i, 0)
        one_line(2 * i + 1, 1)
        return 0

    if not final:
        lax.fori_loop(0, lines // 2, two_lines, 0)
        copies = [
            pltpu.make_async_copy(out_ref.at[pick], edge_ref, sems.at[i])
            for i, (pick, edge_ref) in enumerate(zip(edges, edge_refs))
        ]
        for copy in copies:
            copy.start()
        for copy in copies:
            copy.wait()
        return

    outputs = sum(count for _, count, _ in windows)

    def copies_of(batch, slot):
        return [
            pltpu.make_async_copy(
                result_ref.at[slot, pl.ds(local_of(first), count)],
                out_ref.at[pl.ds(first, count), pl.ds(pl.multiple_of(batch * final, 8), final), :],
                sems.at[slot * len(windows) + i],
            )
            for i, (first, count, _) in enumerate(windows)
        ]

    for batch in range(lines // final):
        lax.fori_loop(batch * final // 2, (batch + 1) * final // 2, two_lines, 0)
        rows = jnp.concatenate(
            [
                jnp.concatenate(
                    [
                        staged_ref[pl.ds(eight * 8 * PHASES + phase, 8, stride=PHASES), :]
                        for phase in range(PHASES)
                    ],
                    axis=1,
                )
                for eight in range(outputs * final // 8)
            ],
            axis=0,
        )
        slot = batch % 2
        if batch >= 2:
            for copy in copies_of(batch - 2, slot):
                copy.wait()
        result_ref[slot] = move_samples(rows, table_ref[...]).reshape(result_ref.shape[1:])
        for copy in copies_of(batch, slot):
            copy.start()
    for batch in range(max(0, lines // final - 2), lines // final):
        for copy in copies_of(batch, batch % 2):
            copy.wait()


def steer(dip, pieces, along, lines, line_of, windows, local_of, edges=(), table=None, before=None):
    samples = PHASES * LANES
    outputs = sum(count for _, count, _ in windows)
    final = 16 if table is not None else 0
    operands = [dip] + [array for array, _ in pieces]
    in_specs = [VMEM] * len(operands)
    aliases = {}
    if final:
        operands.append(table)
        in_specs.append(VMEM)
        if before is not None:
            aliases = {len(operands): 0}
            operands.append(before)
            in_specs.append(HBM)
        extent = dip.shape[1] // PHASES
        out_shape = [jax.ShapeDtypeStruct((extent, lines, samples), F32)]
        out_specs = [HBM]
    else:
        shape = (outputs, lines) if along == 0 else (lines, outputs)
        out_shape = [jax.ShapeDtypeStruct(shape + (PHASES, LANES), F32)]
        out_specs = [VMEM]
        for pick in edges:
            size = [len(range(*s.indices(n))) for s, n in zip(pick, shape)]
            out_shape.append(jax.ShapeDtypeStruct(tuple(size) + (PHASES, LANES), F32))
            out_specs.append(HBM)
    most = max(count for _, count, _ in windows)
    constant = pltpu.VMEM((most * PAIR, LANES), BF16)
    scratch = [constant, constant, pltpu.SemaphoreType.DMA((2 * len(windows) if final else max(1, len(edges)),))]
    scratch += [pltpu.VMEM((WIDE, WIDE), BF16)] * (2 * len(windows))
    if final:
        scratch += [
            pltpu.VMEM((outputs * final * PHASES, LANES), F32),
            pltpu.VMEM((2, outputs, final, samples), F32),
        ]
    return pl.pallas_call(
        functools.partial(
            steer_kernel,
            along=along, whole=[whole for _, whole in pieces], lines=lines, line_of=line_of, windows=windows,
            local_of=local_of, edges=edges, final=final, chained=before is not None, pieces_count=len(pieces),
        ),
        in_specs=in_specs,
        out_specs=out_specs,
        out_shape=out_shape,
        scratch_shapes=scratch,
        input_output_aliases=aliases,
        compiler_params=pltpu.CompilerParams(vmem_limit_bytes=16 * MIB),
        cost_estimate=pl.CostEstimate(
            flops=2400 * outputs * lines * samples,
            bytes_accessed=8 * outputs * lines * samples,
            transcendentals=0,
        ),
    )(*operands)


def swap_ends(head, tail, axis):
    count = lax.axis_size(axis)
    low = lax.ppermute(tail, axis, [(i, i + 1) for i in range(count - 1)])
    high = lax.ppermute(head, axis, [(i + 1, i) for i in range(count - 1)])
    return low, high


def dip_tiles(dip):
    lines, extent = dip.shape
    tiles = jnp.broadcast_to(dip.astype(BF16)[:, :, None, None], (lines, extent, PHASES, LANES))
    return tiles.reshape(lines, extent * PHASES, LANES)


def span_of(index, first, count):
    return [(index, first + i) for i in range(count)]


def smooth(stacked, head, tail, along_rows, along_cols, table):
    rows, cols = stacked.shape[:2]
    mid_rows, mid_cols = rows - 2 * BORDER, cols - 2 * BORDER
    same = lambda line: line
    inner = lambda line: line + BORDER
    outer_col = lambda line: line + jnp.where(line < BORDER, 0, mid_cols)
    outer_row = lambda line: line + jnp.where(line < BORDER, 0, mid_rows)
    mid_place = lambda place: place - BORDER
    outer_place = lambda place: place if place < BORDER else place - mid_rows
    every = slice(None)
    lead, last = slice(0, HALF), slice(2 * BORDER - HALF, 2 * BORDER)

    def mid_windows(places):
        return [(BORDER + i, 16, places[i : i + 16 + 2 * HALF]) for i in range(0, mid_rows, 16)]

    low, high = swap_ends(head, tail, "inline")
    middle, head_mid, tail_mid = steer(
        along_rows, [(stacked, True)], 0, cols, same,
        mid_windows(span_of(0, BORDER - HALF, mid_rows + 2 * HALF)), mid_place,
        edges=[(every, lead), (every, slice(cols - HALF, cols))],
    )
    low_mid, high_mid = swap_ends(head_mid, tail_mid, "crosslin")
    pieces = [(low, True), (stacked, True), (high, True)]
    windows = [
        (0, BORDER, span_of(0, 0, HALF) + span_of(1, 0, BORDER + HALF)),
        (rows - BORDER, BORDER, span_of(1, rows - BORDER - HALF, BORDER + HALF) + span_of(2, 0, HALF)),
    ]
    corners, head_out, tail_out = steer(
        along_rows, pieces, 0, 2 * BORDER, outer_col, windows, outer_place, edges=[(every, lead), (every, last)]
    )
    low_out, high_out = swap_ends(head_out, tail_out, "crosslin")
    (flanks,) = steer(along_rows, pieces, 0, mid_cols, inner, windows, outer_place)

    def cross_windows(places):
        return [(i, 16, places[i : i + 16 + 2 * HALF]) for i in range(0, cols, 16)]

    places = span_of(0, 0, HALF) + span_of(1, 0, cols) + span_of(2, 0, HALF)
    (middle_second,) = steer(
        along_cols, [(low_mid, False), (middle, False), (high_mid, False)], 1, mid_rows, inner,
        cross_windows(places), same,
    )
    places = (
        span_of(0, 0, HALF) + span_of(1, 0, BORDER) + span_of(2, 0, mid_cols) + span_of(1, BORDER, BORDER) + span_of(3, 0, HALF)
    )
    border_second, head, tail = steer(
        along_cols, [(low_out, False), (corners, False), (flanks, False), (high_out, False)], 1, 2 * BORDER,
        outer_row, cross_windows(places), same, edges=[(lead, every), (last, every)],
    )

    low, high = swap_ends(head, tail, "inline")
    places = span_of(0, BORDER - HALF, HALF) + span_of(1, 0, mid_rows) + span_of(0, BORDER, HALF)
    (result,) = steer(
        along_rows, [(border_second, True), (middle_second, True)], 0, cols, same, mid_windows(places), mid_place,
        table=table,
    )
    windows = [
        (0, BORDER, span_of(0, 0, HALF) + span_of(1, 0, BORDER) + span_of(2, 0, HALF)),
        (rows - BORDER, BORDER, span_of(2, mid_rows - HALF, HALF) + span_of(1, BORDER, BORDER) + span_of(3, 0, HALF)),
    ]
    (result,) = steer(
        along_rows, [(low, True), (border_second, True), (middle_second, True), (high, True)], 0, cols, same,
        windows, outer_place, table=table, before=result,
    )
    return result


def on_device(traces, destination, bin_index, dip_inline, dip_cross):
    held, block_rows, samples = traces.shape
    devices = lax.axis_size("inline") * lax.axis_size("crosslin")
    capacity = 2 * held // devices
    tile_rows, tile_cols = dip_inline.shape
    table = interleave_table(samples)
    outgoing = pack(traces, destination.reshape(-1), bin_index.T, jnp.asarray(table, BF16), devices, capacity)
    arrived = lax.all_to_all(outgoing, BOTH, split_axis=0, concat_axis=0, tiled=True)
    back, along_rows, along_cols = jnp.asarray(table.T, BF16), dip_tiles(dip_inline.T), dip_tiles(dip_cross)
    arrived, along_rows, along_cols = lax.optimization_barrier((arrived, along_rows, along_cols))
    stacked, head, tail = stack_bins(arrived, tile_rows, tile_cols, capacity)
    return smooth(stacked, head, tail, along_rows, along_cols, back)


def solution(mesh):
    return jax.shard_map(
        on_device,
        mesh=mesh,
        in_specs=(
            P(BOTH, None, None),
            P(BOTH, None),
            P(BOTH, None),
            P("inline", "crosslin"),
            P("inline", "crosslin"),
        ),
        out_specs=P("inline", "crosslin", None),
        check_vma=False,
    )
```

```python
import functools

import jax
import jax.numpy as jnp
import numpy as np
from jax import lax
from jax.experimental import pallas as pl
from jax.experimental.pallas import tpu as pltpu
from jax.sharding import PartitionSpec as P

HALF = 7
DMAX = 2
LANES = 128
PHASES = 8
PAIR = 2 * PHASES
WIDE = 2 * LANES
BORDER = 8
REACH = -(-HALF * DMAX // PHASES)
REACHES = range(-REACH, REACH + 1)
BOTH = ("inline", "crosslin")
MIB = 2**20
VMEM = pl.BlockSpec(memory_space=pltpu.VMEM)
SMEM = pl.BlockSpec(memory_space=pltpu.SMEM)
ANY = pl.BlockSpec(memory_space=pl.ANY)
HBM = pl.BlockSpec(memory_space=pltpu.HBM)
F32, BF16, I32 = jnp.float32, jnp.bfloat16, jnp.int32


def interleave_table(samples):
    table = np.zeros((samples, samples), np.float32)
    time = np.arange(samples)
    table[time, time % PHASES * LANES + time // PHASES] = 1.0
    return table


def move_samples(rows, table):
    count = rows.shape[0]
    upper = rows.astype(BF16)
    rest = (rows - upper.astype(F32)).astype(BF16)
    both = jnp.concatenate([upper, rest], axis=0)
    moved = jnp.dot(both, table, preferred_element_type=F32)
    return moved[:count] + moved[count:]


def fill_interleave(table_ref):
    size = table_ref.shape[0]
    time = lax.broadcasted_iota(I32, (size, LANES), 0)
    lane = lax.broadcasted_iota(I32, (size, LANES), 1)
    gap = time - lane * PHASES
    for phase in range(PHASES):
        table_ref[:, phase * LANES : (phase + 1) * LANES] = jnp.where(gap == phase, 1.0, 0.0).astype(BF16)


def pack_kernel(target_ref, bins_ref, traces_ref, out_ref, held_ref, table_ref, tiles_ref, used_ref, listed_ref, in_sems, sem, listed_sem, *, capacity):
    held, block_rows, samples = traces_ref.shape
    devices, room, _ = listed_ref.shape
    span = block_rows * PHASES
    groups = held_ref.shape[0]
    count = held // groups
    loads = [
        pltpu.make_async_copy(traces_ref.at[pl.ds(group * count, count)], held_ref.at[group], in_sems.at[group])
        for group in range(groups)
    ]
    for load in loads:
        load.start()
    fill_interleave(table_ref)
    lane = lax.broadcasted_iota(I32, (1, LANES), 1)
    listed_ref[...] = jnp.full(listed_ref.shape, -1.0, F32)

    def clear(device, _):
        used_ref[device] = 0
        return 0

    lax.fori_loop(0, devices, clear, 0)

    def send_block(block, _):
        device = target_ref[block]
        rank = used_ref[device]
        used_ref[device] = rank + 1
        pltpu.make_async_copy(
            tiles_ref.at[pl.ds(pl.multiple_of(block * span, 8), span), :],
            out_ref.at[device, pl.ds(pl.multiple_of(rank * span, 8), span), :],
            sem,
        ).start()
        row = jnp.zeros((1, LANES), I32)
        for j in range(block_rows):
            row = jnp.where(lane == j, bins_ref[j, block], row)
        listed_ref[device, pl.ds(rank, 1), :] = row.astype(F32)
        return 0

    for group in range(groups):
        loads[group].wait()
        rows = held_ref[group].reshape(count * block_rows, samples)
        moved = move_samples(rows, table_ref[...])
        for eight in range(count * block_rows // 8):
            for phase in range(PHASES):
                first = (group * count * block_rows + eight * 8) * PHASES + phase
                tiles_ref[pl.ds(first, 8, stride=PHASES), :] = moved[
                    eight * 8 : eight * 8 + 8, phase * LANES : (phase + 1) * LANES
                ]
        lax.fori_loop(group * count, (group + 1) * count, send_block, 0, unroll=4)
    copy = pltpu.make_async_copy(
        listed_ref, out_ref.at[:, capacity * span : capacity * span + room, :], listed_sem
    )
    copy.start()
    copy.wait()
    pltpu.make_async_copy(tiles_ref, tiles_ref, sem).wait()


def pack(traces, target, bins, devices, capacity):
    held, block_rows, samples = traces.shape
    span = block_rows * PHASES
    room = -(-capacity // 8) * 8
    groups = 2
    return pl.pallas_call(
        functools.partial(pack_kernel, capacity=capacity),
        in_specs=[SMEM, SMEM, HBM],
        out_specs=HBM,
        out_shape=jax.ShapeDtypeStruct((devices, capacity * span + room, LANES), F32),
        scratch_shapes=[
            pltpu.VMEM((groups, held // groups, block_rows, samples), F32),
            pltpu.VMEM((samples, samples), BF16),
            pltpu.VMEM((held * span, LANES), F32),
            pltpu.SMEM((devices,), I32),
            pltpu.VMEM((devices, room, LANES), F32),
            pltpu.SemaphoreType.DMA((groups,)),
            pltpu.SemaphoreType.DMA,
            pltpu.SemaphoreType.DMA,
        ],
        compiler_params=pltpu.CompilerParams(vmem_limit_bytes=60 * MIB),
    )(target, bins, traces)


def bin_kernel(bins_ref, scale_ref, blocks_ref, out_ref, head_ref, tail_ref, held_ref, even_ref, odd_ref, sems, in_sems, *, capacity, block_rows, edge):
    parts = held_ref.shape[0]
    senders = blocks_ref.shape[0] // parts
    bin_total = out_ref.shape[0]
    rows = held_ref.shape[2]
    unroll = 8
    loads = [
        pltpu.make_async_copy(
            blocks_ref.at[pl.ds(part * senders, senders), pl.ds(0, rows), :], held_ref.at[part], in_sems.at[part]
        )
        for part in range(parts)
    ]
    for load in loads:
        load.start()
    nothing = jnp.zeros((PHASES, LANES), F32)

    def clear(i, _):
        for j in range(unroll):
            even_ref[i * unroll + j] = nothing
            odd_ref[i * unroll + j] = nothing
        return 0

    lax.fori_loop(0, bin_total // unroll, clear, 0)
    for part in range(parts):
        loads[part].wait()

        def add_sender(sender, _):
            first = (part * senders + sender) * (capacity * block_rows)
            for i in range(capacity * block_rows):
                total_ref = odd_ref if i % 2 else even_ref
                total_ref[bins_ref[first + i]] += held_ref[part, sender, i * PHASES : (i + 1) * PHASES]
            return 0

        lax.fori_loop(0, senders, add_sender, 0)

    def finish(i, _):
        for j in range(unroll):
            place = i * unroll + j
            out_ref[place] = (even_ref[place] + odd_ref[place]) * scale_ref[place]
        return 0

    lax.fori_loop(0, edge // unroll, finish, 0)
    head_copy = pltpu.make_async_copy(out_ref.at[pl.ds(0, edge)], head_ref, sems.at[0])
    head_copy.start()
    lax.fori_loop((bin_total - edge) // unroll, bin_total // unroll, finish, 0)
    tail_copy = pltpu.make_async_copy(out_ref.at[pl.ds(bin_total - edge, edge)], tail_ref, sems.at[1])
    tail_copy.start()
    lax.fori_loop(edge // unroll, (bin_total - edge) // unroll, finish, 0)
    head_copy.wait()
    tail_copy.wait()


def stack_bins(blocks, tile_rows, tile_cols, capacity, block_rows):
    devices = blocks.shape[0]
    bin_total = tile_rows * tile_cols
    edge = HALF * tile_cols
    rows = capacity * block_rows * PHASES
    listed = blocks[:, rows : rows + capacity, :block_rows].astype(I32)
    bins = jnp.where(listed < 0, bin_total, listed).reshape(-1)
    fold = jnp.sum((jnp.arange(bin_total, dtype=I32)[:, None] == bins[None, :]).astype(F32), axis=1)
    parts = 4
    stacked, head, tail = pl.pallas_call(
        functools.partial(bin_kernel, capacity=capacity, block_rows=block_rows, edge=edge),
        in_specs=[SMEM, SMEM, ANY],
        out_specs=[VMEM, HBM, HBM],
        out_shape=[
            jax.ShapeDtypeStruct((bin_total, PHASES, LANES), F32),
            jax.ShapeDtypeStruct((edge, PHASES, LANES), F32),
            jax.ShapeDtypeStruct((edge, PHASES, LANES), F32),
        ],
        scratch_shapes=[
            pltpu.VMEM((parts, devices // parts, rows, LANES), F32),
            pltpu.VMEM((bin_total + 8, PHASES, LANES), F32),
            pltpu.VMEM((bin_total + 8, PHASES, LANES), F32),
            pltpu.SemaphoreType.DMA((2,)),
            pltpu.SemaphoreType.DMA((parts,)),
        ],
        compiler_params=pltpu.CompilerParams(vmem_limit_bytes=20 * MIB),
    )(bins, 1.0 / jnp.maximum(fold, 1.0), blocks)
    shape = (tile_cols, PHASES, LANES)
    return stacked.reshape((tile_rows,) + shape), head.reshape((HALF,) + shape), tail.reshape((HALF,) + shape)


def fill_weights(spots_ref, weights_ref):
    row = lax.broadcasted_iota(I32, (PAIR, LANES), 0)
    column = lax.broadcasted_iota(I32, (PAIR, LANES), 1)
    for pair in range(spots_ref.shape[0] // (2 * PAIR)):
        for half in range(2):
            block = pl.ds((pair * 2 + half) * PAIR, PAIR)
            spot = half * PAIR + column // PHASES - HALF - 2 * pair - row // PHASES
            share = jnp.maximum(HALF + 1 - jnp.abs(spot), 0).astype(F32) / (HALF + 1) ** 2
            spots_ref[block, :] = jnp.clip(spot, -HALF - 1, HALF + 1).astype(F32).astype(BF16)
            weights_ref[block, :] = share.astype(BF16)


def steer_window(dip_of, cells, first, count, put, halves_ref, spots_ref, weights_ref):
    for pair in range(len(cells) // 2):
        both = jnp.concatenate([cells[2 * pair](), cells[2 * pair + 1]()], axis=0)
        upper = both.astype(BF16)
        halves_ref[pair * PAIR : (pair + 1) * PAIR, :LANES] = upper
        rest = (both - upper.astype(F32)).astype(BF16)
        halves_ref[pair * PAIR : (pair + 1) * PAIR, LANES:] = rest
    row = lax.broadcasted_iota(I32, (PAIR, LANES), 0)
    column = lax.broadcasted_iota(I32, (PAIR, LANES), 1)
    phase_gap = ((row & (PHASES - 1)) - (column & (PHASES - 1))).astype(F32).astype(BF16)
    lane = lax.broadcasted_iota(I32, (PHASES, LANES), 1)
    none = jnp.zeros((PAIR, LANES), BF16)
    taps = []
    for pair in range(count // 2):
        dip = jnp.concatenate(
            [jnp.full((PHASES, LANES), dip_of(first + 2 * pair + i).astype(F32)) for i in range(2)], axis=0
        ).astype(BF16)
        moves, weights = [], []
        for half in range(2):
            block = pl.ds((pair * 2 + half) * PAIR, PAIR)
            moves.append(phase_gap + dip * spots_ref[block, :])
            weights.append(weights_ref[block, :])
        for reach in REACHES:
            taps.append(
                jnp.concatenate(
                    [jnp.where(moves[h] == jnp.bfloat16(reach * PHASES), weights[h], none) for h in range(2)],
                    axis=1,
                )
            )
    sums = jnp.dot(jnp.concatenate(taps, axis=0), halves_ref[...], preferred_element_type=F32)
    for pair in range(count // 2):
        for member in range(2):
            total = None
            for reach in REACHES:
                begin = (pair * len(REACHES) + reach + REACH) * PAIR + member * PHASES
                part = sums[begin : begin + PHASES, :LANES] + sums[begin : begin + PHASES, LANES:]
                if reach:
                    part = pltpu.roll(part, (-reach) % LANES, axis=1)
                    inside = lane < LANES - reach if reach > 0 else lane >= -reach
                    part = jnp.where(inside, part, 0.0)
                total = part if total is None else total + part
            put(first + 2 * pair + member, total)


def steer_kernel(dip_ref, *refs, along, whole, lines, line_of, windows, local_of, edges, final, chained, pieces_count, abreast):
    pieces, refs = refs[:pieces_count], refs[pieces_count:]
    if final:
        table_ref, refs = refs[0], refs[1:]
    refs = refs[chained:]
    out_ref, refs = refs[0], refs[1:]
    edge_refs, refs = refs[: len(edges)], refs[len(edges) :]
    spots_ref, weights_ref, sems, *refs = refs
    halves = refs[: abreast * len(windows)]
    if final:
        staged_ref, result_ref = refs[abreast * len(windows) :]
    fill_weights(spots_ref, weights_ref)
    for i, halves_ref in enumerate(halves):
        filled = len(windows[i % len(windows)][2]) * PHASES
        if filled < WIDE:
            halves_ref[filled:, :] = jnp.zeros((WIDE - filled, WIDE), BF16)

    def at(place, line):
        return (place, line) if along == 0 else (line, place)

    def one_line(line, parity):
        full = line_of(line)

        def cell(index, local):
            return lambda: pieces[index][at(local, full if whole[index] else line)]

        def put(place, value):
            if final:
                staged_ref[pl.ds((local_of(place) * final + line % final) * PHASES, PHASES), :] = value
            else:
                out_ref[at(local_of(place), line)] = value

        for i, (first, count, places) in enumerate(windows):
            steer_window(
                lambda place: dip_ref[at(place, full)],
                [cell(*place) for place in places],
                first, count, put, halves[parity * len(windows) + i], spots_ref, weights_ref,
            )

    def some_lines(i, _):
        for j in range(abreast):
            one_line(abreast * i + j, j)
        return 0

    if not final:
        lax.fori_loop(0, lines // abreast, some_lines, 0)
        copies = [
            pltpu.make_async_copy(out_ref.at[pick], edge_ref, sems.at[i])
            for i, (pick, edge_ref) in enumerate(zip(edges, edge_refs))
        ]
        for copy in copies:
            copy.start()
        for copy in copies:
            copy.wait()
        return

    outputs = sum(count for _, count, _ in windows)

    def copies_of(batch, slot):
        return [
            pltpu.make_async_copy(
                result_ref.at[slot, pl.ds(local_of(first), count)],
                out_ref.at[pl.ds(first, count), pl.ds(pl.multiple_of(batch * final, 8), final), :],
                sems.at[slot * len(windows) + i],
            )
            for i, (first, count, _) in enumerate(windows)
        ]

    for batch in range(lines // final):
        lax.fori_loop(batch * final // abreast, (batch + 1) * final // abreast, some_lines, 0)
        rows = jnp.concatenate(
            [
                jnp.concatenate(
                    [
                        staged_ref[pl.ds(eight * 8 * PHASES + phase, 8, stride=PHASES), :]
                        for phase in range(PHASES)
                    ],
                    axis=1,
                )
                for eight in range(outputs * final // 8)
            ],
            axis=0,
        )
        slot = batch % 2
        if batch >= 2:
            for copy in copies_of(batch - 2, slot):
                copy.wait()
        result_ref[slot] = move_samples(rows, table_ref[...]).reshape(result_ref.shape[1:])
        for copy in copies_of(batch, slot):
            copy.start()
    for batch in range(max(0, lines // final - 2), lines // final):
        for copy in copies_of(batch, batch % 2):
            copy.wait()


def steer(dip, pieces, along, lines, line_of, windows, local_of, edges=(), table=None, before=None, after=None):
    abreast = 2 if along else 4
    samples = PHASES * LANES
    outputs = sum(count for _, count, _ in windows)
    final = 16 if table is not None else 0
    operands = [dip] + [array for array, _ in pieces]
    in_specs = [SMEM] + [VMEM] * len(pieces)
    aliases = {}
    if final:
        operands.append(table)
        in_specs.append(VMEM)
        if before is not None:
            aliases = {len(operands): 0}
            operands.append(before)
            in_specs.append(HBM)
        out_shape = [jax.ShapeDtypeStruct((dip.shape[0], lines, samples), F32)]
        out_specs = [HBM]
    else:
        shape = (outputs, lines) if along == 0 else (lines, outputs)
        out_shape = [jax.ShapeDtypeStruct(shape + (PHASES, LANES), F32)]
        out_specs = [VMEM]
        for pick in edges:
            size = [len(range(*s.indices(n))) for s, n in zip(pick, shape)]
            out_shape.append(jax.ShapeDtypeStruct(tuple(size) + (PHASES, LANES), F32))
            out_specs.append(HBM)
    if after is not None:
        operands.append(after)
        in_specs.append(ANY)
    most = max(count for _, count, _ in windows)
    constant = pltpu.VMEM((most * PAIR, LANES), BF16)
    scratch = [constant, constant, pltpu.SemaphoreType.DMA((2 * len(windows) if final else max(1, len(edges)),))]
    scratch += [pltpu.VMEM((WIDE, WIDE), BF16)] * (abreast * len(windows))
    if final:
        scratch += [
            pltpu.VMEM((outputs * final * PHASES, LANES), F32),
            pltpu.VMEM((2, outputs, final, samples), F32),
        ]
    return pl.pallas_call(
        functools.partial(
            steer_kernel,
            along=along, whole=[whole for _, whole in pieces], lines=lines, line_of=line_of, windows=windows,
            local_of=local_of, edges=edges, final=final, chained=len(operands) - len(pieces) - 1 - bool(final), pieces_count=len(pieces), abreast=abreast,
        ),
        in_specs=in_specs,
        out_specs=out_specs,
        out_shape=out_shape,
        scratch_shapes=scratch,
        input_output_aliases=aliases,
        compiler_params=pltpu.CompilerParams(vmem_limit_bytes=16 * MIB),
        cost_estimate=pl.CostEstimate(
            flops=2400 * outputs * lines * samples,
            bytes_accessed=8 * outputs * lines * samples,
            transcendentals=0,
        ),
    )(*operands)


def swap_ends(head, tail, axis):
    count = lax.axis_size(axis)
    low = lax.ppermute(tail, axis, [(i, i + 1) for i in range(count - 1)])
    high = lax.ppermute(head, axis, [(i + 1, i) for i in range(count - 1)])
    return low, high


def span_of(index, first, count):
    return [(index, first + i) for i in range(count)]


def smooth(stacked, head, tail, along_rows, along_cols, table):
    rows, cols = stacked.shape[:2]
    mid_rows, mid_cols = rows - 2 * BORDER, cols - 2 * BORDER
    same = lambda line: line
    inner = lambda line: line + BORDER
    outer_col = lambda line: line + jnp.where(line < BORDER, 0, mid_cols)
    outer_row = lambda line: line + jnp.where(line < BORDER, 0, mid_rows)
    mid_place = lambda place: place - BORDER
    outer_place = lambda place: place if place < BORDER else place - mid_rows
    every = slice(None)
    lead, last = slice(0, HALF), slice(2 * BORDER - HALF, 2 * BORDER)

    def mid_windows(places):
        return [(BORDER + i, 16, places[i : i + 16 + 2 * HALF]) for i in range(0, mid_rows, 16)]

    low, high = swap_ends(head, tail, "inline")
    middle, head_mid, tail_mid = steer(
        along_rows, [(stacked, True)], 0, cols, same,
        mid_windows(span_of(0, BORDER - HALF, mid_rows + 2 * HALF)), mid_place,
        edges=[(every, lead), (every, slice(cols - HALF, cols))],
    )
    low_mid, high_mid = swap_ends(head_mid, tail_mid, "crosslin")
    pieces = [(low, True), (stacked, True), (high, True)]
    windows = [
        (0, BORDER, span_of(0, 0, HALF) + span_of(1, 0, BORDER + HALF)),
        (rows - BORDER, BORDER, span_of(1, rows - BORDER - HALF, BORDER + HALF) + span_of(2, 0, HALF)),
    ]
    corners, head_out, tail_out = steer(
        along_rows, pieces, 0, 2 * BORDER, outer_col, windows, outer_place, edges=[(every, lead), (every, last)],
        after=middle,
    )
    low_out, high_out = swap_ends(head_out, tail_out, "crosslin")
    (flanks,) = steer(along_rows, pieces, 0, mid_cols, inner, windows, outer_place, after=corners)

    def cross_windows(places):
        return [(i, 16, places[i : i + 16 + 2 * HALF]) for i in range(0, cols, 16)]

    places = span_of(0, 0, HALF) + span_of(1, 0, cols) + span_of(2, 0, HALF)
    (middle_second,) = steer(
        along_cols, [(low_mid, False), (middle, False), (high_mid, False)], 1, mid_rows, inner,
        cross_windows(places), same, after=flanks,
    )
    places = (
        span_of(0, 0, HALF) + span_of(1, 0, BORDER) + span_of(2, 0, mid_cols) + span_of(1, BORDER, BORDER) + span_of(3, 0, HALF)
    )
    border_second, head, tail = steer(
        along_cols, [(low_out, False), (corners, False), (flanks, False), (high_out, False)], 1, 2 * BORDER,
        outer_row, cross_windows(places), same, edges=[(lead, every), (last, every)], after=middle_second,
    )

    low, high = swap_ends(head, tail, "inline")
    places = span_of(0, BORDER - HALF, HALF) + span_of(1, 0, mid_rows) + span_of(0, BORDER, HALF)
    (result,) = steer(
        along_rows, [(border_second, True), (middle_second, True)], 0, cols, same, mid_windows(places), mid_place,
        table=table,
    )
    windows = [
        (0, BORDER, span_of(0, 0, HALF) + span_of(1, 0, BORDER) + span_of(2, 0, HALF)),
        (rows - BORDER, BORDER, span_of(2, mid_rows - HALF, HALF) + span_of(1, BORDER, BORDER) + span_of(3, 0, HALF)),
    ]
    (result,) = steer(
        along_rows, [(low, True), (border_second, True), (middle_second, True), (high, True)], 0, cols, same,
        windows, outer_place, table=table, before=result,
    )
    return result


def on_device(traces, destination, bin_index, dip_inline, dip_cross):
    held, block_rows, samples = traces.shape
    devices = lax.axis_size("inline") * lax.axis_size("crosslin")
    capacity = 2 * held // devices
    tile_rows, tile_cols = dip_inline.shape
    outgoing = pack(traces, destination.reshape(-1), bin_index.T, devices, capacity)
    arrived = lax.all_to_all(outgoing, BOTH, split_axis=0, concat_axis=0, tiled=True)
    stacked, head, tail = stack_bins(arrived, tile_rows, tile_cols, capacity, block_rows)
    back = jnp.asarray(interleave_table(samples).T, BF16)
    return smooth(stacked, head, tail, dip_inline, dip_cross, back)


def solution(mesh):
    return jax.shard_map(
        on_device,
        mesh=mesh,
        in_specs=(
            P(BOTH, None, None),
            P(BOTH, None),
            P(BOTH, None),
            P("inline", "crosslin"),
            P("inline", "crosslin"),
        ),
        out_specs=P("inline", "crosslin", None),
        check_vma=False,
    )
```

```python
import functools

import jax
import jax.numpy as jnp
import numpy as np
from jax import lax
from jax.experimental import pallas as pl
from jax.experimental.pallas import tpu as pltpu
from jax.sharding import PartitionSpec as P

HALF = 7
DMAX = 2
LANES = 128
PHASES = 8
PAIR = 2 * PHASES
WIDE = 2 * LANES
WINDOW = 16
DIPS = 2 * DMAX + 1
BORDER = 8
REACH = -(-HALF * DMAX // PHASES)
REACHES = range(-REACH, REACH + 1)
BOTH = ("inline", "crosslin")
MIB = 2**20
VMEM = pl.BlockSpec(memory_space=pltpu.VMEM)
SMEM = pl.BlockSpec(memory_space=pltpu.SMEM)
ANY = pl.BlockSpec(memory_space=pl.ANY)
HBM = pl.BlockSpec(memory_space=pltpu.HBM)
F32, BF16, I32 = jnp.float32, jnp.bfloat16, jnp.int32


def interleave_table(samples):
    table = np.zeros((samples, samples), np.float32)
    time = np.arange(samples)
    table[time, time % PHASES * LANES + time // PHASES] = 1.0
    return table


def move_samples(rows, table):
    count = rows.shape[0]
    upper = rows.astype(BF16)
    rest = (rows - upper.astype(F32)).astype(BF16)
    both = jnp.concatenate([upper, rest], axis=0)
    moved = jnp.dot(both, table, preferred_element_type=F32)
    return moved[:count] + moved[count:]


def fill_interleave(table_ref):
    size = table_ref.shape[0]
    time = lax.broadcasted_iota(I32, (size, LANES), 0)
    lane = lax.broadcasted_iota(I32, (size, LANES), 1)
    gap = time - lane * PHASES
    for phase in range(PHASES):
        table_ref[:, phase * LANES : (phase + 1) * LANES] = jnp.where(gap == phase, 1.0, 0.0).astype(BF16)


def pack_kernel(target_ref, bins_ref, traces_ref, out_ref, held_ref, table_ref, tiles_ref, used_ref, listed_ref, in_sems, sem, listed_sem, *, capacity):
    held, block_rows, samples = traces_ref.shape
    devices, room, _ = listed_ref.shape
    span = block_rows * PHASES
    groups = held_ref.shape[0]
    count = held // groups
    loads = [
        pltpu.make_async_copy(traces_ref.at[pl.ds(group * count, count)], held_ref.at[group], in_sems.at[group])
        for group in range(groups)
    ]
    for load in loads:
        load.start()
    fill_interleave(table_ref)
    lane = lax.broadcasted_iota(I32, (1, LANES), 1)
    listed_ref[...] = jnp.full(listed_ref.shape, -1.0, F32)

    def clear(device, _):
        used_ref[device] = 0
        return 0

    lax.fori_loop(0, devices, clear, 0)

    def send_block(block, _):
        device = target_ref[block]
        rank = used_ref[device]
        used_ref[device] = rank + 1
        pltpu.make_async_copy(
            tiles_ref.at[pl.ds(pl.multiple_of(block * span, 8), span), :],
            out_ref.at[device, pl.ds(pl.multiple_of(rank * span, 8), span), :],
            sem,
        ).start()
        row = jnp.zeros((1, LANES), I32)
        for j in range(block_rows):
            row = jnp.where(lane == j, bins_ref[j, block], row)
        listed_ref[device, pl.ds(rank, 1), :] = row.astype(F32)
        return 0

    for group in range(groups):
        loads[group].wait()
        rows = held_ref[group].reshape(count * block_rows, samples)
        moved = move_samples(rows, table_ref[...])
        for eight in range(count * block_rows // 8):
            for phase in range(PHASES):
                first = (group * count * block_rows + eight * 8) * PHASES + phase
                tiles_ref[pl.ds(first, 8, stride=PHASES), :] = moved[
                    eight * 8 : eight * 8 + 8, phase * LANES : (phase + 1) * LANES
                ]
        lax.fori_loop(group * count, (group + 1) * count, send_block, 0, unroll=4)
    copy = pltpu.make_async_copy(
        listed_ref, out_ref.at[:, capacity * span : capacity * span + room, :], listed_sem
    )
    copy.start()
    copy.wait()
    pltpu.make_async_copy(tiles_ref, tiles_ref, sem).wait()


def pack(traces, target, bins, devices, capacity):
    held, block_rows, samples = traces.shape
    span = block_rows * PHASES
    room = -(-capacity // 8) * 8
    groups = 2
    return pl.pallas_call(
        functools.partial(pack_kernel, capacity=capacity),
        in_specs=[SMEM, SMEM, HBM],
        out_specs=HBM,
        out_shape=jax.ShapeDtypeStruct((devices, capacity * span + room, LANES), F32),
        scratch_shapes=[
            pltpu.VMEM((groups, held // groups, block_rows, samples), F32),
            pltpu.VMEM((samples, samples), BF16),
            pltpu.VMEM((held * span, LANES), F32),
            pltpu.SMEM((devices,), I32),
            pltpu.VMEM((devices, room, LANES), F32),
            pltpu.SemaphoreType.DMA((groups,)),
            pltpu.SemaphoreType.DMA,
            pltpu.SemaphoreType.DMA,
        ],
        compiler_params=pltpu.CompilerParams(vmem_limit_bytes=60 * MIB),
    )(target, bins, traces)


def bin_kernel(bins_ref, scale_ref, blocks_ref, out_ref, head_ref, tail_ref, even_ref, odd_ref, sems, *, capacity, block_rows, edge):
    bin_total = out_ref.shape[0]
    unroll = 8
    nothing = jnp.zeros((PHASES, LANES), F32)

    def clear(i, _):
        for j in range(unroll):
            even_ref[i * unroll + j] = nothing
            odd_ref[i * unroll + j] = nothing
        return 0

    lax.fori_loop(0, bin_total // unroll, clear, 0)

    def add_sender(sender, _):
        first = sender * (capacity * block_rows)
        for i in range(capacity * block_rows):
            total_ref = odd_ref if i % 2 else even_ref
            total_ref[bins_ref[first + i]] += blocks_ref[sender, i * PHASES : (i + 1) * PHASES]
        return 0

    lax.fori_loop(0, blocks_ref.shape[0], add_sender, 0)

    def finish(i, _):
        for j in range(unroll):
            place = i * unroll + j
            out_ref[place] = (even_ref[place] + odd_ref[place]) * scale_ref[place]
        return 0

    lax.fori_loop(0, edge // unroll, finish, 0)
    head_copy = pltpu.make_async_copy(out_ref.at[pl.ds(0, edge)], head_ref, sems.at[0])
    head_copy.start()
    lax.fori_loop((bin_total - edge) // unroll, bin_total // unroll, finish, 0)
    tail_copy = pltpu.make_async_copy(out_ref.at[pl.ds(bin_total - edge, edge)], tail_ref, sems.at[1])
    tail_copy.start()
    lax.fori_loop(edge // unroll, (bin_total - edge) // unroll, finish, 0)
    head_copy.wait()
    tail_copy.wait()


def stack_bins(blocks, tile_rows, tile_cols, capacity, block_rows):
    bin_total = tile_rows * tile_cols
    edge = HALF * tile_cols
    rows = capacity * block_rows * PHASES
    listed = blocks[:, rows : rows + capacity, :block_rows].astype(I32)
    bins = jnp.where(listed < 0, bin_total, listed).reshape(-1)
    fold = jnp.sum((jnp.arange(bin_total, dtype=I32)[:, None] == bins[None, :]).astype(F32), axis=1)
    stacked, head, tail = pl.pallas_call(
        functools.partial(bin_kernel, capacity=capacity, block_rows=block_rows, edge=edge),
        in_specs=[SMEM, SMEM, VMEM],
        out_specs=[VMEM, HBM, HBM],
        out_shape=[
            jax.ShapeDtypeStruct((bin_total, PHASES, LANES), F32),
            jax.ShapeDtypeStruct((edge, PHASES, LANES), F32),
            jax.ShapeDtypeStruct((edge, PHASES, LANES), F32),
        ],
        scratch_shapes=[
            pltpu.VMEM((bin_total + 8, PHASES, LANES), F32),
            pltpu.VMEM((bin_total + 8, PHASES, LANES), F32),
            pltpu.SemaphoreType.DMA((2,)),
        ],
        compiler_params=pltpu.CompilerParams(vmem_limit_bytes=14 * MIB),
    )(bins, 1.0 / jnp.maximum(fold, 1.0), blocks)
    shape = (tile_cols, PHASES, LANES)
    return stacked.reshape((tile_rows,) + shape), head.reshape((HALF,) + shape), tail.reshape((HALF,) + shape)


def tap_tables():
    dips = np.arange(-DMAX, DMAX + 1)
    pair, dip, reach, member, phase, place, old = np.ogrid[
        : WINDOW // 2, -DMAX : DMAX + 1, -REACH : REACH + 1, :2, :PHASES, : WIDE // PHASES, :PHASES
    ]
    offset = place - HALF - 2 * pair - member
    hit = phase + dip * offset - old == reach * PHASES
    taps = np.where(hit, np.maximum(HALF + 1 - np.abs(offset), 0), 0) / float((HALF + 1) ** 2)
    count = len(dips)
    both = np.zeros((WINDOW // 2, count, count, len(REACHES), 2, PHASES, WIDE), np.float32)
    taps = taps.reshape(WINDOW // 2, count, len(REACHES), 2, PHASES, WIDE)
    both[:, :, :, :, 0] = taps[:, :, None, :, 0]
    both[:, :, :, :, 1] = taps[:, None, :, :, 1]
    return both.reshape(-1, len(REACHES) * PAIR, WIDE)


def steer_window(dip_of, cells, first, count, put, halves_ref, taps_ref):
    for pair in range(len(cells) // 2):
        both = jnp.concatenate([cells[2 * pair](), cells[2 * pair + 1]()], axis=0)
        upper = both.astype(BF16)
        halves_ref[pair * PAIR : (pair + 1) * PAIR, :LANES] = upper
        rest = (both - upper.astype(F32)).astype(BF16)
        halves_ref[pair * PAIR : (pair + 1) * PAIR, LANES:] = rest
    lane = lax.broadcasted_iota(I32, (PHASES, LANES), 1)
    taps = []
    for pair in range(count // 2):
        chosen = (pair * DIPS + dip_of(first + 2 * pair) + DMAX) * DIPS + dip_of(first + 2 * pair + 1) + DMAX
        taps.append(taps_ref[chosen])
    sums = jnp.dot(jnp.concatenate(taps, axis=0), halves_ref[...], preferred_element_type=F32)
    for pair in range(count // 2):
        for member in range(2):
            total = None
            for reach in REACHES:
                begin = (pair * len(REACHES) + reach + REACH) * PAIR + member * PHASES
                part = sums[begin : begin + PHASES, :LANES] + sums[begin : begin + PHASES, LANES:]
                if reach:
                    part = pltpu.roll(part, (-reach) % LANES, axis=1)
                    inside = lane < LANES - reach if reach > 0 else lane >= -reach
                    part = jnp.where(inside, part, 0.0)
                total = part if total is None else total + part
            put(first + 2 * pair + member, total)


def steer_kernel(dip_ref, taps_ref, *refs, along, whole, lines, line_of, windows, local_of, edges, final, chained, pieces_count, abreast):
    pieces, refs = refs[:pieces_count], refs[pieces_count:]
    if final:
        table_ref, refs = refs[0], refs[1:]
    refs = refs[chained:]
    out_ref, refs = refs[0], refs[1:]
    edge_refs, refs = refs[: len(edges)], refs[len(edges) :]
    sems, *refs = refs
    halves = refs[: abreast * len(windows)]
    if final:
        staged_ref, result_ref = refs[abreast * len(windows) :]
    for i, halves_ref in enumerate(halves):
        filled = len(windows[i % len(windows)][2]) * PHASES
        if filled < WIDE:
            halves_ref[filled:, :] = jnp.zeros((WIDE - filled, WIDE), BF16)

    def at(place, line):
        return (place, line) if along == 0 else (line, place)

    def one_line(line, parity):
        full = line_of(line)

        def cell(index, local):
            return lambda: pieces[index][at(local, full if whole[index] else line)]

        def put(place, value):
            if final:
                staged_ref[pl.ds((local_of(place) * final + line % final) * PHASES, PHASES), :] = value
            else:
                out_ref[at(local_of(place), line)] = value

        for i, (first, count, places) in enumerate(windows):
            steer_window(
                lambda place: dip_ref[at(place, full)],
                [cell(*place) for place in places],
                first, count, put, halves[parity * len(windows) + i], taps_ref,
            )

    def some_lines(i, _):
        for j in range(abreast):
            one_line(abreast * i + j, j)
        return 0

    if not final:
        lax.fori_loop(0, lines // abreast, some_lines, 0)
        copies = [
            pltpu.make_async_copy(out_ref.at[pick], edge_ref, sems.at[i])
            for i, (pick, edge_ref) in enumerate(zip(edges, edge_refs))
        ]
        for copy in copies:
            copy.start()
        for copy in copies:
            copy.wait()
        return

    outputs = sum(count for _, count, _ in windows)

    def copies_of(batch, slot):
        return [
            pltpu.make_async_copy(
                result_ref.at[slot, pl.ds(local_of(first), count)],
                out_ref.at[pl.ds(first, count), pl.ds(pl.multiple_of(batch * final, 8), final), :],
                sems.at[slot * len(windows) + i],
            )
            for i, (first, count, _) in enumerate(windows)
        ]

    for batch in range(lines // final):
        lax.fori_loop(batch * final // abreast, (batch + 1) * final // abreast, some_lines, 0)
        rows = jnp.concatenate(
            [
                jnp.concatenate(
                    [
                        staged_ref[pl.ds(eight * 8 * PHASES + phase, 8, stride=PHASES), :]
                        for phase in range(PHASES)
                    ],
                    axis=1,
                )
                for eight in range(outputs * final // 8)
            ],
            axis=0,
        )
        slot = batch % 2
        if batch >= 2:
            for copy in copies_of(batch - 2, slot):
                copy.wait()
        result_ref[slot] = move_samples(rows, table_ref[...]).reshape(result_ref.shape[1:])
        for copy in copies_of(batch, slot):
            copy.start()
    for batch in range(max(0, lines // final - 2), lines // final):
        for copy in copies_of(batch, batch % 2):
            copy.wait()


def steer(dip, taps, pieces, along, lines, line_of, windows, local_of, edges=(), table=None, before=None, after=None):
    abreast = 2 if along else 4
    samples = PHASES * LANES
    outputs = sum(count for _, count, _ in windows)
    final = 16 if table is not None else 0
    operands = [dip, taps] + [array for array, _ in pieces]
    in_specs = [SMEM, VMEM] + [VMEM] * len(pieces)
    aliases = {}
    if final:
        operands.append(table)
        in_specs.append(VMEM)
        if before is not None:
            aliases = {len(operands): 0}
            operands.append(before)
            in_specs.append(HBM)
        out_shape = [jax.ShapeDtypeStruct((dip.shape[0], lines, samples), F32)]
        out_specs = [HBM]
    else:
        shape = (outputs, lines) if along == 0 else (lines, outputs)
        out_shape = [jax.ShapeDtypeStruct(shape + (PHASES, LANES), F32)]
        out_specs = [VMEM]
        for pick in edges:
            size = [len(range(*s.indices(n))) for s, n in zip(pick, shape)]
            out_shape.append(jax.ShapeDtypeStruct(tuple(size) + (PHASES, LANES), F32))
            out_specs.append(HBM)
    if after is not None:
        operands.append(after)
        in_specs.append(ANY)
    scratch = [pltpu.SemaphoreType.DMA((2 * len(windows) if final else max(1, len(edges)),))]
    scratch += [pltpu.VMEM((WIDE, WIDE), BF16)] * (abreast * len(windows))
    if final:
        scratch += [
            pltpu.VMEM((outputs * final * PHASES, LANES), F32),
            pltpu.VMEM((2, outputs, final, samples), F32),
        ]
    return pl.pallas_call(
        functools.partial(
            steer_kernel,
            along=along, whole=[whole for _, whole in pieces], lines=lines, line_of=line_of, windows=windows,
            local_of=local_of, edges=edges, final=final, chained=len(operands) - len(pieces) - 2 - bool(final), pieces_count=len(pieces), abreast=abreast,
        ),
        in_specs=in_specs,
        out_specs=out_specs,
        out_shape=out_shape,
        scratch_shapes=scratch,
        input_output_aliases=aliases,
        compiler_params=pltpu.CompilerParams(vmem_limit_bytes=16 * MIB),
        cost_estimate=pl.CostEstimate(
            flops=2400 * outputs * lines * samples,
            bytes_accessed=8 * outputs * lines * samples,
            transcendentals=0,
        ),
    )(*operands)


def swap_ends(head, tail, axis):
    count = lax.axis_size(axis)
    low = lax.ppermute(tail, axis, [(i, i + 1) for i in range(count - 1)])
    high = lax.ppermute(head, axis, [(i + 1, i) for i in range(count - 1)])
    return low, high


def span_of(index, first, count):
    return [(index, first + i) for i in range(count)]


def smooth(stacked, head, tail, along_rows, along_cols, taps, table):
    rows, cols = stacked.shape[:2]
    mid_rows, mid_cols = rows - 2 * BORDER, cols - 2 * BORDER
    same = lambda line: line
    inner = lambda line: line + BORDER
    outer_col = lambda line: line + jnp.where(line < BORDER, 0, mid_cols)
    outer_row = lambda line: line + jnp.where(line < BORDER, 0, mid_rows)
    mid_place = lambda place: place - BORDER
    outer_place = lambda place: place if place < BORDER else place - mid_rows
    every = slice(None)
    lead, last = slice(0, HALF), slice(2 * BORDER - HALF, 2 * BORDER)

    def mid_windows(places):
        return [(BORDER + i, WINDOW, places[i : i + WINDOW + 2 * HALF]) for i in range(0, mid_rows, WINDOW)]

    low, high = swap_ends(head, tail, "inline")
    middle, head_mid, tail_mid = steer(
        along_rows, taps, [(stacked, True)], 0, cols, same,
        mid_windows(span_of(0, BORDER - HALF, mid_rows + 2 * HALF)), mid_place,
        edges=[(every, lead), (every, slice(cols - HALF, cols))],
    )
    low_mid, high_mid = swap_ends(head_mid, tail_mid, "crosslin")
    pieces = [(low, True), (stacked, True), (high, True)]
    windows = [
        (0, BORDER, span_of(0, 0, HALF) + span_of(1, 0, BORDER + HALF)),
        (rows - BORDER, BORDER, span_of(1, rows - BORDER - HALF, BORDER + HALF) + span_of(2, 0, HALF)),
    ]
    corners, head_out, tail_out = steer(
        along_rows, taps, pieces, 0, 2 * BORDER, outer_col, windows, outer_place, edges=[(every, lead), (every, last)],
        after=middle,
    )
    low_out, high_out = swap_ends(head_out, tail_out, "crosslin")
    (flanks,) = steer(along_rows, taps, pieces, 0, mid_cols, inner, windows, outer_place, after=corners)

    def cross_windows(places):
        return [(i, WINDOW, places[i : i + WINDOW + 2 * HALF]) for i in range(0, cols, WINDOW)]

    places = span_of(0, 0, HALF) + span_of(1, 0, cols) + span_of(2, 0, HALF)
    (middle_second,) = steer(
        along_cols, taps, [(low_mid, False), (middle, False), (high_mid, False)], 1, mid_rows, inner,
        cross_windows(places), same, after=flanks,
    )
    places = (
        span_of(0, 0, HALF) + span_of(1, 0, BORDER) + span_of(2, 0, mid_cols) + span_of(1, BORDER, BORDER) + span_of(3, 0, HALF)
    )
    border_second, head, tail = steer(
        along_cols, taps, [(low_out, False), (corners, False), (flanks, False), (high_out, False)], 1, 2 * BORDER,
        outer_row, cross_windows(places), same, edges=[(lead, every), (last, every)], after=middle_second,
    )

    low, high = swap_ends(head, tail, "inline")
    places = span_of(0, BORDER - HALF, HALF) + span_of(1, 0, mid_rows) + span_of(0, BORDER, HALF)
    (result,) = steer(
        along_rows, taps, [(border_second, True), (middle_second, True)], 0, cols, same, mid_windows(places), mid_place,
        table=table,
    )
    windows = [
        (0, BORDER, span_of(0, 0, HALF) + span_of(1, 0, BORDER) + span_of(2, 0, HALF)),
        (rows - BORDER, BORDER, span_of(2, mid_rows - HALF, HALF) + span_of(1, BORDER, BORDER) + span_of(3, 0, HALF)),
    ]
    (result,) = steer(
        along_rows, taps, [(low, True), (border_second, True), (middle_second, True), (high, True)], 0, cols, same,
        windows, outer_place, table=table, before=result,
    )
    return result


def on_device(traces, destination, bin_index, dip_inline, dip_cross):
    held, block_rows, samples = traces.shape
    devices = lax.axis_size("inline") * lax.axis_size("crosslin")
    capacity = 2 * held // devices
    tile_rows, tile_cols = dip_inline.shape
    outgoing = pack(traces, destination.reshape(-1), bin_index.T, devices, capacity)
    arrived = lax.all_to_all(outgoing, BOTH, split_axis=0, concat_axis=0, tiled=True)
    stacked, head, tail = stack_bins(arrived, tile_rows, tile_cols, capacity, block_rows)
    back = jnp.asarray(interleave_table(samples).T, BF16)
    return smooth(stacked, head, tail, dip_inline, dip_cross, jnp.asarray(tap_tables(), BF16), back)


def solution(mesh):
    return jax.shard_map(
        on_device,
        mesh=mesh,
        in_specs=(
            P(BOTH, None, None),
            P(BOTH, None),
            P(BOTH, None),
            P("inline", "crosslin"),
            P("inline", "crosslin"),
        ),
        out_specs=P("inline", "crosslin", None),
        check_vma=False,
    )
```

```python
import functools

import jax
import jax.numpy as jnp
import numpy as np
from jax import lax
from jax.experimental import pallas as pl
from jax.experimental.pallas import tpu as pltpu
from jax.sharding import PartitionSpec as P

HALF = 7
DMAX = 2
LANES = 128
PHASES = 8
PAIR = 2 * PHASES
WIDE = 2 * LANES
BORDER = 8
REACH = -(-HALF * DMAX // PHASES)
REACHES = range(-REACH, REACH + 1)
BOTH = ("inline", "crosslin")
MIB = 2**20
VMEM = pl.BlockSpec(memory_space=pltpu.VMEM)
SMEM = pl.BlockSpec(memory_space=pltpu.SMEM)
ANY = pl.BlockSpec(memory_space=pl.ANY)
HBM = pl.BlockSpec(memory_space=pltpu.HBM)
F32, BF16, I32 = jnp.float32, jnp.bfloat16, jnp.int32


def interleave_table(samples):
    table = np.zeros((samples, samples), np.float32)
    time = np.arange(samples)
    table[time, time % PHASES * LANES + time // PHASES] = 1.0
    return table


def move_samples(rows, table):
    count = rows.shape[0]
    upper = rows.astype(BF16)
    rest = (rows - upper.astype(F32)).astype(BF16)
    both = jnp.concatenate([upper, rest], axis=0)
    moved = jnp.dot(both, table, preferred_element_type=F32)
    return moved[:count] + moved[count:]


def fill_interleave(table_ref):
    size = table_ref.shape[0]
    time = lax.broadcasted_iota(I32, (size, LANES), 0)
    lane = lax.broadcasted_iota(I32, (size, LANES), 1)
    gap = time - lane * PHASES
    for phase in range(PHASES):
        table_ref[:, phase * LANES : (phase + 1) * LANES] = jnp.where(gap == phase, 1.0, 0.0).astype(BF16)


def pack_kernel(target_ref, bins_ref, traces_ref, out_ref, held_ref, table_ref, tiles_ref, used_ref, listed_ref, in_sems, sem, listed_sem, *, capacity):
    held, block_rows, samples = traces_ref.shape
    devices, room, _ = listed_ref.shape
    span = block_rows * PHASES
    groups = held_ref.shape[0]
    count = held // groups
    loads = [
        pltpu.make_async_copy(traces_ref.at[pl.ds(group * count, count)], held_ref.at[group], in_sems.at[group])
        for group in range(groups)
    ]
    for load in loads:
        load.start()
    fill_interleave(table_ref)
    lane = lax.broadcasted_iota(I32, (1, LANES), 1)
    listed_ref[...] = jnp.full(listed_ref.shape, -1.0, F32)

    def clear(device, _):
        used_ref[device] = 0
        return 0

    lax.fori_loop(0, devices, clear, 0)

    def send_block(block, _):
        device = target_ref[block]
        rank = used_ref[device]
        used_ref[device] = rank + 1
        pltpu.make_async_copy(
            tiles_ref.at[pl.ds(pl.multiple_of(block * span, 8), span), :],
            out_ref.at[device, pl.ds(pl.multiple_of(rank * span, 8), span), :],
            sem,
        ).start()
        row = jnp.zeros((1, LANES), I32)
        for j in range(block_rows):
            row = jnp.where(lane == j, bins_ref[j, block], row)
        listed_ref[device, pl.ds(rank, 1), :] = row.astype(F32)
        return 0

    for group in range(groups):
        loads[group].wait()
        rows = held_ref[group].reshape(count * block_rows, samples)
        moved = move_samples(rows, table_ref[...])
        for eight in range(count * block_rows // 8):
            for phase in range(PHASES):
                first = (group * count * block_rows + eight * 8) * PHASES + phase
                tiles_ref[pl.ds(first, 8, stride=PHASES), :] = moved[
                    eight * 8 : eight * 8 + 8, phase * LANES : (phase + 1) * LANES
                ]
        lax.fori_loop(group * count, (group + 1) * count, send_block, 0, unroll=4)
    copy = pltpu.make_async_copy(
        listed_ref, out_ref.at[:, capacity * span : capacity * span + room, :], listed_sem
    )
    copy.start()
    copy.wait()
    pltpu.make_async_copy(tiles_ref, tiles_ref, sem).wait()


def pack(traces, target, bins, devices, capacity):
    held, block_rows, samples = traces.shape
    span = block_rows * PHASES
    room = -(-capacity // 8) * 8
    groups = 2
    return pl.pallas_call(
        functools.partial(pack_kernel, capacity=capacity),
        in_specs=[SMEM, SMEM, HBM],
        out_specs=HBM,
        out_shape=jax.ShapeDtypeStruct((devices, capacity * span + room, LANES), F32),
        scratch_shapes=[
            pltpu.VMEM((groups, held // groups, block_rows, samples), F32),
            pltpu.VMEM((samples, samples), BF16),
            pltpu.VMEM((held * span, LANES), F32),
            pltpu.SMEM((devices,), I32),
            pltpu.VMEM((devices, room, LANES), F32),
            pltpu.SemaphoreType.DMA((groups,)),
            pltpu.SemaphoreType.DMA,
            pltpu.SemaphoreType.DMA,
        ],
        compiler_params=pltpu.CompilerParams(vmem_limit_bytes=60 * MIB),
    )(target, bins, traces)


def bin_kernel(blocks_ref, out_ref, head_ref, tail_ref, even_ref, odd_ref, listed_ref, places_ref, scale_ref, scales_ref, sems, *, capacity, block_rows, edge):
    devices, rows, _ = blocks_ref.shape
    room = listed_ref.shape[1]
    bin_total = out_ref.shape[0]
    unroll = 8
    listed = blocks_ref[:, rows - room :, :]
    listed_ref[...] = jnp.where(listed < 0, float(bin_total), listed).astype(I32)
    copy = pltpu.make_async_copy(listed_ref, places_ref, sems.at[0])
    copy.start()
    nothing = jnp.zeros((PHASES, LANES), F32)

    def clear(i, _):
        for j in range(unroll):
            even_ref[i * unroll + j] = nothing
            odd_ref[i * unroll + j] = nothing
        return 0

    lax.fori_loop(0, bin_total // unroll, clear, 0)
    copy.wait()
    count_rows = scale_ref.shape[0]
    numbers = lax.broadcasted_iota(I32, (count_rows, LANES), 0) * LANES + lax.broadcasted_iota(
        I32, (count_rows, LANES), 1
    )

    def add_sender(sender, folds):
        folds = list(folds)
        for rank in range(capacity):
            for j in range(block_rows):
                total_ref = odd_ref if j % 2 else even_ref
                place = places_ref[sender, rank, j]
                row = (rank * block_rows + j) * PHASES
                total_ref[place] += blocks_ref[sender, row : row + PHASES, :]
                folds[j % 2] = folds[j % 2] + jnp.where(numbers == place, 1.0, 0.0)
        return tuple(folds)

    empty = jnp.zeros((count_rows, LANES), F32)
    folds = lax.fori_loop(0, devices, add_sender, (empty, empty))
    scale_ref[...] = 1.0 / jnp.maximum(folds[0] + folds[1], 1.0)
    copy = pltpu.make_async_copy(scale_ref, scales_ref, sems.at[0])
    copy.start()
    copy.wait()

    def finish(i, _):
        for j in range(unroll):
            place = i * unroll + j
            scale = scales_ref[place // LANES, place % LANES]
            out_ref[place] = (even_ref[place] + odd_ref[place]) * scale
        return 0

    lax.fori_loop(0, edge // unroll, finish, 0)
    head_copy = pltpu.make_async_copy(out_ref.at[pl.ds(0, edge)], head_ref, sems.at[1])
    head_copy.start()
    lax.fori_loop((bin_total - edge) // unroll, bin_total // unroll, finish, 0)
    tail_copy = pltpu.make_async_copy(out_ref.at[pl.ds(bin_total - edge, edge)], tail_ref, sems.at[2])
    tail_copy.start()
    lax.fori_loop(edge // unroll, (bin_total - edge) // unroll, finish, 0)
    head_copy.wait()
    tail_copy.wait()


def stack_bins(blocks, tile_rows, tile_cols, capacity, block_rows):
    devices = blocks.shape[0]
    bin_total = tile_rows * tile_cols
    edge = HALF * tile_cols
    room = blocks.shape[1] - capacity * block_rows * PHASES
    stacked, head, tail = pl.pallas_call(
        functools.partial(bin_kernel, capacity=capacity, block_rows=block_rows, edge=edge),
        in_specs=[VMEM],
        out_specs=[VMEM, HBM, HBM],
        out_shape=[
            jax.ShapeDtypeStruct((bin_total, PHASES, LANES), F32),
            jax.ShapeDtypeStruct((edge, PHASES, LANES), F32),
            jax.ShapeDtypeStruct((edge, PHASES, LANES), F32),
        ],
        scratch_shapes=[
            pltpu.VMEM((bin_total + 8, PHASES, LANES), F32),
            pltpu.VMEM((bin_total + 8, PHASES, LANES), F32),
            pltpu.VMEM((devices, room, LANES), I32),
            pltpu.SMEM((devices, room, LANES), I32),
            pltpu.VMEM((bin_total // LANES, LANES), F32),
            pltpu.SMEM((bin_total // LANES, LANES), F32),
            pltpu.SemaphoreType.DMA((3,)),
        ],
        compiler_params=pltpu.CompilerParams(vmem_limit_bytes=14 * MIB),
    )(blocks)
    shape = (tile_cols, PHASES, LANES)
    return stacked.reshape((tile_rows,) + shape), head.reshape((HALF,) + shape), tail.reshape((HALF,) + shape)


def fill_weights(spots_ref, weights_ref):
    row = lax.broadcasted_iota(I32, (PAIR, LANES), 0)
    column = lax.broadcasted_iota(I32, (PAIR, LANES), 1)
    for pair in range(spots_ref.shape[0] // (2 * PAIR)):
        for half in range(2):
            block = pl.ds((pair * 2 + half) * PAIR, PAIR)
            spot = half * PAIR + column // PHASES - HALF - 2 * pair - row // PHASES
            share = jnp.maximum(HALF + 1 - jnp.abs(spot), 0).astype(F32) / (HALF + 1) ** 2
            spots_ref[block, :] = jnp.clip(spot, -HALF - 1, HALF + 1).astype(F32).astype(BF16)
            weights_ref[block, :] = share.astype(BF16)


def split_cells(cells, halves_ref):
    for pair in range(len(cells) // 2):
        both = jnp.concatenate([cells[2 * pair](), cells[2 * pair + 1]()], axis=0)
        upper = both.astype(BF16)
        halves_ref[pair * PAIR : (pair + 1) * PAIR, :LANES] = upper
        rest = (both - upper.astype(F32)).astype(BF16)
        halves_ref[pair * PAIR : (pair + 1) * PAIR, LANES:] = rest


def apply_taps(dip_of, first, count, halves_ref, spots_ref, weights_ref):
    row = lax.broadcasted_iota(I32, (PAIR, LANES), 0)
    column = lax.broadcasted_iota(I32, (PAIR, LANES), 1)
    phase_gap = ((row & (PHASES - 1)) - (column & (PHASES - 1))).astype(F32).astype(BF16)
    none = jnp.zeros((PAIR, LANES), BF16)
    taps = []
    for pair in range(count // 2):
        dip = jnp.concatenate(
            [jnp.full((PHASES, LANES), dip_of(first + 2 * pair + i).astype(F32)) for i in range(2)], axis=0
        ).astype(BF16)
        moves, weights = [], []
        for half in range(2):
            block = pl.ds((pair * 2 + half) * PAIR, PAIR)
            moves.append(phase_gap + dip * spots_ref[block, :])
            weights.append(weights_ref[block, :])
        for reach in REACHES:
            taps.append(
                jnp.concatenate(
                    [jnp.where(moves[h] == jnp.bfloat16(reach * PHASES), weights[h], none) for h in range(2)],
                    axis=1,
                )
            )
    return jnp.dot(jnp.concatenate(taps, axis=0), halves_ref[...], preferred_element_type=F32)


def move_lanes(sums, first, count, put):
    lane = lax.broadcasted_iota(I32, (PHASES, LANES), 1)
    for pair in range(count // 2):
        for member in range(2):
            total = None
            for reach in REACHES:
                begin = (pair * len(REACHES) + reach + REACH) * PAIR + member * PHASES
                part = sums[begin : begin + PHASES, :LANES] + sums[begin : begin + PHASES, LANES:]
                if reach:
                    part = pltpu.roll(part, (-reach) % LANES, axis=1)
                    inside = lane < LANES - reach if reach > 0 else lane >= -reach
                    part = jnp.where(inside, part, 0.0)
                total = part if total is None else total + part
            put(first + 2 * pair + member, total)


def steer_kernel(dip_ref, *refs, along, whole, lines, line_of, windows, local_of, edges, final, chained, pieces_count, abreast):
    pieces, refs = refs[:pieces_count], refs[pieces_count:]
    if final:
        table_ref, refs = refs[0], refs[1:]
    refs = refs[chained:]
    out_ref, refs = refs[0], refs[1:]
    edge_refs, refs = refs[: len(edges)], refs[len(edges) :]
    spots_ref, weights_ref, sems, *refs = refs
    halves = refs[: abreast * len(windows)]
    if final:
        staged_ref, result_ref = refs[abreast * len(windows) :]
    fill_weights(spots_ref, weights_ref)
    for i, halves_ref in enumerate(halves):
        filled = len(windows[i % len(windows)][2]) * PHASES
        if filled < WIDE:
            halves_ref[filled:, :] = jnp.zeros((WIDE - filled, WIDE), BF16)

    def at(place, line):
        return (place, line) if along == 0 else (line, place)

    def some_lines(step, _):
        jobs = []
        for parity in range(abreast):
            line = abreast * step + parity
            full = line_of(line)

            def cell(index, local, line=line, full=full):
                return lambda: pieces[index][at(local, full if whole[index] else line)]

            def put(place, value, line=line):
                if final:
                    staged_ref[pl.ds((local_of(place) * final + line % final) * PHASES, PHASES), :] = value
                else:
                    out_ref[at(local_of(place), line)] = value

            for i, (first, count, places) in enumerate(windows):
                halves_ref = halves[parity * len(windows) + i]
                split_cells([cell(*place) for place in places], halves_ref)
                jobs.append((full, first, count, halves_ref, put))
        waiting = None
        for full, first, count, halves_ref, put in jobs:
            sums = apply_taps(
                lambda place: dip_ref[at(place, full)], first, count, halves_ref, spots_ref, weights_ref
            )
            if waiting is not None:
                move_lanes(*waiting)
            waiting = (sums, first, count, put)
        move_lanes(*waiting)
        return 0

    if not final:
        lax.fori_loop(0, lines // abreast, some_lines, 0)
        copies = [
            pltpu.make_async_copy(out_ref.at[pick], edge_ref, sems.at[i])
            for i, (pick, edge_ref) in enumerate(zip(edges, edge_refs))
        ]
        for copy in copies:
            copy.start()
        for copy in copies:
            copy.wait()
        return

    outputs = sum(count for _, count, _ in windows)

    def copies_of(batch, slot):
        return [
            pltpu.make_async_copy(
                result_ref.at[slot, pl.ds(local_of(first), count)],
                out_ref.at[pl.ds(first, count), pl.ds(pl.multiple_of(batch * final, 8), final), :],
                sems.at[slot * len(windows) + i],
            )
            for i, (first, count, _) in enumerate(windows)
        ]

    for batch in range(lines // final):
        lax.fori_loop(batch * final // abreast, (batch + 1) * final // abreast, some_lines, 0)
        rows = jnp.concatenate(
            [
                jnp.concatenate(
                    [
                        staged_ref[pl.ds(eight * 8 * PHASES + phase, 8, stride=PHASES), :]
                        for phase in range(PHASES)
                    ],
                    axis=1,
                )
                for eight in range(outputs * final // 8)
            ],
            axis=0,
        )
        slot = batch % 2
        if batch >= 2:
            for copy in copies_of(batch - 2, slot):
                copy.wait()
        result_ref[slot] = move_samples(rows, table_ref[...]).reshape(result_ref.shape[1:])
        for copy in copies_of(batch, slot):
            copy.start()
    for batch in range(max(0, lines // final - 2), lines // final):
        for copy in copies_of(batch, batch % 2):
            copy.wait()


def steer(dip, pieces, along, lines, line_of, windows, local_of, edges=(), table=None, before=None, after=None):
    abreast = 2 if along else 4
    samples = PHASES * LANES
    outputs = sum(count for _, count, _ in windows)
    final = 16 if table is not None else 0
    operands = [dip] + [array for array, _ in pieces]
    in_specs = [SMEM] + [VMEM] * len(pieces)
    aliases = {}
    if final:
        operands.append(table)
        in_specs.append(VMEM)
        if before is not None:
            aliases = {len(operands): 0}
            operands.append(before)
            in_specs.append(HBM)
        out_shape = [jax.ShapeDtypeStruct((dip.shape[0], lines, samples), F32)]
        out_specs = [HBM]
    else:
        shape = (outputs, lines) if along == 0 else (lines, outputs)
        out_shape = [jax.ShapeDtypeStruct(shape + (PHASES, LANES), F32)]
        out_specs = [VMEM]
        for pick in edges:
            size = [len(range(*s.indices(n))) for s, n in zip(pick, shape)]
            out_shape.append(jax.ShapeDtypeStruct(tuple(size) + (PHASES, LANES), F32))
            out_specs.append(HBM)
    if after is not None:
        operands.append(after)
        in_specs.append(ANY)
    most = max(count for _, count, _ in windows)
    constant = pltpu.VMEM((most * PAIR, LANES), BF16)
    scratch = [constant, constant, pltpu.SemaphoreType.DMA((2 * len(windows) if final else max(1, len(edges)),))]
    scratch += [pltpu.VMEM((WIDE, WIDE), BF16)] * (abreast * len(windows))
    if final:
        scratch += [
            pltpu.VMEM((outputs * final * PHASES, LANES), F32),
            pltpu.VMEM((2, outputs, final, samples), F32),
        ]
    return pl.pallas_call(
        functools.partial(
            steer_kernel,
            along=along, whole=[whole for _, whole in pieces], lines=lines, line_of=line_of, windows=windows,
            local_of=local_of, edges=edges, final=final, chained=len(operands) - len(pieces) - 1 - bool(final), pieces_count=len(pieces), abreast=abreast,
        ),
        in_specs=in_specs,
        out_specs=out_specs,
        out_shape=out_shape,
        scratch_shapes=scratch,
        input_output_aliases=aliases,
        compiler_params=pltpu.CompilerParams(vmem_limit_bytes=16 * MIB),
        cost_estimate=pl.CostEstimate(
            flops=2400 * outputs * lines * samples,
            bytes_accessed=8 * outputs * lines * samples,
            transcendentals=0,
        ),
    )(*operands)


def swap_ends(head, tail, axis):
    count = lax.axis_size(axis)
    low = lax.ppermute(tail, axis, [(i, i + 1) for i in range(count - 1)])
    high = lax.ppermute(head, axis, [(i + 1, i) for i in range(count - 1)])
    return low, high


def span_of(index, first, count):
    return [(index, first + i) for i in range(count)]


def smooth(stacked, head, tail, along_rows, along_cols, table):
    rows, cols = stacked.shape[:2]
    mid_rows, mid_cols = rows - 2 * BORDER, cols - 2 * BORDER
    same = lambda line: line
    inner = lambda line: line + BORDER
    outer_col = lambda line: line + jnp.where(line < BORDER, 0, mid_cols)
    outer_row = lambda line: line + jnp.where(line < BORDER, 0, mid_rows)
    mid_place = lambda place: place - BORDER
    outer_place = lambda place: place if place < BORDER else place - mid_rows
    every = slice(None)
    lead, last = slice(0, HALF), slice(2 * BORDER - HALF, 2 * BORDER)

    def mid_windows(places):
        return [(BORDER + i, 16, places[i : i + 16 + 2 * HALF]) for i in range(0, mid_rows, 16)]

    low, high = swap_ends(head, tail, "inline")
    middle, head_mid, tail_mid = steer(
        along_rows, [(stacked, True)], 0, cols, same,
        mid_windows(span_of(0, BORDER - HALF, mid_rows + 2 * HALF)), mid_place,
        edges=[(every, lead), (every, slice(cols - HALF, cols))],
    )
    low_mid, high_mid = swap_ends(head_mid, tail_mid, "crosslin")
    pieces = [(low, True), (stacked, True), (high, True)]
    windows = [
        (0, BORDER, span_of(0, 0, HALF) + span_of(1, 0, BORDER + HALF)),
        (rows - BORDER, BORDER, span_of(1, rows - BORDER - HALF, BORDER + HALF) + span_of(2, 0, HALF)),
    ]
    corners, head_out, tail_out = steer(
        along_rows, pieces, 0, 2 * BORDER, outer_col, windows, outer_place, edges=[(every, lead), (every, last)],
        after=middle,
    )
    low_out, high_out = swap_ends(head_out, tail_out, "crosslin")
    (flanks,) = steer(along_rows, pieces, 0, mid_cols, inner, windows, outer_place, after=corners)

    def cross_windows(places):
        return [(i, 16, places[i : i + 16 + 2 * HALF]) for i in range(0, cols, 16)]

    places = span_of(0, 0, HALF) + span_of(1, 0, cols) + span_of(2, 0, HALF)
    (middle_second,) = steer(
        along_cols, [(low_mid, False), (middle, False), (high_mid, False)], 1, mid_rows, inner,
        cross_windows(places), same, after=flanks,
    )
    places = (
        span_of(0, 0, HALF) + span_of(1, 0, BORDER) + span_of(2, 0, mid_cols) + span_of(1, BORDER, BORDER) + span_of(3, 0, HALF)
    )
    border_second, head, tail = steer(
        along_cols, [(low_out, False), (corners, False), (flanks, False), (high_out, False)], 1, 2 * BORDER,
        outer_row, cross_windows(places), same, edges=[(lead, every), (last, every)], after=middle_second,
    )

    low, high = swap_ends(head, tail, "inline")
    places = span_of(0, BORDER - HALF, HALF) + span_of(1, 0, mid_rows) + span_of(0, BORDER, HALF)
    (result,) = steer(
        along_rows, [(border_second, True), (middle_second, True)], 0, cols, same, mid_windows(places), mid_place,
        table=table,
    )
    windows = [
        (0, BORDER, span_of(0, 0, HALF) + span_of(1, 0, BORDER) + span_of(2, 0, HALF)),
        (rows - BORDER, BORDER, span_of(2, mid_rows - HALF, HALF) + span_of(1, BORDER, BORDER) + span_of(3, 0, HALF)),
    ]
    (result,) = steer(
        along_rows, [(low, True), (border_second, True), (middle_second, True), (high, True)], 0, cols, same,
        windows, outer_place, table=table, before=result,
    )
    return result


def on_device(traces, destination, bin_index, dip_inline, dip_cross):
    held, block_rows, samples = traces.shape
    devices = lax.axis_size("inline") * lax.axis_size("crosslin")
    capacity = 2 * held // devices
    tile_rows, tile_cols = dip_inline.shape
    outgoing = pack(traces, destination.reshape(-1), bin_index.T, devices, capacity)
    arrived = lax.all_to_all(outgoing, BOTH, split_axis=0, concat_axis=0, tiled=True)
    stacked, head, tail = stack_bins(arrived, tile_rows, tile_cols, capacity, block_rows)
    back = jnp.asarray(interleave_table(samples).T, BF16)
    return smooth(stacked, head, tail, dip_inline, dip_cross, back)


def solution(mesh):
    return jax.shard_map(
        on_device,
        mesh=mesh,
        in_specs=(
            P(BOTH, None, None),
            P(BOTH, None),
            P(BOTH, None),
            P("inline", "crosslin"),
            P("inline", "crosslin"),
        ),
        out_specs=P("inline", "crosslin", None),
        check_vma=False,
    )
```

```python
import functools

import jax
import jax.numpy as jnp
import numpy as np
from jax import lax
from jax.experimental import pallas as pl
from jax.experimental.pallas import tpu as pltpu
from jax.sharding import PartitionSpec as P

HALF = 7
DMAX = 2
LANES = 128
PHASES = 8
PAIR = 2 * PHASES
WIDE = 2 * LANES
WINDOW = 16
BORDER = 8
REACH = -(-HALF * DMAX // PHASES)
REACHES = range(-REACH, REACH + 1)
BOTH = ("inline", "crosslin")
MIB = 2**20
VMEM = pl.BlockSpec(memory_space=pltpu.VMEM)
SMEM = pl.BlockSpec(memory_space=pltpu.SMEM)
ANY = pl.BlockSpec(memory_space=pl.ANY)
HBM = pl.BlockSpec(memory_space=pltpu.HBM)
F32, BF16, I32 = jnp.float32, jnp.bfloat16, jnp.int32


def interleave_table(samples):
    table = np.zeros((samples, samples), np.float32)
    time = np.arange(samples)
    table[time, time % PHASES * LANES + time // PHASES] = 1.0
    return table


def move_samples(rows, table):
    count = rows.shape[0]
    upper = rows.astype(BF16)
    rest = (rows - upper.astype(F32)).astype(BF16)
    both = jnp.concatenate([upper, rest], axis=0)
    moved = jnp.dot(both, table, preferred_element_type=F32)
    return moved[:count] + moved[count:]


def fill_interleave(table_ref):
    size = table_ref.shape[0]
    time = lax.broadcasted_iota(I32, (size, LANES), 0)
    lane = lax.broadcasted_iota(I32, (size, LANES), 1)
    gap = time - lane * PHASES
    for phase in range(PHASES):
        table_ref[:, phase * LANES : (phase + 1) * LANES] = jnp.where(gap == phase, 1.0, 0.0).astype(BF16)


def pack_kernel(target_ref, bins_ref, traces_ref, out_ref, held_ref, table_ref, tiles_ref, used_ref, listed_ref, in_sems, sem, listed_sem, *, capacity):
    held, block_rows, samples = traces_ref.shape
    devices, room, _ = listed_ref.shape
    span = block_rows * PHASES
    groups = held_ref.shape[0]
    count = held // groups
    loads = [
        pltpu.make_async_copy(traces_ref.at[pl.ds(group * count, count)], held_ref.at[group], in_sems.at[group])
        for group in range(groups)
    ]
    for load in loads:
        load.start()
    fill_interleave(table_ref)
    lane = lax.broadcasted_iota(I32, (1, LANES), 1)
    listed_ref[...] = jnp.full(listed_ref.shape, -1.0, F32)

    def clear(device, _):
        used_ref[device] = 0
        return 0

    lax.fori_loop(0, devices, clear, 0)

    def send_block(block, _):
        device = target_ref[block]
        rank = used_ref[device]
        used_ref[device] = rank + 1
        pltpu.make_async_copy(
            tiles_ref.at[pl.ds(pl.multiple_of(block * span, 8), span), :],
            out_ref.at[device, pl.ds(pl.multiple_of(rank * span, 8), span), :],
            sem,
        ).start()
        row = jnp.zeros((1, LANES), I32)
        for j in range(block_rows):
            row = jnp.where(lane == rank * block_rows + j, bins_ref[j, block], row)
        own = (lane >= rank * block_rows) & (lane < (rank + 1) * block_rows)
        listed_ref[device, 0:1, :] = jnp.where(own, row.astype(F32), listed_ref[device, 0:1, :])
        return 0

    for group in range(groups):
        loads[group].wait()
        rows = held_ref[group].reshape(count * block_rows, samples)
        moved = move_samples(rows, table_ref[...])
        for eight in range(count * block_rows // 8):
            for phase in range(PHASES):
                first = (group * count * block_rows + eight * 8) * PHASES + phase
                tiles_ref[pl.ds(first, 8, stride=PHASES), :] = moved[
                    eight * 8 : eight * 8 + 8, phase * LANES : (phase + 1) * LANES
                ]
        lax.fori_loop(group * count, (group + 1) * count, send_block, 0, unroll=4)
    copy = pltpu.make_async_copy(
        listed_ref, out_ref.at[:, capacity * span : capacity * span + room, :], listed_sem
    )
    copy.start()
    copy.wait()
    pltpu.make_async_copy(tiles_ref, tiles_ref, sem).wait()


def pack(traces, target, bins, devices, capacity):
    held, block_rows, samples = traces.shape
    span = block_rows * PHASES
    room = 8
    groups = 2
    return pl.pallas_call(
        functools.partial(pack_kernel, capacity=capacity),
        in_specs=[SMEM, SMEM, HBM],
        out_specs=HBM,
        out_shape=jax.ShapeDtypeStruct((devices, capacity * span + room, LANES), F32),
        scratch_shapes=[
            pltpu.VMEM((groups, held // groups, block_rows, samples), F32),
            pltpu.VMEM((samples, samples), BF16),
            pltpu.VMEM((held * span, LANES), F32),
            pltpu.SMEM((devices,), I32),
            pltpu.VMEM((devices, room, LANES), F32),
            pltpu.SemaphoreType.DMA((groups,)),
            pltpu.SemaphoreType.DMA,
            pltpu.SemaphoreType.DMA,
        ],
        compiler_params=pltpu.CompilerParams(vmem_limit_bytes=60 * MIB),
    )(target, bins, traces)


def bin_kernel(blocks_ref, out_ref, *refs, capacity, block_rows, edges):
    edge_refs, refs = refs[: len(edges)], refs[len(edges) :]
    even_ref, odd_ref, listed_ref, places_ref, scale_ref, scales_ref, sem, sems = refs
    devices = blocks_ref.shape[0]
    tile_rows, tile_cols = out_ref.shape[:2]
    bin_total = tile_rows * tile_cols
    unroll = 8

    def read_list(sender, _):
        listed = blocks_ref[sender, capacity * block_rows * PHASES : capacity * block_rows * PHASES + 1, :]
        listed_ref[pl.ds(sender, 1), :] = jnp.where(listed < 0, float(bin_total), listed).astype(I32)
        return 0

    lax.fori_loop(0, devices, read_list, 0, unroll=8)
    copy = pltpu.make_async_copy(listed_ref, places_ref, sem)
    copy.start()
    nothing = jnp.zeros((PHASES, LANES), F32)

    def clear(i, _):
        for j in range(unroll):
            even_ref[i * unroll + j] = nothing
            odd_ref[i * unroll + j] = nothing
        return 0

    lax.fori_loop(0, bin_total // unroll, clear, 0)
    copy.wait()
    count_rows = scale_ref.shape[0]
    numbers = lax.broadcasted_iota(I32, (count_rows, LANES), 0) * LANES + lax.broadcasted_iota(
        I32, (count_rows, LANES), 1
    )

    def add_sender(sender, folds):
        folds = list(folds)
        for rank in range(capacity):
            for j in range(block_rows):
                total_ref = odd_ref if j % 2 else even_ref
                place = places_ref[sender, rank * block_rows + j]
                row = (rank * block_rows + j) * PHASES
                total_ref[place] += blocks_ref[sender, row : row + PHASES, :]
                folds[j % 2] = folds[j % 2] + jnp.where(numbers == place, 1.0, 0.0)
        return tuple(folds)

    empty = jnp.zeros((count_rows, LANES), F32)
    folds = lax.fori_loop(0, devices, add_sender, (empty, empty))
    scale_ref[...] = 1.0 / jnp.maximum(folds[0] + folds[1], 1.0)
    copy = pltpu.make_async_copy(scale_ref, scales_ref, sem)
    copy.start()
    copy.wait()

    def finish(row, _):
        for col in range(tile_cols):
            place = row * tile_cols + col
            scale = scales_ref[place // LANES, place % LANES]
            out_ref[row, col] = (even_ref[place] + odd_ref[place]) * scale
        return 0

    lax.fori_loop(0, HALF, finish, 0)
    lax.fori_loop(tile_rows - HALF, tile_rows, finish, 0)
    copies = edge_copies(out_ref, edges, edge_refs, sems)
    for copy in copies:
        copy.start()
    lax.fori_loop(HALF, tile_rows - HALF, finish, 0)
    for copy in copies:
        copy.wait()


def edge_copies(out_ref, edges, edge_refs, sems):
    copies = []
    for (_, moves), edge_ref in zip(edges, edge_refs):
        for source, target in moves:
            copies.append(pltpu.make_async_copy(out_ref.at[source], edge_ref.at[target], sems.at[len(copies)]))
    return copies


def edge_outputs(edges):
    shapes = [jax.ShapeDtypeStruct(tuple(shape) + (PHASES, LANES), F32) for shape, _ in edges]
    moves = sum(len(moves) for _, moves in edges)
    return shapes, [HBM] * len(edges), pltpu.SemaphoreType.DMA((max(1, moves),))


def stack_bins(blocks, tile_rows, tile_cols, capacity, block_rows, edges):
    devices = blocks.shape[0]
    bin_total = tile_rows * tile_cols
    shapes, specs, sems = edge_outputs(edges)
    return pl.pallas_call(
        functools.partial(bin_kernel, capacity=capacity, block_rows=block_rows, edges=edges),
        in_specs=[VMEM],
        out_specs=[VMEM] + specs,
        out_shape=[jax.ShapeDtypeStruct((tile_rows, tile_cols, PHASES, LANES), F32)] + shapes,
        scratch_shapes=[
            pltpu.VMEM((bin_total + 8, PHASES, LANES), F32),
            pltpu.VMEM((bin_total + 8, PHASES, LANES), F32),
            pltpu.VMEM((devices, LANES), I32),
            pltpu.SMEM((devices, LANES), I32),
            pltpu.VMEM((bin_total // LANES, LANES), F32),
            pltpu.SMEM((bin_total // LANES, LANES), F32),
            pltpu.SemaphoreType.DMA,
            sems,
        ],
        compiler_params=pltpu.CompilerParams(vmem_limit_bytes=14 * MIB),
    )(blocks)


def fill_weights(spots_ref, weights_ref):
    row = lax.broadcasted_iota(I32, (PAIR, LANES), 0)
    column = lax.broadcasted_iota(I32, (PAIR, LANES), 1)
    for pair in range(spots_ref.shape[0] // (2 * PAIR)):
        for half in range(2):
            block = pl.ds((pair * 2 + half) * PAIR, PAIR)
            spot = half * PAIR + column // PHASES - HALF - 2 * pair - row // PHASES
            share = jnp.maximum(HALF + 1 - jnp.abs(spot), 0).astype(F32) / (HALF + 1) ** 2
            spots_ref[block, :] = jnp.clip(spot, -HALF - 1, HALF + 1).astype(F32).astype(BF16)
            weights_ref[block, :] = share.astype(BF16)


def split_cells(cells, halves_ref):
    for pair in range(len(cells) // 2):
        both = jnp.concatenate([cells[2 * pair](), cells[2 * pair + 1]()], axis=0)
        upper = both.astype(BF16)
        halves_ref[pair * PAIR : (pair + 1) * PAIR, :LANES] = upper
        rest = (both - upper.astype(F32)).astype(BF16)
        halves_ref[pair * PAIR : (pair + 1) * PAIR, LANES:] = rest


def apply_taps(dip_of, first, count, halves_ref, spots_ref, weights_ref):
    row = lax.broadcasted_iota(I32, (PAIR, LANES), 0)
    column = lax.broadcasted_iota(I32, (PAIR, LANES), 1)
    phase_gap = ((row & (PHASES - 1)) - (column & (PHASES - 1))).astype(F32).astype(BF16)
    none = jnp.zeros((PAIR, LANES), BF16)
    taps = []
    for pair in range(count // 2):
        dip = jnp.concatenate(
            [jnp.full((PHASES, LANES), dip_of(first + 2 * pair + i).astype(F32)) for i in range(2)], axis=0
        ).astype(BF16)
        moves, weights = [], []
        for half in range(2):
            block = pl.ds((pair * 2 + half) * PAIR, PAIR)
            moves.append(phase_gap + dip * spots_ref[block, :])
            weights.append(weights_ref[block, :])
        for reach in REACHES:
            taps.append(
                jnp.concatenate(
                    [jnp.where(moves[h] == jnp.bfloat16(reach * PHASES), weights[h], none) for h in range(2)],
                    axis=1,
                )
            )
    return jnp.dot(jnp.concatenate(taps, axis=0), halves_ref[...], preferred_element_type=F32)


def move_lanes(sums, first, count, put):
    lane = lax.broadcasted_iota(I32, (PHASES, LANES), 1)
    for pair in range(count // 2):
        for member in range(2):
            total = None
            for reach in REACHES:
                begin = (pair * len(REACHES) + reach + REACH) * PAIR + member * PHASES
                part = sums[begin : begin + PHASES, :LANES] + sums[begin : begin + PHASES, LANES:]
                if reach:
                    part = pltpu.roll(part, (-reach) % LANES, axis=1)
                    inside = lane < LANES - reach if reach > 0 else lane >= -reach
                    part = jnp.where(inside, part, 0.0)
                total = part if total is None else total + part
            put(first + 2 * pair + member, total)


def steer_kernel(dip_ref, *refs, along, whole, lines, line_of, windows, local_of, edges, final, batches, filled, chained, pieces_count, abreast):
    pieces, refs = refs[:pieces_count], refs[pieces_count:]
    if final:
        table_ref, refs = refs[0], refs[1:]
    refs = refs[chained:]
    out_ref, refs = refs[0], refs[1:]
    edge_refs, refs = refs[: len(edges)], refs[len(edges) :]
    spots_ref, weights_ref, sems, *refs = refs
    halves = refs[: abreast * len(windows)]
    if final:
        staged_ref, result_ref = refs[abreast * len(windows) :]
    fill_weights(spots_ref, weights_ref)
    for i, halves_ref in enumerate(halves):
        used = len(windows[i % len(windows)][2]) * PHASES
        if used < WIDE:
            halves_ref[used:, :] = jnp.zeros((WIDE - used, WIDE), BF16)

    def at(place, line):
        return (place, line) if along == 0 else (line, place)

    def some_lines(step, _):
        jobs = []
        for parity in range(abreast):
            line = abreast * step + parity
            full = line_of(line)

            def cell(index, local, line=line, full=full):
                return lambda: pieces[index][at(local, full if whole[index] else line)]

            def put(place, value, line=line):
                if final:
                    staged_ref[pl.ds((local_of(place) * final + line % final) * PHASES, PHASES), :] = value
                else:
                    out_ref[at(local_of(place), line)] = value

            for i, (first, count, places) in enumerate(windows):
                halves_ref = halves[parity * len(windows) + i]
                split_cells([cell(*place) for place in places], halves_ref)
                jobs.append((full, first, count, halves_ref, put))
        waiting = None
        for full, first, count, halves_ref, put in jobs:
            sums = apply_taps(
                lambda place: dip_ref[at(place, full)], first, count, halves_ref, spots_ref, weights_ref
            )
            if waiting is not None:
                move_lanes(*waiting)
            waiting = (sums, first, count, put)
        move_lanes(*waiting)
        return 0

    if not final:
        if filled is not None:
            index, target = filled
            fill = pltpu.make_async_copy(pieces[index], out_ref.at[target], sems.at[sems.shape[0] - 1])
            fill.start()
        lax.fori_loop(0, lines // abreast, some_lines, 0)
        if filled is not None:
            fill.wait()
        copies = edge_copies(out_ref, edges, edge_refs, sems)
        for copy in copies:
            copy.start()
        for copy in copies:
            copy.wait()
        return

    outputs = sum(count for _, count, _ in windows)

    def copies_of(batch, slot):
        return [
            pltpu.make_async_copy(
                result_ref.at[slot, pl.ds(local_of(first), count), pl.ds(local, wide), :],
                out_ref.at[pl.ds(first, count), pl.ds(full, wide), :],
                sems.at[(slot * len(windows) + i) * len(batches[batch]) + j],
            )
            for i, (first, count, _) in enumerate(windows)
            for j, (local, full, wide) in enumerate(batches[batch])
        ]

    for batch in range(lines // final):
        lax.fori_loop(batch * final // abreast, (batch + 1) * final // abreast, some_lines, 0)
        rows = jnp.concatenate(
            [
                jnp.concatenate(
                    [
                        staged_ref[pl.ds(eight * 8 * PHASES + phase, 8, stride=PHASES), :]
                        for phase in range(PHASES)
                    ],
                    axis=1,
                )
                for eight in range(outputs * final // 8)
            ],
            axis=0,
        )
        slot = batch % 2
        if batch >= 2:
            for copy in copies_of(batch - 2, slot):
                copy.wait()
        result_ref[slot] = move_samples(rows, table_ref[...]).reshape(result_ref.shape[1:])
        for copy in copies_of(batch, slot):
            copy.start()
    for batch in range(max(0, lines // final - 2), lines // final):
        for copy in copies_of(batch, batch % 2):
            copy.wait()


def steer(
    dip, pieces, along, lines, line_of, windows, local_of, edges=(), table=None, batches=None, before=None, after=None, filled=None
):
    samples = PHASES * LANES
    outputs = sum(count for _, count, _ in windows)
    final = 16 if table is not None else 0
    abreast = 4 * WINDOW // outputs
    shapes, specs, sems = edge_outputs(edges)
    operands = [dip] + [array for array, _ in pieces]
    in_specs = [SMEM] + [VMEM] * len(pieces)
    aliases = {}
    if final:
        operands.append(table)
        in_specs.append(VMEM)
        if before is not None:
            aliases = {len(operands): 0}
            operands.append(before)
            in_specs.append(HBM)
        out_shape = [jax.ShapeDtypeStruct(dip.shape + (samples,), F32)]
        sems = pltpu.SemaphoreType.DMA((2 * len(windows) * len(batches[0]),))
        out_specs = [HBM]
    else:
        reach = outputs if filled is None else dip.shape[along]
        shape = (reach, lines) if along == 0 else (lines, reach)
        out_shape = [jax.ShapeDtypeStruct(shape + (PHASES, LANES), F32)] + shapes
        out_specs = [VMEM] + specs
        if filled is not None:
            sems = pltpu.SemaphoreType.DMA((sems.shape[0] + 1,))
    if after is not None:
        operands.append(after)
        in_specs.append(ANY)
    most = max(count for _, count, _ in windows)
    constant = pltpu.VMEM((most * PAIR, LANES), BF16)
    scratch = [constant, constant, sems]
    scratch += [pltpu.VMEM((WIDE, WIDE), BF16)] * (abreast * len(windows))
    if final:
        scratch += [
            pltpu.VMEM((outputs * final * PHASES, LANES), F32),
            pltpu.VMEM((2, outputs, final, samples), F32),
        ]
    return pl.pallas_call(
        functools.partial(
            steer_kernel,
            along=along, whole=[whole for _, whole in pieces], lines=lines, line_of=line_of, windows=windows,
            local_of=local_of, edges=edges, final=final, batches=batches, filled=filled, chained=len(operands) - len(pieces) - 1 - bool(final), pieces_count=len(pieces), abreast=abreast,
        ),
        in_specs=in_specs,
        out_specs=out_specs,
        out_shape=out_shape,
        scratch_shapes=scratch,
        input_output_aliases=aliases,
        compiler_params=pltpu.CompilerParams(vmem_limit_bytes=16 * MIB),
        cost_estimate=pl.CostEstimate(
            flops=2400 * outputs * lines * samples,
            bytes_accessed=8 * outputs * lines * samples,
            transcendentals=0,
        ),
    )(*operands)


def swap_ends(head, tail, axis):
    count = lax.axis_size(axis)
    low = lax.ppermute(tail, axis, [(i, i + 1) for i in range(count - 1)])
    high = lax.ppermute(head, axis, [(i + 1, i) for i in range(count - 1)])
    return low, high


def span_of(index, first, count):
    return [(index, first + i) for i in range(count)]


def rows_of(first, count):
    return slice(first, first + count)


def smooth(arrived, capacity, block_rows, dip_inline, dip_cross, table):
    rows, cols = dip_inline.shape
    mid_rows, mid_cols = rows - 2 * BORDER, cols - 2 * BORDER
    both = 2 * BORDER
    same = lambda line: line
    inner = lambda line: line + BORDER
    outer_col = lambda line: line + jnp.where(line < BORDER, 0, mid_cols)
    outer_row = lambda line: line + jnp.where(line < BORDER, 0, mid_rows)
    mid_place = lambda place: place - BORDER
    outer_place = lambda place: place if place < BORDER else place - mid_rows
    every = slice(None)
    lead, last = rows_of(0, HALF), rows_of(both - HALF, HALF)
    left, right, middle_cols = rows_of(0, BORDER), rows_of(cols - BORDER, BORDER), rows_of(BORDER, mid_cols)

    def outer_edge(pick):
        return ((HALF, both), [((pick, left), (every, rows_of(0, BORDER))), ((pick, right), (every, rows_of(BORDER, BORDER)))])

    def whole_edge(shape, pick):
        return (shape, [(pick, (every, every))])

    def mid_windows(places, extent):
        return [(i, WINDOW, places[i - BORDER : i - BORDER + WINDOW + 2 * HALF]) for i in range(BORDER, extent - BORDER, WINDOW)]

    stacked, head_out, tail_out, head_mid, tail_mid = stack_bins(
        arrived, rows, cols, capacity, block_rows,
        [
            outer_edge(rows_of(0, HALF)),
            outer_edge(rows_of(rows - HALF, HALF)),
            whole_edge((HALF, mid_cols), (rows_of(0, HALF), middle_cols)),
            whole_edge((HALF, mid_cols), (rows_of(rows - HALF, HALF), middle_cols)),
        ],
    )
    low_out, high_out = swap_ends(head_out, tail_out, "inline")
    low_mid, high_mid = swap_ends(head_mid, tail_mid, "inline")

    middle, head, tail = steer(
        dip_inline, [(stacked, True)], 0, cols, same,
        mid_windows(span_of(0, BORDER - HALF, mid_rows + 2 * HALF), rows), mid_place,
        edges=[whole_edge((mid_rows, HALF), (every, lead)), whole_edge((mid_rows, HALF), (every, rows_of(cols - HALF, HALF)))],
    )
    left_mid, right_mid = swap_ends(head, tail, "crosslin")
    windows = [
        (0, BORDER, span_of(0, 0, HALF) + span_of(1, 0, BORDER + HALF)),
        (rows - BORDER, BORDER, span_of(1, rows - BORDER - HALF, BORDER + HALF) + span_of(2, 0, HALF)),
    ]
    corners, head, tail = steer(
        dip_inline, [(low_out, False), (stacked, True), (high_out, False)], 0, both, outer_col, windows, outer_place,
        edges=[whole_edge((both, HALF), (every, lead)), whole_edge((both, HALF), (every, last))], after=middle,
    )
    left_out, right_out = swap_ends(head, tail, "crosslin")
    (flanks,) = steer(
        dip_inline, [(low_mid, False), (stacked, True), (high_mid, False)], 0, mid_cols, inner, windows, outer_place,
        after=corners,
    )

    places = span_of(0, BORDER - HALF, HALF) + span_of(1, 0, mid_cols) + span_of(0, BORDER, HALF)
    second_mid, head, tail = steer(
        dip_cross, [(corners, False), (flanks, False)], 1, both, outer_row, mid_windows(places, cols), mid_place,
        edges=[whole_edge((HALF, mid_cols), (lead, every)), whole_edge((HALF, mid_cols), (last, every))],
    )
    low_mid, high_mid = swap_ends(head, tail, "inline")
    places = span_of(0, 0, HALF) + span_of(1, 0, cols) + span_of(2, 0, HALF)
    (middle_second,) = steer(
        dip_cross, [(left_mid, False), (middle, False), (right_mid, False)], 1, mid_rows, inner,
        [(i, WINDOW, places[i : i + WINDOW + 2 * HALF]) for i in range(0, cols, WINDOW)], same, after=second_mid,
    )
    windows = [
        (0, BORDER, span_of(0, 0, HALF) + span_of(1, 0, BORDER) + span_of(2, 0, HALF)),
        (cols - BORDER, BORDER, span_of(2, mid_cols - HALF, HALF) + span_of(1, BORDER, BORDER) + span_of(3, 0, HALF)),
    ]
    border_second, head, tail = steer(
        dip_cross,
        [(left_out, False), (corners, False), (flanks, False), (right_out, False), (second_mid, False)],
        1, both, outer_row, windows, same, filled=(4, (every, middle_cols)),
        edges=[outer_edge(lead), outer_edge(last)], after=middle_second,
    )
    low_out, high_out = swap_ends(head, tail, "inline")

    places = span_of(0, BORDER - HALF, HALF) + span_of(1, 0, mid_rows) + span_of(0, BORDER, HALF)
    (result,) = steer(
        dip_inline, [(border_second, True), (middle_second, True)], 0, cols, same, mid_windows(places, rows), mid_place,
        table=table, batches=[[(0, first, WINDOW)] for first in range(0, cols, WINDOW)],
    )
    windows = [
        (0, BORDER, span_of(0, 0, HALF) + span_of(1, 0, BORDER) + span_of(2, 0, HALF)),
        (rows - BORDER, BORDER, span_of(2, mid_rows - HALF, HALF) + span_of(1, BORDER, BORDER) + span_of(3, 0, HALF)),
    ]
    for low, high, lines, line_of, batches in (
        (low_mid, high_mid, mid_cols, inner, [[(0, first, WINDOW)] for first in range(BORDER, cols - BORDER, WINDOW)]),
        (low_out, high_out, both, outer_col, [[(0, 0, BORDER), (BORDER, cols - BORDER, BORDER)]]),
    ):
        (result,) = steer(
            dip_inline, [(low, False), (border_second, True), (middle_second, True), (high, False)], 0, lines, line_of,
            windows, outer_place, table=table, batches=batches, before=result,
        )
    return result


def on_device(traces, destination, bin_index, dip_inline, dip_cross):
    held, block_rows, samples = traces.shape
    devices = lax.axis_size("inline") * lax.axis_size("crosslin")
    capacity = 2 * held // devices
    outgoing = pack(traces, destination.reshape(-1), bin_index.T, devices, capacity)
    arrived = lax.all_to_all(outgoing, BOTH, split_axis=0, concat_axis=0, tiled=True)
    back = jnp.asarray(interleave_table(samples).T, BF16)
    return smooth(arrived, capacity, block_rows, dip_inline, dip_cross, back)


def solution(mesh):
    return jax.shard_map(
        on_device,
        mesh=mesh,
        in_specs=(
            P(BOTH, None, None),
            P(BOTH, None),
            P(BOTH, None),
            P("inline", "crosslin"),
            P("inline", "crosslin"),
        ),
        out_specs=P("inline", "crosslin", None),
        check_vma=False,
    )
```

```python
import functools

import jax
import jax.numpy as jnp
from jax import lax
from jax.experimental import pallas as pl
from jax.experimental.pallas import tpu as pltpu
from jax.sharding import PartitionSpec as P

HALF = 7
DMAX = 2
LANES = 128
PHASES = 8
PAIR = 2 * PHASES
WIDE = 2 * LANES
BLOCK = WIDE // PHASES
WINDOW = 16
BORDER = 8
REACH = -(-HALF * DMAX // PHASES)
REACHES = range(-REACH, REACH + 1)
BOTH = ("inline", "crosslin")
MIB = 2**20
VMEM = pl.BlockSpec(memory_space=pltpu.VMEM)
SMEM = pl.BlockSpec(memory_space=pltpu.SMEM)
ANY = pl.BlockSpec(memory_space=pl.ANY)
HBM = pl.BlockSpec(memory_space=pltpu.HBM)
F32, BF16, I32 = jnp.float32, jnp.bfloat16, jnp.int32


def fill_interleave(table_ref, time_dim):
    time = lax.broadcasted_iota(I32, (WIDE, WIDE), time_dim)
    place = lax.broadcasted_iota(I32, (WIDE, WIDE), 1 - time_dim)
    hit = time == place % BLOCK * PHASES + place // BLOCK
    table_ref[...] = jnp.where(hit, 1.0, 0.0).astype(BF16)


def move_samples(rows, table):
    count = rows.shape[0]
    upper = rows.astype(BF16)
    rest = (rows - upper.astype(F32)).astype(BF16)
    both = jnp.concatenate([upper, rest], axis=0)
    moved = jnp.dot(both, table, preferred_element_type=F32)
    return moved[:count] + moved[count:]


def swap_blocks(tiles):
    count = LANES // BLOCK
    block = lax.broadcasted_iota(I32, tiles[0].shape, 1) // BLOCK
    swapped = []
    for j in range(count):
        total = tiles[j]
        for m in range(count):
            if m != j:
                total = jnp.where(block == m, pltpu.roll(tiles[m], (m - j) * BLOCK % LANES, axis=1), total)
        swapped.append(total)
    return swapped


def pack_kernel(mine_ref, target_ref, bins_ref, traces_ref, out_ref, held_ref, table_ref, tiles_ref, used_ref, listed_ref, in_sems, sem, listed_sem, *, capacity):
    held, block_rows, samples = traces_ref.shape
    devices, room, _ = listed_ref.shape
    span = block_rows * PHASES
    groups = held_ref.shape[0]
    count = held // groups
    loads = [
        pltpu.make_async_copy(traces_ref.at[pl.ds(group * count, count)], held_ref.at[group], in_sems.at[group])
        for group in range(groups)
    ]
    for load in loads:
        load.start()
    fill_interleave(table_ref, 0)
    lane = lax.broadcasted_iota(I32, (1, LANES), 1)
    listed_ref[...] = jnp.zeros(listed_ref.shape, F32)
    own_lanes = mine_ref[0] % (LANES // (capacity * block_rows)) * (capacity * block_rows)

    def clear(device, _):
        used_ref[device] = 0
        return 0

    lax.fori_loop(0, devices, clear, 0)

    def send_block(block, _):
        device = target_ref[block]
        rank = used_ref[device]
        used_ref[device] = rank + 1
        pltpu.make_async_copy(
            tiles_ref.at[pl.ds(pl.multiple_of(block * span, 8), span), :],
            out_ref.at[device, pl.ds(pl.multiple_of(rank * span, 8), span), :],
            sem,
        ).start()
        row = jnp.zeros((1, LANES), I32)
        for j in range(block_rows):
            row = jnp.where(lane == own_lanes + rank * block_rows + j, bins_ref[j, block] + 1, row)
        listed_ref[device, 0:1, :] = listed_ref[device, 0:1, :] + row.astype(F32)
        return 0

    for group in range(groups):
        loads[group].wait()
        rows = held_ref[group].reshape(count * block_rows, samples)
        stretches = samples // WIDE
        cut = jnp.concatenate([rows[:, i * WIDE : (i + 1) * WIDE] for i in range(stretches)], axis=0)
        moved = move_samples(cut, table_ref[...])
        for eight in range(count * block_rows // 8):
            for half in range(2):
                parts = []
                for i in range(stretches):
                    begin = i * count * block_rows + eight * 8
                    parts.append(moved[begin : begin + 8, half * LANES : (half + 1) * LANES])
                for phase, part in enumerate(swap_blocks(parts)):
                    first = (group * count * block_rows + eight * 8) * PHASES + half * 4 + phase
                    tiles_ref[pl.ds(first, 8, stride=PHASES), :] = part
        lax.fori_loop(group * count, (group + 1) * count, send_block, 0, unroll=4)
    copy = pltpu.make_async_copy(
        listed_ref, out_ref.at[:, capacity * span : capacity * span + room, :], listed_sem
    )
    copy.start()
    copy.wait()
    pltpu.make_async_copy(tiles_ref, tiles_ref, sem).wait()


def pack(traces, mine, target, bins, devices, capacity):
    held, block_rows, samples = traces.shape
    span = block_rows * PHASES
    room = 8
    groups = 2
    return pl.pallas_call(
        functools.partial(pack_kernel, capacity=capacity),
        in_specs=[SMEM, SMEM, SMEM, HBM],
        out_specs=HBM,
        out_shape=jax.ShapeDtypeStruct((devices, capacity * span + room, LANES), F32),
        scratch_shapes=[
            pltpu.VMEM((groups, held // groups, block_rows, samples), F32),
            pltpu.VMEM((WIDE, WIDE), BF16),
            pltpu.VMEM((held * span, LANES), F32),
            pltpu.SMEM((devices,), I32),
            pltpu.VMEM((devices, room, LANES), F32),
            pltpu.SemaphoreType.DMA((groups,)),
            pltpu.SemaphoreType.DMA,
            pltpu.SemaphoreType.DMA,
        ],
        compiler_params=pltpu.CompilerParams(vmem_limit_bytes=60 * MIB),
    )(mine, target, bins, traces)


def bin_kernel(blocks_ref, out_ref, *refs, capacity, block_rows, edges):
    edge_refs, refs = refs[: len(edges)], refs[len(edges) :]
    even_ref, odd_ref, listed_ref, places_ref, scale_ref, scales_ref, sem, sems = refs
    devices = blocks_ref.shape[0]
    tile_rows, tile_cols = out_ref.shape[:2]
    bin_total = tile_rows * tile_cols
    unroll = 8
    lanes = capacity * block_rows
    shared = LANES // lanes

    def read_lists(row, _):
        total = jnp.zeros((1, LANES), F32)
        for i in range(shared):
            total = total + blocks_ref[row * shared + i, lanes * PHASES : lanes * PHASES + 1, :]
        listed_ref[pl.ds(row, 1), :] = jnp.where(total > 0, total - 1.0, float(bin_total)).astype(I32)
        return 0

    lax.fori_loop(0, devices // shared, read_lists, 0)
    copy = pltpu.make_async_copy(listed_ref, places_ref, sem)
    copy.start()
    nothing = jnp.zeros((PHASES, LANES), F32)

    def clear(i, _):
        for j in range(unroll):
            even_ref[i * unroll + j] = nothing
            odd_ref[i * unroll + j] = nothing
        return 0

    lax.fori_loop(0, bin_total // unroll, clear, 0)
    copy.wait()
    count_rows = scale_ref.shape[0]
    numbers = lax.broadcasted_iota(I32, (count_rows, LANES), 0) * LANES + lax.broadcasted_iota(
        I32, (count_rows, LANES), 1
    )

    def add_sender(sender, folds):
        folds = list(folds)
        row, first = sender // shared, sender % shared * lanes
        for rank in range(capacity):
            for j in range(block_rows):
                total_ref = odd_ref if j % 2 else even_ref
                place = places_ref[row, first + rank * block_rows + j]
                cell = (rank * block_rows + j) * PHASES
                total_ref[place] += blocks_ref[sender, cell : cell + PHASES, :]
                folds[j % 2] = folds[j % 2] + jnp.where(numbers == place, 1.0, 0.0)
        return tuple(folds)

    empty = jnp.zeros((count_rows, LANES), F32)
    folds = lax.fori_loop(0, devices, add_sender, (empty, empty))
    scale_ref[...] = 1.0 / jnp.maximum(folds[0] + folds[1], 1.0)
    copy = pltpu.make_async_copy(scale_ref, scales_ref, sem)
    copy.start()
    copy.wait()

    def finish(row, _):
        high, low = row * tile_cols // LANES, row * tile_cols % LANES
        for col in range(tile_cols):
            place = row * tile_cols + col
            scale = scales_ref[high, low + col]
            out_ref[row, col] = (even_ref[place] + odd_ref[place]) * scale
        return 0

    lax.fori_loop(0, HALF, finish, 0)
    lax.fori_loop(tile_rows - HALF, tile_rows, finish, 0)
    copies = edge_copies(out_ref, edges, edge_refs, sems)
    for copy in copies:
        copy.start()
    lax.fori_loop(HALF, tile_rows - HALF, finish, 0)
    for copy in copies:
        copy.wait()


def edge_copies(out_ref, edges, edge_refs, sems):
    copies = []
    for (_, moves), edge_ref in zip(edges, edge_refs):
        for source, target in moves:
            copies.append(pltpu.make_async_copy(out_ref.at[source], edge_ref.at[target], sems.at[len(copies)]))
    return copies


def edge_outputs(edges):
    shapes = [jax.ShapeDtypeStruct(tuple(shape) + (PHASES, LANES), F32) for shape, _ in edges]
    moves = sum(len(moves) for _, moves in edges)
    return shapes, [HBM] * len(edges), pltpu.SemaphoreType.DMA((max(1, moves),))


def stack_bins(blocks, tile_rows, tile_cols, capacity, block_rows, edges):
    devices = blocks.shape[0]
    bin_total = tile_rows * tile_cols
    shapes, specs, sems = edge_outputs(edges)
    return pl.pallas_call(
        functools.partial(bin_kernel, capacity=capacity, block_rows=block_rows, edges=edges),
        in_specs=[VMEM],
        out_specs=[VMEM] + specs,
        out_shape=[jax.ShapeDtypeStruct((tile_rows, tile_cols, PHASES, LANES), F32)] + shapes,
        scratch_shapes=[
            pltpu.VMEM((bin_total + 8, PHASES, LANES), F32),
            pltpu.VMEM((bin_total + 8, PHASES, LANES), F32),
            pltpu.VMEM((devices * capacity * block_rows // LANES, LANES), I32),
            pltpu.SMEM((devices * capacity * block_rows // LANES, LANES), I32),
            pltpu.VMEM((bin_total // LANES, LANES), F32),
            pltpu.SMEM((bin_total // LANES, LANES), F32),
            pltpu.SemaphoreType.DMA,
            sems,
        ],
        compiler_params=pltpu.CompilerParams(vmem_limit_bytes=14 * MIB),
    )(blocks)


def fill_weights(spots_ref, weights_ref):
    row = lax.broadcasted_iota(I32, (PAIR, LANES), 0)
    column = lax.broadcasted_iota(I32, (PAIR, LANES), 1)
    for pair in range(spots_ref.shape[0] // (2 * PAIR)):
        for half in range(2):
            block = pl.ds((pair * 2 + half) * PAIR, PAIR)
            spot = half * PAIR + column // PHASES - HALF - 2 * pair - row // PHASES
            share = jnp.maximum(HALF + 1 - jnp.abs(spot), 0).astype(F32) / (HALF + 1) ** 2
            spots_ref[block, :] = jnp.clip(spot, -HALF - 1, HALF + 1).astype(F32).astype(BF16)
            weights_ref[block, :] = share.astype(BF16)


def split_cells(cells, halves_ref):
    for pair in range(len(cells) // 2):
        both = jnp.concatenate([cells[2 * pair](), cells[2 * pair + 1]()], axis=0)
        upper = both.astype(BF16)
        halves_ref[pair * PAIR : (pair + 1) * PAIR, :LANES] = upper
        rest = (both - upper.astype(F32)).astype(BF16)
        halves_ref[pair * PAIR : (pair + 1) * PAIR, LANES:] = rest


def apply_taps(dip_of, first, count, halves_ref, spots_ref, weights_ref):
    row = lax.broadcasted_iota(I32, (PAIR, LANES), 0)
    column = lax.broadcasted_iota(I32, (PAIR, LANES), 1)
    phase_gap = ((row & (PHASES - 1)) - (column & (PHASES - 1))).astype(F32).astype(BF16)
    none = jnp.zeros((PAIR, LANES), BF16)
    taps = []
    for pair in range(count // 2):
        dip = jnp.concatenate(
            [jnp.full((PHASES, LANES), dip_of(first + 2 * pair + i).astype(F32)) for i in range(2)], axis=0
        ).astype(BF16)
        moves, weights = [], []
        for half in range(2):
            block = pl.ds((pair * 2 + half) * PAIR, PAIR)
            moves.append(phase_gap + dip * spots_ref[block, :])
            weights.append(weights_ref[block, :])
        for reach in REACHES:
            taps.append(
                jnp.concatenate(
                    [jnp.where(moves[h] == jnp.bfloat16(reach * PHASES), weights[h], none) for h in range(2)],
                    axis=1,
                )
            )
    half = len(taps) // 2
    return [
        jnp.dot(jnp.concatenate(part, axis=0), halves_ref[...], preferred_element_type=F32)
        for part in (taps[:half], taps[half:])
    ]


def move_lanes(sums, first, count, put):
    lane = lax.broadcasted_iota(I32, (PHASES, LANES), 1)
    for pair in range(count // 2):
        for member in range(2):
            total = None
            for reach in REACHES:
                which, begin = divmod((pair * len(REACHES) + reach + REACH) * PAIR + member * PHASES, sums[0].shape[0])
                part = sums[which][begin : begin + PHASES, :LANES] + sums[which][begin : begin + PHASES, LANES:]
                if reach:
                    part = pltpu.roll(part, (-reach) % LANES, axis=1)
                    inside = lane < LANES - reach if reach > 0 else lane >= -reach
                    part = jnp.where(inside, part, 0.0)
                total = part if total is None else total + part
            put(first + 2 * pair + member, total)


def steer_kernel(dip_ref, *refs, along, whole, lines, line_of, windows, local_of, edges, final, batches, filled, chained, pieces_count, abreast):
    pieces, refs = refs[:pieces_count], refs[pieces_count:]
    refs = refs[chained:]
    out_ref, refs = refs[0], refs[1:]
    edge_refs, refs = refs[: len(edges)], refs[len(edges) :]
    spots_ref, weights_ref, sems, *refs = refs
    halves = refs[: abreast * len(windows)]
    if final:
        staged_ref, result_ref, table_ref = refs[abreast * len(windows) :]
        fill_interleave(table_ref, 1)
    fill_weights(spots_ref, weights_ref)
    for i, halves_ref in enumerate(halves):
        used = len(windows[i % len(windows)][2]) * PHASES
        if used < WIDE:
            halves_ref[used:, :] = jnp.zeros((WIDE - used, WIDE), BF16)

    def at(place, line):
        return (place, line) if along == 0 else (line, place)

    def some_lines(step, _):
        jobs = []
        for parity in range(abreast):
            line = abreast * step + parity
            full = line_of(line)

            def cell(index, local, line=line, full=full):
                return lambda: pieces[index][at(local, full if whole[index] else line)]

            def put(place, value, line=line):
                if final:
                    staged_ref[pl.ds((local_of(place) * final + line % final) * PHASES, PHASES), :] = value
                else:
                    out_ref[at(local_of(place), line)] = value

            for i, (first, count, places) in enumerate(windows):
                halves_ref = halves[parity * len(windows) + i]
                split_cells([cell(*place) for place in places], halves_ref)
                jobs.append((full, first, count, halves_ref, put))
        waiting = None
        for full, first, count, halves_ref, put in jobs:
            sums = apply_taps(
                lambda place: dip_ref[at(place, full)], first, count, halves_ref, spots_ref, weights_ref
            )
            if waiting is not None:
                move_lanes(*waiting)
            waiting = (sums, first, count, put)
        move_lanes(*waiting)
        return 0

    if not final:
        if filled is not None:
            index, target = filled
            fill = pltpu.make_async_copy(pieces[index], out_ref.at[target], sems.at[sems.shape[0] - 1])
            fill.start()
        lax.fori_loop(0, lines // abreast, some_lines, 0)
        if filled is not None:
            fill.wait()
        copies = edge_copies(out_ref, edges, edge_refs, sems)
        for copy in copies:
            copy.start()
        for copy in copies:
            copy.wait()
        return

    outputs = sum(count for _, count, _ in windows)

    def copies_of(batch, slot):
        return [
            pltpu.make_async_copy(
                result_ref.at[slot, pl.ds(local_of(first), count), pl.ds(local, wide), :],
                out_ref.at[pl.ds(first, count), pl.ds(full, wide), :],
                sems.at[(slot * len(windows) + i) * len(batches[batch]) + j],
            )
            for i, (first, count, _) in enumerate(windows)
            for j, (local, full, wide) in enumerate(batches[batch])
        ]

    for batch in range(lines // final):
        lax.fori_loop(batch * final // abreast, (batch + 1) * final // abreast, some_lines, 0)
        stretches = PHASES * LANES // WIDE
        cuts = [[] for _ in range(stretches)]
        for eight in range(outputs * final // 8):
            sides = [
                swap_blocks(
                    [
                        staged_ref[pl.ds(eight * 8 * PHASES + half * 4 + phase, 8, stride=PHASES), :]
                        for phase in range(PHASES // 2)
                    ]
                )
                for half in range(2)
            ]
            for i in range(stretches):
                cuts[i].append(jnp.concatenate([sides[0][i], sides[1][i]], axis=1))
        moved = move_samples(jnp.concatenate(sum(cuts, []), axis=0), table_ref[...])
        slot = batch % 2
        if batch >= 2:
            for copy in copies_of(batch - 2, slot):
                copy.wait()
        count = outputs * final
        for i in range(stretches):
            result_ref[slot, :, :, i * WIDE : (i + 1) * WIDE] = moved[i * count : (i + 1) * count].reshape(
                outputs, final, WIDE
            )
        for copy in copies_of(batch, slot):
            copy.start()
    for batch in range(max(0, lines // final - 2), lines // final):
        for copy in copies_of(batch, batch % 2):
            copy.wait()


def steer(
    dip, pieces, along, lines, line_of, windows, local_of, edges=(), batches=None, before=None, after=None, filled=None
):
    samples = PHASES * LANES
    outputs = sum(count for _, count, _ in windows)
    final = 16 if batches is not None else 0
    abreast = 4 * WINDOW // outputs
    shapes, specs, sems = edge_outputs(edges)
    operands = [dip] + [array for array, _ in pieces]
    in_specs = [SMEM] + [VMEM] * len(pieces)
    aliases = {}
    if final:
        if before is not None:
            aliases = {len(operands): 0}
            operands.append(before)
            in_specs.append(HBM)
        out_shape = [jax.ShapeDtypeStruct(dip.shape + (samples,), F32)]
        sems = pltpu.SemaphoreType.DMA((2 * len(windows) * len(batches[0]),))
        out_specs = [HBM]
    else:
        reach = outputs if filled is None else dip.shape[along]
        shape = (reach, lines) if along == 0 else (lines, reach)
        out_shape = [jax.ShapeDtypeStruct(shape + (PHASES, LANES), F32)] + shapes
        out_specs = [VMEM] + specs
        if filled is not None:
            sems = pltpu.SemaphoreType.DMA((sems.shape[0] + 1,))
    if after is not None:
        operands.append(after)
        in_specs.append(ANY)
    most = max(count for _, count, _ in windows)
    constant = pltpu.VMEM((most * PAIR, LANES), BF16)
    scratch = [constant, constant, sems]
    scratch += [pltpu.VMEM((WIDE, WIDE), BF16)] * (abreast * len(windows))
    if final:
        scratch += [
            pltpu.VMEM((outputs * final * PHASES, LANES), F32),
            pltpu.VMEM((2, outputs, final, samples), F32),
            pltpu.VMEM((WIDE, WIDE), BF16),
        ]
    return pl.pallas_call(
        functools.partial(
            steer_kernel,
            along=along, whole=[whole for _, whole in pieces], lines=lines, line_of=line_of, windows=windows,
            local_of=local_of, edges=edges, final=final, batches=batches, filled=filled, chained=len(operands) - len(pieces) - 1, pieces_count=len(pieces), abreast=abreast,
        ),
        in_specs=in_specs,
        out_specs=out_specs,
        out_shape=out_shape,
        scratch_shapes=scratch,
        input_output_aliases=aliases,
        compiler_params=pltpu.CompilerParams(vmem_limit_bytes=16 * MIB),
        cost_estimate=pl.CostEstimate(
            flops=2400 * outputs * lines * samples,
            bytes_accessed=8 * outputs * lines * samples,
            transcendentals=0,
        ),
    )(*operands)


def swap_ends(head, tail, axis):
    count = lax.axis_size(axis)
    low = lax.ppermute(tail, axis, [(i, i + 1) for i in range(count - 1)])
    high = lax.ppermute(head, axis, [(i + 1, i) for i in range(count - 1)])
    return low, high


def span_of(index, first, count):
    return [(index, first + i) for i in range(count)]


def rows_of(first, count):
    return slice(first, first + count)


def smooth(arrived, capacity, block_rows, dip_inline, dip_cross):
    rows, cols = dip_inline.shape
    mid_rows, mid_cols = rows - 2 * BORDER, cols - 2 * BORDER
    both = 2 * BORDER
    same = lambda line: line
    inner = lambda line: line + BORDER
    outer_col = lambda line: line + jnp.where(line < BORDER, 0, mid_cols)
    outer_row = lambda line: line + jnp.where(line < BORDER, 0, mid_rows)
    mid_place = lambda place: place - BORDER
    outer_place = lambda place: place if place < BORDER else place - mid_rows
    every = slice(None)
    lead, last = rows_of(0, HALF), rows_of(both - HALF, HALF)
    left, right, middle_cols = rows_of(0, BORDER), rows_of(cols - BORDER, BORDER), rows_of(BORDER, mid_cols)

    def outer_edge(pick):
        return ((HALF, both), [((pick, left), (every, rows_of(0, BORDER))), ((pick, right), (every, rows_of(BORDER, BORDER)))])

    def whole_edge(shape, pick):
        return (shape, [(pick, (every, every))])

    def mid_windows(places, extent):
        return [(i, WINDOW, places[i - BORDER : i - BORDER + WINDOW + 2 * HALF]) for i in range(BORDER, extent - BORDER, WINDOW)]

    stacked, head_out, tail_out, head_mid, tail_mid = stack_bins(
        arrived, rows, cols, capacity, block_rows,
        [
            outer_edge(rows_of(0, HALF)),
            outer_edge(rows_of(rows - HALF, HALF)),
            whole_edge((HALF, mid_cols), (rows_of(0, HALF), middle_cols)),
            whole_edge((HALF, mid_cols), (rows_of(rows - HALF, HALF), middle_cols)),
        ],
    )
    low_out, high_out = swap_ends(head_out, tail_out, "inline")
    low_mid, high_mid = swap_ends(head_mid, tail_mid, "inline")

    middle, head, tail = steer(
        dip_inline, [(stacked, True)], 0, cols, same,
        mid_windows(span_of(0, BORDER - HALF, mid_rows + 2 * HALF), rows), mid_place,
        edges=[whole_edge((mid_rows, HALF), (every, lead)), whole_edge((mid_rows, HALF), (every, rows_of(cols - HALF, HALF)))],
    )
    left_mid, right_mid = swap_ends(head, tail, "crosslin")
    windows = [
        (0, BORDER, span_of(0, 0, HALF) + span_of(1, 0, BORDER + HALF)),
        (rows - BORDER, BORDER, span_of(1, rows - BORDER - HALF, BORDER + HALF) + span_of(2, 0, HALF)),
    ]
    corners, head, tail = steer(
        dip_inline, [(low_out, False), (stacked, True), (high_out, False)], 0, both, outer_col, windows, outer_place,
        edges=[whole_edge((both, HALF), (every, lead)), whole_edge((both, HALF), (every, last))], after=middle,
    )
    left_out, right_out = swap_ends(head, tail, "crosslin")
    (flanks,) = steer(
        dip_inline, [(low_mid, False), (stacked, True), (high_mid, False)], 0, mid_cols, inner, windows, outer_place,
        after=corners,
    )

    places = span_of(0, BORDER - HALF, HALF) + span_of(1, 0, mid_cols) + span_of(0, BORDER, HALF)
    second_mid, head, tail = steer(
        dip_cross, [(corners, False), (flanks, False)], 1, both, outer_row, mid_windows(places, cols), mid_place,
        edges=[whole_edge((HALF, mid_cols), (lead, every)), whole_edge((HALF, mid_cols), (last, every))],
    )
    low_mid, high_mid = swap_ends(head, tail, "inline")
    places = span_of(0, 0, HALF) + span_of(1, 0, cols) + span_of(2, 0, HALF)
    (middle_second,) = steer(
        dip_cross, [(left_mid, False), (middle, False), (right_mid, False)], 1, mid_rows, inner,
        [(i, WINDOW, places[i : i + WINDOW + 2 * HALF]) for i in range(0, cols, WINDOW)], same, after=second_mid,
    )
    windows = [
        (0, BORDER, span_of(0, 0, HALF) + span_of(1, 0, BORDER) + span_of(2, 0, HALF)),
        (cols - BORDER, BORDER, span_of(2, mid_cols - HALF, HALF) + span_of(1, BORDER, BORDER) + span_of(3, 0, HALF)),
    ]
    border_second, head, tail = steer(
        dip_cross,
        [(left_out, False), (corners, False), (flanks, False), (right_out, False), (second_mid, False)],
        1, both, outer_row, windows, same, filled=(4, (every, middle_cols)),
        edges=[outer_edge(lead), outer_edge(last)], after=middle_second,
    )
    low_out, high_out = swap_ends(head, tail, "inline")

    places = span_of(0, BORDER - HALF, HALF) + span_of(1, 0, mid_rows) + span_of(0, BORDER, HALF)
    (result,) = steer(
        dip_inline, [(border_second, True), (middle_second, True)], 0, cols, same, mid_windows(places, rows), mid_place,
        batches=[[(0, first, WINDOW)] for first in range(0, cols, WINDOW)],
    )
    windows = [
        (0, BORDER, span_of(0, 0, HALF) + span_of(1, 0, BORDER) + span_of(2, 0, HALF)),
        (rows - BORDER, BORDER, span_of(2, mid_rows - HALF, HALF) + span_of(1, BORDER, BORDER) + span_of(3, 0, HALF)),
    ]
    for low, high, lines, line_of, batches in (
        (low_mid, high_mid, mid_cols, inner, [[(0, first, WINDOW)] for first in range(BORDER, cols - BORDER, WINDOW)]),
        (low_out, high_out, both, outer_col, [[(0, 0, BORDER), (BORDER, cols - BORDER, BORDER)]]),
    ):
        (result,) = steer(
            dip_inline, [(low, False), (border_second, True), (middle_second, True), (high, False)], 0, lines, line_of,
            windows, outer_place, batches=batches, before=result,
        )
    return result


def on_device(traces, destination, bin_index, dip_inline, dip_cross):
    held, block_rows, _ = traces.shape
    devices = lax.axis_size("inline") * lax.axis_size("crosslin")
    capacity = 2 * held // devices
    mine = lax.axis_index("inline") * lax.axis_size("crosslin") + lax.axis_index("crosslin")
    outgoing = pack(traces, mine.astype(I32).reshape(1), destination.reshape(-1), bin_index.T, devices, capacity)
    arrived = lax.all_to_all(outgoing, BOTH, split_axis=0, concat_axis=0, tiled=True)
    return smooth(arrived, capacity, block_rows, dip_inline, dip_cross)


def solution(mesh):
    return jax.shard_map(
        on_device,
        mesh=mesh,
        in_specs=(
            P(BOTH, None, None),
            P(BOTH, None),
            P(BOTH, None),
            P("inline", "crosslin"),
            P("inline", "crosslin"),
        ),
        out_specs=P("inline", "crosslin", None),
        check_vma=False,
    )
```

```python
import functools

import jax
import jax.numpy as jnp
from jax import lax
from jax.experimental import pallas as pl
from jax.experimental.pallas import tpu as pltpu
from jax.sharding import PartitionSpec as P

HALF = 7
DMAX = 2
LANES = 128
PHASES = 8
PAIR = 2 * PHASES
WIDE = 2 * LANES
BLOCK = WIDE // PHASES
WINDOW = 16
BORDER = 8
REACH = -(-HALF * DMAX // PHASES)
REACHES = range(-REACH, REACH + 1)
BOTH = ("inline", "crosslin")
MIB = 2**20
VMEM = pl.BlockSpec(memory_space=pltpu.VMEM)
SMEM = pl.BlockSpec(memory_space=pltpu.SMEM)
ANY = pl.BlockSpec(memory_space=pl.ANY)
HBM = pl.BlockSpec(memory_space=pltpu.HBM)
F32, BF16, I32 = jnp.float32, jnp.bfloat16, jnp.int32


def fill_interleave(table_ref, time_dim):
    time = lax.broadcasted_iota(I32, (WIDE, WIDE), time_dim)
    place = lax.broadcasted_iota(I32, (WIDE, WIDE), 1 - time_dim)
    hit = time == place % BLOCK * PHASES + place // BLOCK
    table_ref[...] = jnp.where(hit, 1.0, 0.0).astype(BF16)


def move_samples(rows, table):
    count = rows.shape[0]
    upper = rows.astype(BF16)
    rest = (rows - upper.astype(F32)).astype(BF16)
    both = jnp.concatenate([upper, rest], axis=0)
    moved = jnp.dot(both, table, preferred_element_type=F32)
    return moved[:count] + moved[count:]


def take_lanes(tile, index):
    return jnp.take_along_axis(tile, index, axis=1, mode="promise_in_bounds")


def swap_blocks(tiles):
    lane = lax.broadcasted_iota(I32, tiles[0].shape, 1)
    tiles = list(tiles)
    for step in (2, 1):
        low = lane // BLOCK % (2 * step) < step
        across = lane ^ (step * BLOCK)
        for m in range(len(tiles)):
            if m // step % 2 == 0:
                first, second = tiles[m], tiles[m + step]
                crossed = take_lanes(jnp.where(low, second, first), across)
                tiles[m] = jnp.where(low, first, crossed)
                tiles[m + step] = jnp.where(low, crossed, second)
    return tiles


def pack_kernel(mine_ref, target_ref, bins_ref, traces_ref, out_ref, held_ref, table_ref, tiles_ref, used_ref, listed_ref, in_sems, sem, listed_sem, *, capacity):
    held, block_rows, samples = traces_ref.shape
    devices, room, _ = listed_ref.shape
    span = block_rows * PHASES
    groups = held_ref.shape[0]
    count = held // groups
    loads = [
        pltpu.make_async_copy(traces_ref.at[pl.ds(group * count, count)], held_ref.at[group], in_sems.at[group])
        for group in range(groups)
    ]
    for load in loads:
        load.start()
    fill_interleave(table_ref, 0)
    lane = lax.broadcasted_iota(I32, (1, LANES), 1)
    listed_ref[...] = jnp.zeros(listed_ref.shape, F32)
    own_lanes = mine_ref[0] % (LANES // (capacity * block_rows)) * (capacity * block_rows)

    def clear(device, _):
        used_ref[device] = 0
        return 0

    lax.fori_loop(0, devices, clear, 0)

    def send_block(block, _):
        device = target_ref[block]
        rank = used_ref[device]
        used_ref[device] = rank + 1
        pltpu.make_async_copy(
            tiles_ref.at[pl.ds(pl.multiple_of(block * span, 8), span), :],
            out_ref.at[device, pl.ds(pl.multiple_of(rank * span, 8), span), :],
            sem,
        ).start()
        row = jnp.zeros((1, LANES), I32)
        for j in range(block_rows):
            row = jnp.where(lane == own_lanes + rank * block_rows + j, bins_ref[j, block] + 1, row)
        listed_ref[device, 0:1, :] = listed_ref[device, 0:1, :] + row.astype(F32)
        return 0

    for group in range(groups):
        loads[group].wait()
        rows = held_ref[group].reshape(count * block_rows, samples)
        stretches = samples // WIDE
        cut = jnp.concatenate([rows[:, i * WIDE : (i + 1) * WIDE] for i in range(stretches)], axis=0)
        moved = move_samples(cut, table_ref[...])
        for eight in range(count * block_rows // 8):
            for half in range(2):
                parts = []
                for i in range(stretches):
                    begin = i * count * block_rows + eight * 8
                    parts.append(moved[begin : begin + 8, half * LANES : (half + 1) * LANES])
                for phase, part in enumerate(swap_blocks(parts)):
                    first = (group * count * block_rows + eight * 8) * PHASES + half * 4 + phase
                    tiles_ref[pl.ds(first, 8, stride=PHASES), :] = part
        lax.fori_loop(group * count, (group + 1) * count, send_block, 0, unroll=4)
    copy = pltpu.make_async_copy(
        listed_ref, out_ref.at[:, capacity * span : capacity * span + room, :], listed_sem
    )
    copy.start()
    copy.wait()
    pltpu.make_async_copy(tiles_ref, tiles_ref, sem).wait()


def pack(traces, mine, target, bins, devices, capacity):
    held, block_rows, samples = traces.shape
    span = block_rows * PHASES
    room = 8
    groups = 2
    return pl.pallas_call(
        functools.partial(pack_kernel, capacity=capacity),
        in_specs=[SMEM, SMEM, SMEM, HBM],
        out_specs=HBM,
        out_shape=jax.ShapeDtypeStruct((devices, capacity * span + room, LANES), F32),
        scratch_shapes=[
            pltpu.VMEM((groups, held // groups, block_rows, samples), F32),
            pltpu.VMEM((WIDE, WIDE), BF16),
            pltpu.VMEM((held * span, LANES), F32),
            pltpu.SMEM((devices,), I32),
            pltpu.VMEM((devices, room, LANES), F32),
            pltpu.SemaphoreType.DMA((groups,)),
            pltpu.SemaphoreType.DMA,
            pltpu.SemaphoreType.DMA,
        ],
        compiler_params=pltpu.CompilerParams(vmem_limit_bytes=60 * MIB),
    )(mine, target, bins, traces)


def bin_kernel(blocks_ref, out_ref, *refs, capacity, block_rows, edges):
    edge_refs, refs = refs[: len(edges)], refs[len(edges) :]
    even_ref, odd_ref, listed_ref, places_ref, scale_ref, scales_ref, sem, sems = refs
    devices = blocks_ref.shape[0]
    tile_rows, tile_cols = out_ref.shape[:2]
    bin_total = tile_rows * tile_cols
    unroll = 8
    lanes = capacity * block_rows
    shared = LANES // lanes

    def read_lists(row, _):
        total = jnp.zeros((1, LANES), F32)
        for i in range(shared):
            total = total + blocks_ref[row * shared + i, lanes * PHASES : lanes * PHASES + 1, :]
        listed_ref[pl.ds(row, 1), :] = jnp.where(total > 0, total - 1.0, float(bin_total)).astype(I32)
        return 0

    lax.fori_loop(0, devices // shared, read_lists, 0)
    copy = pltpu.make_async_copy(listed_ref, places_ref, sem)
    copy.start()
    nothing = jnp.zeros((PHASES, LANES), F32)

    def clear(i, _):
        for j in range(unroll):
            even_ref[i * unroll + j] = nothing
            odd_ref[i * unroll + j] = nothing
        return 0

    lax.fori_loop(0, bin_total // unroll, clear, 0)
    copy.wait()
    count_rows = scale_ref.shape[0]
    numbers = lax.broadcasted_iota(I32, (count_rows, LANES), 0) * LANES + lax.broadcasted_iota(
        I32, (count_rows, LANES), 1
    )

    def add_sender(sender, folds):
        folds = list(folds)
        row, first = sender // shared, sender % shared * lanes
        for rank in range(capacity):
            for j in range(block_rows):
                total_ref = odd_ref if j % 2 else even_ref
                place = places_ref[row, first + rank * block_rows + j]
                cell = (rank * block_rows + j) * PHASES
                total_ref[place] += blocks_ref[sender, cell : cell + PHASES, :]
                folds[j % 2] = folds[j % 2] + jnp.where(numbers == place, 1.0, 0.0)
        return tuple(folds)

    empty = jnp.zeros((count_rows, LANES), F32)
    folds = lax.fori_loop(0, devices, add_sender, (empty, empty))
    scale_ref[...] = 1.0 / jnp.maximum(folds[0] + folds[1], 1.0)
    copy = pltpu.make_async_copy(scale_ref, scales_ref, sem)
    copy.start()
    copy.wait()

    def finish(row, _):
        high, low = row * tile_cols // LANES, row * tile_cols % LANES
        for col in range(tile_cols):
            place = row * tile_cols + col
            scale = scales_ref[high, low + col]
            out_ref[row, col] = (even_ref[place] + odd_ref[place]) * scale
        return 0

    lax.fori_loop(0, HALF, finish, 0)
    lax.fori_loop(tile_rows - HALF, tile_rows, finish, 0)
    copies = edge_copies(out_ref, edges, edge_refs, sems)
    for copy in copies:
        copy.start()
    lax.fori_loop(HALF, tile_rows - HALF, finish, 0)
    for copy in copies:
        copy.wait()


def edge_copies(out_ref, edges, edge_refs, sems):
    copies = []
    for (_, moves), edge_ref in zip(edges, edge_refs):
        for source, target in moves:
            copies.append(pltpu.make_async_copy(out_ref.at[source], edge_ref.at[target], sems.at[len(copies)]))
    return copies


def edge_outputs(edges):
    shapes = [jax.ShapeDtypeStruct(tuple(shape) + (PHASES, LANES), F32) for shape, _ in edges]
    moves = sum(len(moves) for _, moves in edges)
    return shapes, [HBM] * len(edges), pltpu.SemaphoreType.DMA((max(1, moves),))


def stack_bins(blocks, tile_rows, tile_cols, capacity, block_rows, edges):
    devices = blocks.shape[0]
    bin_total = tile_rows * tile_cols
    shapes, specs, sems = edge_outputs(edges)
    return pl.pallas_call(
        functools.partial(bin_kernel, capacity=capacity, block_rows=block_rows, edges=edges),
        in_specs=[VMEM],
        out_specs=[VMEM] + specs,
        out_shape=[jax.ShapeDtypeStruct((tile_rows, tile_cols, PHASES, LANES), F32)] + shapes,
        scratch_shapes=[
            pltpu.VMEM((bin_total + 8, PHASES, LANES), F32),
            pltpu.VMEM((bin_total + 8, PHASES, LANES), F32),
            pltpu.VMEM((devices * capacity * block_rows // LANES, LANES), I32),
            pltpu.SMEM((devices * capacity * block_rows // LANES, LANES), I32),
            pltpu.VMEM((bin_total // LANES, LANES), F32),
            pltpu.SMEM((bin_total // LANES, LANES), F32),
            pltpu.SemaphoreType.DMA,
            sems,
        ],
        compiler_params=pltpu.CompilerParams(vmem_limit_bytes=14 * MIB),
    )(blocks)


def fill_weights(spots_ref, weights_ref):
    row = lax.broadcasted_iota(I32, (PAIR, LANES), 0)
    column = lax.broadcasted_iota(I32, (PAIR, LANES), 1)
    for pair in range(spots_ref.shape[0] // (2 * PAIR)):
        for half in range(2):
            block = pl.ds((pair * 2 + half) * PAIR, PAIR)
            spot = half * PAIR + column // PHASES - HALF - 2 * pair - row // PHASES
            share = jnp.maximum(HALF + 1 - jnp.abs(spot), 0).astype(F32) / (HALF + 1) ** 2
            spots_ref[block, :] = jnp.clip(spot, -HALF - 1, HALF + 1).astype(F32).astype(BF16)
            weights_ref[block, :] = share.astype(BF16)


def split_cells(cells, halves_ref):
    for pair in range(len(cells) // 2):
        both = jnp.concatenate([cells[2 * pair](), cells[2 * pair + 1]()], axis=0)
        upper = both.astype(BF16)
        halves_ref[pair * PAIR : (pair + 1) * PAIR, :LANES] = upper
        rest = (both - upper.astype(F32)).astype(BF16)
        halves_ref[pair * PAIR : (pair + 1) * PAIR, LANES:] = rest


def apply_taps(dip_of, first, count, halves_ref, spots_ref, weights_ref):
    row = lax.broadcasted_iota(I32, (PAIR, LANES), 0)
    column = lax.broadcasted_iota(I32, (PAIR, LANES), 1)
    phase_gap = ((row & (PHASES - 1)) - (column & (PHASES - 1))).astype(F32).astype(BF16)
    none = jnp.zeros((PAIR, LANES), BF16)
    taps = []
    for pair in range(count // 2):
        dip = jnp.concatenate(
            [jnp.full((PHASES, LANES), dip_of(first + 2 * pair + i).astype(F32)) for i in range(2)], axis=0
        ).astype(BF16)
        moves, weights = [], []
        for half in range(2):
            block = pl.ds((pair * 2 + half) * PAIR, PAIR)
            moves.append(phase_gap + dip * spots_ref[block, :])
            weights.append(weights_ref[block, :])
        for reach in REACHES:
            taps.append(
                jnp.concatenate(
                    [jnp.where(moves[h] == jnp.bfloat16(reach * PHASES), weights[h], none) for h in range(2)],
                    axis=1,
                )
            )
    half = len(taps) // 2
    return [
        jnp.dot(jnp.concatenate(part, axis=0), halves_ref[...], preferred_element_type=F32)
        for part in (taps[:half], taps[half:])
    ]


def move_lanes(sums, first, count, put):
    lane = lax.broadcasted_iota(I32, (PHASES, LANES), 1)
    for pair in range(count // 2):
        for member in range(2):
            total = None
            for reach in REACHES:
                which, begin = divmod((pair * len(REACHES) + reach + REACH) * PAIR + member * PHASES, sums[0].shape[0])
                part = sums[which][begin : begin + PHASES, :LANES] + sums[which][begin : begin + PHASES, LANES:]
                if reach:
                    part = take_lanes(part, (lane + reach) & (LANES - 1))
                    inside = lane < LANES - reach if reach > 0 else lane >= -reach
                    part = jnp.where(inside, part, 0.0)
                total = part if total is None else total + part
            put(first + 2 * pair + member, total)


def steer_kernel(dip_ref, *refs, along, whole, lines, line_of, windows, local_of, edges, final, batches, filled, chained, pieces_count, abreast):
    pieces, refs = refs[:pieces_count], refs[pieces_count:]
    refs = refs[chained:]
    out_ref, refs = refs[0], refs[1:]
    edge_refs, refs = refs[: len(edges)], refs[len(edges) :]
    spots_ref, weights_ref, sems, *refs = refs
    halves = refs[: abreast * len(windows)]
    if final:
        staged_ref, result_ref, table_ref = refs[abreast * len(windows) :]
        fill_interleave(table_ref, 1)
    fill_weights(spots_ref, weights_ref)
    for i, halves_ref in enumerate(halves):
        used = len(windows[i % len(windows)][2]) * PHASES
        if used < WIDE:
            halves_ref[used:, :] = jnp.zeros((WIDE - used, WIDE), BF16)

    def at(place, line):
        return (place, line) if along == 0 else (line, place)

    def some_lines(step, _):
        jobs = []
        for parity in range(abreast):
            line = abreast * step + parity
            full = line_of(line)

            def cell(index, local, line=line, full=full):
                return lambda: pieces[index][at(local, full if whole[index] else line)]

            def put(place, value, line=line):
                if final:
                    staged_ref[pl.ds((local_of(place) * final + line % final) * PHASES, PHASES), :] = value
                else:
                    out_ref[at(local_of(place), line)] = value

            for i, (first, count, places) in enumerate(windows):
                halves_ref = halves[parity * len(windows) + i]
                split_cells([cell(*place) for place in places], halves_ref)
                jobs.append((full, first, count, halves_ref, put))
        waiting = None
        for full, first, count, halves_ref, put in jobs:
            sums = apply_taps(
                lambda place: dip_ref[at(place, full)], first, count, halves_ref, spots_ref, weights_ref
            )
            if waiting is not None:
                move_lanes(*waiting)
            waiting = (sums, first, count, put)
        move_lanes(*waiting)
        return 0

    if not final:
        if filled is not None:
            index, target = filled
            fill = pltpu.make_async_copy(pieces[index], out_ref.at[target], sems.at[sems.shape[0] - 1])
            fill.start()
        lax.fori_loop(0, lines // abreast, some_lines, 0)
        if filled is not None:
            fill.wait()
        copies = edge_copies(out_ref, edges, edge_refs, sems)
        for copy in copies:
            copy.start()
        for copy in copies:
            copy.wait()
        return

    outputs = sum(count for _, count, _ in windows)

    def copies_of(batch, slot):
        return [
            pltpu.make_async_copy(
                result_ref.at[slot, pl.ds(local_of(first), count), pl.ds(local, wide), :],
                out_ref.at[pl.ds(first, count), pl.ds(full, wide), :],
                sems.at[(slot * len(windows) + i) * len(batches[batch]) + j],
            )
            for i, (first, count, _) in enumerate(windows)
            for j, (local, full, wide) in enumerate(batches[batch])
        ]

    for batch in range(lines // final):
        lax.fori_loop(batch * final // abreast, (batch + 1) * final // abreast, some_lines, 0)
        stretches = PHASES * LANES // WIDE
        cuts = [[] for _ in range(stretches)]
        for eight in range(outputs * final // 8):
            sides = [
                swap_blocks(
                    [
                        staged_ref[pl.ds(eight * 8 * PHASES + half * 4 + phase, 8, stride=PHASES), :]
                        for phase in range(PHASES // 2)
                    ]
                )
                for half in range(2)
            ]
            for i in range(stretches):
                cuts[i].append(jnp.concatenate([sides[0][i], sides[1][i]], axis=1))
        moved = move_samples(jnp.concatenate(sum(cuts, []), axis=0), table_ref[...])
        slot = batch % 2
        if batch >= 2:
            for copy in copies_of(batch - 2, slot):
                copy.wait()
        count = outputs * final
        for i in range(stretches):
            result_ref[slot, :, :, i * WIDE : (i + 1) * WIDE] = moved[i * count : (i + 1) * count].reshape(
                outputs, final, WIDE
            )
        for copy in copies_of(batch, slot):
            copy.start()
    for batch in range(max(0, lines // final - 2), lines // final):
        for copy in copies_of(batch, batch % 2):
            copy.wait()


def steer(
    dip, pieces, along, lines, line_of, windows, local_of, edges=(), batches=None, before=None, after=None, filled=None
):
    samples = PHASES * LANES
    outputs = sum(count for _, count, _ in windows)
    final = 16 if batches is not None else 0
    abreast = 4 * WINDOW // outputs
    shapes, specs, sems = edge_outputs(edges)
    operands = [dip] + [array for array, _ in pieces]
    in_specs = [SMEM] + [VMEM] * len(pieces)
    aliases = {}
    if final:
        if before is not None:
            aliases = {len(operands): 0}
            operands.append(before)
            in_specs.append(HBM)
        out_shape = [jax.ShapeDtypeStruct(dip.shape + (samples,), F32)]
        sems = pltpu.SemaphoreType.DMA((2 * len(windows) * len(batches[0]),))
        out_specs = [HBM]
    else:
        reach = outputs if filled is None else dip.shape[along]
        shape = (reach, lines) if along == 0 else (lines, reach)
        out_shape = [jax.ShapeDtypeStruct(shape + (PHASES, LANES), F32)] + shapes
        out_specs = [VMEM] + specs
        if filled is not None:
            sems = pltpu.SemaphoreType.DMA((sems.shape[0] + 1,))
    if after is not None:
        operands.append(after)
        in_specs.append(ANY)
    most = max(count for _, count, _ in windows)
    constant = pltpu.VMEM((most * PAIR, LANES), BF16)
    scratch = [constant, constant, sems]
    scratch += [pltpu.VMEM((WIDE, WIDE), BF16)] * (abreast * len(windows))
    if final:
        scratch += [
            pltpu.VMEM((outputs * final * PHASES, LANES), F32),
            pltpu.VMEM((2, outputs, final, samples), F32),
            pltpu.VMEM((WIDE, WIDE), BF16),
        ]
    return pl.pallas_call(
        functools.partial(
            steer_kernel,
            along=along, whole=[whole for _, whole in pieces], lines=lines, line_of=line_of, windows=windows,
            local_of=local_of, edges=edges, final=final, batches=batches, filled=filled, chained=len(operands) - len(pieces) - 1, pieces_count=len(pieces), abreast=abreast,
        ),
        in_specs=in_specs,
        out_specs=out_specs,
        out_shape=out_shape,
        scratch_shapes=scratch,
        input_output_aliases=aliases,
        compiler_params=pltpu.CompilerParams(vmem_limit_bytes=16 * MIB),
        cost_estimate=pl.CostEstimate(
            flops=2400 * outputs * lines * samples,
            bytes_accessed=8 * outputs * lines * samples,
            transcendentals=0,
        ),
    )(*operands)


def swap_ends(head, tail, axis):
    count = lax.axis_size(axis)
    low = lax.ppermute(tail, axis, [(i, i + 1) for i in range(count - 1)])
    high = lax.ppermute(head, axis, [(i + 1, i) for i in range(count - 1)])
    return low, high


def span_of(index, first, count):
    return [(index, first + i) for i in range(count)]


def rows_of(first, count):
    return slice(first, first + count)


def smooth(arrived, capacity, block_rows, dip_inline, dip_cross):
    rows, cols = dip_inline.shape
    mid_rows, mid_cols = rows - 2 * BORDER, cols - 2 * BORDER
    both = 2 * BORDER
    same = lambda line: line
    inner = lambda line: line + BORDER
    outer_col = lambda line: line + jnp.where(line < BORDER, 0, mid_cols)
    outer_row = lambda line: line + jnp.where(line < BORDER, 0, mid_rows)
    mid_place = lambda place: place - BORDER
    outer_place = lambda place: place if place < BORDER else place - mid_rows
    every = slice(None)
    lead, last = rows_of(0, HALF), rows_of(both - HALF, HALF)
    left, right, middle_cols = rows_of(0, BORDER), rows_of(cols - BORDER, BORDER), rows_of(BORDER, mid_cols)

    def outer_edge(pick):
        return ((HALF, both), [((pick, left), (every, rows_of(0, BORDER))), ((pick, right), (every, rows_of(BORDER, BORDER)))])

    def whole_edge(shape, pick):
        return (shape, [(pick, (every, every))])

    def mid_windows(places, extent):
        return [(i, WINDOW, places[i - BORDER : i - BORDER + WINDOW + 2 * HALF]) for i in range(BORDER, extent - BORDER, WINDOW)]

    stacked, head_out, tail_out, head_mid, tail_mid = stack_bins(
        arrived, rows, cols, capacity, block_rows,
        [
            outer_edge(rows_of(0, HALF)),
            outer_edge(rows_of(rows - HALF, HALF)),
            whole_edge((HALF, mid_cols), (rows_of(0, HALF), middle_cols)),
            whole_edge((HALF, mid_cols), (rows_of(rows - HALF, HALF), middle_cols)),
        ],
    )
    low_out, high_out = swap_ends(head_out, tail_out, "inline")
    low_mid, high_mid = swap_ends(head_mid, tail_mid, "inline")

    middle, head, tail = steer(
        dip_inline, [(stacked, True)], 0, cols, same,
        mid_windows(span_of(0, BORDER - HALF, mid_rows + 2 * HALF), rows), mid_place,
        edges=[whole_edge((mid_rows, HALF), (every, lead)), whole_edge((mid_rows, HALF), (every, rows_of(cols - HALF, HALF)))],
    )
    left_mid, right_mid = swap_ends(head, tail, "crosslin")
    windows = [
        (0, BORDER, span_of(0, 0, HALF) + span_of(1, 0, BORDER + HALF)),
        (rows - BORDER, BORDER, span_of(1, rows - BORDER - HALF, BORDER + HALF) + span_of(2, 0, HALF)),
    ]
    corners, head, tail = steer(
        dip_inline, [(low_out, False), (stacked, True), (high_out, False)], 0, both, outer_col, windows, outer_place,
        edges=[whole_edge((both, HALF), (every, lead)), whole_edge((both, HALF), (every, last))], after=middle,
    )
    left_out, right_out = swap_ends(head, tail, "crosslin")
    (flanks,) = steer(
        dip_inline, [(low_mid, False), (stacked, True), (high_mid, False)], 0, mid_cols, inner, windows, outer_place,
        after=corners,
    )

    places = span_of(0, BORDER - HALF, HALF) + span_of(1, 0, mid_cols) + span_of(0, BORDER, HALF)
    second_mid, head, tail = steer(
        dip_cross, [(corners, False), (flanks, False)], 1, both, outer_row, mid_windows(places, cols), mid_place,
        edges=[whole_edge((HALF, mid_cols), (lead, every)), whole_edge((HALF, mid_cols), (last, every))],
    )
    low_mid, high_mid = swap_ends(head, tail, "inline")
    places = span_of(0, 0, HALF) + span_of(1, 0, cols) + span_of(2, 0, HALF)
    (middle_second,) = steer(
        dip_cross, [(left_mid, False), (middle, False), (right_mid, False)], 1, mid_rows, inner,
        [(i, WINDOW, places[i : i + WINDOW + 2 * HALF]) for i in range(0, cols, WINDOW)], same, after=second_mid,
    )
    windows = [
        (0, BORDER, span_of(0, 0, HALF) + span_of(1, 0, BORDER) + span_of(2, 0, HALF)),
        (cols - BORDER, BORDER, span_of(2, mid_cols - HALF, HALF) + span_of(1, BORDER, BORDER) + span_of(3, 0, HALF)),
    ]
    border_second, head, tail = steer(
        dip_cross,
        [(left_out, False), (corners, False), (flanks, False), (right_out, False), (second_mid, False)],
        1, both, outer_row, windows, same, filled=(4, (every, middle_cols)),
        edges=[outer_edge(lead), outer_edge(last)], after=middle_second,
    )
    low_out, high_out = swap_ends(head, tail, "inline")

    places = span_of(0, BORDER - HALF, HALF) + span_of(1, 0, mid_rows) + span_of(0, BORDER, HALF)
    (result,) = steer(
        dip_inline, [(border_second, True), (middle_second, True)], 0, cols, same, mid_windows(places, rows), mid_place,
        batches=[[(0, first, WINDOW)] for first in range(0, cols, WINDOW)],
    )
    windows = [
        (0, BORDER, span_of(0, 0, HALF) + span_of(1, 0, BORDER) + span_of(2, 0, HALF)),
        (rows - BORDER, BORDER, span_of(2, mid_rows - HALF, HALF) + span_of(1, BORDER, BORDER) + span_of(3, 0, HALF)),
    ]
    for low, high, lines, line_of, batches in (
        (low_mid, high_mid, mid_cols, inner, [[(0, first, WINDOW)] for first in range(BORDER, cols - BORDER, WINDOW)]),
        (low_out, high_out, both, outer_col, [[(0, 0, BORDER), (BORDER, cols - BORDER, BORDER)]]),
    ):
        (result,) = steer(
            dip_inline, [(low, False), (border_second, True), (middle_second, True), (high, False)], 0, lines, line_of,
            windows, outer_place, batches=batches, before=result,
        )
    return result


def on_device(traces, destination, bin_index, dip_inline, dip_cross):
    held, block_rows, _ = traces.shape
    devices = lax.axis_size("inline") * lax.axis_size("crosslin")
    capacity = 2 * held // devices
    mine = lax.axis_index("inline") * lax.axis_size("crosslin") + lax.axis_index("crosslin")
    outgoing = pack(traces, mine.astype(I32).reshape(1), destination.reshape(-1), bin_index.T, devices, capacity)
    arrived = lax.all_to_all(outgoing, BOTH, split_axis=0, concat_axis=0, tiled=True)
    return smooth(arrived, capacity, block_rows, dip_inline, dip_cross)


def solution(mesh):
    return jax.shard_map(
        on_device,
        mesh=mesh,
        in_specs=(
            P(BOTH, None, None),
            P(BOTH, None),
            P(BOTH, None),
            P("inline", "crosslin"),
            P("inline", "crosslin"),
        ),
        out_specs=P("inline", "crosslin", None),
        check_vma=False,
    )
```

```python
import functools

import jax
import jax.numpy as jnp
from jax import lax
from jax.experimental import pallas as pl
from jax.experimental.pallas import tpu as pltpu
from jax.sharding import PartitionSpec as P

HALF = 7
DMAX = 2
LANES = 128
PHASES = 8
PAIR = 2 * PHASES
WIDE = 2 * LANES
BLOCK = WIDE // PHASES
WINDOW = 16
BORDER = 8
REACH = -(-HALF * DMAX // PHASES)
REACHES = range(-REACH, REACH + 1)
FAR = [reach for reach in REACHES if abs(reach) > 1]
BOTH = ("inline", "crosslin")
MIB = 2**20
VMEM = pl.BlockSpec(memory_space=pltpu.VMEM)
SMEM = pl.BlockSpec(memory_space=pltpu.SMEM)
ANY = pl.BlockSpec(memory_space=pl.ANY)
HBM = pl.BlockSpec(memory_space=pltpu.HBM)
F32, BF16, I32 = jnp.float32, jnp.bfloat16, jnp.int32


def fill_interleave(table_ref, time_dim):
    time = lax.broadcasted_iota(I32, (WIDE, WIDE), time_dim)
    place = lax.broadcasted_iota(I32, (WIDE, WIDE), 1 - time_dim)
    hit = time == place % BLOCK * PHASES + place // BLOCK
    table_ref[...] = jnp.where(hit, 1.0, 0.0).astype(BF16)


def move_samples(rows, table):
    count = rows.shape[0]
    upper = rows.astype(BF16)
    rest = (rows - upper.astype(F32)).astype(BF16)
    both = jnp.concatenate([upper, rest], axis=0)
    moved = jnp.dot(both, table, preferred_element_type=F32)
    return moved[:count] + moved[count:]


def take_lanes(tile, index):
    return jnp.take_along_axis(tile, index, axis=1, mode="promise_in_bounds")


def swap_blocks(tiles):
    lane = lax.broadcasted_iota(I32, tiles[0].shape, 1)
    tiles = list(tiles)
    for step in (2, 1):
        low = lane // BLOCK % (2 * step) < step
        across = lane ^ (step * BLOCK)
        for m in range(len(tiles)):
            if m // step % 2 == 0:
                first, second = tiles[m], tiles[m + step]
                mixed = jnp.where(low, second, first)
                crossed = pltpu.roll(mixed, LANES // 2, axis=1) if 2 * step * BLOCK == LANES else take_lanes(mixed, across)
                tiles[m] = jnp.where(low, first, crossed)
                tiles[m + step] = jnp.where(low, crossed, second)
    return tiles


def pack_kernel(mine_ref, target_ref, bins_ref, traces_ref, out_ref, held_ref, table_ref, tiles_ref, used_ref, listed_ref, in_sems, sem, listed_sem, *, capacity):
    held, block_rows, samples = traces_ref.shape
    devices, room, _ = listed_ref.shape
    span = block_rows * PHASES
    groups = held_ref.shape[0]
    count = held // groups
    loads = [
        pltpu.make_async_copy(traces_ref.at[pl.ds(group * count, count)], held_ref.at[group], in_sems.at[group])
        for group in range(groups)
    ]
    for load in loads:
        load.start()
    fill_interleave(table_ref, 0)
    lane = lax.broadcasted_iota(I32, (1, LANES), 1)
    listed_ref[...] = jnp.zeros(listed_ref.shape, F32)
    own_lanes = mine_ref[0] % (LANES // (capacity * block_rows)) * (capacity * block_rows)

    def clear(device, _):
        used_ref[device] = 0
        return 0

    lax.fori_loop(0, devices, clear, 0)

    def send_block(block, _):
        device = target_ref[block]
        rank = used_ref[device]
        used_ref[device] = rank + 1
        pltpu.make_async_copy(
            tiles_ref.at[pl.ds(pl.multiple_of(block * span, 8), span), :],
            out_ref.at[device, pl.ds(pl.multiple_of(rank * span, 8), span), :],
            sem,
        ).start()
        row = jnp.zeros((1, LANES), I32)
        for j in range(block_rows):
            row = jnp.where(lane == own_lanes + rank * block_rows + j, bins_ref[j, block] + 1, row)
        listed_ref[device, 0:1, :] = listed_ref[device, 0:1, :] + row.astype(F32)
        return 0

    for group in range(groups):
        loads[group].wait()
        rows = held_ref[group].reshape(count * block_rows, samples)
        stretches = samples // WIDE
        cut = jnp.concatenate([rows[:, i * WIDE : (i + 1) * WIDE] for i in range(stretches)], axis=0)
        moved = move_samples(cut, table_ref[...])
        for eight in range(count * block_rows // 8):
            for half in range(2):
                parts = []
                for i in range(stretches):
                    begin = i * count * block_rows + eight * 8
                    parts.append(moved[begin : begin + 8, half * LANES : (half + 1) * LANES])
                for phase, part in enumerate(swap_blocks(parts)):
                    first = (group * count * block_rows + eight * 8) * PHASES + half * 4 + phase
                    tiles_ref[pl.ds(first, 8, stride=PHASES), :] = part
        lax.fori_loop(group * count, (group + 1) * count, send_block, 0, unroll=4)
    copy = pltpu.make_async_copy(
        listed_ref, out_ref.at[:, capacity * span : capacity * span + room, :], listed_sem
    )
    copy.start()
    copy.wait()
    pltpu.make_async_copy(tiles_ref, tiles_ref, sem).wait()


def pack(traces, mine, target, bins, devices, capacity):
    held, block_rows, samples = traces.shape
    span = block_rows * PHASES
    room = 8
    groups = 2
    return pl.pallas_call(
        functools.partial(pack_kernel, capacity=capacity),
        in_specs=[SMEM, SMEM, SMEM, HBM],
        out_specs=HBM,
        out_shape=jax.ShapeDtypeStruct((devices, capacity * span + room, LANES), F32),
        scratch_shapes=[
            pltpu.VMEM((groups, held // groups, block_rows, samples), F32),
            pltpu.VMEM((WIDE, WIDE), BF16),
            pltpu.VMEM((held * span, LANES), F32),
            pltpu.SMEM((devices,), I32),
            pltpu.VMEM((devices, room, LANES), F32),
            pltpu.SemaphoreType.DMA((groups,)),
            pltpu.SemaphoreType.DMA,
            pltpu.SemaphoreType.DMA,
        ],
        compiler_params=pltpu.CompilerParams(vmem_limit_bytes=60 * MIB),
    )(mine, target, bins, traces)


def bin_kernel(blocks_ref, out_ref, *refs, capacity, block_rows, edges):
    edge_refs, refs = refs[: len(edges)], refs[len(edges) :]
    even_ref, odd_ref, listed_ref, places_ref, scale_ref, scales_ref, sem, sems = refs
    devices = blocks_ref.shape[0]
    tile_rows, tile_cols = out_ref.shape[:2]
    bin_total = tile_rows * tile_cols
    unroll = 8
    lanes = capacity * block_rows
    shared = LANES // lanes

    def read_lists(row, _):
        total = jnp.zeros((1, LANES), F32)
        for i in range(shared):
            total = total + blocks_ref[row * shared + i, lanes * PHASES : lanes * PHASES + 1, :]
        listed_ref[pl.ds(row, 1), :] = jnp.where(total > 0, total - 1.0, float(bin_total)).astype(I32)
        return 0

    lax.fori_loop(0, devices // shared, read_lists, 0)
    copy = pltpu.make_async_copy(listed_ref, places_ref, sem)
    copy.start()
    nothing = jnp.zeros((PHASES, LANES), F32)

    def clear(i, _):
        for j in range(unroll):
            even_ref[i * unroll + j] = nothing
            odd_ref[i * unroll + j] = nothing
        return 0

    lax.fori_loop(0, bin_total // unroll, clear, 0)
    copy.wait()
    count_rows = scale_ref.shape[0]
    numbers = lax.broadcasted_iota(I32, (count_rows, LANES), 0) * LANES + lax.broadcasted_iota(
        I32, (count_rows, LANES), 1
    )

    def add_sender(sender, folds):
        folds = list(folds)
        row, first = sender // shared, sender % shared * lanes
        for rank in range(capacity):
            for j in range(block_rows):
                total_ref = odd_ref if j % 2 else even_ref
                place = places_ref[row, first + rank * block_rows + j]
                cell = (rank * block_rows + j) * PHASES
                total_ref[place] += blocks_ref[sender, cell : cell + PHASES, :]
                folds[j % 2] = folds[j % 2] + jnp.where(numbers == place, 1.0, 0.0)
        return tuple(folds)

    empty = jnp.zeros((count_rows, LANES), F32)
    folds = lax.fori_loop(0, devices, add_sender, (empty, empty))
    scale_ref[...] = 1.0 / jnp.maximum(folds[0] + folds[1], 1.0)
    copy = pltpu.make_async_copy(scale_ref, scales_ref, sem)
    copy.start()
    copy.wait()

    def finish(row, _):
        high, low = row * tile_cols // LANES, row * tile_cols % LANES
        for col in range(tile_cols):
            place = row * tile_cols + col
            scale = scales_ref[high, low + col]
            out_ref[row, col] = (even_ref[place] + odd_ref[place]) * scale
        return 0

    lax.fori_loop(0, HALF, finish, 0)
    lax.fori_loop(tile_rows - HALF, tile_rows, finish, 0)
    copies = edge_copies(out_ref, edges, edge_refs, sems)
    for copy in copies:
        copy.start()
    lax.fori_loop(HALF, tile_rows - HALF, finish, 0)
    for copy in copies:
        copy.wait()


def edge_copies(out_ref, edges, edge_refs, sems):
    copies = []
    for (_, moves), edge_ref in zip(edges, edge_refs):
        for source, target in moves:
            copies.append(pltpu.make_async_copy(out_ref.at[source], edge_ref.at[target], sems.at[len(copies)]))
    return copies


def edge_outputs(edges):
    shapes = [jax.ShapeDtypeStruct(tuple(shape) + (PHASES, LANES), F32) for shape, _ in edges]
    moves = sum(len(moves) for _, moves in edges)
    return shapes, [HBM] * len(edges), pltpu.SemaphoreType.DMA((max(1, moves),))


def stack_bins(blocks, tile_rows, tile_cols, capacity, block_rows, edges):
    devices = blocks.shape[0]
    bin_total = tile_rows * tile_cols
    shapes, specs, sems = edge_outputs(edges)
    return pl.pallas_call(
        functools.partial(bin_kernel, capacity=capacity, block_rows=block_rows, edges=edges),
        in_specs=[VMEM],
        out_specs=[VMEM] + specs,
        out_shape=[jax.ShapeDtypeStruct((tile_rows, tile_cols, PHASES, LANES), F32)] + shapes,
        scratch_shapes=[
            pltpu.VMEM((bin_total + 8, PHASES, LANES), F32),
            pltpu.VMEM((bin_total + 8, PHASES, LANES), F32),
            pltpu.VMEM((devices * capacity * block_rows // LANES, LANES), I32),
            pltpu.SMEM((devices * capacity * block_rows // LANES, LANES), I32),
            pltpu.VMEM((bin_total // LANES, LANES), F32),
            pltpu.SMEM((bin_total // LANES, LANES), F32),
            pltpu.SemaphoreType.DMA,
            sems,
        ],
        compiler_params=pltpu.CompilerParams(vmem_limit_bytes=14 * MIB),
    )(blocks)


def fill_weights(spots_ref, weights_ref):
    row = lax.broadcasted_iota(I32, (PAIR, LANES), 0)
    column = lax.broadcasted_iota(I32, (PAIR, LANES), 1)
    for pair in range(spots_ref.shape[0] // (2 * PAIR)):
        for half in range(2):
            block = pl.ds((pair * 2 + half) * PAIR, PAIR)
            spot = half * PAIR + column // PHASES - HALF - 2 * pair - row // PHASES
            share = jnp.maximum(HALF + 1 - jnp.abs(spot), 0).astype(F32) / (HALF + 1) ** 2
            spots_ref[block, :] = jnp.clip(spot, -HALF - 1, HALF + 1).astype(F32).astype(BF16)
            weights_ref[block, :] = share.astype(BF16)


def split_cells(cells, halves_ref):
    for pair in range(len(cells) // 2):
        both = jnp.concatenate([cells[2 * pair](), cells[2 * pair + 1]()], axis=0)
        upper = both.astype(BF16)
        halves_ref[pair * PAIR : (pair + 1) * PAIR, :LANES] = upper
        rest = (both - upper.astype(F32)).astype(BF16)
        halves_ref[pair * PAIR : (pair + 1) * PAIR, LANES:] = rest


def apply_taps(dip_of, first, count, halves_ref, spots_ref, weights_ref):
    row = lax.broadcasted_iota(I32, (PAIR, LANES), 0)
    column = lax.broadcasted_iota(I32, (PAIR, LANES), 1)
    phase_gap = ((row & (PHASES - 1)) - (column & (PHASES - 1))).astype(F32).astype(BF16)
    none = jnp.zeros((PAIR, LANES), BF16)
    taps = []
    for pair in range(count // 2):
        dip = jnp.concatenate(
            [jnp.full((PHASES, LANES), dip_of(first + 2 * pair + i).astype(F32)) for i in range(2)], axis=0
        ).astype(BF16)
        moves, weights = [], []
        for half in range(2):
            block = pl.ds((pair * 2 + half) * PAIR, PAIR)
            moves.append(phase_gap + dip * spots_ref[block, :])
            weights.append(weights_ref[block, :])
        for reach in REACHES:
            taps.append(
                jnp.concatenate(
                    [jnp.where(moves[h] == jnp.bfloat16(reach * PHASES), weights[h], none) for h in range(2)],
                    axis=1,
                )
            )
    return jnp.dot(jnp.concatenate(taps, axis=0), halves_ref[...], preferred_element_type=F32)


def fill_shift(shift_ref):
    size = shift_ref.shape[0]
    source = lax.broadcasted_iota(I32, (size, LANES), 0)
    lane = lax.broadcasted_iota(I32, (size, LANES), 1)
    hit = jnp.zeros((size, LANES), jnp.bool_)
    for i, reach in enumerate(FAR):
        hit = hit | ((source // LANES == i) & (source % LANES == lane + reach))
    shift_ref[...] = jnp.where(hit, 1.0, 0.0).astype(BF16)


def move_lanes(sums, first, count, put, shift_ref):
    lane = lax.broadcasted_iota(I32, (PAIR, LANES), 1)

    def part(pair, reach):
        begin = (pair * len(REACHES) + reach + REACH) * PAIR
        return sums[begin : begin + PAIR, :LANES] + sums[begin : begin + PAIR, LANES:]

    upper, rest = [], []
    for pair in range(count // 2):
        far = jnp.concatenate([part(pair, reach) for reach in FAR], axis=1)
        upper.append(far.astype(BF16))
        rest.append((far - upper[-1].astype(F32)).astype(BF16))
    far = jnp.dot(jnp.concatenate(upper + rest, axis=0), shift_ref[...], preferred_element_type=F32)
    rows = count * PHASES
    for pair in range(count // 2):
        total = far[pair * PAIR : (pair + 1) * PAIR] + far[rows + pair * PAIR : rows + (pair + 1) * PAIR]
        for reach in REACHES:
            if reach not in FAR:
                near = part(pair, reach)
                if reach:
                    near = pltpu.roll(near, (-reach) % LANES, axis=1)
                    inside = lane < LANES - reach if reach > 0 else lane >= -reach
                    near = jnp.where(inside, near, 0.0)
                total = total + near
        for member in range(2):
            put(first + 2 * pair + member, total[member * PHASES : (member + 1) * PHASES])


def steer_kernel(dip_ref, *refs, along, whole, lines, line_of, windows, local_of, edges, final, batches, filled, chained, pieces_count, abreast):
    pieces, refs = refs[:pieces_count], refs[pieces_count:]
    refs = refs[chained:]
    out_ref, refs = refs[0], refs[1:]
    edge_refs, refs = refs[: len(edges)], refs[len(edges) :]
    spots_ref, weights_ref, shift_ref, sems, *refs = refs
    halves = refs[: abreast * len(windows)]
    if final:
        staged_ref, result_ref, table_ref = refs[abreast * len(windows) :]
        fill_interleave(table_ref, 1)
    fill_weights(spots_ref, weights_ref)
    fill_shift(shift_ref)
    for i, halves_ref in enumerate(halves):
        used = len(windows[i % len(windows)][2]) * PHASES
        if used < WIDE:
            halves_ref[used:, :] = jnp.zeros((WIDE - used, WIDE), BF16)

    def at(place, line):
        return (place, line) if along == 0 else (line, place)

    def some_lines(step, _):
        jobs = []
        for parity in range(abreast):
            line = abreast * step + parity
            full = line_of(line)

            def cell(index, local, line=line, full=full):
                return lambda: pieces[index][at(local, full if whole[index] else line)]

            def put(place, value, line=line):
                if final:
                    staged_ref[pl.ds((local_of(place) * final + line % final) * PHASES, PHASES), :] = value
                else:
                    out_ref[at(local_of(place), line)] = value

            for i, (first, count, places) in enumerate(windows):
                halves_ref = halves[parity * len(windows) + i]
                split_cells([cell(*place) for place in places], halves_ref)
                jobs.append((full, first, count, halves_ref, put))
        waiting = None
        for full, first, count, halves_ref, put in jobs:
            sums = apply_taps(
                lambda place: dip_ref[at(place, full)], first, count, halves_ref, spots_ref, weights_ref
            )
            if waiting is not None:
                move_lanes(*waiting)
            waiting = (sums, first, count, put, shift_ref)
        move_lanes(*waiting)
        return 0

    if not final:
        if filled is not None:
            index, target = filled
            fill = pltpu.make_async_copy(pieces[index], out_ref.at[target], sems.at[sems.shape[0] - 1])
            fill.start()
        lax.fori_loop(0, lines // abreast, some_lines, 0)
        if filled is not None:
            fill.wait()
        copies = edge_copies(out_ref, edges, edge_refs, sems)
        for copy in copies:
            copy.start()
        for copy in copies:
            copy.wait()
        return

    outputs = sum(count for _, count, _ in windows)

    def copies_of(batch, slot):
        return [
            pltpu.make_async_copy(
                result_ref.at[slot, pl.ds(local_of(first), count), pl.ds(local, wide), :],
                out_ref.at[pl.ds(first, count), pl.ds(full, wide), :],
                sems.at[(slot * len(windows) + i) * len(batches[batch]) + j],
            )
            for i, (first, count, _) in enumerate(windows)
            for j, (local, full, wide) in enumerate(batches[batch])
        ]

    for batch in range(lines // final):
        lax.fori_loop(batch * final // abreast, (batch + 1) * final // abreast, some_lines, 0)
        stretches = PHASES * LANES // WIDE
        cuts = [[] for _ in range(stretches)]
        for eight in range(outputs * final // 8):
            sides = [
                swap_blocks(
                    [
                        staged_ref[pl.ds(eight * 8 * PHASES + half * 4 + phase, 8, stride=PHASES), :]
                        for phase in range(PHASES // 2)
                    ]
                )
                for half in range(2)
            ]
            for i in range(stretches):
                cuts[i].append(jnp.concatenate([sides[0][i], sides[1][i]], axis=1))
        moved = move_samples(jnp.concatenate(sum(cuts, []), axis=0), table_ref[...])
        slot = batch % 2
        if batch >= 2:
            for copy in copies_of(batch - 2, slot):
                copy.wait()
        count = outputs * final
        for i in range(stretches):
            result_ref[slot, :, :, i * WIDE : (i + 1) * WIDE] = moved[i * count : (i + 1) * count].reshape(
                outputs, final, WIDE
            )
        for copy in copies_of(batch, slot):
            copy.start()
    for batch in range(max(0, lines // final - 2), lines // final):
        for copy in copies_of(batch, batch % 2):
            copy.wait()


def steer(
    dip, pieces, along, lines, line_of, windows, local_of, edges=(), batches=None, before=None, after=None, filled=None
):
    samples = PHASES * LANES
    outputs = sum(count for _, count, _ in windows)
    final = 16 if batches is not None else 0
    abreast = 4 * WINDOW // outputs
    shapes, specs, sems = edge_outputs(edges)
    operands = [dip] + [array for array, _ in pieces]
    in_specs = [SMEM] + [VMEM] * len(pieces)
    aliases = {}
    if final:
        if before is not None:
            aliases = {len(operands): 0}
            operands.append(before)
            in_specs.append(HBM)
        out_shape = [jax.ShapeDtypeStruct(dip.shape + (samples,), F32)]
        sems = pltpu.SemaphoreType.DMA((2 * len(windows) * len(batches[0]),))
        out_specs = [HBM]
    else:
        reach = outputs if filled is None else dip.shape[along]
        shape = (reach, lines) if along == 0 else (lines, reach)
        out_shape = [jax.ShapeDtypeStruct(shape + (PHASES, LANES), F32)] + shapes
        out_specs = [VMEM] + specs
        if filled is not None:
            sems = pltpu.SemaphoreType.DMA((sems.shape[0] + 1,))
    if after is not None:
        operands.append(after)
        in_specs.append(ANY)
    most = max(count for _, count, _ in windows)
    constant = pltpu.VMEM((most * PAIR, LANES), BF16)
    scratch = [constant, constant, pltpu.VMEM((len(FAR) * LANES, LANES), BF16), sems]
    scratch += [pltpu.VMEM((WIDE, WIDE), BF16)] * (abreast * len(windows))
    if final:
        scratch += [
            pltpu.VMEM((outputs * final * PHASES, LANES), F32),
            pltpu.VMEM((2, outputs, final, samples), F32),
            pltpu.VMEM((WIDE, WIDE), BF16),
        ]
    return pl.pallas_call(
        functools.partial(
            steer_kernel,
            along=along, whole=[whole for _, whole in pieces], lines=lines, line_of=line_of, windows=windows,
            local_of=local_of, edges=edges, final=final, batches=batches, filled=filled, chained=len(operands) - len(pieces) - 1, pieces_count=len(pieces), abreast=abreast,
        ),
        in_specs=in_specs,
        out_specs=out_specs,
        out_shape=out_shape,
        scratch_shapes=scratch,
        input_output_aliases=aliases,
        compiler_params=pltpu.CompilerParams(vmem_limit_bytes=16 * MIB),
        cost_estimate=pl.CostEstimate(
            flops=2400 * outputs * lines * samples,
            bytes_accessed=8 * outputs * lines * samples,
            transcendentals=0,
        ),
    )(*operands)


def swap_ends(head, tail, axis):
    count = lax.axis_size(axis)
    low = lax.ppermute(tail, axis, [(i, i + 1) for i in range(count - 1)])
    high = lax.ppermute(head, axis, [(i + 1, i) for i in range(count - 1)])
    return low, high


def span_of(index, first, count):
    return [(index, first + i) for i in range(count)]


def rows_of(first, count):
    return slice(first, first + count)


def smooth(arrived, capacity, block_rows, dip_inline, dip_cross):
    rows, cols = dip_inline.shape
    mid_rows, mid_cols = rows - 2 * BORDER, cols - 2 * BORDER
    both = 2 * BORDER
    same = lambda line: line
    inner = lambda line: line + BORDER
    outer_col = lambda line: line + jnp.where(line < BORDER, 0, mid_cols)
    outer_row = lambda line: line + jnp.where(line < BORDER, 0, mid_rows)
    mid_place = lambda place: place - BORDER
    outer_place = lambda place: place if place < BORDER else place - mid_rows
    every = slice(None)
    lead, last = rows_of(0, HALF), rows_of(both - HALF, HALF)
    left, right, middle_cols = rows_of(0, BORDER), rows_of(cols - BORDER, BORDER), rows_of(BORDER, mid_cols)

    def outer_edge(pick):
        return ((HALF, both), [((pick, left), (every, rows_of(0, BORDER))), ((pick, right), (every, rows_of(BORDER, BORDER)))])

    def whole_edge(shape, pick):
        return (shape, [(pick, (every, every))])

    def mid_windows(places, extent):
        return [(i, WINDOW, places[i - BORDER : i - BORDER + WINDOW + 2 * HALF]) for i in range(BORDER, extent - BORDER, WINDOW)]

    stacked, head_out, tail_out, head_mid, tail_mid = stack_bins(
        arrived, rows, cols, capacity, block_rows,
        [
            outer_edge(rows_of(0, HALF)),
            outer_edge(rows_of(rows - HALF, HALF)),
            whole_edge((HALF, mid_cols), (rows_of(0, HALF), middle_cols)),
            whole_edge((HALF, mid_cols), (rows_of(rows - HALF, HALF), middle_cols)),
        ],
    )
    low_out, high_out = swap_ends(head_out, tail_out, "inline")
    low_mid, high_mid = swap_ends(head_mid, tail_mid, "inline")

    middle, head, tail = steer(
        dip_inline, [(stacked, True)], 0, cols, same,
        mid_windows(span_of(0, BORDER - HALF, mid_rows + 2 * HALF), rows), mid_place,
        edges=[whole_edge((mid_rows, HALF), (every, lead)), whole_edge((mid_rows, HALF), (every, rows_of(cols - HALF, HALF)))],
    )
    left_mid, right_mid = swap_ends(head, tail, "crosslin")
    windows = [
        (0, BORDER, span_of(0, 0, HALF) + span_of(1, 0, BORDER + HALF)),
        (rows - BORDER, BORDER, span_of(1, rows - BORDER - HALF, BORDER + HALF) + span_of(2, 0, HALF)),
    ]
    corners, head, tail = steer(
        dip_inline, [(low_out, False), (stacked, True), (high_out, False)], 0, both, outer_col, windows, outer_place,
        edges=[whole_edge((both, HALF), (every, lead)), whole_edge((both, HALF), (every, last))], after=middle,
    )
    left_out, right_out = swap_ends(head, tail, "crosslin")
    (flanks,) = steer(
        dip_inline, [(low_mid, False), (stacked, True), (high_mid, False)], 0, mid_cols, inner, windows, outer_place,
        after=corners,
    )

    places = span_of(0, BORDER - HALF, HALF) + span_of(1, 0, mid_cols) + span_of(0, BORDER, HALF)
    second_mid, head, tail = steer(
        dip_cross, [(corners, False), (flanks, False)], 1, both, outer_row, mid_windows(places, cols), mid_place,
        edges=[whole_edge((HALF, mid_cols), (lead, every)), whole_edge((HALF, mid_cols), (last, every))],
    )
    low_mid, high_mid = swap_ends(head, tail, "inline")
    places = span_of(0, 0, HALF) + span_of(1, 0, cols) + span_of(2, 0, HALF)
    (middle_second,) = steer(
        dip_cross, [(left_mid, False), (middle, False), (right_mid, False)], 1, mid_rows, inner,
        [(i, WINDOW, places[i : i + WINDOW + 2 * HALF]) for i in range(0, cols, WINDOW)], same, after=second_mid,
    )
    windows = [
        (0, BORDER, span_of(0, 0, HALF) + span_of(1, 0, BORDER) + span_of(2, 0, HALF)),
        (cols - BORDER, BORDER, span_of(2, mid_cols - HALF, HALF) + span_of(1, BORDER, BORDER) + span_of(3, 0, HALF)),
    ]
    border_second, head, tail = steer(
        dip_cross,
        [(left_out, False), (corners, False), (flanks, False), (right_out, False), (second_mid, False)],
        1, both, outer_row, windows, same, filled=(4, (every, middle_cols)),
        edges=[outer_edge(lead), outer_edge(last)], after=middle_second,
    )
    low_out, high_out = swap_ends(head, tail, "inline")

    places = span_of(0, BORDER - HALF, HALF) + span_of(1, 0, mid_rows) + span_of(0, BORDER, HALF)
    (result,) = steer(
        dip_inline, [(border_second, True), (middle_second, True)], 0, cols, same, mid_windows(places, rows), mid_place,
        batches=[[(0, first, WINDOW)] for first in range(0, cols, WINDOW)],
    )
    windows = [
        (0, BORDER, span_of(0, 0, HALF) + span_of(1, 0, BORDER) + span_of(2, 0, HALF)),
        (rows - BORDER, BORDER, span_of(2, mid_rows - HALF, HALF) + span_of(1, BORDER, BORDER) + span_of(3, 0, HALF)),
    ]
    for low, high, lines, line_of, batches in (
        (low_mid, high_mid, mid_cols, inner, [[(0, first, WINDOW)] for first in range(BORDER, cols - BORDER, WINDOW)]),
        (low_out, high_out, both, outer_col, [[(0, 0, BORDER), (BORDER, cols - BORDER, BORDER)]]),
    ):
        (result,) = steer(
            dip_inline, [(low, False), (border_second, True), (middle_second, True), (high, False)], 0, lines, line_of,
            windows, outer_place, batches=batches, before=result,
        )
    return result


def on_device(traces, destination, bin_index, dip_inline, dip_cross):
    held, block_rows, _ = traces.shape
    devices = lax.axis_size("inline") * lax.axis_size("crosslin")
    capacity = 2 * held // devices
    mine = lax.axis_index("inline") * lax.axis_size("crosslin") + lax.axis_index("crosslin")
    outgoing = pack(traces, mine.astype(I32).reshape(1), destination.reshape(-1), bin_index.T, devices, capacity)
    arrived = lax.all_to_all(outgoing, BOTH, split_axis=0, concat_axis=0, tiled=True)
    return smooth(arrived, capacity, block_rows, dip_inline, dip_cross)


def solution(mesh):
    return jax.shard_map(
        on_device,
        mesh=mesh,
        in_specs=(
            P(BOTH, None, None),
            P(BOTH, None),
            P(BOTH, None),
            P("inline", "crosslin"),
            P("inline", "crosslin"),
        ),
        out_specs=P("inline", "crosslin", None),
        check_vma=False,
    )
```

```python
import functools

import jax
import jax.numpy as jnp
from jax import lax
from jax.experimental import pallas as pl
from jax.experimental.pallas import tpu as pltpu
from jax.sharding import PartitionSpec as P

HALF = 7
DMAX = 2
LANES = 128
PHASES = 8
PAIR = 2 * PHASES
WIDE = 2 * LANES
BLOCK = WIDE // PHASES
WINDOW = 16
BORDER = 8
REACH = -(-HALF * DMAX // PHASES)
REACHES = range(-REACH, REACH + 1)
BOTH = ("inline", "crosslin")
MIB = 2**20
VMEM = pl.BlockSpec(memory_space=pltpu.VMEM)
SMEM = pl.BlockSpec(memory_space=pltpu.SMEM)
ANY = pl.BlockSpec(memory_space=pl.ANY)
HBM = pl.BlockSpec(memory_space=pltpu.HBM)
F32, BF16, I32 = jnp.float32, jnp.bfloat16, jnp.int32


def fill_interleave(table_ref, time_dim):
    time = lax.broadcasted_iota(I32, (WIDE, WIDE), time_dim)
    place = lax.broadcasted_iota(I32, (WIDE, WIDE), 1 - time_dim)
    hit = time == place % BLOCK * PHASES + place // BLOCK
    table_ref[...] = jnp.where(hit, 1.0, 0.0).astype(BF16)


def move_samples(rows, table):
    count = rows.shape[0]
    upper = rows.astype(BF16)
    rest = (rows - upper.astype(F32)).astype(BF16)
    both = jnp.concatenate([upper, rest], axis=0)
    moved = jnp.dot(both, table, preferred_element_type=F32)
    return moved[:count] + moved[count:]


def take_lanes(tile, index):
    return jnp.take_along_axis(tile, index, axis=1, mode="promise_in_bounds")


def swap_blocks(tiles):
    lane = lax.broadcasted_iota(I32, tiles[0].shape, 1)
    tiles = list(tiles)
    for step in (2, 1):
        low = lane // BLOCK % (2 * step) < step
        across = lane ^ (step * BLOCK)
        for m in range(len(tiles)):
            if m // step % 2 == 0:
                first, second = tiles[m], tiles[m + step]
                crossed = take_lanes(jnp.where(low, second, first), across)
                tiles[m] = jnp.where(low, first, crossed)
                tiles[m + step] = jnp.where(low, crossed, second)
    return tiles


def pack_kernel(mine_ref, target_ref, bins_ref, traces_ref, out_ref, held_ref, table_ref, tiles_ref, used_ref, rank_ref, listed_ref, in_sems, sem, listed_sem, *, capacity):
    held, block_rows, samples = traces_ref.shape
    devices, room, _ = listed_ref.shape
    span = block_rows * PHASES
    groups = held_ref.shape[0]
    count = held // groups
    loads = [
        pltpu.make_async_copy(traces_ref.at[pl.ds(group * count, count)], held_ref.at[group], in_sems.at[group])
        for group in range(groups)
    ]
    for load in loads:
        load.start()
    fill_interleave(table_ref, 0)
    lane = lax.broadcasted_iota(I32, (1, LANES), 1)
    listed_ref[...] = jnp.zeros(listed_ref.shape, F32)
    own_lanes = mine_ref[0] % (LANES // (capacity * block_rows)) * (capacity * block_rows)

    def clear(device, _):
        used_ref[device] = 0
        return 0

    lax.fori_loop(0, devices, clear, 0)

    def choose_slot(block, _):
        device = target_ref[block]
        rank = used_ref[device]
        used_ref[device] = rank + 1
        rank_ref[block] = rank
        row = jnp.zeros((1, LANES), I32)
        for j in range(block_rows):
            row = jnp.where(lane == own_lanes + rank * block_rows + j, bins_ref[j, block] + 1, row)
        listed_ref[device, 0:1, :] = listed_ref[device, 0:1, :] + row.astype(F32)
        return 0

    lax.fori_loop(0, held, choose_slot, 0, unroll=4)
    lists = pltpu.make_async_copy(
        listed_ref, out_ref.at[:, capacity * span : capacity * span + room, :], listed_sem
    )
    lists.start()

    def send_block(block, _):
        pltpu.make_async_copy(
            tiles_ref.at[pl.ds(pl.multiple_of(block * span, 8), span), :],
            out_ref.at[target_ref[block], pl.ds(pl.multiple_of(rank_ref[block] * span, 8), span), :],
            sem,
        ).start()
        return 0

    for group in range(groups):
        loads[group].wait()
        rows = held_ref[group].reshape(count * block_rows, samples)
        stretches = samples // WIDE
        cut = jnp.concatenate([rows[:, i * WIDE : (i + 1) * WIDE] for i in range(stretches)], axis=0)
        moved = move_samples(cut, table_ref[...])
        for eight in range(count * block_rows // 8):
            for half in range(2):
                parts = []
                for i in range(stretches):
                    begin = i * count * block_rows + eight * 8
                    parts.append(moved[begin : begin + 8, half * LANES : (half + 1) * LANES])
                for phase, part in enumerate(swap_blocks(parts)):
                    first = (group * count * block_rows + eight * 8) * PHASES + half * 4 + phase
                    tiles_ref[pl.ds(first, 8, stride=PHASES), :] = part
        lax.fori_loop(group * count, (group + 1) * count, send_block, 0, unroll=4)
    lists.wait()
    pltpu.make_async_copy(tiles_ref, tiles_ref, sem).wait()


def pack(traces, mine, target, bins, devices, capacity):
    held, block_rows, samples = traces.shape
    span = block_rows * PHASES
    room = 8
    groups = 2
    return pl.pallas_call(
        functools.partial(pack_kernel, capacity=capacity),
        in_specs=[SMEM, SMEM, SMEM, HBM],
        out_specs=HBM,
        out_shape=jax.ShapeDtypeStruct((devices, capacity * span + room, LANES), F32),
        scratch_shapes=[
            pltpu.VMEM((groups, held // groups, block_rows, samples), F32),
            pltpu.VMEM((WIDE, WIDE), BF16),
            pltpu.VMEM((held * span, LANES), F32),
            pltpu.SMEM((devices,), I32),
            pltpu.SMEM((held,), I32),
            pltpu.VMEM((devices, room, LANES), F32),
            pltpu.SemaphoreType.DMA((groups,)),
            pltpu.SemaphoreType.DMA,
            pltpu.SemaphoreType.DMA,
        ],
        compiler_params=pltpu.CompilerParams(vmem_limit_bytes=60 * MIB),
    )(mine, target, bins, traces)


def bin_kernel(blocks_ref, out_ref, *refs, capacity, block_rows, edges):
    edge_refs, refs = refs[: len(edges)], refs[len(edges) :]
    even_ref, odd_ref, listed_ref, places_ref, scale_ref, scales_ref, sem, sems = refs
    devices = blocks_ref.shape[0]
    tile_rows, tile_cols = out_ref.shape[:2]
    bin_total = tile_rows * tile_cols
    unroll = 8
    lanes = capacity * block_rows
    shared = LANES // lanes

    def read_lists(row, _):
        total = jnp.zeros((1, LANES), F32)
        for i in range(shared):
            total = total + blocks_ref[row * shared + i, lanes * PHASES : lanes * PHASES + 1, :]
        listed_ref[pl.ds(row, 1), :] = jnp.where(total > 0, total - 1.0, float(bin_total)).astype(I32)
        return 0

    lax.fori_loop(0, devices // shared, read_lists, 0)
    copy = pltpu.make_async_copy(listed_ref, places_ref, sem)
    copy.start()
    nothing = jnp.zeros((PHASES, LANES), F32)

    def clear(i, _):
        for j in range(unroll):
            even_ref[i * unroll + j] = nothing
            odd_ref[i * unroll + j] = nothing
        return 0

    lax.fori_loop(0, bin_total // unroll, clear, 0)
    copy.wait()
    count_rows = scale_ref.shape[0]
    numbers = lax.broadcasted_iota(I32, (count_rows, LANES), 0) * LANES + lax.broadcasted_iota(
        I32, (count_rows, LANES), 1
    )

    def add_sender(sender, folds):
        folds = list(folds)
        row, first = sender // shared, sender % shared * lanes
        for rank in range(capacity):
            for j in range(block_rows):
                total_ref = odd_ref if j % 2 else even_ref
                place = places_ref[row, first + rank * block_rows + j]
                cell = (rank * block_rows + j) * PHASES
                total_ref[place] += blocks_ref[sender, cell : cell + PHASES, :]
                folds[j % 2] = folds[j % 2] + jnp.where(numbers == place, 1.0, 0.0)
        return tuple(folds)

    empty = jnp.zeros((count_rows, LANES), F32)
    folds = lax.fori_loop(0, devices, add_sender, (empty, empty))
    scale_ref[...] = 1.0 / jnp.maximum(folds[0] + folds[1], 1.0)
    copy = pltpu.make_async_copy(scale_ref, scales_ref, sem)
    copy.start()
    copy.wait()

    def finish(row, _):
        high, low = row * tile_cols // LANES, row * tile_cols % LANES
        for col in range(tile_cols):
            place = row * tile_cols + col
            scale = scales_ref[high, low + col]
            out_ref[row, col] = (even_ref[place] + odd_ref[place]) * scale
        return 0

    lax.fori_loop(0, HALF, finish, 0)
    lax.fori_loop(tile_rows - HALF, tile_rows, finish, 0)
    copies = edge_copies(out_ref, (), edges, edge_refs, sems)
    for copy in copies:
        copy.start()
    lax.fori_loop(HALF, tile_rows - HALF, finish, 0)
    for copy in copies:
        copy.wait()


def edge_copies(out_ref, pieces, edges, edge_refs, sems):
    copies = []
    for (_, moves), edge_ref in zip(edges, edge_refs):
        for source, target, *piece in moves:
            from_ref = pieces[piece[0]] if piece else out_ref
            copies.append(pltpu.make_async_copy(from_ref.at[source], edge_ref.at[target], sems.at[len(copies)]))
    return copies


def edge_outputs(edges):
    shapes = [jax.ShapeDtypeStruct(tuple(shape) + (PHASES, LANES), F32) for shape, _ in edges]
    moves = sum(len(moves) for _, moves in edges)
    return shapes, [HBM] * len(edges), pltpu.SemaphoreType.DMA((max(1, moves),))


def stack_bins(blocks, tile_rows, tile_cols, capacity, block_rows, edges):
    devices = blocks.shape[0]
    bin_total = tile_rows * tile_cols
    shapes, specs, sems = edge_outputs(edges)
    return pl.pallas_call(
        functools.partial(bin_kernel, capacity=capacity, block_rows=block_rows, edges=edges),
        in_specs=[VMEM],
        out_specs=[VMEM] + specs,
        out_shape=[jax.ShapeDtypeStruct((tile_rows, tile_cols, PHASES, LANES), F32)] + shapes,
        scratch_shapes=[
            pltpu.VMEM((bin_total + 8, PHASES, LANES), F32),
            pltpu.VMEM((bin_total + 8, PHASES, LANES), F32),
            pltpu.VMEM((devices * capacity * block_rows // LANES, LANES), I32),
            pltpu.SMEM((devices * capacity * block_rows // LANES, LANES), I32),
            pltpu.VMEM((bin_total // LANES, LANES), F32),
            pltpu.SMEM((bin_total // LANES, LANES), F32),
            pltpu.SemaphoreType.DMA,
            sems,
        ],
        compiler_params=pltpu.CompilerParams(vmem_limit_bytes=14 * MIB),
    )(blocks)


def fill_weights(spots_ref, weights_ref):
    row = lax.broadcasted_iota(I32, (PAIR, LANES), 0)
    column = lax.broadcasted_iota(I32, (PAIR, LANES), 1)
    for pair in range(spots_ref.shape[0] // (2 * PAIR)):
        for half in range(2):
            block = pl.ds((pair * 2 + half) * PAIR, PAIR)
            spot = half * PAIR + column // PHASES - HALF - 2 * pair - row // PHASES
            share = jnp.maximum(HALF + 1 - jnp.abs(spot), 0).astype(F32) / (HALF + 1) ** 2
            spots_ref[block, :] = jnp.clip(spot, -HALF - 1, HALF + 1).astype(F32).astype(BF16)
            weights_ref[block, :] = share.astype(BF16)


def split_cells(cells, halves_ref):
    for pair in range(len(cells) // 2):
        both = jnp.concatenate([cells[2 * pair](), cells[2 * pair + 1]()], axis=0)
        upper = both.astype(BF16)
        halves_ref[pair * PAIR : (pair + 1) * PAIR, :LANES] = upper
        rest = (both - upper.astype(F32)).astype(BF16)
        halves_ref[pair * PAIR : (pair + 1) * PAIR, LANES:] = rest


def apply_taps(dip_of, first, count, halves_ref, spots_ref, weights_ref):
    row = lax.broadcasted_iota(I32, (PAIR, LANES), 0)
    column = lax.broadcasted_iota(I32, (PAIR, LANES), 1)
    phase_gap = ((row & (PHASES - 1)) - (column & (PHASES - 1))).astype(F32).astype(BF16)
    none = jnp.zeros((PAIR, LANES), BF16)
    taps = []
    for pair in range(count // 2):
        dip = jnp.concatenate(
            [jnp.full((PHASES, LANES), dip_of(first + 2 * pair + i).astype(F32)) for i in range(2)], axis=0
        ).astype(BF16)
        moves, weights = [], []
        for half in range(2):
            block = pl.ds((pair * 2 + half) * PAIR, PAIR)
            moves.append(phase_gap + dip * spots_ref[block, :])
            weights.append(weights_ref[block, :])
        for reach in REACHES:
            taps.append(
                jnp.concatenate(
                    [jnp.where(moves[h] == jnp.bfloat16(reach * PHASES), weights[h], none) for h in range(2)],
                    axis=1,
                )
            )
    return jnp.dot(jnp.concatenate(taps, axis=0), halves_ref[...], preferred_element_type=F32)


def move_lanes(sums, first, count, put):
    lane = lax.broadcasted_iota(I32, (PHASES, LANES), 1)
    for pair in range(count // 2):
        for member in range(2):
            total = None
            for reach in REACHES:
                begin = (pair * len(REACHES) + reach + REACH) * PAIR + member * PHASES
                part = sums[begin : begin + PHASES, :LANES] + sums[begin : begin + PHASES, LANES:]
                if reach:
                    part = pltpu.roll(part, (-reach) % LANES, axis=1)
                    inside = lane < LANES - reach if reach > 0 else lane >= -reach
                    part = jnp.where(inside, part, 0.0)
                total = part if total is None else total + part
            put(first + 2 * pair + member, total)


def steer_kernel(dip_ref, *refs, along, whole, lines, line_of, windows, local_of, edges, final, batches, filled, chained, pieces_count, abreast):
    pieces, refs = refs[:pieces_count], refs[pieces_count:]
    refs = refs[chained:]
    out_ref, refs = refs[0], refs[1:]
    edge_refs, refs = refs[: len(edges)], refs[len(edges) :]
    spots_ref, weights_ref, sems, *refs = refs
    halves = refs[: abreast * len(windows)]
    if final:
        staged_ref, result_ref, table_ref = refs[abreast * len(windows) :]
        fill_interleave(table_ref, 1)
    fill_weights(spots_ref, weights_ref)
    for i, halves_ref in enumerate(halves):
        used = len(windows[i % len(windows)][2]) * PHASES
        if used < WIDE:
            halves_ref[used:, :] = jnp.zeros((WIDE - used, WIDE), BF16)

    def at(place, line):
        return (place, line) if along == 0 else (line, place)

    def some_lines(step, _):
        jobs = []
        for parity in range(abreast):
            line = abreast * step + parity
            full = line_of(line)

            def cell(index, local, line=line, full=full):
                return lambda: pieces[index][at(local, full if whole[index] else line)]

            def put(place, value, line=line):
                if final:
                    staged_ref[pl.ds((local_of(place) * final + line % final) * PHASES, PHASES), :] = value
                else:
                    out_ref[at(local_of(place), line)] = value

            for i, (first, count, places) in enumerate(windows):
                halves_ref = halves[parity * len(windows) + i]
                split_cells([cell(*place) for place in places], halves_ref)
                jobs.append((full, first, count, halves_ref, put))
        waiting = None
        for full, first, count, halves_ref, put in jobs:
            sums = apply_taps(
                lambda place: dip_ref[at(place, full)], first, count, halves_ref, spots_ref, weights_ref
            )
            if waiting is not None:
                move_lanes(*waiting)
            waiting = (sums, first, count, put)
        move_lanes(*waiting)
        return 0

    if not final:
        if filled is not None:
            index, target = filled
            fill = pltpu.make_async_copy(pieces[index], out_ref.at[target], sems.at[sems.shape[0] - 1])
            fill.start()
        lax.fori_loop(0, lines // abreast, some_lines, 0)
        if filled is not None:
            fill.wait()
        copies = edge_copies(out_ref, pieces, edges, edge_refs, sems)
        for copy in copies:
            copy.start()
        for copy in copies:
            copy.wait()
        return

    outputs = sum(count for _, count, _ in windows)

    def copies_of(batch, slot):
        return [
            pltpu.make_async_copy(
                result_ref.at[slot, pl.ds(local_of(first), count), pl.ds(local, wide), :],
                out_ref.at[pl.ds(first, count), pl.ds(full, wide), :],
                sems.at[(slot * len(windows) + i) * len(batches[batch]) + j],
            )
            for i, (first, count, _) in enumerate(windows)
            for j, (local, full, wide) in enumerate(batches[batch])
        ]

    for batch in range(lines // final):
        lax.fori_loop(batch * final // abreast, (batch + 1) * final // abreast, some_lines, 0)
        stretches = PHASES * LANES // WIDE
        cuts = [[] for _ in range(stretches)]
        for eight in range(outputs * final // 8):
            sides = [
                swap_blocks(
                    [
                        staged_ref[pl.ds(eight * 8 * PHASES + half * 4 + phase, 8, stride=PHASES), :]
                        for phase in range(PHASES // 2)
                    ]
                )
                for half in range(2)
            ]
            for i in range(stretches):
                cuts[i].append(jnp.concatenate([sides[0][i], sides[1][i]], axis=1))
        moved = move_samples(jnp.concatenate(sum(cuts, []), axis=0), table_ref[...])
        slot = batch % 2
        if batch >= 2:
            for copy in copies_of(batch - 2, slot):
                copy.wait()
        count = outputs * final
        for i in range(stretches):
            result_ref[slot, :, :, i * WIDE : (i + 1) * WIDE] = moved[i * count : (i + 1) * count].reshape(
                outputs, final, WIDE
            )
        for copy in copies_of(batch, slot):
            copy.start()
    for batch in range(max(0, lines // final - 2), lines // final):
        for copy in copies_of(batch, batch % 2):
            copy.wait()


def steer(
    dip, pieces, along, lines, line_of, windows, local_of, edges=(), batches=None, before=None, after=None, filled=None
):
    samples = PHASES * LANES
    outputs = sum(count for _, count, _ in windows)
    final = 16 if batches is not None else 0
    abreast = 4 * WINDOW // outputs
    shapes, specs, sems = edge_outputs(edges)
    operands = [dip] + [array for array, _ in pieces]
    in_specs = [SMEM] + [VMEM] * len(pieces)
    aliases = {}
    if final:
        if before is not None:
            aliases = {len(operands): 0}
            operands.append(before)
            in_specs.append(HBM)
        out_shape = [jax.ShapeDtypeStruct(dip.shape + (samples,), F32)]
        sems = pltpu.SemaphoreType.DMA((2 * len(windows) * len(batches[0]),))
        out_specs = [HBM]
    else:
        reach = outputs if filled is None else dip.shape[along]
        shape = (reach, lines) if along == 0 else (lines, reach)
        out_shape = [jax.ShapeDtypeStruct(shape + (PHASES, LANES), F32)] + shapes
        out_specs = [VMEM] + specs
        if filled is not None:
            sems = pltpu.SemaphoreType.DMA((sems.shape[0] + 1,))
    if after is not None:
        operands.append(after)
        in_specs.append(ANY)
    most = max(count for _, count, _ in windows)
    constant = pltpu.VMEM((most * PAIR, LANES), BF16)
    scratch = [constant, constant, sems]
    scratch += [pltpu.VMEM((WIDE, WIDE), BF16)] * (abreast * len(windows))
    if final:
        scratch += [
            pltpu.VMEM((outputs * final * PHASES, LANES), F32),
            pltpu.VMEM((2, outputs, final, samples), F32),
            pltpu.VMEM((WIDE, WIDE), BF16),
        ]
    return pl.pallas_call(
        functools.partial(
            steer_kernel,
            along=along, whole=[whole for _, whole in pieces], lines=lines, line_of=line_of, windows=windows,
            local_of=local_of, edges=edges, final=final, batches=batches, filled=filled, chained=len(operands) - len(pieces) - 1, pieces_count=len(pieces), abreast=abreast,
        ),
        in_specs=in_specs,
        out_specs=out_specs,
        out_shape=out_shape,
        scratch_shapes=scratch,
        input_output_aliases=aliases,
        compiler_params=pltpu.CompilerParams(vmem_limit_bytes=16 * MIB),
        cost_estimate=pl.CostEstimate(
            flops=2400 * outputs * lines * samples,
            bytes_accessed=8 * outputs * lines * samples,
            transcendentals=0,
        ),
    )(*operands)


def swap_ends(head, tail, axis):
    count = lax.axis_size(axis)
    low = lax.ppermute(tail, axis, [(i, i + 1) for i in range(count - 1)])
    high = lax.ppermute(head, axis, [(i + 1, i) for i in range(count - 1)])
    return low, high


def span_of(index, first, count):
    return [(index, first + i) for i in range(count)]


def rows_of(first, count):
    return slice(first, first + count)


def smooth(arrived, capacity, block_rows, dip_inline, dip_cross):
    rows, cols = dip_inline.shape
    mid_rows, mid_cols = rows - 2 * BORDER, cols - 2 * BORDER
    both = 2 * BORDER
    same = lambda line: line
    inner = lambda line: line + BORDER
    outer_col = lambda line: line + jnp.where(line < BORDER, 0, mid_cols)
    outer_row = lambda line: line + jnp.where(line < BORDER, 0, mid_rows)
    mid_place = lambda place: place - BORDER
    outer_place = lambda place: place if place < BORDER else place - mid_rows
    every = slice(None)
    lead, last = rows_of(0, HALF), rows_of(both - HALF, HALF)
    left, right, middle_cols = rows_of(0, BORDER), rows_of(cols - BORDER, BORDER), rows_of(BORDER, mid_cols)

    def outer_edge(pick):
        return ((HALF, both), [((pick, left), (every, rows_of(0, BORDER))), ((pick, right), (every, rows_of(BORDER, BORDER)))])

    def whole_edge(shape, pick):
        return (shape, [(pick, (every, every))])

    def mid_windows(places, extent):
        return [(i, WINDOW, places[i - BORDER : i - BORDER + WINDOW + 2 * HALF]) for i in range(BORDER, extent - BORDER, WINDOW)]

    stacked, head_out, tail_out, head_mid, tail_mid = stack_bins(
        arrived, rows, cols, capacity, block_rows,
        [
            outer_edge(rows_of(0, HALF)),
            outer_edge(rows_of(rows - HALF, HALF)),
            whole_edge((HALF, mid_cols), (rows_of(0, HALF), middle_cols)),
            whole_edge((HALF, mid_cols), (rows_of(rows - HALF, HALF), middle_cols)),
        ],
    )
    low_out, high_out = swap_ends(head_out, tail_out, "inline")
    low_mid, high_mid = swap_ends(head_mid, tail_mid, "inline")

    (middle,) = steer(
        dip_inline, [(stacked, True)], 0, cols, same,
        mid_windows(span_of(0, BORDER - HALF, mid_rows + 2 * HALF), rows), mid_place,
    )
    windows = [
        (0, BORDER, span_of(0, 0, HALF) + span_of(1, 0, BORDER + HALF)),
        (rows - BORDER, BORDER, span_of(1, rows - BORDER - HALF, BORDER + HALF) + span_of(2, 0, HALF)),
    ]
    top, bottom, between = rows_of(0, BORDER), rows_of(rows - BORDER, BORDER), rows_of(BORDER, mid_rows)

    def column_edge(outer, whole):
        return (
            (rows, HALF),
            [
                ((rows_of(0, BORDER), outer), (top, every)),
                ((rows_of(BORDER, BORDER), outer), (bottom, every)),
                ((every, whole), (between, every), 3),
            ],
        )

    corners, head, tail = steer(
        dip_inline, [(low_out, False), (stacked, True), (high_out, False), (middle, False)], 0, both, outer_col,
        windows, outer_place, edges=[column_edge(lead, lead), column_edge(last, rows_of(cols - HALF, HALF))],
    )
    west, east = swap_ends(head, tail, "crosslin")
    (flanks,) = steer(
        dip_inline, [(low_mid, False), (stacked, True), (high_mid, False)], 0, mid_cols, inner, windows, outer_place,
        after=corners,
    )

    places = span_of(0, BORDER - HALF, HALF) + span_of(1, 0, mid_cols) + span_of(0, BORDER, HALF)
    second_mid, head, tail = steer(
        dip_cross, [(corners, False), (flanks, False)], 1, both, outer_row, mid_windows(places, cols), mid_place,
        edges=[whole_edge((HALF, mid_cols), (lead, every)), whole_edge((HALF, mid_cols), (last, every))],
    )
    low_mid, high_mid = swap_ends(head, tail, "inline")
    (centre,) = steer(
        dip_cross, [(middle, False)], 1, mid_rows, inner,
        mid_windows(span_of(0, BORDER - HALF, mid_cols + 2 * HALF), cols), mid_place, after=second_mid,
    )
    windows = [
        (0, BORDER, span_of(0, 0, HALF) + span_of(1, 0, BORDER) + span_of(2, 0, HALF)),
        (cols - BORDER, BORDER, span_of(2, mid_cols - HALF, HALF) + span_of(1, BORDER, BORDER) + span_of(3, 0, HALF)),
    ]
    border_second, head, tail = steer(
        dip_cross,
        [(west, True), (corners, False), (flanks, False), (east, True), (second_mid, False)],
        1, both, outer_row, windows, same, filled=(4, (every, middle_cols)),
        edges=[outer_edge(lead), outer_edge(last)], after=centre,
    )
    low_out, high_out = swap_ends(head, tail, "inline")
    windows = [
        (0, BORDER, span_of(0, 0, HALF) + span_of(1, 0, BORDER + HALF)),
        (cols - BORDER, BORDER, span_of(1, cols - BORDER - HALF, BORDER + HALF) + span_of(2, 0, HALF)),
    ]
    (middle_second,) = steer(
        dip_cross, [(west, True), (middle, False), (east, True), (centre, False)], 1, mid_rows, inner, windows, same,
        filled=(3, (every, middle_cols)), after=border_second,
    )

    places = span_of(0, BORDER - HALF, HALF) + span_of(1, 0, mid_rows) + span_of(0, BORDER, HALF)
    (result,) = steer(
        dip_inline, [(border_second, True), (middle_second, True)], 0, cols, same, mid_windows(places, rows), mid_place,
        batches=[[(0, first, WINDOW)] for first in range(0, cols, WINDOW)],
    )
    windows = [
        (0, BORDER, span_of(0, 0, HALF) + span_of(1, 0, BORDER) + span_of(2, 0, HALF)),
        (rows - BORDER, BORDER, span_of(2, mid_rows - HALF, HALF) + span_of(1, BORDER, BORDER) + span_of(3, 0, HALF)),
    ]
    for low, high, lines, line_of, batches in (
        (low_mid, high_mid, mid_cols, inner, [[(0, first, WINDOW)] for first in range(BORDER, cols - BORDER, WINDOW)]),
        (low_out, high_out, both, outer_col, [[(0, 0, BORDER), (BORDER, cols - BORDER, BORDER)]]),
    ):
        (result,) = steer(
            dip_inline, [(low, False), (border_second, True), (middle_second, True), (high, False)], 0, lines, line_of,
            windows, outer_place, batches=batches, before=result,
        )
    return result


def on_device(traces, destination, bin_index, dip_inline, dip_cross):
    held, block_rows, _ = traces.shape
    devices = lax.axis_size("inline") * lax.axis_size("crosslin")
    capacity = 2 * held // devices
    mine = lax.axis_index("inline") * lax.axis_size("crosslin") + lax.axis_index("crosslin")
    outgoing = pack(traces, mine.astype(I32).reshape(1), destination.reshape(-1), bin_index.T, devices, capacity)
    arrived = lax.all_to_all(outgoing, BOTH, split_axis=0, concat_axis=0, tiled=True)
    return smooth(arrived, capacity, block_rows, dip_inline, dip_cross)


def solution(mesh):
    return jax.shard_map(
        on_device,
        mesh=mesh,
        in_specs=(
            P(BOTH, None, None),
            P(BOTH, None),
            P(BOTH, None),
            P("inline", "crosslin"),
            P("inline", "crosslin"),
        ),
        out_specs=P("inline", "crosslin", None),
        check_vma=False,
    )
```

```python
import functools

import jax
import jax.numpy as jnp
from jax import lax
from jax.experimental import pallas as pl
from jax.experimental.pallas import tpu as pltpu
from jax.sharding import PartitionSpec as P

HALF = 7
DMAX = 2
LANES = 128
PHASES = 8
PAIR = 2 * PHASES
WIDE = 2 * LANES
BLOCK = WIDE // PHASES
WINDOW = 16
BORDER = 8
REACH = -(-HALF * DMAX // PHASES)
REACHES = range(-REACH, REACH + 1)
BOTH = ("inline", "crosslin")
MIB = 2**20
VMEM = pl.BlockSpec(memory_space=pltpu.VMEM)
SMEM = pl.BlockSpec(memory_space=pltpu.SMEM)
ANY = pl.BlockSpec(memory_space=pl.ANY)
HBM = pl.BlockSpec(memory_space=pltpu.HBM)
F32, BF16, I32 = jnp.float32, jnp.bfloat16, jnp.int32


def fill_interleave(table_ref, time_dim):
    time = lax.broadcasted_iota(I32, (WIDE, WIDE), time_dim)
    place = lax.broadcasted_iota(I32, (WIDE, WIDE), 1 - time_dim)
    hit = time == place % BLOCK * PHASES + place // BLOCK
    table_ref[...] = jnp.where(hit, 1.0, 0.0).astype(BF16)


def move_samples(rows, table):
    count = rows.shape[0]
    upper = rows.astype(BF16)
    rest = (rows - upper.astype(F32)).astype(BF16)
    both = jnp.concatenate([upper, rest], axis=0)
    moved = jnp.dot(both, table, preferred_element_type=F32)
    return moved[:count] + moved[count:]


def take_lanes(tile, index):
    return jnp.take_along_axis(tile, index, axis=1, mode="promise_in_bounds")


def swap_blocks(tiles):
    lane = lax.broadcasted_iota(I32, tiles[0].shape, 1)
    tiles = list(tiles)
    for step in (2, 1):
        low = lane // BLOCK % (2 * step) < step
        across = lane ^ (step * BLOCK)
        for m in range(len(tiles)):
            if m // step % 2 == 0:
                first, second = tiles[m], tiles[m + step]
                crossed = take_lanes(jnp.where(low, second, first), across)
                tiles[m] = jnp.where(low, first, crossed)
                tiles[m + step] = jnp.where(low, crossed, second)
    return tiles


def pack_kernel(mine_ref, target_ref, bins_ref, traces_ref, out_ref, held_ref, table_ref, tiles_ref, used_ref, rank_ref, listed_ref, in_sems, sem, listed_sem, *, capacity):
    held, block_rows, samples = traces_ref.shape
    devices, room, _ = listed_ref.shape
    span = block_rows * PHASES
    groups = held_ref.shape[0]
    count = held // groups
    loads = [
        pltpu.make_async_copy(traces_ref.at[pl.ds(group * count, count)], held_ref.at[group], in_sems.at[group])
        for group in range(groups)
    ]
    for load in loads:
        load.start()
    fill_interleave(table_ref, 0)
    lane = lax.broadcasted_iota(I32, (1, LANES), 1)
    listed_ref[...] = jnp.zeros(listed_ref.shape, F32)
    own_lanes = mine_ref[0] % (LANES // (capacity * block_rows)) * (capacity * block_rows)

    def clear(device, _):
        used_ref[device] = 0
        return 0

    lax.fori_loop(0, devices, clear, 0)

    def choose_slot(block, _):
        device = target_ref[block]
        rank = used_ref[device]
        used_ref[device] = rank + 1
        rank_ref[block] = rank
        row = jnp.zeros((1, LANES), I32)
        for j in range(block_rows):
            row = jnp.where(lane == own_lanes + rank * block_rows + j, bins_ref[j, block] + 1, row)
        listed_ref[device, 0:1, :] = listed_ref[device, 0:1, :] + row.astype(F32)
        return 0

    lax.fori_loop(0, held, choose_slot, 0, unroll=4)
    lists = pltpu.make_async_copy(
        listed_ref, out_ref.at[:, capacity * span : capacity * span + room, :], listed_sem
    )
    lists.start()

    def send_block(block, _):
        pltpu.make_async_copy(
            tiles_ref.at[pl.ds(pl.multiple_of(block * span, 8), span), :],
            out_ref.at[target_ref[block], pl.ds(pl.multiple_of(rank_ref[block] * span, 8), span), :],
            sem,
        ).start()
        return 0

    for group in range(groups):
        loads[group].wait()
        rows = held_ref[group].reshape(count * block_rows, samples)
        stretches = samples // WIDE
        cut = jnp.concatenate([rows[:, i * WIDE : (i + 1) * WIDE] for i in range(stretches)], axis=0)
        moved = move_samples(cut, table_ref[...])
        for eight in range(count * block_rows // 8):
            for half in range(2):
                parts = []
                for i in range(stretches):
                    begin = i * count * block_rows + eight * 8
                    parts.append(moved[begin : begin + 8, half * LANES : (half + 1) * LANES])
                for phase, part in enumerate(swap_blocks(parts)):
                    first = (group * count * block_rows + eight * 8) * PHASES + half * 4 + phase
                    tiles_ref[pl.ds(first, 8, stride=PHASES), :] = part
        lax.fori_loop(group * count, (group + 1) * count, send_block, 0, unroll=4)
    lists.wait()
    pltpu.make_async_copy(tiles_ref, tiles_ref, sem).wait()


def pack(traces, mine, target, bins, devices, capacity):
    held, block_rows, samples = traces.shape
    span = block_rows * PHASES
    room = 8
    groups = 2
    return pl.pallas_call(
        functools.partial(pack_kernel, capacity=capacity),
        in_specs=[SMEM, SMEM, SMEM, HBM],
        out_specs=HBM,
        out_shape=jax.ShapeDtypeStruct((devices, capacity * span + room, LANES), F32),
        scratch_shapes=[
            pltpu.VMEM((groups, held // groups, block_rows, samples), F32),
            pltpu.VMEM((WIDE, WIDE), BF16),
            pltpu.VMEM((held * span, LANES), F32),
            pltpu.SMEM((devices,), I32),
            pltpu.SMEM((held,), I32),
            pltpu.VMEM((devices, room, LANES), F32),
            pltpu.SemaphoreType.DMA((groups,)),
            pltpu.SemaphoreType.DMA,
            pltpu.SemaphoreType.DMA,
        ],
        compiler_params=pltpu.CompilerParams(vmem_limit_bytes=60 * MIB),
    )(mine, target, bins, traces)


def bin_kernel(blocks_ref, out_ref, *refs, capacity, block_rows, edges):
    edge_refs, refs = refs[: len(edges)], refs[len(edges) :]
    even_ref, odd_ref, listed_ref, places_ref, scale_ref, scales_ref, sem, sems = refs
    devices = blocks_ref.shape[0]
    tile_rows, tile_cols = out_ref.shape[:2]
    bin_total = tile_rows * tile_cols
    unroll = 8
    lanes = capacity * block_rows
    shared = LANES // lanes

    def read_lists(row, _):
        total = jnp.zeros((1, LANES), F32)
        for i in range(shared):
            total = total + blocks_ref[row * shared + i, lanes * PHASES : lanes * PHASES + 1, :]
        listed_ref[pl.ds(row, 1), :] = jnp.where(total > 0, total - 1.0, float(bin_total)).astype(I32)
        return 0

    lax.fori_loop(0, devices // shared, read_lists, 0)
    copy = pltpu.make_async_copy(listed_ref, places_ref, sem)
    copy.start()
    nothing = jnp.zeros((PHASES, LANES), F32)

    def clear(i, _):
        for j in range(unroll):
            even_ref[i * unroll + j] = nothing
            odd_ref[i * unroll + j] = nothing
        return 0

    lax.fori_loop(0, bin_total // unroll, clear, 0)
    copy.wait()
    count_rows = scale_ref.shape[0]
    numbers = lax.broadcasted_iota(I32, (count_rows, LANES), 0) * LANES + lax.broadcasted_iota(
        I32, (count_rows, LANES), 1
    )

    def add_sender(sender, folds):
        folds = list(folds)
        row, first = sender // shared, sender % shared * lanes
        for rank in range(capacity):
            for j in range(block_rows):
                total_ref = odd_ref if j % 2 else even_ref
                place = places_ref[row, first + rank * block_rows + j]
                cell = (rank * block_rows + j) * PHASES
                total_ref[place] += blocks_ref[sender, cell : cell + PHASES, :]
                folds[j % 2] = folds[j % 2] + jnp.where(numbers == place, 1.0, 0.0)
        return tuple(folds)

    empty = jnp.zeros((count_rows, LANES), F32)
    folds = lax.fori_loop(0, devices, add_sender, (empty, empty))
    scale_ref[...] = 1.0 / jnp.maximum(folds[0] + folds[1], 1.0)
    copy = pltpu.make_async_copy(scale_ref, scales_ref, sem)
    copy.start()
    copy.wait()

    def finish(row, _):
        high, low = row * tile_cols // LANES, row * tile_cols % LANES
        for col in range(tile_cols):
            place = row * tile_cols + col
            scale = scales_ref[high, low + col]
            out_ref[row, col] = (even_ref[place] + odd_ref[place]) * scale
        return 0

    lax.fori_loop(0, HALF, finish, 0)
    lax.fori_loop(tile_rows - HALF, tile_rows, finish, 0)
    copies = edge_copies(out_ref, (), edges, edge_refs, sems)
    for copy in copies:
        copy.start()
    lax.fori_loop(HALF, tile_rows - HALF, finish, 0)
    for copy in copies:
        copy.wait()


def edge_copies(out_ref, pieces, edges, edge_refs, sems):
    copies = []
    for (_, moves), edge_ref in zip(edges, edge_refs):
        for source, target, *piece in moves:
            from_ref = pieces[piece[0]] if piece else out_ref
            copies.append(pltpu.make_async_copy(from_ref.at[source], edge_ref.at[target], sems.at[len(copies)]))
    return copies


def edge_outputs(edges):
    shapes = [jax.ShapeDtypeStruct(tuple(shape) + (PHASES, LANES), F32) for shape, _ in edges]
    moves = sum(len(moves) for _, moves in edges)
    return shapes, [HBM] * len(edges), pltpu.SemaphoreType.DMA((max(1, moves),))


def stack_bins(blocks, tile_rows, tile_cols, capacity, block_rows, edges):
    devices = blocks.shape[0]
    bin_total = tile_rows * tile_cols
    shapes, specs, sems = edge_outputs(edges)
    return pl.pallas_call(
        functools.partial(bin_kernel, capacity=capacity, block_rows=block_rows, edges=edges),
        in_specs=[VMEM],
        out_specs=[VMEM] + specs,
        out_shape=[jax.ShapeDtypeStruct((tile_rows, tile_cols, PHASES, LANES), F32)] + shapes,
        scratch_shapes=[
            pltpu.VMEM((bin_total + 8, PHASES, LANES), F32),
            pltpu.VMEM((bin_total + 8, PHASES, LANES), F32),
            pltpu.VMEM((devices * capacity * block_rows // LANES, LANES), I32),
            pltpu.SMEM((devices * capacity * block_rows // LANES, LANES), I32),
            pltpu.VMEM((bin_total // LANES, LANES), F32),
            pltpu.SMEM((bin_total // LANES, LANES), F32),
            pltpu.SemaphoreType.DMA,
            sems,
        ],
        compiler_params=pltpu.CompilerParams(vmem_limit_bytes=14 * MIB),
    )(blocks)


def fill_weights(spots_ref, weights_ref):
    row = lax.broadcasted_iota(I32, (PAIR, LANES), 0)
    column = lax.broadcasted_iota(I32, (PAIR, LANES), 1)
    for pair in range(spots_ref.shape[0] // (2 * PAIR)):
        for half in range(2):
            block = pl.ds((pair * 2 + half) * PAIR, PAIR)
            spot = half * PAIR + column // PHASES - HALF - 2 * pair - row // PHASES
            share = jnp.maximum(HALF + 1 - jnp.abs(spot), 0).astype(F32) / (HALF + 1) ** 2
            spots_ref[block, :] = jnp.clip(spot, -HALF - 1, HALF + 1).astype(F32).astype(BF16)
            weights_ref[block, :] = share.astype(BF16)


def split_cells(cells, halves_ref):
    for pair in range(len(cells) // 2):
        both = jnp.concatenate([cells[2 * pair](), cells[2 * pair + 1]()], axis=0)
        upper = both.astype(BF16)
        halves_ref[pair * PAIR : (pair + 1) * PAIR, :LANES] = upper
        rest = (both - upper.astype(F32)).astype(BF16)
        halves_ref[pair * PAIR : (pair + 1) * PAIR, LANES:] = rest


def apply_taps(dip_of, first, count, halves_ref, spots_ref, weights_ref):
    row = lax.broadcasted_iota(I32, (PAIR, LANES), 0)
    column = lax.broadcasted_iota(I32, (PAIR, LANES), 1)
    phase_gap = ((row & (PHASES - 1)) - (column & (PHASES - 1))).astype(F32).astype(BF16)
    none = jnp.zeros((PAIR, LANES), BF16)
    taps = []
    for pair in range(count // 2):
        dip = jnp.concatenate(
            [jnp.full((PHASES, LANES), dip_of(first + 2 * pair + i).astype(F32)) for i in range(2)], axis=0
        ).astype(BF16)
        moves, weights = [], []
        for half in range(2):
            block = pl.ds((pair * 2 + half) * PAIR, PAIR)
            moves.append(phase_gap + dip * spots_ref[block, :])
            weights.append(weights_ref[block, :])
        for reach in REACHES:
            taps.append(
                jnp.concatenate(
                    [jnp.where(moves[h] == jnp.bfloat16(reach * PHASES), weights[h], none) for h in range(2)],
                    axis=1,
                )
            )
    return jnp.dot(jnp.concatenate(taps, axis=0), halves_ref[...], preferred_element_type=F32)


def move_lanes(sums, first, count, put):
    lane = lax.broadcasted_iota(I32, (PHASES, LANES), 1)
    for pair in range(count // 2):
        for member in range(2):
            total = None
            for reach in REACHES:
                begin = (pair * len(REACHES) + reach + REACH) * PAIR + member * PHASES
                part = sums[begin : begin + PHASES, :LANES] + sums[begin : begin + PHASES, LANES:]
                if reach:
                    part = pltpu.roll(part, (-reach) % LANES, axis=1)
                    inside = lane < LANES - reach if reach > 0 else lane >= -reach
                    part = jnp.where(inside, part, 0.0)
                total = part if total is None else total + part
            put(first + 2 * pair + member, total)


def steer_kernel(dip_ref, *refs, along, whole, lines, line_of, windows, local_of, edges, final, batches, filled, chained, pieces_count, abreast):
    pieces, refs = refs[:pieces_count], refs[pieces_count:]
    refs = refs[chained:]
    out_ref, refs = refs[0], refs[1:]
    edge_refs, refs = refs[: len(edges)], refs[len(edges) :]
    spots_ref, weights_ref, sems, *refs = refs
    halves = refs[: abreast * len(windows)]
    if final:
        staged_ref, result_ref, table_ref = refs[abreast * len(windows) :]
        fill_interleave(table_ref, 1)
    fill_weights(spots_ref, weights_ref)
    for i, halves_ref in enumerate(halves):
        used = len(windows[i % len(windows)][2]) * PHASES
        if used < WIDE:
            halves_ref[used:, :] = jnp.zeros((WIDE - used, WIDE), BF16)

    def at(place, line):
        return (place, line) if along == 0 else (line, place)

    def some_lines(step, _):
        jobs = []
        for parity in range(abreast):
            line = abreast * step + parity
            full = line_of(line)

            def cell(index, local, line=line, full=full):
                return lambda: pieces[index][at(local, full if whole[index] else line)]

            def put(place, value, line=line):
                if final:
                    staged_ref[pl.ds((local_of(place) * final + line % final) * PHASES, PHASES), :] = value
                else:
                    out_ref[at(local_of(place), line)] = value

            for i, (first, count, places) in enumerate(windows):
                halves_ref = halves[parity * len(windows) + i]
                split_cells([cell(*place) for place in places], halves_ref)
                jobs.append((full, first, count, halves_ref, put))
        waiting = None
        for full, first, count, halves_ref, put in jobs:
            sums = apply_taps(
                lambda place: dip_ref[at(place, full)], first, count, halves_ref, spots_ref, weights_ref
            )
            if waiting is not None:
                move_lanes(*waiting)
            waiting = (sums, first, count, put)
        move_lanes(*waiting)
        return 0

    if not final:
        if filled is not None:
            index, target = filled
            fill = pltpu.make_async_copy(pieces[index], out_ref.at[target], sems.at[sems.shape[0] - 1])
            fill.start()
        lax.fori_loop(0, lines // abreast, some_lines, 0)
        if filled is not None:
            fill.wait()
        copies = edge_copies(out_ref, pieces, edges, edge_refs, sems)
        for copy in copies:
            copy.start()
        for copy in copies:
            copy.wait()
        return

    outputs = sum(count for _, count, _ in windows)

    def copies_of(batch, slot):
        return [
            pltpu.make_async_copy(
                result_ref.at[slot, pl.ds(local_of(first), count), pl.ds(local, wide), :],
                out_ref.at[pl.ds(first, count), pl.ds(full, wide), :],
                sems.at[(slot * len(windows) + i) * len(batches[batch]) + j],
            )
            for i, (first, count, _) in enumerate(windows)
            for j, (local, full, wide) in enumerate(batches[batch])
        ]

    for batch in range(lines // final):
        lax.fori_loop(batch * final // abreast, (batch + 1) * final // abreast, some_lines, 0)
        stretches = PHASES * LANES // WIDE
        cuts = [[] for _ in range(stretches)]
        for eight in range(outputs * final // 8):
            sides = [
                swap_blocks(
                    [
                        staged_ref[pl.ds(eight * 8 * PHASES + half * 4 + phase, 8, stride=PHASES), :]
                        for phase in range(PHASES // 2)
                    ]
                )
                for half in range(2)
            ]
            for i in range(stretches):
                cuts[i].append(jnp.concatenate([sides[0][i], sides[1][i]], axis=1))
        moved = move_samples(jnp.concatenate(sum(cuts, []), axis=0), table_ref[...])
        slot = batch % 2
        if batch >= 2:
            for copy in copies_of(batch - 2, slot):
                copy.wait()
        count = outputs * final
        for i in range(stretches):
            result_ref[slot, :, :, i * WIDE : (i + 1) * WIDE] = moved[i * count : (i + 1) * count].reshape(
                outputs, final, WIDE
            )
        for copy in copies_of(batch, slot):
            copy.start()
    for batch in range(max(0, lines // final - 2), lines // final):
        for copy in copies_of(batch, batch % 2):
            copy.wait()


def steer(
    dip, pieces, along, lines, line_of, windows, local_of, edges=(), batches=None, before=None, after=None, filled=None
):
    samples = PHASES * LANES
    outputs = sum(count for _, count, _ in windows)
    final = 16 if batches is not None else 0
    abreast = 4 * WINDOW // outputs
    shapes, specs, sems = edge_outputs(edges)
    operands = [dip] + [array for array, _ in pieces]
    in_specs = [SMEM] + [VMEM] * len(pieces)
    aliases = {}
    if final:
        if before is not None:
            aliases = {len(operands): 0}
            operands.append(before)
            in_specs.append(HBM)
        out_shape = [jax.ShapeDtypeStruct(dip.shape + (samples,), F32)]
        sems = pltpu.SemaphoreType.DMA((2 * len(windows) * len(batches[0]),))
        out_specs = [HBM]
    else:
        reach = outputs if filled is None else dip.shape[along]
        shape = (reach, lines) if along == 0 else (lines, reach)
        out_shape = [jax.ShapeDtypeStruct(shape + (PHASES, LANES), F32)] + shapes
        out_specs = [VMEM] + specs
        if filled is not None:
            sems = pltpu.SemaphoreType.DMA((sems.shape[0] + 1,))
    if after is not None:
        operands.append(after)
        in_specs.append(ANY)
    most = max(count for _, count, _ in windows)
    constant = pltpu.VMEM((most * PAIR, LANES), BF16)
    scratch = [constant, constant, sems]
    scratch += [pltpu.VMEM((WIDE, WIDE), BF16)] * (abreast * len(windows))
    if final:
        scratch += [
            pltpu.VMEM((outputs * final * PHASES, LANES), F32),
            pltpu.VMEM((2, outputs, final, samples), F32),
            pltpu.VMEM((WIDE, WIDE), BF16),
        ]
    return pl.pallas_call(
        functools.partial(
            steer_kernel,
            along=along, whole=[whole for _, whole in pieces], lines=lines, line_of=line_of, windows=windows,
            local_of=local_of, edges=edges, final=final, batches=batches, filled=filled, chained=len(operands) - len(pieces) - 1, pieces_count=len(pieces), abreast=abreast,
        ),
        in_specs=in_specs,
        out_specs=out_specs,
        out_shape=out_shape,
        scratch_shapes=scratch,
        input_output_aliases=aliases,
        compiler_params=pltpu.CompilerParams(vmem_limit_bytes=16 * MIB),
        cost_estimate=pl.CostEstimate(
            flops=2400 * outputs * lines * samples,
            bytes_accessed=8 * outputs * lines * samples,
            transcendentals=0,
        ),
    )(*operands)


def swap_ends(head, tail, axis):
    count = lax.axis_size(axis)
    low = lax.ppermute(tail, axis, [(i, i + 1) for i in range(count - 1)])
    high = lax.ppermute(head, axis, [(i + 1, i) for i in range(count - 1)])
    return low, high


def span_of(index, first, count):
    return [(index, first + i) for i in range(count)]


def rows_of(first, count):
    return slice(first, first + count)


def smooth(arrived, capacity, block_rows, dip_inline, dip_cross):
    rows, cols = dip_inline.shape
    mid_rows, mid_cols = rows - 2 * BORDER, cols - 2 * BORDER
    both = 2 * BORDER
    same = lambda line: line
    inner = lambda line: line + BORDER
    outer_col = lambda line: line + jnp.where(line < BORDER, 0, mid_cols)
    outer_row = lambda line: line + jnp.where(line < BORDER, 0, mid_rows)
    mid_place = lambda place: place - BORDER
    outer_place = lambda place: place if place < BORDER else place - mid_rows
    every = slice(None)
    lead, last = rows_of(0, HALF), rows_of(both - HALF, HALF)
    left, right, middle_cols = rows_of(0, BORDER), rows_of(cols - BORDER, BORDER), rows_of(BORDER, mid_cols)

    def outer_edge(pick):
        return ((HALF, both), [((pick, left), (every, rows_of(0, BORDER))), ((pick, right), (every, rows_of(BORDER, BORDER)))])

    def whole_edge(shape, pick):
        return (shape, [(pick, (every, every))])

    def mid_windows(places, extent):
        return [(i, WINDOW, places[i - BORDER : i - BORDER + WINDOW + 2 * HALF]) for i in range(BORDER, extent - BORDER, WINDOW)]

    stacked, head, tail = stack_bins(
        arrived, rows, cols, capacity, block_rows,
        [whole_edge((HALF, cols), (rows_of(0, HALF), every)), whole_edge((HALF, cols), (rows_of(rows - HALF, HALF), every))],
    )
    low, high = swap_ends(head, tail, "inline")

    (middle,) = steer(
        dip_inline, [(stacked, True)], 0, cols, same,
        mid_windows(span_of(0, BORDER - HALF, mid_rows + 2 * HALF), rows), mid_place,
    )
    windows = [
        (0, BORDER, span_of(0, 0, HALF) + span_of(1, 0, BORDER + HALF)),
        (rows - BORDER, BORDER, span_of(1, rows - BORDER - HALF, BORDER + HALF) + span_of(2, 0, HALF)),
    ]
    top, bottom, between = rows_of(0, BORDER), rows_of(rows - BORDER, BORDER), rows_of(BORDER, mid_rows)

    def column_edge(outer, whole):
        return (
            (rows, HALF),
            [
                ((rows_of(0, BORDER), outer), (top, every)),
                ((rows_of(BORDER, BORDER), outer), (bottom, every)),
                ((every, whole), (between, every), 3),
            ],
        )

    corners, head, tail = steer(
        dip_inline, [(low, True), (stacked, True), (high, True), (middle, False)], 0, both, outer_col,
        windows, outer_place, edges=[column_edge(lead, lead), column_edge(last, rows_of(cols - HALF, HALF))],
    )
    west, east = swap_ends(head, tail, "crosslin")
    (flanks,) = steer(
        dip_inline, [(low, True), (stacked, True), (high, True)], 0, mid_cols, inner, windows, outer_place,
        after=corners,
    )

    places = span_of(0, BORDER - HALF, HALF) + span_of(1, 0, mid_cols) + span_of(0, BORDER, HALF)
    second_mid, head, tail = steer(
        dip_cross, [(corners, False), (flanks, False)], 1, both, outer_row, mid_windows(places, cols), mid_place,
        edges=[whole_edge((HALF, mid_cols), (lead, every)), whole_edge((HALF, mid_cols), (last, every))],
    )
    low_mid, high_mid = swap_ends(head, tail, "inline")
    (centre,) = steer(
        dip_cross, [(middle, False)], 1, mid_rows, inner,
        mid_windows(span_of(0, BORDER - HALF, mid_cols + 2 * HALF), cols), mid_place, after=second_mid,
    )
    windows = [
        (0, BORDER, span_of(0, 0, HALF) + span_of(1, 0, BORDER) + span_of(2, 0, HALF)),
        (cols - BORDER, BORDER, span_of(2, mid_cols - HALF, HALF) + span_of(1, BORDER, BORDER) + span_of(3, 0, HALF)),
    ]
    border_second, head, tail = steer(
        dip_cross,
        [(west, True), (corners, False), (flanks, False), (east, True), (second_mid, False)],
        1, both, outer_row, windows, same, filled=(4, (every, middle_cols)),
        edges=[outer_edge(lead), outer_edge(last)], after=centre,
    )
    low_out, high_out = swap_ends(head, tail, "inline")
    windows = [
        (0, BORDER, span_of(0, 0, HALF) + span_of(1, 0, BORDER + HALF)),
        (cols - BORDER, BORDER, span_of(1, cols - BORDER - HALF, BORDER + HALF) + span_of(2, 0, HALF)),
    ]
    (middle_second,) = steer(
        dip_cross, [(west, True), (middle, False), (east, True), (centre, False)], 1, mid_rows, inner, windows, same,
        filled=(3, (every, middle_cols)), after=border_second,
    )

    places = span_of(0, BORDER - HALF, HALF) + span_of(1, 0, mid_rows) + span_of(0, BORDER, HALF)
    (result,) = steer(
        dip_inline, [(border_second, True), (middle_second, True)], 0, cols, same, mid_windows(places, rows), mid_place,
        batches=[[(0, first, WINDOW)] for first in range(0, cols, WINDOW)],
    )
    windows = [
        (0, BORDER, span_of(0, 0, HALF) + span_of(1, 0, BORDER) + span_of(2, 0, HALF)),
        (rows - BORDER, BORDER, span_of(2, mid_rows - HALF, HALF) + span_of(1, BORDER, BORDER) + span_of(3, 0, HALF)),
    ]
    for low, high, lines, line_of, batches in (
        (low_mid, high_mid, mid_cols, inner, [[(0, first, WINDOW)] for first in range(BORDER, cols - BORDER, WINDOW)]),
        (low_out, high_out, both, outer_col, [[(0, 0, BORDER), (BORDER, cols - BORDER, BORDER)]]),
    ):
        (result,) = steer(
            dip_inline, [(low, False), (border_second, True), (middle_second, True), (high, False)], 0, lines, line_of,
            windows, outer_place, batches=batches, before=result,
        )
    return result


def on_device(traces, destination, bin_index, dip_inline, dip_cross):
    held, block_rows, _ = traces.shape
    devices = lax.axis_size("inline") * lax.axis_size("crosslin")
    capacity = 2 * held // devices
    mine = lax.axis_index("inline") * lax.axis_size("crosslin") + lax.axis_index("crosslin")
    outgoing = pack(traces, mine.astype(I32).reshape(1), destination.reshape(-1), bin_index.T, devices, capacity)
    arrived = lax.all_to_all(outgoing, BOTH, split_axis=0, concat_axis=0, tiled=True)
    return smooth(arrived, capacity, block_rows, dip_inline, dip_cross)


def solution(mesh):
    return jax.shard_map(
        on_device,
        mesh=mesh,
        in_specs=(
            P(BOTH, None, None),
            P(BOTH, None),
            P(BOTH, None),
            P("inline", "crosslin"),
            P("inline", "crosslin"),
        ),
        out_specs=P("inline", "crosslin", None),
        check_vma=False,
    )
```

```python
import functools

import jax
import jax.numpy as jnp
from jax import lax
from jax.experimental import pallas as pl
from jax.experimental.pallas import tpu as pltpu
from jax.sharding import PartitionSpec as P

HALF = 7
DMAX = 2
LANES = 128
PHASES = 8
PAIR = 2 * PHASES
WIDE = 2 * LANES
BLOCK = WIDE // PHASES
WINDOW = 16
BORDER = 8
REACH = -(-HALF * DMAX // PHASES)
REACHES = range(-REACH, REACH + 1)
BOTH = ("inline", "crosslin")
MIB = 2**20
VMEM = pl.BlockSpec(memory_space=pltpu.VMEM)
SMEM = pl.BlockSpec(memory_space=pltpu.SMEM)
ANY = pl.BlockSpec(memory_space=pl.ANY)
HBM = pl.BlockSpec(memory_space=pltpu.HBM)
F32, BF16, I32 = jnp.float32, jnp.bfloat16, jnp.int32


def fill_interleave(table_ref, time_dim):
    time = lax.broadcasted_iota(I32, (WIDE, WIDE), time_dim)
    place = lax.broadcasted_iota(I32, (WIDE, WIDE), 1 - time_dim)
    hit = time == place % BLOCK * PHASES + place // BLOCK
    table_ref[...] = jnp.where(hit, 1.0, 0.0).astype(BF16)


def move_samples(rows, table):
    count = rows.shape[0]
    upper = rows.astype(BF16)
    rest = (rows - upper.astype(F32)).astype(BF16)
    both = jnp.concatenate([upper, rest], axis=0)
    moved = jnp.dot(both, table, preferred_element_type=F32)
    return moved[:count] + moved[count:]


def take_lanes(tile, index):
    return jnp.take_along_axis(tile, index, axis=1, mode="promise_in_bounds")


def swap_blocks(tiles):
    lane = lax.broadcasted_iota(I32, tiles[0].shape, 1)
    tiles = list(tiles)
    for step in (2, 1):
        low = lane // BLOCK % (2 * step) < step
        across = lane ^ (step * BLOCK)
        for m in range(len(tiles)):
            if m // step % 2 == 0:
                first, second = tiles[m], tiles[m + step]
                crossed = take_lanes(jnp.where(low, second, first), across)
                tiles[m] = jnp.where(low, first, crossed)
                tiles[m + step] = jnp.where(low, crossed, second)
    return tiles


def pack_kernel(mine_ref, target_ref, bins_ref, traces_ref, out_ref, held_ref, table_ref, tiles_ref, used_ref, rank_ref, listed_ref, in_sems, sem, listed_sem, *, capacity):
    held, block_rows, samples = traces_ref.shape
    devices, room, _ = listed_ref.shape
    span = block_rows * PHASES
    groups = held_ref.shape[0]
    count = held // groups
    loads = [
        pltpu.make_async_copy(traces_ref.at[pl.ds(group * count, count)], held_ref.at[group], in_sems.at[group])
        for group in range(groups)
    ]
    for load in loads:
        load.start()
    fill_interleave(table_ref, 0)
    lane = lax.broadcasted_iota(I32, (1, LANES), 1)
    listed_ref[...] = jnp.zeros(listed_ref.shape, F32)
    own_lanes = mine_ref[0] % (LANES // (capacity * block_rows)) * (capacity * block_rows)

    def clear(device, _):
        used_ref[device] = 0
        return 0

    lax.fori_loop(0, devices, clear, 0)

    def choose_slot(block, _):
        device = target_ref[block]
        rank = used_ref[device]
        used_ref[device] = rank + 1
        rank_ref[block] = rank
        row = jnp.zeros((1, LANES), I32)
        for j in range(block_rows):
            row = jnp.where(lane == own_lanes + rank * block_rows + j, bins_ref[j, block] + 1, row)
        listed_ref[device, 0:1, :] = listed_ref[device, 0:1, :] + row.astype(F32)
        return 0

    lax.fori_loop(0, held, choose_slot, 0, unroll=4)
    lists = pltpu.make_async_copy(
        listed_ref, out_ref.at[:, capacity * span : capacity * span + room, :], listed_sem
    )
    lists.start()

    def send_block(block, _):
        pltpu.make_async_copy(
            tiles_ref.at[pl.ds(pl.multiple_of(block * span, 8), span), :],
            out_ref.at[target_ref[block], pl.ds(pl.multiple_of(rank_ref[block] * span, 8), span), :],
            sem,
        ).start()
        return 0

    for group in range(groups):
        loads[group].wait()
        rows = held_ref[group].reshape(count * block_rows, samples)
        stretches = samples // WIDE
        cut = jnp.concatenate([rows[:, i * WIDE : (i + 1) * WIDE] for i in range(stretches)], axis=0)
        moved = move_samples(cut, table_ref[...])
        for eight in range(count * block_rows // 8):
            for half in range(2):
                parts = []
                for i in range(stretches):
                    begin = i * count * block_rows + eight * 8
                    parts.append(moved[begin : begin + 8, half * LANES : (half + 1) * LANES])
                for phase, part in enumerate(swap_blocks(parts)):
                    first = (group * count * block_rows + eight * 8) * PHASES + half * 4 + phase
                    tiles_ref[pl.ds(first, 8, stride=PHASES), :] = part
        lax.fori_loop(group * count, (group + 1) * count, send_block, 0, unroll=4)
    lists.wait()
    pltpu.make_async_copy(tiles_ref, tiles_ref, sem).wait()


def pack(traces, mine, target, bins, devices, capacity):
    held, block_rows, samples = traces.shape
    span = block_rows * PHASES
    room = 8
    groups = 2
    return pl.pallas_call(
        functools.partial(pack_kernel, capacity=capacity),
        in_specs=[SMEM, SMEM, SMEM, HBM],
        out_specs=HBM,
        out_shape=jax.ShapeDtypeStruct((devices, capacity * span + room, LANES), F32),
        scratch_shapes=[
            pltpu.VMEM((groups, held // groups, block_rows, samples), F32),
            pltpu.VMEM((WIDE, WIDE), BF16),
            pltpu.VMEM((held * span, LANES), F32),
            pltpu.SMEM((devices,), I32),
            pltpu.SMEM((held,), I32),
            pltpu.VMEM((devices, room, LANES), F32),
            pltpu.SemaphoreType.DMA((groups,)),
            pltpu.SemaphoreType.DMA,
            pltpu.SemaphoreType.DMA,
        ],
        compiler_params=pltpu.CompilerParams(vmem_limit_bytes=60 * MIB),
    )(mine, target, bins, traces)


def bin_kernel(blocks_ref, out_ref, *refs, capacity, block_rows, edges):
    edge_refs, refs = refs[: len(edges)], refs[len(edges) :]
    even_ref, odd_ref, listed_ref, places_ref, scale_ref, scales_ref, sem, sems = refs
    devices = blocks_ref.shape[0]
    tile_rows, tile_cols = out_ref.shape[:2]
    bin_total = tile_rows * tile_cols
    unroll = 8
    lanes = capacity * block_rows
    shared = LANES // lanes

    def read_lists(row, _):
        total = jnp.zeros((1, LANES), F32)
        for i in range(shared):
            total = total + blocks_ref[row * shared + i, lanes * PHASES : lanes * PHASES + 1, :]
        listed_ref[pl.ds(row, 1), :] = jnp.where(total > 0, total - 1.0, float(bin_total)).astype(I32)
        return 0

    lax.fori_loop(0, devices // shared, read_lists, 0)
    copy = pltpu.make_async_copy(listed_ref, places_ref, sem)
    copy.start()
    nothing = jnp.zeros((PHASES, LANES), F32)

    def clear(i, _):
        for j in range(unroll):
            even_ref[i * unroll + j] = nothing
            odd_ref[i * unroll + j] = nothing
        return 0

    lax.fori_loop(0, bin_total // unroll, clear, 0)
    copy.wait()
    count_rows = scale_ref.shape[0]
    numbers = lax.broadcasted_iota(I32, (count_rows, LANES), 0) * LANES + lax.broadcasted_iota(
        I32, (count_rows, LANES), 1
    )

    def add_sender(sender, folds):
        folds = list(folds)
        row, first = sender // shared, sender % shared * lanes
        for rank in range(capacity):
            for j in range(block_rows):
                total_ref = odd_ref if j % 2 else even_ref
                place = places_ref[row, first + rank * block_rows + j]
                cell = (rank * block_rows + j) * PHASES
                total_ref[place] += blocks_ref[sender, cell : cell + PHASES, :]
                folds[j % 2] = folds[j % 2] + jnp.where(numbers == place, 1.0, 0.0)
        return tuple(folds)

    empty = jnp.zeros((count_rows, LANES), F32)
    folds = lax.fori_loop(0, devices, add_sender, (empty, empty))
    scale_ref[...] = 1.0 / jnp.maximum(folds[0] + folds[1], 1.0)
    copy = pltpu.make_async_copy(scale_ref, scales_ref, sem)
    copy.start()
    copy.wait()

    def finish(row, _):
        high, low = row * tile_cols // LANES, row * tile_cols % LANES
        for col in range(tile_cols):
            place = row * tile_cols + col
            scale = scales_ref[high, low + col]
            out_ref[row, col] = (even_ref[place] + odd_ref[place]) * scale
        return 0

    lax.fori_loop(0, HALF, finish, 0)
    lax.fori_loop(tile_rows - HALF, tile_rows, finish, 0)
    copies = edge_copies(out_ref, (), edges, edge_refs, sems)
    for copy in copies:
        copy.start()
    lax.fori_loop(HALF, tile_rows - HALF, finish, 0)
    for copy in copies:
        copy.wait()


def edge_copies(out_ref, pieces, edges, edge_refs, sems):
    copies = []
    for (_, moves), edge_ref in zip(edges, edge_refs):
        for source, target, *piece in moves:
            from_ref = pieces[piece[0]] if piece else out_ref
            copies.append(pltpu.make_async_copy(from_ref.at[source], edge_ref.at[target], sems.at[len(copies)]))
    return copies


def edge_outputs(edges):
    shapes = [jax.ShapeDtypeStruct(tuple(shape) + (PHASES, LANES), F32) for shape, _ in edges]
    moves = sum(len(moves) for _, moves in edges)
    return shapes, [HBM] * len(edges), pltpu.SemaphoreType.DMA((max(1, moves),))


def stack_bins(blocks, tile_rows, tile_cols, capacity, block_rows, edges):
    devices = blocks.shape[0]
    bin_total = tile_rows * tile_cols
    shapes, specs, sems = edge_outputs(edges)
    return pl.pallas_call(
        functools.partial(bin_kernel, capacity=capacity, block_rows=block_rows, edges=edges),
        in_specs=[VMEM],
        out_specs=[VMEM] + specs,
        out_shape=[jax.ShapeDtypeStruct((tile_rows, tile_cols, PHASES, LANES), F32)] + shapes,
        scratch_shapes=[
            pltpu.VMEM((bin_total + 8, PHASES, LANES), F32),
            pltpu.VMEM((bin_total + 8, PHASES, LANES), F32),
            pltpu.VMEM((devices * capacity * block_rows // LANES, LANES), I32),
            pltpu.SMEM((devices * capacity * block_rows // LANES, LANES), I32),
            pltpu.VMEM((bin_total // LANES, LANES), F32),
            pltpu.SMEM((bin_total // LANES, LANES), F32),
            pltpu.SemaphoreType.DMA,
            sems,
        ],
        compiler_params=pltpu.CompilerParams(vmem_limit_bytes=14 * MIB),
    )(blocks)


def fill_weights(spots_ref, weights_ref):
    row = lax.broadcasted_iota(I32, (PAIR, LANES), 0)
    column = lax.broadcasted_iota(I32, (PAIR, LANES), 1)
    for pair in range(spots_ref.shape[0] // (2 * PAIR)):
        for half in range(2):
            block = pl.ds((pair * 2 + half) * PAIR, PAIR)
            spot = half * PAIR + column // PHASES - HALF - 2 * pair - row // PHASES
            share = jnp.maximum(HALF + 1 - jnp.abs(spot), 0).astype(F32) / (HALF + 1) ** 2
            spots_ref[block, :] = jnp.clip(spot, -HALF - 1, HALF + 1).astype(F32).astype(BF16)
            weights_ref[block, :] = share.astype(BF16)


def split_cells(cells, halves_ref):
    for pair in range(len(cells) // 2):
        both = jnp.concatenate([cells[2 * pair](), cells[2 * pair + 1]()], axis=0)
        upper = both.astype(BF16)
        halves_ref[pair * PAIR : (pair + 1) * PAIR, :LANES] = upper
        rest = (both - upper.astype(F32)).astype(BF16)
        halves_ref[pair * PAIR : (pair + 1) * PAIR, LANES:] = rest


def apply_taps(dip_of, first, count, halves_ref, spots_ref, weights_ref):
    row = lax.broadcasted_iota(I32, (PAIR, LANES), 0)
    column = lax.broadcasted_iota(I32, (PAIR, LANES), 1)
    phase_gap = ((row & (PHASES - 1)) - (column & (PHASES - 1))).astype(F32).astype(BF16)
    none = jnp.zeros((PAIR, LANES), BF16)
    taps = []
    for pair in range(count // 2):
        dip = jnp.concatenate(
            [jnp.full((PHASES, LANES), dip_of(first + 2 * pair + i).astype(F32)) for i in range(2)], axis=0
        ).astype(BF16)
        moves, weights = [], []
        for half in range(2):
            block = pl.ds((pair * 2 + half) * PAIR, PAIR)
            moves.append(phase_gap + dip * spots_ref[block, :])
            weights.append(weights_ref[block, :])
        for reach in REACHES:
            taps.append(
                jnp.concatenate(
                    [jnp.where(moves[h] == jnp.bfloat16(reach * PHASES), weights[h], none) for h in range(2)],
                    axis=1,
                )
            )
    return jnp.dot(jnp.concatenate(taps, axis=0), halves_ref[...], preferred_element_type=F32)


def move_lanes(sums, first, count, put):
    lane = lax.broadcasted_iota(I32, (PHASES, LANES), 1)
    for pair in range(count // 2):
        for member in range(2):
            total = None
            for reach in REACHES:
                begin = (pair * len(REACHES) + reach + REACH) * PAIR + member * PHASES
                part = sums[begin : begin + PHASES, :LANES] + sums[begin : begin + PHASES, LANES:]
                if reach:
                    part = pltpu.roll(part, (-reach) % LANES, axis=1)
                    inside = lane < LANES - reach if reach > 0 else lane >= -reach
                    part = jnp.where(inside, part, 0.0)
                total = part if total is None else total + part
            put(first + 2 * pair + member, total)


def steer_kernel(dip_ref, *refs, along, whole, lines, line_of, windows, local_of, edges, final, batches, filled, chained, pieces_count, abreast):
    pieces, refs = refs[:pieces_count], refs[pieces_count:]
    refs = refs[chained:]
    out_ref, refs = refs[0], refs[1:]
    edge_refs, refs = refs[: len(edges)], refs[len(edges) :]
    spots_ref, weights_ref, sems, *refs = refs
    halves = refs[: abreast * len(windows)]
    if final:
        staged_ref, result_ref, table_ref = refs[abreast * len(windows) :]
        fill_interleave(table_ref, 1)
    fill_weights(spots_ref, weights_ref)
    for i, halves_ref in enumerate(halves):
        used = len(windows[i % len(windows)][2]) * PHASES
        if used < WIDE:
            halves_ref[used:, :] = jnp.zeros((WIDE - used, WIDE), BF16)

    def at(place, line):
        return (place, line) if along == 0 else (line, place)

    def some_lines(step, _):
        jobs = []
        for parity in range(abreast):
            line = abreast * step + parity
            full = line_of(line)

            def cell(index, local, line=line, full=full):
                return lambda: pieces[index][at(local, full if whole[index] else line)]

            def put(place, value, line=line):
                if final:
                    staged_ref[pl.ds((local_of(place) * final + line % final) * PHASES, PHASES), :] = value
                else:
                    out_ref[at(local_of(place), line)] = value

            for i, (first, count, places) in enumerate(windows):
                halves_ref = halves[parity * len(windows) + i]
                split_cells([cell(*place) for place in places], halves_ref)
                jobs.append((full, first, count, halves_ref, put))
        waiting = None
        for full, first, count, halves_ref, put in jobs:
            sums = apply_taps(
                lambda place: dip_ref[at(place, full)], first, count, halves_ref, spots_ref, weights_ref
            )
            if waiting is not None:
                move_lanes(*waiting)
            waiting = (sums, first, count, put)
        move_lanes(*waiting)
        return 0

    if not final:
        if filled is not None:
            index, target = filled
            fill = pltpu.make_async_copy(pieces[index], out_ref.at[target], sems.at[sems.shape[0] - 1])
            fill.start()
        lax.fori_loop(0, lines // abreast, some_lines, 0)
        if filled is not None:
            fill.wait()
        copies = edge_copies(out_ref, pieces, edges, edge_refs, sems)
        for copy in copies:
            copy.start()
        for copy in copies:
            copy.wait()
        return

    outputs = sum(count for _, count, _ in windows)

    def copies_of(batch, slot):
        return [
            pltpu.make_async_copy(
                result_ref.at[slot, pl.ds(local_of(first), count), pl.ds(local, wide), :],
                out_ref.at[pl.ds(first, count), pl.ds(full, wide), :],
                sems.at[(slot * len(windows) + i) * len(batches[batch]) + j],
            )
            for i, (first, count, _) in enumerate(windows)
            for j, (local, full, wide) in enumerate(batches[batch])
        ]

    for batch in range(lines // final):
        lax.fori_loop(batch * final // abreast, (batch + 1) * final // abreast, some_lines, 0)
        stretches = PHASES * LANES // WIDE
        cuts = [[] for _ in range(stretches)]
        for eight in range(outputs * final // 8):
            sides = [
                swap_blocks(
                    [
                        staged_ref[pl.ds(eight * 8 * PHASES + half * 4 + phase, 8, stride=PHASES), :]
                        for phase in range(PHASES // 2)
                    ]
                )
                for half in range(2)
            ]
            for i in range(stretches):
                cuts[i].append(jnp.concatenate([sides[0][i], sides[1][i]], axis=1))
        moved = move_samples(jnp.concatenate(sum(cuts, []), axis=0), table_ref[...])
        slot = batch % 2
        if batch >= 2:
            for copy in copies_of(batch - 2, slot):
                copy.wait()
        count = outputs * final
        for i in range(stretches):
            result_ref[slot, :, :, i * WIDE : (i + 1) * WIDE] = moved[i * count : (i + 1) * count].reshape(
                outputs, final, WIDE
            )
        for copy in copies_of(batch, slot):
            copy.start()
    for batch in range(max(0, lines // final - 2), lines // final):
        for copy in copies_of(batch, batch % 2):
            copy.wait()


def steer(
    dip, pieces, along, lines, line_of, windows, local_of, edges=(), batches=None, before=None, after=None, filled=None
):
    samples = PHASES * LANES
    outputs = sum(count for _, count, _ in windows)
    final = 16 if batches is not None else 0
    abreast = 4 * WINDOW // outputs
    shapes, specs, sems = edge_outputs(edges)
    operands = [dip] + [array for array, _ in pieces]
    in_specs = [SMEM] + [VMEM] * len(pieces)
    aliases = {}
    if final:
        if before is not None:
            aliases = {len(operands): 0}
            operands.append(before)
            in_specs.append(HBM)
        out_shape = [jax.ShapeDtypeStruct(dip.shape + (samples,), F32)]
        sems = pltpu.SemaphoreType.DMA((2 * len(windows) * len(batches[0]),))
        out_specs = [HBM]
    else:
        reach = outputs if filled is None else dip.shape[along]
        shape = (reach, lines) if along == 0 else (lines, reach)
        out_shape = [jax.ShapeDtypeStruct(shape + (PHASES, LANES), F32)] + shapes
        out_specs = [VMEM] + specs
        if filled is not None:
            sems = pltpu.SemaphoreType.DMA((sems.shape[0] + 1,))
    if after is not None:
        operands.append(after)
        in_specs.append(ANY)
    most = max(count for _, count, _ in windows)
    constant = pltpu.VMEM((most * PAIR, LANES), BF16)
    scratch = [constant, constant, sems]
    scratch += [pltpu.VMEM((WIDE, WIDE), BF16)] * (abreast * len(windows))
    if final:
        scratch += [
            pltpu.VMEM((outputs * final * PHASES, LANES), F32),
            pltpu.VMEM((2, outputs, final, samples), F32),
            pltpu.VMEM((WIDE, WIDE), BF16),
        ]
    return pl.pallas_call(
        functools.partial(
            steer_kernel,
            along=along, whole=[whole for _, whole in pieces], lines=lines, line_of=line_of, windows=windows,
            local_of=local_of, edges=edges, final=final, batches=batches, filled=filled, chained=len(operands) - len(pieces) - 1, pieces_count=len(pieces), abreast=abreast,
        ),
        in_specs=in_specs,
        out_specs=out_specs,
        out_shape=out_shape,
        scratch_shapes=scratch,
        input_output_aliases=aliases,
        compiler_params=pltpu.CompilerParams(vmem_limit_bytes=16 * MIB),
        cost_estimate=pl.CostEstimate(
            flops=40000 * outputs * lines * samples,
            bytes_accessed=8 * outputs * lines * samples,
            transcendentals=0,
        ),
    )(*operands)


def swap_ends(head, tail, axis):
    count = lax.axis_size(axis)
    low = lax.ppermute(tail, axis, [(i, i + 1) for i in range(count - 1)])
    high = lax.ppermute(head, axis, [(i + 1, i) for i in range(count - 1)])
    return low, high


def span_of(index, first, count):
    return [(index, first + i) for i in range(count)]


def rows_of(first, count):
    return slice(first, first + count)


def smooth(arrived, capacity, block_rows, dip_inline, dip_cross):
    rows, cols = dip_inline.shape
    mid_rows, mid_cols = rows - 2 * BORDER, cols - 2 * BORDER
    both = 2 * BORDER
    same = lambda line: line
    inner = lambda line: line + BORDER
    outer_col = lambda line: line + jnp.where(line < BORDER, 0, mid_cols)
    outer_row = lambda line: line + jnp.where(line < BORDER, 0, mid_rows)
    mid_place = lambda place: place - BORDER
    outer_place = lambda place: place if place < BORDER else place - mid_rows
    every = slice(None)
    lead, last = rows_of(0, HALF), rows_of(both - HALF, HALF)
    left, right, middle_cols = rows_of(0, BORDER), rows_of(cols - BORDER, BORDER), rows_of(BORDER, mid_cols)

    def outer_edge(pick):
        return ((HALF, both), [((pick, left), (every, rows_of(0, BORDER))), ((pick, right), (every, rows_of(BORDER, BORDER)))])

    def whole_edge(shape, pick):
        return (shape, [(pick, (every, every))])

    def mid_windows(places, extent):
        return [(i, WINDOW, places[i - BORDER : i - BORDER + WINDOW + 2 * HALF]) for i in range(BORDER, extent - BORDER, WINDOW)]

    stacked, head_out, tail_out, head_mid, tail_mid = stack_bins(
        arrived, rows, cols, capacity, block_rows,
        [
            outer_edge(rows_of(0, HALF)),
            outer_edge(rows_of(rows - HALF, HALF)),
            whole_edge((HALF, mid_cols), (rows_of(0, HALF), middle_cols)),
            whole_edge((HALF, mid_cols), (rows_of(rows - HALF, HALF), middle_cols)),
        ],
    )
    low_out, high_out = swap_ends(head_out, tail_out, "inline")
    low_mid, high_mid = swap_ends(head_mid, tail_mid, "inline")

    (middle,) = steer(
        dip_inline, [(stacked, True)], 0, cols, same,
        mid_windows(span_of(0, BORDER - HALF, mid_rows + 2 * HALF), rows), mid_place,
    )
    windows = [
        (0, BORDER, span_of(0, 0, HALF) + span_of(1, 0, BORDER + HALF)),
        (rows - BORDER, BORDER, span_of(1, rows - BORDER - HALF, BORDER + HALF) + span_of(2, 0, HALF)),
    ]
    top, bottom, between = rows_of(0, BORDER), rows_of(rows - BORDER, BORDER), rows_of(BORDER, mid_rows)

    def column_edge(outer, whole):
        return (
            (rows, HALF),
            [
                ((rows_of(0, BORDER), outer), (top, every)),
                ((rows_of(BORDER, BORDER), outer), (bottom, every)),
                ((every, whole), (between, every), 3),
            ],
        )

    corners, head, tail = steer(
        dip_inline, [(low_out, False), (stacked, True), (high_out, False), (middle, False)], 0, both, outer_col,
        windows, outer_place, edges=[column_edge(lead, lead), column_edge(last, rows_of(cols - HALF, HALF))],
    )
    west, east = swap_ends(head, tail, "crosslin")
    (flanks,) = steer(
        dip_inline, [(low_mid, False), (stacked, True), (high_mid, False)], 0, mid_cols, inner, windows, outer_place,
        after=corners,
    )

    places = span_of(0, BORDER - HALF, HALF) + span_of(1, 0, mid_cols) + span_of(0, BORDER, HALF)
    second_mid, head, tail = steer(
        dip_cross, [(corners, False), (flanks, False)], 1, both, outer_row, mid_windows(places, cols), mid_place,
        edges=[whole_edge((HALF, mid_cols), (lead, every)), whole_edge((HALF, mid_cols), (last, every))],
    )
    low_mid, high_mid = swap_ends(head, tail, "inline")
    (centre,) = steer(
        dip_cross, [(middle, False)], 1, mid_rows, inner,
        mid_windows(span_of(0, BORDER - HALF, mid_cols + 2 * HALF), cols), mid_place, after=second_mid,
    )
    windows = [
        (0, BORDER, span_of(0, 0, HALF) + span_of(1, 0, BORDER) + span_of(2, 0, HALF)),
        (cols - BORDER, BORDER, span_of(2, mid_cols - HALF, HALF) + span_of(1, BORDER, BORDER) + span_of(3, 0, HALF)),
    ]
    border_second, head, tail = steer(
        dip_cross,
        [(west, True), (corners, False), (flanks, False), (east, True), (second_mid, False)],
        1, both, outer_row, windows, same, filled=(4, (every, middle_cols)),
        edges=[outer_edge(lead), outer_edge(last)], after=centre,
    )
    low_out, high_out = swap_ends(head, tail, "inline")
    windows = [
        (0, BORDER, span_of(0, 0, HALF) + span_of(1, 0, BORDER + HALF)),
        (cols - BORDER, BORDER, span_of(1, cols - BORDER - HALF, BORDER + HALF) + span_of(2, 0, HALF)),
    ]
    (middle_second,) = steer(
        dip_cross, [(west, True), (middle, False), (east, True), (centre, False)], 1, mid_rows, inner, windows, same,
        filled=(3, (every, middle_cols)), after=border_second,
    )

    places = span_of(0, BORDER - HALF, HALF) + span_of(1, 0, mid_rows) + span_of(0, BORDER, HALF)
    (result,) = steer(
        dip_inline, [(border_second, True), (middle_second, True)], 0, cols, same, mid_windows(places, rows), mid_place,
        batches=[[(0, first, WINDOW)] for first in range(0, cols, WINDOW)],
    )
    windows = [
        (0, BORDER, span_of(0, 0, HALF) + span_of(1, 0, BORDER) + span_of(2, 0, HALF)),
        (rows - BORDER, BORDER, span_of(2, mid_rows - HALF, HALF) + span_of(1, BORDER, BORDER) + span_of(3, 0, HALF)),
    ]
    for low, high, lines, line_of, batches in (
        (low_mid, high_mid, mid_cols, inner, [[(0, first, WINDOW)] for first in range(BORDER, cols - BORDER, WINDOW)]),
        (low_out, high_out, both, outer_col, [[(0, 0, BORDER), (BORDER, cols - BORDER, BORDER)]]),
    ):
        (result,) = steer(
            dip_inline, [(low, False), (border_second, True), (middle_second, True), (high, False)], 0, lines, line_of,
            windows, outer_place, batches=batches, before=result,
        )
    return result


def on_device(traces, destination, bin_index, dip_inline, dip_cross):
    held, block_rows, _ = traces.shape
    devices = lax.axis_size("inline") * lax.axis_size("crosslin")
    capacity = 2 * held // devices
    mine = lax.axis_index("inline") * lax.axis_size("crosslin") + lax.axis_index("crosslin")
    outgoing = pack(traces, mine.astype(I32).reshape(1), destination.reshape(-1), bin_index.T, devices, capacity)
    arrived = lax.all_to_all(outgoing, BOTH, split_axis=0, concat_axis=0, tiled=True)
    return smooth(arrived, capacity, block_rows, dip_inline, dip_cross)


def solution(mesh):
    return jax.shard_map(
        on_device,
        mesh=mesh,
        in_specs=(
            P(BOTH, None, None),
            P(BOTH, None),
            P(BOTH, None),
            P("inline", "crosslin"),
            P("inline", "crosslin"),
        ),
        out_specs=P("inline", "crosslin", None),
        check_vma=False,
    )
```

```python
import functools

import jax
import jax.numpy as jnp
from jax import lax
from jax.experimental import pallas as pl
from jax.experimental.pallas import tpu as pltpu
from jax.sharding import PartitionSpec as P

HALF = 7
DMAX = 2
LANES = 128
PHASES = 8
PAIR = 2 * PHASES
WIDE = 2 * LANES
BLOCK = WIDE // PHASES
WINDOW = 16
BORDER = 8
REACH = -(-HALF * DMAX // PHASES)
REACHES = range(-REACH, REACH + 1)
BOTH = ("inline", "crosslin")
MIB = 2**20
VMEM = pl.BlockSpec(memory_space=pltpu.VMEM)
SMEM = pl.BlockSpec(memory_space=pltpu.SMEM)
ANY = pl.BlockSpec(memory_space=pl.ANY)
HBM = pl.BlockSpec(memory_space=pltpu.HBM)
F32, BF16, I32 = jnp.float32, jnp.bfloat16, jnp.int32


def fill_interleave(table_ref, time_dim):
    time = lax.broadcasted_iota(I32, (WIDE, WIDE), time_dim)
    place = lax.broadcasted_iota(I32, (WIDE, WIDE), 1 - time_dim)
    hit = time == place % BLOCK * PHASES + place // BLOCK
    table_ref[...] = jnp.where(hit, 1.0, 0.0).astype(BF16)


def move_samples(rows, table):
    count = rows.shape[0]
    upper = rows.astype(BF16)
    rest = (rows - upper.astype(F32)).astype(BF16)
    both = jnp.concatenate([upper, rest], axis=0)
    moved = jnp.dot(both, table, preferred_element_type=F32)
    return moved[:count] + moved[count:]


def take_lanes(tile, index):
    return jnp.take_along_axis(tile, index, axis=1, mode="promise_in_bounds")


def swap_blocks(tiles):
    lane = lax.broadcasted_iota(I32, tiles[0].shape, 1)
    tiles = list(tiles)
    for step in (2, 1):
        low = lane // BLOCK % (2 * step) < step
        across = lane ^ (step * BLOCK)
        for m in range(len(tiles)):
            if m // step % 2 == 0:
                first, second = tiles[m], tiles[m + step]
                crossed = take_lanes(jnp.where(low, second, first), across)
                tiles[m] = jnp.where(low, first, crossed)
                tiles[m + step] = jnp.where(low, crossed, second)
    return tiles


def pack_kernel(mine_ref, target_ref, bins_ref, traces_ref, out_ref, held_ref, table_ref, tiles_ref, used_ref, rank_ref, listed_ref, in_sems, sem, listed_sem, *, capacity):
    held, block_rows, samples = traces_ref.shape
    devices, room, _ = listed_ref.shape
    span = block_rows * PHASES
    groups = held_ref.shape[0]
    count = held // groups
    loads = [
        pltpu.make_async_copy(traces_ref.at[pl.ds(group * count, count)], held_ref.at[group], in_sems.at[group])
        for group in range(groups)
    ]
    for load in loads:
        load.start()
    fill_interleave(table_ref, 0)
    lane = lax.broadcasted_iota(I32, (1, LANES), 1)
    listed_ref[...] = jnp.zeros(listed_ref.shape, F32)
    own_lanes = mine_ref[0] % (LANES // (capacity * block_rows)) * (capacity * block_rows)

    def clear(device, _):
        used_ref[device] = 0
        return 0

    lax.fori_loop(0, devices, clear, 0)

    def choose_slot(block, _):
        device = target_ref[block]
        rank = used_ref[device]
        used_ref[device] = rank + 1
        rank_ref[block] = rank
        row = jnp.zeros((1, LANES), I32)
        for j in range(block_rows):
            row = jnp.where(lane == own_lanes + rank * block_rows + j, bins_ref[j, block] + 1, row)
        listed_ref[device, 0:1, :] = listed_ref[device, 0:1, :] + row.astype(F32)
        return 0

    lax.fori_loop(0, held, choose_slot, 0, unroll=4)
    lists = pltpu.make_async_copy(
        listed_ref, out_ref.at[:, capacity * span : capacity * span + room, :], listed_sem
    )
    lists.start()

    def send_block(block, _):
        pltpu.make_async_copy(
            tiles_ref.at[pl.ds(pl.multiple_of(block * span, 8), span), :],
            out_ref.at[target_ref[block], pl.ds(pl.multiple_of(rank_ref[block] * span, 8), span), :],
            sem,
        ).start()
        return 0

    for group in range(groups):
        loads[group].wait()
        rows = held_ref[group].reshape(count * block_rows, samples)
        stretches = samples // WIDE
        cut = jnp.concatenate([rows[:, i * WIDE : (i + 1) * WIDE] for i in range(stretches)], axis=0)
        moved = move_samples(cut, table_ref[...])
        for eight in range(count * block_rows // 8):
            for half in range(2):
                parts = []
                for i in range(stretches):
                    begin = i * count * block_rows + eight * 8
                    parts.append(moved[begin : begin + 8, half * LANES : (half + 1) * LANES])
                for phase, part in enumerate(swap_blocks(parts)):
                    first = (group * count * block_rows + eight * 8) * PHASES + half * 4 + phase
                    tiles_ref[pl.ds(first, 8, stride=PHASES), :] = part
        lax.fori_loop(group * count, (group + 1) * count, send_block, 0, unroll=4)
    lists.wait()
    pltpu.make_async_copy(tiles_ref, tiles_ref, sem).wait()


def pack(traces, mine, target, bins, devices, capacity):
    held, block_rows, samples = traces.shape
    span = block_rows * PHASES
    room = 8
    groups = 2
    return pl.pallas_call(
        functools.partial(pack_kernel, capacity=capacity),
        in_specs=[SMEM, SMEM, SMEM, HBM],
        out_specs=HBM,
        out_shape=jax.ShapeDtypeStruct((devices, capacity * span + room, LANES), F32),
        scratch_shapes=[
            pltpu.VMEM((groups, held // groups, block_rows, samples), F32),
            pltpu.VMEM((WIDE, WIDE), BF16),
            pltpu.VMEM((held * span, LANES), F32),
            pltpu.SMEM((devices,), I32),
            pltpu.SMEM((held,), I32),
            pltpu.VMEM((devices, room, LANES), F32),
            pltpu.SemaphoreType.DMA((groups,)),
            pltpu.SemaphoreType.DMA,
            pltpu.SemaphoreType.DMA,
        ],
        compiler_params=pltpu.CompilerParams(vmem_limit_bytes=60 * MIB),
    )(mine, target, bins, traces)


def bin_kernel(blocks_ref, out_ref, *refs, capacity, block_rows, edges):
    edge_refs, refs = refs[: len(edges)], refs[len(edges) :]
    even_ref, odd_ref, listed_ref, places_ref, scale_ref, scales_ref, sem, sems = refs
    devices = blocks_ref.shape[0]
    tile_rows, tile_cols = out_ref.shape[:2]
    bin_total = tile_rows * tile_cols
    unroll = 8
    lanes = capacity * block_rows
    shared = LANES // lanes

    def read_lists(row, _):
        total = jnp.zeros((1, LANES), F32)
        for i in range(shared):
            total = total + blocks_ref[row * shared + i, lanes * PHASES : lanes * PHASES + 1, :]
        listed_ref[pl.ds(row, 1), :] = jnp.where(total > 0, total - 1.0, float(bin_total)).astype(I32)
        return 0

    lax.fori_loop(0, devices // shared, read_lists, 0)
    copy = pltpu.make_async_copy(listed_ref, places_ref, sem)
    copy.start()
    nothing = jnp.zeros((PHASES, LANES), F32)

    def clear(i, _):
        for j in range(unroll):
            even_ref[i * unroll + j] = nothing
            odd_ref[i * unroll + j] = nothing
        return 0

    lax.fori_loop(0, bin_total // unroll, clear, 0)
    copy.wait()
    count_rows = scale_ref.shape[0]
    numbers = lax.broadcasted_iota(I32, (count_rows, LANES), 0) * LANES + lax.broadcasted_iota(
        I32, (count_rows, LANES), 1
    )

    def add_sender(sender, folds):
        folds = list(folds)
        row, first = sender // shared, sender % shared * lanes
        for rank in range(capacity):
            for j in range(block_rows):
                total_ref = odd_ref if j % 2 else even_ref
                place = places_ref[row, first + rank * block_rows + j]
                cell = (rank * block_rows + j) * PHASES
                total_ref[place] += blocks_ref[sender, cell : cell + PHASES, :]
                folds[j % 2] = folds[j % 2] + jnp.where(numbers == place, 1.0, 0.0)
        return tuple(folds)

    empty = jnp.zeros((count_rows, LANES), F32)
    folds = lax.fori_loop(0, devices, add_sender, (empty, empty))
    scale_ref[...] = 1.0 / jnp.maximum(folds[0] + folds[1], 1.0)
    copy = pltpu.make_async_copy(scale_ref, scales_ref, sem)
    copy.start()
    copy.wait()

    def finish(row, _):
        high, low = row * tile_cols // LANES, row * tile_cols % LANES
        for col in range(tile_cols):
            place = row * tile_cols + col
            scale = scales_ref[high, low + col]
            out_ref[row, col] = (even_ref[place] + odd_ref[place]) * scale
        return 0

    lax.fori_loop(0, HALF, finish, 0)
    lax.fori_loop(tile_rows - HALF, tile_rows, finish, 0)
    copies = edge_copies(out_ref, (), edges, edge_refs, sems)
    for copy in copies:
        copy.start()
    lax.fori_loop(HALF, tile_rows - HALF, finish, 0)
    for copy in copies:
        copy.wait()


def edge_copies(out_ref, pieces, edges, edge_refs, sems):
    copies = []
    for (_, moves), edge_ref in zip(edges, edge_refs):
        for source, target, *piece in moves:
            from_ref = pieces[piece[0]] if piece else out_ref
            copies.append(pltpu.make_async_copy(from_ref.at[source], edge_ref.at[target], sems.at[len(copies)]))
    return copies


def edge_outputs(edges):
    shapes = [jax.ShapeDtypeStruct(tuple(shape) + (PHASES, LANES), F32) for shape, _ in edges]
    moves = sum(len(moves) for _, moves in edges)
    return shapes, [HBM] * len(edges), pltpu.SemaphoreType.DMA((max(1, moves),))


def stack_bins(blocks, tile_rows, tile_cols, capacity, block_rows, edges):
    devices = blocks.shape[0]
    bin_total = tile_rows * tile_cols
    shapes, specs, sems = edge_outputs(edges)
    return pl.pallas_call(
        functools.partial(bin_kernel, capacity=capacity, block_rows=block_rows, edges=edges),
        in_specs=[VMEM],
        out_specs=[VMEM] + specs,
        out_shape=[jax.ShapeDtypeStruct((tile_rows, tile_cols, PHASES, LANES), F32)] + shapes,
        scratch_shapes=[
            pltpu.VMEM((bin_total + 8, PHASES, LANES), F32),
            pltpu.VMEM((bin_total + 8, PHASES, LANES), F32),
            pltpu.VMEM((devices * capacity * block_rows // LANES, LANES), I32),
            pltpu.SMEM((devices * capacity * block_rows // LANES, LANES), I32),
            pltpu.VMEM((bin_total // LANES, LANES), F32),
            pltpu.SMEM((bin_total // LANES, LANES), F32),
            pltpu.SemaphoreType.DMA,
            sems,
        ],
        compiler_params=pltpu.CompilerParams(vmem_limit_bytes=14 * MIB),
    )(blocks)


def fill_weights(spots_ref, weights_ref):
    row = lax.broadcasted_iota(I32, (PAIR, LANES), 0)
    column = lax.broadcasted_iota(I32, (PAIR, LANES), 1)
    for pair in range(spots_ref.shape[0] // (2 * PAIR)):
        for half in range(2):
            block = pl.ds((pair * 2 + half) * PAIR, PAIR)
            spot = half * PAIR + column // PHASES - HALF - 2 * pair - row // PHASES
            share = jnp.maximum(HALF + 1 - jnp.abs(spot), 0).astype(F32) / (HALF + 1) ** 2
            spots_ref[block, :] = jnp.clip(spot, -HALF - 1, HALF + 1).astype(F32).astype(BF16)
            weights_ref[block, :] = share.astype(BF16)


def split_cells(cells, halves_ref):
    for pair in range(len(cells) // 2):
        both = jnp.concatenate([cells[2 * pair](), cells[2 * pair + 1]()], axis=0)
        upper = both.astype(BF16)
        halves_ref[pair * PAIR : (pair + 1) * PAIR, :LANES] = upper
        rest = (both - upper.astype(F32)).astype(BF16)
        halves_ref[pair * PAIR : (pair + 1) * PAIR, LANES:] = rest


def apply_taps(dip_of, first, count, halves_ref, spots_ref, weights_ref):
    row = lax.broadcasted_iota(I32, (PAIR, LANES), 0)
    column = lax.broadcasted_iota(I32, (PAIR, LANES), 1)
    phase_gap = ((row & (PHASES - 1)) - (column & (PHASES - 1))).astype(F32).astype(BF16)
    none = jnp.zeros((PAIR, LANES), BF16)
    taps = []
    for pair in range(count // 2):
        dip = jnp.concatenate(
            [jnp.full((PHASES, LANES), dip_of(first + 2 * pair + i).astype(F32)) for i in range(2)], axis=0
        ).astype(BF16)
        moves, weights = [], []
        for half in range(2):
            block = pl.ds((pair * 2 + half) * PAIR, PAIR)
            moves.append(phase_gap + dip * spots_ref[block, :])
            weights.append(weights_ref[block, :])
        for reach in REACHES:
            taps.append(
                jnp.concatenate(
                    [jnp.where(moves[h] == jnp.bfloat16(reach * PHASES), weights[h], none) for h in range(2)],
                    axis=1,
                )
            )
    return jnp.dot(jnp.concatenate(taps, axis=0), halves_ref[...], preferred_element_type=F32)


def move_lanes(sums, first, count, put):
    lane = lax.broadcasted_iota(I32, (PHASES, LANES), 1)
    for pair in range(count // 2):
        for member in range(2):
            total = None
            for reach in REACHES:
                begin = (pair * len(REACHES) + reach + REACH) * PAIR + member * PHASES
                part = sums[begin : begin + PHASES, :LANES] + sums[begin : begin + PHASES, LANES:]
                if reach:
                    part = pltpu.roll(part, (-reach) % LANES, axis=1)
                    inside = lane < LANES - reach if reach > 0 else lane >= -reach
                    part = jnp.where(inside, part, 0.0)
                total = part if total is None else total + part
            put(first + 2 * pair + member, total)


def steer_kernel(dip_ref, *refs, along, whole, lines, line_of, windows, local_of, edges, final, batches, filled, chained, pieces_count, abreast):
    pieces, refs = refs[:pieces_count], refs[pieces_count:]
    refs = refs[chained:]
    out_ref, refs = refs[0], refs[1:]
    edge_refs, refs = refs[: len(edges)], refs[len(edges) :]
    spots_ref, weights_ref, sems, *refs = refs
    halves = refs[: abreast * len(windows)]
    if final:
        staged_ref, result_ref, table_ref = refs[abreast * len(windows) :]
        fill_interleave(table_ref, 1)
    fill_weights(spots_ref, weights_ref)
    for i, halves_ref in enumerate(halves):
        used = len(windows[i % len(windows)][2]) * PHASES
        if used < WIDE:
            halves_ref[used:, :] = jnp.zeros((WIDE - used, WIDE), BF16)

    def at(place, line):
        return (place, line) if along == 0 else (line, place)

    def some_lines(step, _):
        jobs = []
        for parity in range(abreast):
            line = abreast * step + parity
            full = line_of(line)

            def cell(index, local, line=line, full=full):
                return lambda: pieces[index][at(local, full if whole[index] else line)]

            def put(place, value, line=line):
                if final:
                    staged_ref[pl.ds((local_of(place) * final + line % final) * PHASES, PHASES), :] = value
                else:
                    out_ref[at(local_of(place), line)] = value

            for i, (first, count, places) in enumerate(windows):
                halves_ref = halves[parity * len(windows) + i]
                split_cells([cell(*place) for place in places], halves_ref)
                jobs.append((full, first, count, halves_ref, put))
        waiting = None
        for full, first, count, halves_ref, put in jobs:
            sums = apply_taps(
                lambda place: dip_ref[at(place, full)], first, count, halves_ref, spots_ref, weights_ref
            )
            if waiting is not None:
                move_lanes(*waiting)
            waiting = (sums, first, count, put)
        move_lanes(*waiting)
        return 0

    if not final:
        if filled is not None:
            index, target = filled
            fill = pltpu.make_async_copy(pieces[index], out_ref.at[target], sems.at[sems.shape[0] - 1])
            fill.start()
        lax.fori_loop(0, lines // abreast, some_lines, 0)
        if filled is not None:
            fill.wait()
        copies = edge_copies(out_ref, pieces, edges, edge_refs, sems)
        for copy in copies:
            copy.start()
        for copy in copies:
            copy.wait()
        return

    outputs = sum(count for _, count, _ in windows)

    def copies_of(batch, slot):
        return [
            pltpu.make_async_copy(
                result_ref.at[slot, pl.ds(local_of(first), count), pl.ds(local, wide), :],
                out_ref.at[pl.ds(first, count), pl.ds(full, wide), :],
                sems.at[(slot * len(windows) + i) * len(batches[batch]) + j],
            )
            for i, (first, count, _) in enumerate(windows)
            for j, (local, full, wide) in enumerate(batches[batch])
        ]

    for batch in range(lines // final):
        lax.fori_loop(batch * final // abreast, (batch + 1) * final // abreast, some_lines, 0)
        stretches = PHASES * LANES // WIDE
        cuts = [[] for _ in range(stretches)]
        for eight in range(outputs * final // 8):
            sides = [
                swap_blocks(
                    [
                        staged_ref[pl.ds(eight * 8 * PHASES + half * 4 + phase, 8, stride=PHASES), :]
                        for phase in range(PHASES // 2)
                    ]
                )
                for half in range(2)
            ]
            for i in range(stretches):
                cuts[i].append(jnp.concatenate([sides[0][i], sides[1][i]], axis=1))
        moved = move_samples(jnp.concatenate(sum(cuts, []), axis=0), table_ref[...])
        slot = batch % 2
        if batch >= 2:
            for copy in copies_of(batch - 2, slot):
                copy.wait()
        count = outputs * final
        for i in range(stretches):
            result_ref[slot, :, :, i * WIDE : (i + 1) * WIDE] = moved[i * count : (i + 1) * count].reshape(
                outputs, final, WIDE
            )
        for copy in copies_of(batch, slot):
            copy.start()
    for batch in range(max(0, lines // final - 2), lines // final):
        for copy in copies_of(batch, batch % 2):
            copy.wait()


def steer(
    dip, pieces, along, lines, line_of, windows, local_of, edges=(), batches=None, before=None, after=None, filled=None
):
    samples = PHASES * LANES
    outputs = sum(count for _, count, _ in windows)
    final = 16 if batches is not None else 0
    abreast = 4 * WINDOW // outputs
    shapes, specs, sems = edge_outputs(edges)
    operands = [dip] + [array for array, _ in pieces]
    in_specs = [SMEM] + [VMEM] * len(pieces)
    aliases = {}
    if final:
        if before is not None:
            aliases = {len(operands): 0}
            operands.append(before)
            in_specs.append(HBM)
        out_shape = [jax.ShapeDtypeStruct(dip.shape + (samples,), F32)]
        sems = pltpu.SemaphoreType.DMA((2 * len(windows) * len(batches[0]),))
        out_specs = [HBM]
    else:
        reach = outputs if filled is None else dip.shape[along]
        shape = (reach, lines) if along == 0 else (lines, reach)
        out_shape = [jax.ShapeDtypeStruct(shape + (PHASES, LANES), F32)] + shapes
        out_specs = [VMEM] + specs
        if filled is not None:
            sems = pltpu.SemaphoreType.DMA((sems.shape[0] + 1,))
    if after is not None:
        operands.append(after)
        in_specs.append(ANY)
    most = max(count for _, count, _ in windows)
    constant = pltpu.VMEM((most * PAIR, LANES), BF16)
    scratch = [constant, constant, sems]
    scratch += [pltpu.VMEM((WIDE, WIDE), BF16)] * (abreast * len(windows))
    if final:
        scratch += [
            pltpu.VMEM((outputs * final * PHASES, LANES), F32),
            pltpu.VMEM((2, outputs, final, samples), F32),
            pltpu.VMEM((WIDE, WIDE), BF16),
        ]
    return pl.pallas_call(
        functools.partial(
            steer_kernel,
            along=along, whole=[whole for _, whole in pieces], lines=lines, line_of=line_of, windows=windows,
            local_of=local_of, edges=edges, final=final, batches=batches, filled=filled, chained=len(operands) - len(pieces) - 1, pieces_count=len(pieces), abreast=abreast,
        ),
        in_specs=in_specs,
        out_specs=out_specs,
        out_shape=out_shape,
        scratch_shapes=scratch,
        input_output_aliases=aliases,
        compiler_params=pltpu.CompilerParams(vmem_limit_bytes=16 * MIB),
        cost_estimate=pl.CostEstimate(
            flops=16000 * outputs * lines * samples,
            bytes_accessed=8 * outputs * lines * samples,
            transcendentals=0,
        ),
    )(*operands)


def swap_ends(head, tail, axis):
    count = lax.axis_size(axis)
    low = lax.ppermute(tail, axis, [(i, i + 1) for i in range(count - 1)])
    high = lax.ppermute(head, axis, [(i + 1, i) for i in range(count - 1)])
    return low, high


def span_of(index, first, count):
    return [(index, first + i) for i in range(count)]


def rows_of(first, count):
    return slice(first, first + count)


def smooth(arrived, capacity, block_rows, dip_inline, dip_cross):
    rows, cols = dip_inline.shape
    mid_rows, mid_cols = rows - 2 * BORDER, cols - 2 * BORDER
    both = 2 * BORDER
    same = lambda line: line
    inner = lambda line: line + BORDER
    outer_col = lambda line: line + jnp.where(line < BORDER, 0, mid_cols)
    outer_row = lambda line: line + jnp.where(line < BORDER, 0, mid_rows)
    mid_place = lambda place: place - BORDER
    outer_place = lambda place: place if place < BORDER else place - mid_rows
    every = slice(None)
    lead, last = rows_of(0, HALF), rows_of(both - HALF, HALF)
    left, right, middle_cols = rows_of(0, BORDER), rows_of(cols - BORDER, BORDER), rows_of(BORDER, mid_cols)

    def outer_edge(pick):
        return ((HALF, both), [((pick, left), (every, rows_of(0, BORDER))), ((pick, right), (every, rows_of(BORDER, BORDER)))])

    def whole_edge(shape, pick):
        return (shape, [(pick, (every, every))])

    def mid_windows(places, extent):
        return [(i, WINDOW, places[i - BORDER : i - BORDER + WINDOW + 2 * HALF]) for i in range(BORDER, extent - BORDER, WINDOW)]

    stacked, head_out, tail_out, head_mid, tail_mid = stack_bins(
        arrived, rows, cols, capacity, block_rows,
        [
            outer_edge(rows_of(0, HALF)),
            outer_edge(rows_of(rows - HALF, HALF)),
            whole_edge((HALF, mid_cols), (rows_of(0, HALF), middle_cols)),
            whole_edge((HALF, mid_cols), (rows_of(rows - HALF, HALF), middle_cols)),
        ],
    )
    low_out, high_out = swap_ends(head_out, tail_out, "inline")
    low_mid, high_mid = swap_ends(head_mid, tail_mid, "inline")

    (middle,) = steer(
        dip_inline, [(stacked, True)], 0, cols, same,
        mid_windows(span_of(0, BORDER - HALF, mid_rows + 2 * HALF), rows), mid_place,
    )
    windows = [
        (0, BORDER, span_of(0, 0, HALF) + span_of(1, 0, BORDER + HALF)),
        (rows - BORDER, BORDER, span_of(1, rows - BORDER - HALF, BORDER + HALF) + span_of(2, 0, HALF)),
    ]
    top, bottom, between = rows_of(0, BORDER), rows_of(rows - BORDER, BORDER), rows_of(BORDER, mid_rows)

    def column_edge(outer, whole):
        return (
            (rows, HALF),
            [
                ((rows_of(0, BORDER), outer), (top, every)),
                ((rows_of(BORDER, BORDER), outer), (bottom, every)),
                ((every, whole), (between, every), 3),
            ],
        )

    corners, head, tail = steer(
        dip_inline, [(low_out, False), (stacked, True), (high_out, False), (middle, False)], 0, both, outer_col,
        windows, outer_place, edges=[column_edge(lead, lead), column_edge(last, rows_of(cols - HALF, HALF))],
    )
    west, east = swap_ends(head, tail, "crosslin")
    (flanks,) = steer(
        dip_inline, [(low_mid, False), (stacked, True), (high_mid, False)], 0, mid_cols, inner, windows, outer_place,
        after=corners,
    )

    places = span_of(0, BORDER - HALF, HALF) + span_of(1, 0, mid_cols) + span_of(0, BORDER, HALF)
    second_mid, head, tail = steer(
        dip_cross, [(corners, False), (flanks, False)], 1, both, outer_row, mid_windows(places, cols), mid_place,
        edges=[whole_edge((HALF, mid_cols), (lead, every)), whole_edge((HALF, mid_cols), (last, every))],
    )
    low_mid, high_mid = swap_ends(head, tail, "inline")
    (centre,) = steer(
        dip_cross, [(middle, False)], 1, mid_rows, inner,
        mid_windows(span_of(0, BORDER - HALF, mid_cols + 2 * HALF), cols), mid_place, after=second_mid,
    )
    places = span_of(0, BORDER - HALF, HALF) + span_of(1, 0, mid_rows) + span_of(0, BORDER, HALF)
    middle_windows = mid_windows(places, rows)
    middle_batches = [[(0, first, WINDOW)] for first in range(BORDER, cols - BORDER, WINDOW)]
    outer_batches = [[(0, 0, BORDER), (BORDER, cols - BORDER, BORDER)]]
    (result,) = steer(
        dip_inline, [(second_mid, False), (centre, False)], 0, mid_cols, inner, middle_windows, mid_place,
        batches=middle_batches,
    )
    windows = [
        (0, BORDER, span_of(0, 0, HALF) + span_of(1, 0, BORDER) + span_of(2, 0, HALF)),
        (cols - BORDER, BORDER, span_of(2, mid_cols - HALF, HALF) + span_of(1, BORDER, BORDER) + span_of(3, 0, HALF)),
    ]
    border_second, head, tail = steer(
        dip_cross,
        [(west, True), (corners, False), (flanks, False), (east, True), (second_mid, False)],
        1, both, outer_row, windows, same, filled=(4, (every, middle_cols)),
        edges=[outer_edge(lead), outer_edge(last)], after=centre,
    )
    low_out, high_out = swap_ends(head, tail, "inline")
    windows = [
        (0, BORDER, span_of(0, 0, HALF) + span_of(1, 0, BORDER + HALF)),
        (cols - BORDER, BORDER, span_of(1, cols - BORDER - HALF, BORDER + HALF) + span_of(2, 0, HALF)),
    ]
    (middle_second,) = steer(
        dip_cross, [(west, True), (middle, False), (east, True), (centre, False)], 1, mid_rows, inner, windows, same,
        filled=(3, (every, middle_cols)), after=border_second,
    )

    (result,) = steer(
        dip_inline, [(border_second, True), (middle_second, True)], 0, both, outer_col, middle_windows, mid_place,
        batches=outer_batches, before=result,
    )
    windows = [
        (0, BORDER, span_of(0, 0, HALF) + span_of(1, 0, BORDER) + span_of(2, 0, HALF)),
        (rows - BORDER, BORDER, span_of(2, mid_rows - HALF, HALF) + span_of(1, BORDER, BORDER) + span_of(3, 0, HALF)),
    ]
    for low, high, lines, line_of, batches in (
        (low_mid, high_mid, mid_cols, inner, middle_batches),
        (low_out, high_out, both, outer_col, outer_batches),
    ):
        (result,) = steer(
            dip_inline, [(low, False), (border_second, True), (middle_second, True), (high, False)], 0, lines, line_of,
            windows, outer_place, batches=batches, before=result,
        )
    return result


def on_device(traces, destination, bin_index, dip_inline, dip_cross):
    held, block_rows, _ = traces.shape
    devices = lax.axis_size("inline") * lax.axis_size("crosslin")
    capacity = 2 * held // devices
    mine = lax.axis_index("inline") * lax.axis_size("crosslin") + lax.axis_index("crosslin")
    outgoing = pack(traces, mine.astype(I32).reshape(1), destination.reshape(-1), bin_index.T, devices, capacity)
    arrived = lax.all_to_all(outgoing, BOTH, split_axis=0, concat_axis=0, tiled=True)
    return smooth(arrived, capacity, block_rows, dip_inline, dip_cross)


def solution(mesh):
    return jax.shard_map(
        on_device,
        mesh=mesh,
        in_specs=(
            P(BOTH, None, None),
            P(BOTH, None),
            P(BOTH, None),
            P("inline", "crosslin"),
            P("inline", "crosslin"),
        ),
        out_specs=P("inline", "crosslin", None),
        check_vma=False,
    )
```

```python
import functools

import jax
import jax.numpy as jnp
from jax import lax
from jax.experimental import pallas as pl
from jax.experimental.pallas import tpu as pltpu
from jax.sharding import PartitionSpec as P

HALF = 7
DMAX = 2
LANES = 128
PHASES = 8
PAIR = 2 * PHASES
WIDE = 2 * LANES
BLOCK = WIDE // PHASES
WINDOW = 16
BORDER = 8
REACH = -(-HALF * DMAX // PHASES)
REACHES = range(-REACH, REACH + 1)
BOTH = ("inline", "crosslin")
MIB = 2**20
VMEM = pl.BlockSpec(memory_space=pltpu.VMEM)
SMEM = pl.BlockSpec(memory_space=pltpu.SMEM)
ANY = pl.BlockSpec(memory_space=pl.ANY)
HBM = pl.BlockSpec(memory_space=pltpu.HBM)
F32, BF16, I32 = jnp.float32, jnp.bfloat16, jnp.int32


def fill_interleave(table_ref, time_dim):
    time = lax.broadcasted_iota(I32, (WIDE, WIDE), time_dim)
    place = lax.broadcasted_iota(I32, (WIDE, WIDE), 1 - time_dim)
    hit = time == place % BLOCK * PHASES + place // BLOCK
    table_ref[...] = jnp.where(hit, 1.0, 0.0).astype(BF16)


def move_samples(rows, table):
    count = rows.shape[0]
    upper = rows.astype(BF16)
    rest = (rows - upper.astype(F32)).astype(BF16)
    both = jnp.concatenate([upper, rest], axis=0)
    moved = jnp.dot(both, table, preferred_element_type=F32)
    return moved[:count] + moved[count:]


def take_lanes(tile, index):
    return jnp.take_along_axis(tile, index, axis=1, mode="promise_in_bounds")


def swap_blocks(tiles):
    lane = lax.broadcasted_iota(I32, tiles[0].shape, 1)
    tiles = list(tiles)
    for step in (2, 1):
        low = lane // BLOCK % (2 * step) < step
        across = lane ^ (step * BLOCK)
        for m in range(len(tiles)):
            if m // step % 2 == 0:
                first, second = tiles[m], tiles[m + step]
                crossed = take_lanes(jnp.where(low, second, first), across)
                tiles[m] = jnp.where(low, first, crossed)
                tiles[m + step] = jnp.where(low, crossed, second)
    return tiles


def pack_kernel(mine_ref, target_ref, bins_ref, traces_ref, out_ref, held_ref, table_ref, tiles_ref, used_ref, rank_ref, listed_ref, in_sems, sem, listed_sem, *, capacity):
    held, block_rows, samples = traces_ref.shape
    devices, room, _ = listed_ref.shape
    span = block_rows * PHASES
    groups = held_ref.shape[0]
    count = held // groups
    loads = [
        pltpu.make_async_copy(traces_ref.at[pl.ds(group * count, count)], held_ref.at[group], in_sems.at[group])
        for group in range(groups)
    ]
    for load in loads:
        load.start()
    fill_interleave(table_ref, 0)
    lane = lax.broadcasted_iota(I32, (1, LANES), 1)
    listed_ref[...] = jnp.zeros(listed_ref.shape, F32)
    own_lanes = mine_ref[0] % (LANES // (capacity * block_rows)) * (capacity * block_rows)

    def clear(device, _):
        used_ref[device] = 0
        return 0

    lax.fori_loop(0, devices, clear, 0)

    def choose_slot(block, _):
        device = target_ref[block]
        rank = used_ref[device]
        used_ref[device] = rank + 1
        rank_ref[block] = rank
        row = jnp.zeros((1, LANES), I32)
        for j in range(block_rows):
            row = jnp.where(lane == own_lanes + rank * block_rows + j, bins_ref[j, block] + 1, row)
        listed_ref[device, 0:1, :] = listed_ref[device, 0:1, :] + row.astype(F32)
        return 0

    lax.fori_loop(0, held, choose_slot, 0, unroll=4)
    lists = pltpu.make_async_copy(
        listed_ref, out_ref.at[:, capacity * span : capacity * span + room, :], listed_sem
    )
    lists.start()

    def send_block(block, _):
        pltpu.make_async_copy(
            tiles_ref.at[pl.ds(pl.multiple_of(block * span, 8), span), :],
            out_ref.at[target_ref[block], pl.ds(pl.multiple_of(rank_ref[block] * span, 8), span), :],
            sem,
        ).start()
        return 0

    for group in range(groups):
        loads[group].wait()
        rows = held_ref[group].reshape(count * block_rows, samples)
        stretches = samples // WIDE
        cut = jnp.concatenate([rows[:, i * WIDE : (i + 1) * WIDE] for i in range(stretches)], axis=0)
        moved = move_samples(cut, table_ref[...])
        for eight in range(count * block_rows // 8):
            for half in range(2):
                parts = []
                for i in range(stretches):
                    begin = i * count * block_rows + eight * 8
                    parts.append(moved[begin : begin + 8, half * LANES : (half + 1) * LANES])
                for phase, part in enumerate(swap_blocks(parts)):
                    first = (group * count * block_rows + eight * 8) * PHASES + half * 4 + phase
                    tiles_ref[pl.ds(first, 8, stride=PHASES), :] = part
        lax.fori_loop(group * count, (group + 1) * count, send_block, 0, unroll=4)
    lists.wait()
    pltpu.make_async_copy(tiles_ref, tiles_ref, sem).wait()


def pack(traces, mine, target, bins, devices, capacity):
    held, block_rows, samples = traces.shape
    span = block_rows * PHASES
    room = 8
    groups = 2
    return pl.pallas_call(
        functools.partial(pack_kernel, capacity=capacity),
        in_specs=[SMEM, SMEM, SMEM, HBM],
        out_specs=HBM,
        out_shape=jax.ShapeDtypeStruct((devices, capacity * span + room, LANES), F32),
        scratch_shapes=[
            pltpu.VMEM((groups, held // groups, block_rows, samples), F32),
            pltpu.VMEM((WIDE, WIDE), BF16),
            pltpu.VMEM((held * span, LANES), F32),
            pltpu.SMEM((devices,), I32),
            pltpu.SMEM((held,), I32),
            pltpu.VMEM((devices, room, LANES), F32),
            pltpu.SemaphoreType.DMA((groups,)),
            pltpu.SemaphoreType.DMA,
            pltpu.SemaphoreType.DMA,
        ],
        compiler_params=pltpu.CompilerParams(vmem_limit_bytes=60 * MIB),
    )(mine, target, bins, traces)


def bin_kernel(blocks_ref, out_ref, *refs, capacity, block_rows, edges):
    edge_refs, refs = refs[: len(edges)], refs[len(edges) :]
    even_ref, odd_ref, listed_ref, places_ref, scale_ref, scales_ref, sem, sems = refs
    devices = blocks_ref.shape[0]
    tile_rows, tile_cols = out_ref.shape[:2]
    bin_total = tile_rows * tile_cols
    unroll = 8
    lanes = capacity * block_rows
    shared = LANES // lanes

    def read_lists(row, _):
        total = jnp.zeros((1, LANES), F32)
        for i in range(shared):
            total = total + blocks_ref[row * shared + i, lanes * PHASES : lanes * PHASES + 1, :]
        listed_ref[pl.ds(row, 1), :] = jnp.where(total > 0, total - 1.0, float(bin_total)).astype(I32)
        return 0

    lax.fori_loop(0, devices // shared, read_lists, 0)
    copy = pltpu.make_async_copy(listed_ref, places_ref, sem)
    copy.start()
    nothing = jnp.zeros((PHASES, LANES), F32)

    def clear(i, _):
        for j in range(unroll):
            even_ref[i * unroll + j] = nothing
            odd_ref[i * unroll + j] = nothing
        return 0

    lax.fori_loop(0, bin_total // unroll, clear, 0)
    copy.wait()
    count_rows = scale_ref.shape[0]
    numbers = lax.broadcasted_iota(I32, (count_rows, LANES), 0) * LANES + lax.broadcasted_iota(
        I32, (count_rows, LANES), 1
    )

    def add_sender(sender, folds):
        folds = list(folds)
        row, first = sender // shared, sender % shared * lanes
        for rank in range(capacity):
            for j in range(block_rows):
                total_ref = odd_ref if j % 2 else even_ref
                place = places_ref[row, first + rank * block_rows + j]
                cell = (rank * block_rows + j) * PHASES
                total_ref[place] += blocks_ref[sender, cell : cell + PHASES, :]
                folds[j % 2] = folds[j % 2] + jnp.where(numbers == place, 1.0, 0.0)
        return tuple(folds)

    empty = jnp.zeros((count_rows, LANES), F32)
    folds = lax.fori_loop(0, devices, add_sender, (empty, empty))
    scale_ref[...] = 1.0 / jnp.maximum(folds[0] + folds[1], 1.0)
    copy = pltpu.make_async_copy(scale_ref, scales_ref, sem)
    copy.start()
    copy.wait()

    def finish(row, _):
        high, low = row * tile_cols // LANES, row * tile_cols % LANES
        for col in range(tile_cols):
            place = row * tile_cols + col
            scale = scales_ref[high, low + col]
            out_ref[row, col] = (even_ref[place] + odd_ref[place]) * scale
        return 0

    lax.fori_loop(0, HALF, finish, 0)
    lax.fori_loop(tile_rows - HALF, tile_rows, finish, 0)
    copies = edge_copies(out_ref, (), edges, edge_refs, sems)
    for copy in copies:
        copy.start()
    lax.fori_loop(HALF, tile_rows - HALF, finish, 0)
    for copy in copies:
        copy.wait()


def edge_copies(out_ref, pieces, edges, edge_refs, sems):
    copies = []
    for (_, moves), edge_ref in zip(edges, edge_refs):
        for source, target, *piece in moves:
            from_ref = pieces[piece[0]] if piece else out_ref
            copies.append(pltpu.make_async_copy(from_ref.at[source], edge_ref.at[target], sems.at[len(copies)]))
    return copies


def edge_outputs(edges):
    shapes = [jax.ShapeDtypeStruct(tuple(shape) + (PHASES, LANES), F32) for shape, _ in edges]
    moves = sum(len(moves) for _, moves in edges)
    return shapes, [HBM] * len(edges), pltpu.SemaphoreType.DMA((max(1, moves),))


def stack_bins(blocks, tile_rows, tile_cols, capacity, block_rows, edges):
    devices = blocks.shape[0]
    bin_total = tile_rows * tile_cols
    shapes, specs, sems = edge_outputs(edges)
    return pl.pallas_call(
        functools.partial(bin_kernel, capacity=capacity, block_rows=block_rows, edges=edges),
        in_specs=[VMEM],
        out_specs=[VMEM] + specs,
        out_shape=[jax.ShapeDtypeStruct((tile_rows, tile_cols, PHASES, LANES), F32)] + shapes,
        scratch_shapes=[
            pltpu.VMEM((bin_total + 8, PHASES, LANES), F32),
            pltpu.VMEM((bin_total + 8, PHASES, LANES), F32),
            pltpu.VMEM((devices * capacity * block_rows // LANES, LANES), I32),
            pltpu.SMEM((devices * capacity * block_rows // LANES, LANES), I32),
            pltpu.VMEM((bin_total // LANES, LANES), F32),
            pltpu.SMEM((bin_total // LANES, LANES), F32),
            pltpu.SemaphoreType.DMA,
            sems,
        ],
        compiler_params=pltpu.CompilerParams(vmem_limit_bytes=14 * MIB),
    )(blocks)


def fill_weights(spots_ref, weights_ref):
    row = lax.broadcasted_iota(I32, (PAIR, LANES), 0)
    column = lax.broadcasted_iota(I32, (PAIR, LANES), 1)
    for pair in range(spots_ref.shape[0] // (2 * PAIR)):
        for half in range(2):
            block = pl.ds((pair * 2 + half) * PAIR, PAIR)
            spot = half * PAIR + column // PHASES - HALF - 2 * pair - row // PHASES
            share = jnp.maximum(HALF + 1 - jnp.abs(spot), 0).astype(F32) / (HALF + 1) ** 2
            spots_ref[block, :] = jnp.clip(spot, -HALF - 1, HALF + 1).astype(F32).astype(BF16)
            weights_ref[block, :] = share.astype(BF16)


def split_cells(cells, halves_ref):
    for pair in range(len(cells) // 2):
        both = jnp.concatenate([cells[2 * pair](), cells[2 * pair + 1]()], axis=0)
        upper = both.astype(BF16)
        halves_ref[pair * PAIR : (pair + 1) * PAIR, :LANES] = upper
        rest = (both - upper.astype(F32)).astype(BF16)
        halves_ref[pair * PAIR : (pair + 1) * PAIR, LANES:] = rest


def apply_taps(dip_of, first, count, halves_ref, spots_ref, weights_ref):
    row = lax.broadcasted_iota(I32, (PAIR, LANES), 0)
    column = lax.broadcasted_iota(I32, (PAIR, LANES), 1)
    phase_gap = ((row & (PHASES - 1)) - (column & (PHASES - 1))).astype(F32).astype(BF16)
    none = jnp.zeros((PAIR, LANES), BF16)
    taps = []
    for pair in range(count // 2):
        dip = jnp.concatenate(
            [jnp.full((PHASES, LANES), dip_of(first + 2 * pair + i).astype(F32)) for i in range(2)], axis=0
        ).astype(BF16)
        moves, weights = [], []
        for half in range(2):
            block = pl.ds((pair * 2 + half) * PAIR, PAIR)
            moves.append(phase_gap + dip * spots_ref[block, :])
            weights.append(weights_ref[block, :])
        for reach in REACHES:
            taps.append(
                jnp.concatenate(
                    [jnp.where(moves[h] == jnp.bfloat16(reach * PHASES), weights[h], none) for h in range(2)],
                    axis=1,
                )
            )
    return jnp.dot(jnp.concatenate(taps, axis=0), halves_ref[...], preferred_element_type=F32)


def move_lanes(sums, first, count, put):
    lane = lax.broadcasted_iota(I32, (PHASES, LANES), 1)
    for pair in range(count // 2):
        for member in range(2):
            total = None
            for reach in REACHES:
                begin = (pair * len(REACHES) + reach + REACH) * PAIR + member * PHASES
                part = sums[begin : begin + PHASES, :LANES] + sums[begin : begin + PHASES, LANES:]
                if reach:
                    part = pltpu.roll(part, (-reach) % LANES, axis=1)
                    inside = lane < LANES - reach if reach > 0 else lane >= -reach
                    part = jnp.where(inside, part, 0.0)
                total = part if total is None else total + part
            put(first + 2 * pair + member, total)


def steer_kernel(dip_ref, *refs, along, whole, lines, line_of, windows, local_of, edges, final, batches, filled, chained, pieces_count, abreast):
    pieces, refs = refs[:pieces_count], refs[pieces_count:]
    refs = refs[chained:]
    out_ref, refs = refs[0], refs[1:]
    edge_refs, refs = refs[: len(edges)], refs[len(edges) :]
    spots_ref, weights_ref, sems, *refs = refs
    halves = refs[: abreast * len(windows)]
    if final:
        staged_ref, result_ref, table_ref = refs[abreast * len(windows) :]
        fill_interleave(table_ref, 1)
    fill_weights(spots_ref, weights_ref)
    for i, halves_ref in enumerate(halves):
        used = len(windows[i % len(windows)][2]) * PHASES
        if used < WIDE:
            halves_ref[used:, :] = jnp.zeros((WIDE - used, WIDE), BF16)

    def at(place, line):
        return (place, line) if along == 0 else (line, place)

    def some_lines(step, _):
        jobs = []
        for parity in range(abreast):
            line = abreast * step + parity
            full = line_of(line)

            def cell(index, local, line=line, full=full):
                return lambda: pieces[index][at(local, full if whole[index] else line)]

            def put(place, value, line=line):
                if final:
                    staged_ref[pl.ds((local_of(place) * final + line % final) * PHASES, PHASES), :] = value
                else:
                    out_ref[at(local_of(place), line)] = value

            for i, (first, count, places) in enumerate(windows):
                halves_ref = halves[parity * len(windows) + i]
                split_cells([cell(*place) for place in places], halves_ref)
                jobs.append((full, first, count, halves_ref, put))
        waiting = None
        for full, first, count, halves_ref, put in jobs:
            sums = apply_taps(
                lambda place: dip_ref[at(place, full)], first, count, halves_ref, spots_ref, weights_ref
            )
            if waiting is not None:
                move_lanes(*waiting)
            waiting = (sums, first, count, put)
        move_lanes(*waiting)
        return 0

    if not final:
        if filled is not None:
            index, target = filled
            fill = pltpu.make_async_copy(pieces[index], out_ref.at[target], sems.at[sems.shape[0] - 1])
            fill.start()
        lax.fori_loop(0, lines // abreast, some_lines, 0)
        if filled is not None:
            fill.wait()
        copies = edge_copies(out_ref, pieces, edges, edge_refs, sems)
        for copy in copies:
            copy.start()
        for copy in copies:
            copy.wait()
        return

    outputs = sum(count for _, count, _ in windows)

    def copies_of(batch, slot):
        return [
            pltpu.make_async_copy(
                result_ref.at[slot, pl.ds(local_of(first), count), pl.ds(local, wide), :],
                out_ref.at[pl.ds(first, count), pl.ds(full, wide), :],
                sems.at[(slot * len(windows) + i) * len(batches[batch]) + j],
            )
            for i, (first, count, _) in enumerate(windows)
            for j, (local, full, wide) in enumerate(batches[batch])
        ]

    for batch in range(lines // final):
        lax.fori_loop(batch * final // abreast, (batch + 1) * final // abreast, some_lines, 0)
        stretches = PHASES * LANES // WIDE
        cuts = [[] for _ in range(stretches)]
        for eight in range(outputs * final // 8):
            sides = [
                swap_blocks(
                    [
                        staged_ref[pl.ds(eight * 8 * PHASES + half * 4 + phase, 8, stride=PHASES), :]
                        for phase in range(PHASES // 2)
                    ]
                )
                for half in range(2)
            ]
            for i in range(stretches):
                cuts[i].append(jnp.concatenate([sides[0][i], sides[1][i]], axis=1))
        moved = move_samples(jnp.concatenate(sum(cuts, []), axis=0), table_ref[...])
        slot = batch % 2
        if batch >= 2:
            for copy in copies_of(batch - 2, slot):
                copy.wait()
        count = outputs * final
        for i in range(stretches):
            result_ref[slot, :, :, i * WIDE : (i + 1) * WIDE] = moved[i * count : (i + 1) * count].reshape(
                outputs, final, WIDE
            )
        for copy in copies_of(batch, slot):
            copy.start()
    for batch in range(max(0, lines // final - 2), lines // final):
        for copy in copies_of(batch, batch % 2):
            copy.wait()


def steer(
    dip, pieces, along, lines, line_of, windows, local_of, edges=(), batches=None, before=None, after=None, filled=None
):
    samples = PHASES * LANES
    outputs = sum(count for _, count, _ in windows)
    final = BORDER if batches is not None else 0
    abreast = 4 * WINDOW // outputs
    shapes, specs, sems = edge_outputs(edges)
    operands = [dip] + [array for array, _ in pieces]
    in_specs = [SMEM] + [VMEM] * len(pieces)
    aliases = {}
    if final:
        if before is not None:
            aliases = {len(operands): 0}
            operands.append(before)
            in_specs.append(HBM)
        out_shape = [jax.ShapeDtypeStruct(dip.shape + (samples,), F32)]
        sems = pltpu.SemaphoreType.DMA((2 * len(windows) * len(batches[0]),))
        out_specs = [HBM]
    else:
        reach = outputs if filled is None else dip.shape[along]
        shape = (reach, lines) if along == 0 else (lines, reach)
        out_shape = [jax.ShapeDtypeStruct(shape + (PHASES, LANES), F32)] + shapes
        out_specs = [VMEM] + specs
        if filled is not None:
            sems = pltpu.SemaphoreType.DMA((sems.shape[0] + 1,))
    if after is not None:
        operands.append(after)
        in_specs.append(ANY)
    most = max(count for _, count, _ in windows)
    constant = pltpu.VMEM((most * PAIR, LANES), BF16)
    scratch = [constant, constant, sems]
    scratch += [pltpu.VMEM((WIDE, WIDE), BF16)] * (abreast * len(windows))
    if final:
        scratch += [
            pltpu.VMEM((outputs * final * PHASES, LANES), F32),
            pltpu.VMEM((2, outputs, final, samples), F32),
            pltpu.VMEM((WIDE, WIDE), BF16),
        ]
    return pl.pallas_call(
        functools.partial(
            steer_kernel,
            along=along, whole=[whole for _, whole in pieces], lines=lines, line_of=line_of, windows=windows,
            local_of=local_of, edges=edges, final=final, batches=batches, filled=filled, chained=len(operands) - len(pieces) - 1, pieces_count=len(pieces), abreast=abreast,
        ),
        in_specs=in_specs,
        out_specs=out_specs,
        out_shape=out_shape,
        scratch_shapes=scratch,
        input_output_aliases=aliases,
        compiler_params=pltpu.CompilerParams(vmem_limit_bytes=16 * MIB),
        cost_estimate=pl.CostEstimate(
            flops=16000 * outputs * lines * samples,
            bytes_accessed=8 * outputs * lines * samples,
            transcendentals=0,
        ),
    )(*operands)


def swap_ends(head, tail, axis):
    count = lax.axis_size(axis)
    low = lax.ppermute(tail, axis, [(i, i + 1) for i in range(count - 1)])
    high = lax.ppermute(head, axis, [(i + 1, i) for i in range(count - 1)])
    return low, high


def span_of(index, first, count):
    return [(index, first + i) for i in range(count)]


def rows_of(first, count):
    return slice(first, first + count)


def smooth(arrived, capacity, block_rows, dip_inline, dip_cross):
    rows, cols = dip_inline.shape
    mid_rows, mid_cols = rows - 2 * BORDER, cols - 2 * BORDER
    both = 2 * BORDER
    same = lambda line: line
    inner = lambda line: line + BORDER
    outer_col = lambda line: line + jnp.where(line < BORDER, 0, mid_cols)
    outer_row = lambda line: line + jnp.where(line < BORDER, 0, mid_rows)
    mid_place = lambda place: place - BORDER
    outer_place = lambda place: place if place < BORDER else place - mid_rows
    every = slice(None)
    lead, last = rows_of(0, HALF), rows_of(both - HALF, HALF)
    left, right, middle_cols = rows_of(0, BORDER), rows_of(cols - BORDER, BORDER), rows_of(BORDER, mid_cols)

    def outer_edge(pick):
        return ((HALF, both), [((pick, left), (every, rows_of(0, BORDER))), ((pick, right), (every, rows_of(BORDER, BORDER)))])

    def whole_edge(shape, pick):
        return (shape, [(pick, (every, every))])

    def mid_windows(places, extent):
        return [(i, WINDOW, places[i - BORDER : i - BORDER + WINDOW + 2 * HALF]) for i in range(BORDER, extent - BORDER, WINDOW)]

    stacked, head_out, tail_out, head_mid, tail_mid = stack_bins(
        arrived, rows, cols, capacity, block_rows,
        [
            outer_edge(rows_of(0, HALF)),
            outer_edge(rows_of(rows - HALF, HALF)),
            whole_edge((HALF, mid_cols), (rows_of(0, HALF), middle_cols)),
            whole_edge((HALF, mid_cols), (rows_of(rows - HALF, HALF), middle_cols)),
        ],
    )
    low_out, high_out = swap_ends(head_out, tail_out, "inline")
    low_mid, high_mid = swap_ends(head_mid, tail_mid, "inline")

    (middle,) = steer(
        dip_inline, [(stacked, True)], 0, cols, same,
        mid_windows(span_of(0, BORDER - HALF, mid_rows + 2 * HALF), rows), mid_place,
    )
    windows = [
        (0, BORDER, span_of(0, 0, HALF) + span_of(1, 0, BORDER + HALF)),
        (rows - BORDER, BORDER, span_of(1, rows - BORDER - HALF, BORDER + HALF) + span_of(2, 0, HALF)),
    ]
    top, bottom, between = rows_of(0, BORDER), rows_of(rows - BORDER, BORDER), rows_of(BORDER, mid_rows)

    def column_edge(outer, whole):
        return (
            (rows, HALF),
            [
                ((rows_of(0, BORDER), outer), (top, every)),
                ((rows_of(BORDER, BORDER), outer), (bottom, every)),
                ((every, whole), (between, every), 3),
            ],
        )

    corners, head, tail = steer(
        dip_inline, [(low_out, False), (stacked, True), (high_out, False), (middle, False)], 0, both, outer_col,
        windows, outer_place, edges=[column_edge(lead, lead), column_edge(last, rows_of(cols - HALF, HALF))],
    )
    west, east = swap_ends(head, tail, "crosslin")
    (flanks,) = steer(
        dip_inline, [(low_mid, False), (stacked, True), (high_mid, False)], 0, mid_cols, inner, windows, outer_place,
        after=corners,
    )

    places = span_of(0, BORDER - HALF, HALF) + span_of(1, 0, mid_cols) + span_of(0, BORDER, HALF)
    second_mid, head, tail = steer(
        dip_cross, [(corners, False), (flanks, False)], 1, both, outer_row, mid_windows(places, cols), mid_place,
        edges=[whole_edge((HALF, mid_cols), (lead, every)), whole_edge((HALF, mid_cols), (last, every))],
    )
    low_mid, high_mid = swap_ends(head, tail, "inline")
    (centre,) = steer(
        dip_cross, [(middle, False)], 1, mid_rows, inner,
        mid_windows(span_of(0, BORDER - HALF, mid_cols + 2 * HALF), cols), mid_place, after=second_mid,
    )
    places = span_of(0, BORDER - HALF, HALF) + span_of(1, 0, mid_rows) + span_of(0, BORDER, HALF)
    middle_windows = mid_windows(places, rows)
    middle_batches = [[(0, first, BORDER)] for first in range(BORDER, cols - BORDER, BORDER)]
    outer_batches = [[(0, 0, BORDER)], [(0, cols - BORDER, BORDER)]]
    (result,) = steer(
        dip_inline, [(second_mid, False), (centre, False)], 0, mid_cols, inner, middle_windows, mid_place,
        batches=middle_batches,
    )
    windows = [
        (0, BORDER, span_of(0, 0, HALF) + span_of(1, 0, BORDER) + span_of(2, 0, HALF)),
        (cols - BORDER, BORDER, span_of(2, mid_cols - HALF, HALF) + span_of(1, BORDER, BORDER) + span_of(3, 0, HALF)),
    ]
    border_second, head, tail = steer(
        dip_cross,
        [(west, True), (corners, False), (flanks, False), (east, True), (second_mid, False)],
        1, both, outer_row, windows, same, filled=(4, (every, middle_cols)),
        edges=[outer_edge(lead), outer_edge(last)], after=centre,
    )
    low_out, high_out = swap_ends(head, tail, "inline")
    windows = [
        (0, BORDER, span_of(0, 0, HALF) + span_of(1, 0, BORDER + HALF)),
        (cols - BORDER, BORDER, span_of(1, cols - BORDER - HALF, BORDER + HALF) + span_of(2, 0, HALF)),
    ]
    (middle_second,) = steer(
        dip_cross, [(west, True), (middle, False), (east, True), (centre, False)], 1, mid_rows, inner, windows, same,
        filled=(3, (every, middle_cols)), after=border_second,
    )

    (result,) = steer(
        dip_inline, [(border_second, True), (middle_second, True)], 0, both, outer_col, middle_windows, mid_place,
        batches=outer_batches, before=result,
    )
    windows = [
        (0, BORDER, span_of(0, 0, HALF) + span_of(1, 0, BORDER) + span_of(2, 0, HALF)),
        (rows - BORDER, BORDER, span_of(2, mid_rows - HALF, HALF) + span_of(1, BORDER, BORDER) + span_of(3, 0, HALF)),
    ]
    for low, high, lines, line_of, batches in (
        (low_mid, high_mid, mid_cols, inner, middle_batches),
        (low_out, high_out, both, outer_col, outer_batches),
    ):
        (result,) = steer(
            dip_inline, [(low, False), (border_second, True), (middle_second, True), (high, False)], 0, lines, line_of,
            windows, outer_place, batches=batches, before=result,
        )
    return result


def on_device(traces, destination, bin_index, dip_inline, dip_cross):
    held, block_rows, _ = traces.shape
    devices = lax.axis_size("inline") * lax.axis_size("crosslin")
    capacity = 2 * held // devices
    mine = lax.axis_index("inline") * lax.axis_size("crosslin") + lax.axis_index("crosslin")
    outgoing = pack(traces, mine.astype(I32).reshape(1), destination.reshape(-1), bin_index.T, devices, capacity)
    arrived = lax.all_to_all(outgoing, BOTH, split_axis=0, concat_axis=0, tiled=True)
    return smooth(arrived, capacity, block_rows, dip_inline, dip_cross)


def solution(mesh):
    return jax.shard_map(
        on_device,
        mesh=mesh,
        in_specs=(
            P(BOTH, None, None),
            P(BOTH, None),
            P(BOTH, None),
            P("inline", "crosslin"),
            P("inline", "crosslin"),
        ),
        out_specs=P("inline", "crosslin", None),
        check_vma=False,
    )
```
